32 devices in a mesh: gx: 4 (over z), gy: 4 (over x, core), gz: 2 (over y).
Axes of the slice: x: 2, y: 2, z: 4, core: 2. Of those that a mesh axis runs over, the one named last changes fastest.
Arguments:
- phase_mask: int32 [64, 128, 256], P('gx', 'gy', 'gz'), may hold values from 0 to 2
- pressure: float32 [64, 128, 256], P('gx', 'gy', 'gz'), may hold values from -6 to 6
- velocity_cot: float32 [3, 64, 128, 256], P(None, 'gx', 'gy', 'gz'), may hold values from -30 to 30
Outputs:
- ustar_cot: float32 [3, 64, 128, 256], P(None, 'gx', 'gy', 'gz')
- coef_cot: float32 [64, 128, 256], P('gx', 'gy', 'gz')
The draws below stay inside these ranges and needn't reach their ends.
Inputs may be any that keep to these rules, and one draw needn't show every extreme that they name: `phase_mask`: 0 air, 1 water, 2 interface band.
All inputs are finite; a program needn't handle non-finite values.
Results may differ from the reference program's by a relative error of at most 0.0001.
Values sent between devices are 32-bit elements; how exact they have to be, the bound alone decides.
No kernel may reach another device: no remote copies, remote signals or barrier semaphores. Data moves between devices by JAX's collectives and lax.ppermute only.
A program may use at most 64 MiB of HBM per device.

```python
import math
import jax
import jax.numpy as jnp
from jax import lax

ITERS = 3
NX = 64
NY = 128
NZ = 256


def draw_velocity_cot(key, part):
    shape = (3, NX, NY, NZ)
    frac_x = lax.broadcasted_iota(jnp.float32, shape, 1) / NX
    frac_y = lax.broadcasted_iota(jnp.float32, shape, 2) / NY
    frac_z = lax.broadcasted_iota(jnp.float32, shape, 3) / NZ
    scale = jnp.exp(math.log(3.0) * (frac_x + frac_y + frac_z - 1.5))
    base = jnp.clip(jax.random.normal(key, shape, jnp.float32), -5.0, 5.0)
    return (base * scale).astype(jnp.float32)


def touch_ends(values, key, low, top_value):
    spot = [jax.random.randint(jax.random.fold_in(key, axis), (), 0, length) for axis, length in enumerate(values.shape)]
    widest = values.shape.index(max(values.shape))
    beside = spot[:widest] + [(spot[widest] + 1) % values.shape[widest]] + spot[widest + 1:]
    return values.at[tuple(spot)].set(low).at[tuple(beside)].set(top_value)


def block_levels(own_key, shape, pieces, smallest, high):
    def one(position, parts):
        draws = jax.random.uniform(jax.random.fold_in(jax.random.fold_in(own_key, 6), position), (parts,), jnp.float32, smallest / len(pieces), high / len(pieces))
        return jnp.repeat(jnp.exp(draws), shape[position] // parts).reshape((-1,) + (1,) * (len(shape) - position - 1))

    level = one(*pieces[0])
    for cut in pieces[1:]:
        level = level * one(*cut)
    return level


def gaussian(own_key, shape, scale, limit, split=(), held_as=jnp.bfloat16):
    values = scale * jax.random.normal(own_key, shape, jnp.float32)
    if split:
        values = values * block_levels(own_key, shape, split, -0.22, 0.18)
    return jnp.clip(values, -limit, limit).astype(held_as)


def setup_inputs(seed: int = 0) -> dict:
    arg_keys = jax.random.split(jax.random.key(seed), 4)
    phase_mask = touch_ends(jax.random.randint(arg_keys[0], (NX, NY, NZ), 0, 3), jax.random.fold_in(arg_keys[0], 1), 0, 2).astype(jnp.int32)
    pressure = gaussian(arg_keys[1], (NX, NY, NZ), 1.0, 6.0, ((0, 4), (1, 4), (2, 2)), jnp.float32)
    velocity_cot = draw_velocity_cot(jax.random.fold_in(arg_keys[3], 71), 0)
    return dict(phase_mask=phase_mask, pressure=pressure, velocity_cot=velocity_cot)


def coefficient(phase_mask):
    return jnp.where(phase_mask == 0, 8.0, jnp.where(phase_mask == 1, 1.0, 2.0)).astype(jnp.float32)


def face_pair(padded, dim_idx):
    count = padded.shape[dim_idx]
    lower = lax.slice_in_dim(padded, 0, count - 1, axis=dim_idx)
    upper = lax.slice_in_dim(padded, 1, count, axis=dim_idx)
    for other in range(3):
        if other != dim_idx:
            width = padded.shape[other]
            lower = lax.slice_in_dim(lower, 1, width - 1, axis=other)
            upper = lax.slice_in_dim(upper, 1, width - 1, axis=other)
    return upper, lower


def face_grads(padded):
    result = []
    for dim_idx in range(3):
        upper, lower = face_pair(padded, dim_idx)
        result.append(upper - lower)
    return tuple(result)


def face_weights(coef_padded):
    result = []
    for dim_idx in range(3):
        upper, lower = face_pair(coef_padded, dim_idx)
        result.append(0.5 * (upper + lower))
    return tuple(result)


def diverge(fluxes):
    total = None
    for dim_idx in range(3):
        flux = fluxes[dim_idx]
        count = flux.shape[dim_idx]
        term = lax.slice_in_dim(flux, 0, count - 1, axis=dim_idx) - lax.slice_in_dim(flux, 1, count, axis=dim_idx)
        total = term if total is None else total + term
    return total


def spread(fluxes):
    total = None
    for dim_idx in range(3):
        flux = fluxes[dim_idx]
        count = flux.shape[dim_idx]
        term = lax.slice_in_dim(flux, 0, count - 1, axis=dim_idx) + lax.slice_in_dim(flux, 1, count, axis=dim_idx)
        total = term if total is None else total + term
    return total


def operate(padded, weights):
    grads = face_grads(padded)
    return diverge(tuple(weights[dim_idx] * grads[dim_idx] for dim_idx in range(3)))


def prepare(coef_padded, press_padded, vel_padded):
    weights = face_weights(coef_padded)
    precond = 1.0 / spread(weights)
    vel_faces = tuple(face_pair(vel_padded[dim_idx], dim_idx)[1] for dim_idx in range(3))
    rhs = -diverge(tuple(weights[dim_idx] * vel_faces[dim_idx] for dim_idx in range(3)))
    press_grads = face_grads(press_padded)
    return weights, precond, rhs, press_grads, vel_faces


def finish(lam_padded, velocity_cot, press_grads, vel_faces):
    lam_grads = face_grads(lam_padded)
    columns = []
    for dim_idx in range(3):
        count = lam_grads[dim_idx].shape[dim_idx]
        columns.append(velocity_cot[dim_idx] + lax.slice_in_dim(lam_grads[dim_idx], 1, count, axis=dim_idx))
    ustar_cot = jnp.stack(columns, 0)
    wbar = tuple(-press_grads[dim_idx] * (vel_faces[dim_idx] + lam_grads[dim_idx]) for dim_idx in range(3))
    coef_cot = 0.5 * spread(wbar)
    return ustar_cot, coef_cot


def pad_cells(field):
    return jnp.pad(field, ((1, 1), (1, 1), (1, 1)))


def reference(phase_mask, pressure, velocity_cot):
    stacked = jnp.concatenate([coefficient(phase_mask)[None], pressure[None], velocity_cot], 0)
    padded = jnp.pad(stacked, ((0, 0), (1, 1), (1, 1), (1, 1)))
    weights, precond, rhs, press_grads, vel_faces = prepare(padded[0], padded[1], padded[2:])
    solution = jnp.zeros_like(rhs)
    resid = rhs
    precd = precond * resid
    direction = precd
    rz_now = jnp.sum(resid * precd)
    for iteration in range(ITERS):
        image = operate(pad_cells(direction), weights)
        step_len = rz_now / jnp.sum(direction * image)
        solution = solution + step_len * direction
        resid = resid - step_len * image
        if iteration + 1 < ITERS:
            precd = precond * resid
            rz_next = jnp.sum(resid * precd)
            direction = precd + (rz_next / rz_now) * direction
            rz_now = rz_next
    return finish(pad_cells(solution), velocity_cot, press_grads, vel_faces)
```

```python
import functools

import jax
import jax.numpy as jnp
from jax import lax
from jax.experimental import pallas as pl
from jax.experimental.pallas import tpu as pltpu
from jax.sharding import PartitionSpec as P

AXES = ("gx", "gy", "gz")
DEPTH = 4
GROUP = 4 * DEPTH
LANES = 128
ROWS = 8
VMEM = pl.BlockSpec(memory_space=pltpu.VMEM)
SMEM = pl.BlockSpec(memory_space=pltpu.SMEM)
ANY = pl.BlockSpec(memory_space=pl.ANY)
PARAMS = pltpu.CompilerParams(vmem_limit_bytes=48 * 1024 * 1024)


def swaps(count, first):
    pairs = []
    for i in range(first, count - 1, 2):
        pairs += [(i, i + 1), (i + 1, i)]
    return pairs


def exchange(sends, axis):
    count = lax.axis_size(axis)
    return [lax.ppermute(send, axis, swaps(count, turn)) for turn, send in enumerate(sends)]


def turns(axis):
    return min(2, lax.axis_size(axis) - 1)


def coefficient(phase):
    return jnp.where(phase == 0, 8.0, jnp.where(phase == 1, 1.0, 2.0)).astype(jnp.float32)


def sides(even, got, load):
    one = load(got[0])
    two = load(got[1]) if len(got) > 1 else jnp.zeros_like(one)
    return jnp.where(even, two, one), jnp.where(even, one, two)


def lane_index(shape):
    return lax.broadcasted_iota(jnp.int32, shape, len(shape) - 1)


def row_index(shape):
    return lax.broadcasted_iota(jnp.int32, shape, len(shape) - 2)


def roll_rows(plane, shift):
    return pltpu.roll(plane, shift % plane.shape[0], 0)


def roll_lanes(plane, shift):
    return pltpu.roll(plane, shift % plane.shape[1], 1)


def pack_x(nx, parity, phase, press, vel, *refs):
    count = (len(refs) - 2) // 1
    outs, held, sem = refs[:count], refs[count], refs[count + 1]
    copies = []
    for turn, out in enumerate(outs):
        top = parity[0] == turn
        deep = jnp.where(top, nx - DEPTH, 0)
        less = jnp.where(top, nx - DEPTH + 1, 0)
        last = jnp.where(top, nx - 1, 0)
        parts = [
            (phase.at[pl.ds(deep, DEPTH)], held.at[turn]),
            (vel.at[0, pl.ds(deep, DEPTH)], out.at[pl.ds(DEPTH, DEPTH)]),
            (vel.at[1, pl.ds(less, DEPTH - 1)], out.at[pl.ds(2 * DEPTH, DEPTH - 1)]),
            (vel.at[2, pl.ds(less, DEPTH - 1)], out.at[pl.ds(3 * DEPTH - 1, DEPTH - 1)]),
            (press.at[pl.ds(last, 1)], out.at[pl.ds(4 * DEPTH - 2, 1)]),
        ]
        for which, (src, dst) in enumerate(parts):
            copy = pltpu.make_async_copy(src, dst, sem.at[turn, which])
            copy.start()
            copies.append(copy)
    for copy in copies:
        copy.wait()
    for turn, out in enumerate(outs):
        out[:DEPTH] = coefficient(held[turn])


def halo_planes(nx, even_x, got_x, row, height):
    def load(field, plane):
        above = plane < nx + DEPTH
        layer = plane - nx if above else plane - nx - DEPTH
        if field >= 2:
            layer = layer if above else layer - 1
            if layer < 0 or layer >= DEPTH - 1:
                return jnp.zeros((height, LANES), jnp.float32)
        base = (0, DEPTH, 2 * DEPTH, 3 * DEPTH - 1)[field]
        low, high = sides(even_x, got_x, lambda ref: ref[base + layer, pl.ds(row, height), :])
        return high if above else low

    return load


def pack_y(nx, ny, n_x, parity, phase, press, vel, *refs):
    got_x, outs = refs[:n_x], refs[n_x:]
    even_x = parity[0] == 0
    rows = row_index((ROWS, LANES))
    for turn, out in enumerate(outs):
        top = parity[1] == turn
        row = pl.multiple_of(jnp.where(top, ny - ROWS, 0), ROWS)
        halo = halo_planes(nx, even_x, got_x, row, ROWS)
        for plane in range(nx + 2 * DEPTH):
            if plane < nx:
                fields = [coefficient(phase[plane, pl.ds(row, ROWS), :])]
                fields += [vel[k, plane, pl.ds(row, ROWS), :] for k in range(3)]
            else:
                fields = [halo(f, plane) for f in range(4)]
            for half in range(2):
                one, two = fields[2 * half], fields[2 * half + 1]
                one = jnp.where(top, roll_rows(one, DEPTH), one)
                two = jnp.where(top, two, roll_rows(two, DEPTH))
                out[plane, half * ROWS : (half + 1) * ROWS, :] = jnp.where(rows < DEPTH, one, two)
        for plane in range(nx):
            tile = press[plane, pl.ds(row, ROWS), :]
            edge = jnp.where(top, tile[ROWS - 1 : ROWS], tile[0:1])
            at = nx + 2 * DEPTH + plane // GROUP
            out[at, plane % GROUP : plane % GROUP + 1, :] = edge


def pack_z(nx, ny, n_x, n_y, n_z, parity, phase, press, vel, *refs):
    got_x, got_y = refs[:n_x], refs[n_x : n_x + n_y]
    full, ends, *sends = refs[n_x + n_y :]
    even_x, even_y = parity[0] == 0, parity[1] == 0
    total, height = nx + 2 * DEPTH, ny + 2 * DEPTH
    groups = total // ROWS
    rows = row_index((ROWS, LANES))
    lanes = lane_index((height, LANES))
    halo = halo_planes(nx, even_x, got_x, 0, ny)
    for group in range(groups):
        tops = bottoms = jnp.zeros((height, LANES), jnp.float32)
        for seat in range(ROWS):
            plane = seat * groups + group
            for f in range(4):
                if plane >= nx:
                    own = halo(f, plane)
                elif f == 0:
                    own = coefficient(phase[plane])
                else:
                    own = vel[f - 1, plane]
                half = slice(f // 2 * ROWS, f // 2 * ROWS + ROWS)
                low, high = sides(even_y, got_y, lambda ref: ref[plane, half, :])
                if f % 2 == 0:
                    low = roll_rows(low, DEPTH)
                else:
                    high = roll_rows(high, DEPTH)
                cells = jnp.concatenate([own, jnp.where(rows < DEPTH, high, low)], 0)
                full[f, plane] = cells
                at = GROUP * seat + DEPTH * f
                here = (lanes >= at) & (lanes < at + DEPTH)
                tops = jnp.where(here, roll_lanes(cells, at + DEPTH), tops)
                bottoms = jnp.where(here, roll_lanes(cells, at), bottoms)
        ends[0, group] = tops
        ends[1, group] = bottoms
    tops = bottoms = jnp.zeros((ny, LANES), jnp.float32)
    lanes = lane_index((ny, LANES))
    for plane in range(nx):
        here = lanes == 2 * plane
        tops = jnp.where(here, roll_lanes(press[plane], 2 * plane + 1), tops)
        bottoms = jnp.where(here, roll_lanes(press[plane], 2 * plane), bottoms)
    pad = jnp.zeros((2 * DEPTH, LANES), jnp.float32)
    for turn, send in enumerate(sends):
        top = parity[2] == turn
        send[:groups] = jnp.where(top, ends[0], ends[1])
        send[groups] = jnp.concatenate([jnp.where(top, tops, bottoms), pad], 0)


def tree_sum(parts):
    while len(parts) > 1:
        parts = [parts[i] + parts[i + 1] if i + 1 < len(parts) else parts[i] for i in range(0, len(parts), 2)]
    return parts[0]


class Totals:
    def __init__(self):
        self.stack = []

    def add(self, tile):
        level = 0
        while self.stack and self.stack[-1][0] == level:
            tile = self.stack.pop()[1] + tile
            level += 1
        self.stack.append((level, tile))

    def value(self):
        tiles = [tile for _, tile in self.stack]
        total = tiles.pop()
        while tiles:
            total = tiles.pop() + total
        return total


def krylov(nx, ny, n_z, parity, full, ends, *refs):
    got_z = refs[:n_z]
    basis, basis_z, sums = refs[n_z : n_z + 3]
    wx, wy, wz, inverse, pw, pinv, pv, spill = refs[n_z + 3 :]
    even_z = parity[2] == 0
    total, height = nx + 2 * DEPTH, ny + 2 * DEPTH
    groups = total // ROWS
    lanes = lane_index((height, LANES))
    seat_lane = lanes % GROUP
    at_low, at_high = lanes == 0, lanes == LANES - 1
    edge = at_low | at_high

    def px(planes, group, step):
        if 0 <= group + step < groups:
            return planes[group + step]
        return roll_lanes(planes[(group + step) % groups], -GROUP * step)

    def spilled(which, group, up, down):
        spill[which, group] = jnp.where(seat_lane == 10, roll_lanes(up, 7), down)

    packed = []
    for f in range(4):
        planes = []
        for group in range(groups):
            low, high = sides(even_z, got_z, lambda ref: ref[group])
            parts = (ends[0, group], high, low, ends[1, group])
            cells = parts[3]
            cells = roll_lanes(cells, 3 * DEPTH - DEPTH * f)
            for seat in range(3):
                moved = roll_lanes(parts[seat], DEPTH * (seat - f))
                here = (seat_lane >= DEPTH * seat) & (seat_lane < DEPTH * (seat + 1))
                cells = jnp.where(here, moved, cells)
            planes.append(cells)
        packed.append(planes)
    coef, vx, vy, vz = packed
    for g in range(groups):
        pw[0, g] = 0.5 * (coef[g] + px(coef, g, 1))
        pw[1, g] = 0.5 * (coef[g] + roll_rows(coef[g], -1))
        pw[2, g] = 0.5 * (coef[g] + roll_lanes(coef[g], -1))
    flux = [pw[0, g] * vx[g] for g in range(groups)]
    weight = [pw[0, g] for g in range(groups)]
    for g in range(groups):
        wy_, wz_ = pw[1, g], pw[2, g]
        fy, fz = wy_ * vy[g], wz_ * vz[g]
        spilled(0, g, wz_, wz_)
        spilled(1, g, fz, -fz)
        diag = weight[g] + px(weight, g, -1) + wy_ + roll_rows(wy_, 1) + wz_ + roll_lanes(wz_, 1)
        rhs = flux[g] - px(flux, g, -1) + fy - roll_rows(fy, 1) + fz - roll_lanes(fz, 1)
        scale = jnp.where(coef[g] > 0, 1.0 / jnp.where(coef[g] > 0, diag, 1.0), 0.0)
        pinv[g] = scale
        basis_z[0, g] = scale * rhs
    for n in range(3):
        field = [basis_z[n, g] for g in range(groups)]
        flux = [pw[0, g] * (px(field, g, 1) - field[g]) for g in range(groups)]
        for g in range(groups):
            fy = pw[1, g] * (roll_rows(field[g], -1) - field[g])
            fz = pw[2, g] * (roll_lanes(field[g], -1) - field[g])
            spilled(2 + n, g, -fz, fz)
            if n < 2:
                image = px(flux, g, -1) - flux[g] + roll_rows(fy, 1) - fy + roll_lanes(fz, 1) - fz
                basis_z[n + 1, g] = pinv[g] * image
    for g in range(groups):
        basis_z[3, g] = vz[g]

    def inject(which, plane):
        group, seat = plane % groups, plane // groups
        return jnp.where(edge, roll_lanes(spill[which, group], LANES - 1 - 10 - GROUP * seat), 0.0)

    totals = [Totals() for _ in range(6)]

    def count(which, left, right):
        product = left[:ny] * right[:ny]
        totals[which].add(tree_sum([product[i : i + ROWS] for i in range(0, ny, ROWS)]))

    old_weight = old_flux = None
    for x in range(-DEPTH, nx + DEPTH - 1):
        e = x % total
        here, above = full[0, e], full[0, (e + 1) % total]
        weight = 0.5 * (here + above)
        wx[e] = weight
        flux = weight * full[1, e]
        if x > -DEPTH:
            wy_ = 0.5 * (here + roll_rows(here, -1))
            wz_ = jnp.where(at_high, 0.0, 0.5 * (here + roll_lanes(here, -1)))
            wy[e], wz[e] = wy_, wz_
            fy, fz = wy_ * full[2, e], wz_ * full[3, e]
            diag = weight + old_weight + wy_ + roll_rows(wy_, 1) + wz_ + roll_lanes(wz_, 1) + inject(0, e)
            rhs = flux - old_flux + fy - roll_rows(fy, 1) + fz - roll_lanes(fz, 1) + inject(1, e)
            inside = here > 0
            scale = jnp.where(inside, 1.0 / jnp.where(inside, diag, 1.0), 0.0)
            inverse[e] = scale
            field = scale * rhs
            basis[0, e] = field
            if 0 <= x < nx:
                count(0, field, rhs)
        old_weight, old_flux = weight, flux
    for n in range(3):
        reach = 2 - n
        old_flux = None
        here = basis[n, (-reach - 1) % total]
        for x in range(-reach - 1, nx + reach):
            e = x % total
            above = basis[n, (e + 1) % total]
            flux = wx[e] * (above - here)
            if x >= -reach:
                fy = wy[e] * (roll_rows(here, -1) - here)
                fz = wz[e] * (roll_lanes(here, -1) - here)
                image = old_flux - flux + roll_rows(fy, 1) - fy + roll_lanes(fz, 1) - fz + inject(2 + n, e)
                own = 0 <= x < nx
                if own:
                    count(2 * n + 1, here, image)
                if n < 2:
                    following = inverse[e] * image
                    basis[n + 1, e] = following
                    if own:
                        count(2 * n + 2, following, image)
            old_flux, here = flux, above
    lane = lane_index((1, LANES))
    row = jnp.zeros((1, LANES), jnp.float32)
    for which, total_ in enumerate(totals):
        value = jnp.sum(jnp.sum(total_.value(), 0, keepdims=True), 1, keepdims=True)
        row = jnp.where(lane == which, value, row)
    sums[...] = row


def finish(nx, ny, n_x, n_y, n_z, parity, gathered, press, vel, basis, basis_z, *refs):
    got_x, got_y, got_z = refs[:n_x], refs[n_x : n_x + n_y], refs[n_x + n_y : n_x + n_y + n_z]
    ustar, coef_cot = refs[n_x + n_y + n_z :]
    even_x, even_y, even_z = parity[0] == 0, parity[1] == 0, parity[2] == 0
    total, height = nx + 2 * DEPTH, ny + 2 * DEPTH
    groups = total // ROWS
    parts = gathered[...]
    while parts.shape[0] > ROWS:
        half = parts.shape[0] // 2
        parts = parts[:half] + parts[half:]
    sums = jnp.sum(parts, 0, keepdims=True)
    lane = lane_index((1, LANES))
    m0, m1, m2, m3, m4, m5 = [
        jnp.sum(jnp.where(lane == which, sums, 0.0), 1, keepdims=True) for which in range(6)
    ]
    l1, l2 = m2 / m1, m3 / m1
    d1, cross, d2 = m3 - l1 * m2, m4 - l1 * m3, m5 - l2 * m3
    l21 = cross / d1
    d2 = d2 - l21 * cross
    y1 = -l1 * m0 + m1
    y2 = m2 - l2 * m0 - l21 * y1
    c2 = y2 / d2
    c1 = y1 / d1 - l21 * c2
    c0 = m0 / m1 - l1 * c1 - l2 * c2

    lanes = lane_index((height, LANES))
    seat_lane = lanes % GROUP
    spill = []
    for g in range(groups):
        cells = c0 * basis_z[0, g] + c1 * basis_z[1, g] + c2 * basis_z[2, g]
        spill.append(jnp.where(seat_lane == 10, roll_lanes(cells, 6), cells))
    lanes = lane_index((ny, LANES))
    at_low, at_high = lanes == 0, lanes == LANES - 1
    low_z, high_z = sides(even_z, got_z, lambda ref: ref[groups, :ny, :])
    press_z = jnp.where(lanes % 2 == 0, high_z, roll_lanes(low_z, 1))
    p_base, layer = 4 * DEPTH - 2, 2 * DEPTH - 1
    p_low, p_high = sides(even_x, got_x, lambda ref: ref[p_base])
    u_low, _ = sides(even_x, got_x, lambda ref: ref[layer])

    def solved(x):
        e = x % total
        return c0 * basis[0, e] + c1 * basis[1, e] + c2 * basis[2, e]

    rows = row_index((ROWS, LANES))
    below, here = solved(-1), solved(0)
    face_low = (p_low - press[0]) * (u_low + here[:ny] - below[:ny])
    for x in range(nx):
        above = solved(x + 1)
        group, seat = x % groups, x // groups
        own, p = here[:ny], press[x]
        out = vel[0, x] + (above[:ny] - own)
        ustar[0, x] = out
        face = (p - (press[x + 1] if x + 1 < nx else p_high)) * out
        answer = face_low + face
        face_low = face
        low, high = sides(even_y, got_y, lambda ref: ref[nx + 2 * DEPTH + x // GROUP, x % GROUP : x % GROUP + 1, :])
        shape = (ROWS, LANES)
        p_tile = jnp.where(rows == 0, jnp.broadcast_to(high, shape), jnp.broadcast_to(low, shape))
        p_tall = jnp.concatenate([p, p_tile], 0)
        u_row, _ = sides(even_y, got_y, lambda ref: ref[x, 3 * DEPTH - 1 : 3 * DEPTH, :])
        u_tall = jnp.concatenate([vel[1, x], jnp.broadcast_to(u_row, shape)], 0)
        out = u_tall + (roll_rows(here, -1) - here)
        ustar[1, x] = out[:ny]
        face = (p_tall - roll_rows(p_tall, -1)) * out
        answer = answer + (face + roll_rows(face, 1))[:ny]
        shift = LANES - 1 - 10 - GROUP * seat
        lam_end = roll_lanes(spill[group][:ny], shift)
        u_end = roll_lanes(basis_z[3, group, :ny, :], shift)
        p_end = roll_lanes(press_z, LANES - 1 - 2 * x)
        out = vel[2, x] + (jnp.where(at_high, lam_end, roll_lanes(own, -1)) - own)
        ustar[2, x] = out
        face = (p - jnp.where(at_high, p_end, roll_lanes(p, -1))) * out
        first = (p_end - p) * (u_end + own - lam_end)
        answer = answer + face + jnp.where(at_low, first, roll_lanes(face, 1))
        coef_cot[x] = 0.5 * answer
        here = above


def on_device(phase, press, vel):
    nx, ny, nz = phase.shape
    total, height = nx + 2 * DEPTH, ny + 2 * DEPTH
    groups = total // ROWS
    devices = lax.axis_size(AXES)
    n_x, n_y, n_z = (turns(axis) for axis in AXES)
    f32 = lambda *shape: jax.ShapeDtypeStruct(shape, jnp.float32)
    parity = jnp.stack([lax.axis_index(axis) % 2 for axis in AXES]).astype(jnp.int32)
    scratch = lambda *shape: pltpu.VMEM(shape, jnp.float32)

    send = pl.pallas_call(
        functools.partial(pack_x, nx),
        out_shape=[f32(4 * DEPTH - 1, ny, nz)] * n_x,
        in_specs=[SMEM, ANY, ANY, ANY],
        out_specs=[VMEM] * n_x,
        scratch_shapes=[pltpu.VMEM((n_x, DEPTH, ny, nz), jnp.int32), pltpu.SemaphoreType.DMA((n_x, 5))],
        compiler_params=PARAMS,
        name="pack_x",
    )(parity, phase, press, vel)
    got_x = exchange(send, "gx")
    send = pl.pallas_call(
        functools.partial(pack_y, nx, ny, n_x),
        out_shape=[f32(total + -(-nx // GROUP), GROUP, nz)] * n_y,
        in_specs=[SMEM] + [VMEM] * (3 + n_x),
        out_specs=[VMEM] * n_y,
        compiler_params=PARAMS,
        name="pack_y",
    )(parity, phase, press, vel, *got_x)
    got_y = exchange(send, "gy")
    full, ends, *send = pl.pallas_call(
        functools.partial(pack_z, nx, ny, n_x, n_y, n_z),
        out_shape=[f32(4, total, height, nz), f32(2, groups, height, LANES)] + [f32(groups + 1, height, LANES)] * n_z,
        in_specs=[SMEM] + [VMEM] * (3 + n_x + n_y),
        out_specs=[VMEM] * (2 + n_z),
        compiler_params=PARAMS,
        name="pack_z",
    )(parity, phase, press, vel, *got_x, *got_y)
    got_z = exchange(send, "gz")
    basis, basis_z, sums = pl.pallas_call(
        functools.partial(krylov, nx, ny, n_z),
        out_shape=[f32(3, total, height, nz), f32(4, groups, height, LANES), f32(1, LANES)],
        in_specs=[SMEM] + [VMEM] * (2 + n_z),
        out_specs=[VMEM] * 3,
        scratch_shapes=[scratch(total, height, nz)] * 4
        + [scratch(3, groups, height, LANES), scratch(groups, height, LANES), scratch(groups, height, LANES)]
        + [scratch(5, groups, height, LANES)],
        compiler_params=PARAMS,
        name="krylov",
    )(parity, full, ends, *got_z)
    spread = jnp.broadcast_to(sums[None], (devices, 1, LANES))
    gathered = lax.all_to_all(spread, AXES, 0, 0).reshape(devices, LANES)
    return pl.pallas_call(
        functools.partial(finish, nx, ny, n_x, n_y, n_z),
        out_shape=[f32(*vel.shape), f32(nx, ny, nz)],
        in_specs=[SMEM] + [VMEM] * (5 + n_x + n_y + n_z),
        out_specs=[VMEM] * 2,
        compiler_params=PARAMS,
        name="finish",
    )(parity, gathered, press, vel, basis, basis_z, *got_x, *got_y, *got_z)


def solution(mesh):
    cells, faces = P(*AXES), P(None, *AXES)
    return jax.shard_map(
        on_device, mesh=mesh, in_specs=(cells, cells, faces), out_specs=(faces, cells), check_vma=False
    )
```

```python
import functools

import jax
import jax.numpy as jnp
from jax import lax
from jax.experimental import pallas as pl
from jax.experimental.pallas import tpu as pltpu
from jax.sharding import PartitionSpec as P

AXES = ("gx", "gy", "gz")
DEPTH = 4
GROUP = 4 * DEPTH
LANES = 128
ROWS = 8
VMEM = pl.BlockSpec(memory_space=pltpu.VMEM)
SMEM = pl.BlockSpec(memory_space=pltpu.SMEM)
HBM = pl.BlockSpec(memory_space=pltpu.HBM)
ANY = pl.BlockSpec(memory_space=pl.ANY)
PARAMS = pltpu.CompilerParams(vmem_limit_bytes=40 * 1024 * 1024)


def swaps(count, first):
    pairs = []
    for i in range(first, count - 1, 2):
        pairs += [(i, i + 1), (i + 1, i)]
    return pairs


def exchange(sends, axis):
    count = lax.axis_size(axis)
    return [lax.ppermute(send, axis, swaps(count, turn)) for turn, send in enumerate(sends)]


def turns(axis):
    return min(2, lax.axis_size(axis) - 1)


def coefficient(phase):
    return jnp.where(phase == 0, 8.0, jnp.where(phase == 1, 1.0, 2.0)).astype(jnp.float32)


def sides(even, got, load):
    one = load(got[0])
    two = load(got[1]) if len(got) > 1 else jnp.zeros_like(one)
    return jnp.where(even, two, one), jnp.where(even, one, two)


def lane_index(shape):
    return lax.broadcasted_iota(jnp.int32, shape, len(shape) - 1)


def row_index(shape):
    return lax.broadcasted_iota(jnp.int32, shape, len(shape) - 2)


def roll_rows(plane, shift):
    return pltpu.roll(plane, shift % plane.shape[0], 0)


def roll_lanes(plane, shift):
    return pltpu.roll(plane, shift % plane.shape[1], 1)


def pack_x(nx, parity, phase, press, vel, *refs):
    count = (len(refs) - 2) // 1
    outs, held, sem = refs[:count], refs[count], refs[count + 1]
    copies = []
    for turn, out in enumerate(outs):
        top = parity[0] == turn
        deep = jnp.where(top, nx - DEPTH, 0)
        less = jnp.where(top, nx - DEPTH + 1, 0)
        last = jnp.where(top, nx - 1, 0)
        parts = [
            (phase.at[pl.ds(deep, DEPTH)], held.at[turn]),
            (vel.at[0, pl.ds(deep, DEPTH)], out.at[pl.ds(DEPTH, DEPTH)]),
            (vel.at[1, pl.ds(less, DEPTH - 1)], out.at[pl.ds(2 * DEPTH, DEPTH - 1)]),
            (vel.at[2, pl.ds(less, DEPTH - 1)], out.at[pl.ds(3 * DEPTH - 1, DEPTH - 1)]),
            (press.at[pl.ds(last, 1)], out.at[pl.ds(4 * DEPTH - 2, 1)]),
        ]
        for which, (src, dst) in enumerate(parts):
            copy = pltpu.make_async_copy(src, dst, sem.at[turn, which])
            copy.start()
            copies.append(copy)
    for copy in copies:
        copy.wait()
    for turn, out in enumerate(outs):
        out[:DEPTH] = coefficient(held[turn])


def load(phase, press, vel, after, coef, press_out, vel_out, held, sem):
    del after
    copies = []
    for which, (src, dst) in enumerate(((phase, held), (press, press_out), (vel, vel_out))):
        copies.append(pltpu.make_async_copy(src, dst, sem.at[which]))
        copies[-1].start()
    copies[0].wait()
    for plane in range(coef.shape[0]):
        coef[plane] = coefficient(held[plane])
    copies[1].wait()
    copies[2].wait()


def halo_planes(nx, even_x, got_x, row, height):
    def load(field, plane):
        above = plane < nx + DEPTH
        layer = plane - nx if above else plane - nx - DEPTH
        if field >= 2:
            layer = layer if above else layer - 1
            if layer < 0 or layer >= DEPTH - 1:
                return jnp.zeros((height, LANES), jnp.float32)
        base = (0, DEPTH, 2 * DEPTH, 3 * DEPTH - 1)[field]
        low, high = sides(even_x, got_x, lambda ref: ref[base + layer, pl.ds(row, height), :])
        return high if above else low

    return load


def pack_y(nx, ny, n_x, parity, coef, press, vel, *refs):
    got_x, outs = refs[:n_x], refs[n_x:]
    even_x = parity[0] == 0
    rows = row_index((ROWS, LANES))
    for turn, out in enumerate(outs):
        top = parity[1] == turn
        row = pl.multiple_of(jnp.where(top, ny - ROWS, 0), ROWS)
        halo = halo_planes(nx, even_x, got_x, row, ROWS)
        for plane in range(nx + 2 * DEPTH):
            if plane < nx:
                fields = [coef[plane, pl.ds(row, ROWS), :]]
                fields += [vel[k, plane, pl.ds(row, ROWS), :] for k in range(3)]
            else:
                fields = [halo(f, plane) for f in range(4)]
            for half in range(2):
                one, two = fields[2 * half], fields[2 * half + 1]
                one = jnp.where(top, roll_rows(one, DEPTH), one)
                two = jnp.where(top, two, roll_rows(two, DEPTH))
                out[plane, half * ROWS : (half + 1) * ROWS, :] = jnp.where(rows < DEPTH, one, two)
        for plane in range(nx):
            tile = press[plane, pl.ds(row, ROWS), :]
            edge = jnp.where(top, tile[ROWS - 1 : ROWS], tile[0:1])
            at = nx + 2 * DEPTH + plane // GROUP
            out[at, plane % GROUP : plane % GROUP + 1, :] = edge


def tall_planes(nx, ny, parity, coef, vel, got_x, got_y):
    even_x, even_y = parity[0] == 0, parity[1] == 0
    rows = row_index((ROWS, LANES))
    halo = halo_planes(nx, even_x, got_x, 0, ny)

    def cells(field, plane):
        if plane >= nx:
            own = halo(field, plane)
        elif field == 0:
            own = coef[plane]
        else:
            own = vel[field - 1, plane]
        half = slice(field // 2 * ROWS, field // 2 * ROWS + ROWS)
        low, high = sides(even_y, got_y, lambda ref: ref[plane, half, :])
        if field % 2 == 0:
            low = roll_rows(low, DEPTH)
        else:
            high = roll_rows(high, DEPTH)
        return jnp.concatenate([own, jnp.where(rows < DEPTH, high, low)], 0)

    return cells


def pack_z(nx, ny, n_x, n_y, parity, coef, press, vel, *refs):
    got_x, got_y, sends = refs[:n_x], refs[n_x : n_x + n_y], refs[n_x + n_y :]
    groups = (nx + 2 * DEPTH) // ROWS
    lanes = lane_index((ny + 2 * DEPTH, LANES))
    cells = tall_planes(nx, ny, parity, coef, vel, got_x, got_y)
    low_lanes = lane_index((ny, LANES))
    pad = jnp.zeros((2 * DEPTH, LANES), jnp.float32)
    for turn, send in enumerate(sends):
        top = parity[2] == turn
        for group in range(groups):
            parts = jnp.zeros((ny + 2 * DEPTH, LANES), jnp.float32)
            for seat in range(ROWS):
                for f in range(4):
                    at = GROUP * seat + DEPTH * f
                    here = (lanes >= at) & (lanes < at + DEPTH)
                    shift = jnp.where(top, (at + DEPTH) % LANES, at)
                    parts = jnp.where(here, pltpu.roll(cells(f, seat * groups + group), shift, 1), parts)
            send[group] = parts
        parts = jnp.zeros((ny, LANES), jnp.float32)
        for plane in range(nx):
            shift = jnp.where(top, 2 * plane + 1, 2 * plane)
            parts = jnp.where(low_lanes == 2 * plane, pltpu.roll(press[plane], shift, 1), parts)
        send[groups] = jnp.concatenate([parts, pad], 0)


def prepare(nx, ny, n_x, n_y, parity, coef, vel, after, *refs):
    del after
    got_x, got_y = refs[:n_x], refs[n_x : n_x + n_y]
    wx, wy, wz, diag_out, rhs_out, ends = refs[n_x + n_y :]
    total, height = nx + 2 * DEPTH, ny + 2 * DEPTH
    groups = total // ROWS
    lanes = lane_index((height, LANES))
    cells = tall_planes(nx, ny, parity, coef, vel, got_x, got_y)
    for group in range(groups):
        tops = bottoms = jnp.zeros((height, LANES), jnp.float32)
        for seat in range(ROWS):
            for f in range(4):
                plane = cells(f, seat * groups + group)
                at = GROUP * seat + DEPTH * f
                here = (lanes >= at) & (lanes < at + DEPTH)
                tops = jnp.where(here, roll_lanes(plane, at + DEPTH), tops)
                bottoms = jnp.where(here, roll_lanes(plane, at), bottoms)
        ends[0, group] = tops
        ends[1, group] = bottoms
    old_weight = old_flux = None
    here = cells(0, nx + DEPTH)
    for x in range(-DEPTH, nx + DEPTH - 1):
        e = x % total
        above = cells(0, (e + 1) % total)
        weight = 0.5 * (here + above)
        wx[e] = weight
        flux = weight * cells(1, e)
        if x > -DEPTH:
            vy, vz = cells(2, e), cells(3, e)
            up, down = 0.5 * (here + roll_rows(here, -1)), 0.5 * (here + roll_rows(here, 1))
            right = jnp.where(lanes == LANES - 1, 0.0, 0.5 * (here + roll_lanes(here, -1)))
            left = jnp.where(lanes == 0, 0.0, 0.5 * (here + roll_lanes(here, 1)))
            wy[0, e], wy[1, e], wz[0, e], wz[1, e] = up, down, right, left
            diag = (weight + old_weight) + (up + down) + (right + left)
            diag_out[e] = jnp.where(here > 0, diag, 0.0)
            rhs_out[e] = (
                (flux - old_flux) + (up * vy - down * roll_rows(vy, 1)) + (right * vz - left * roll_lanes(vz, 1))
            )
        old_weight, old_flux, here = weight, flux, above


def tree_sum(parts):
    while len(parts) > 1:
        parts = [parts[i] + parts[i + 1] if i + 1 < len(parts) else parts[i] for i in range(0, len(parts), 2)]
    return parts[0]


class Totals:
    def __init__(self):
        self.stack = []

    def add(self, tile):
        level = 0
        while self.stack and self.stack[-1][0] == level:
            tile = self.stack.pop()[1] + tile
            level += 1
        self.stack.append((level, tile))

    def value(self):
        tiles = [tile for _, tile in self.stack]
        total = tiles.pop()
        while tiles:
            total = tiles.pop() + total
        return total


def krylov(nx, ny, n_z, parity, wx, wy, wz, diag_in, rhs_in, ends, *refs):
    got_z = refs[:n_z]
    basis, basis_z, sums = refs[n_z : n_z + 3]
    inverse, pw, pinv, spill = refs[n_z + 3 :]
    even_z = parity[2] == 0
    total, height = nx + 2 * DEPTH, ny + 2 * DEPTH
    groups = total // ROWS
    lanes = lane_index((height, LANES))
    seat_lane = lanes % GROUP
    edge = (lanes == 0) | (lanes == LANES - 1)

    def along(planes, group, step):
        if 0 <= group + step < groups:
            return planes[group + step]
        return roll_lanes(planes[(group + step) % groups], -GROUP * step)

    def spilled(which, group, up, down):
        spill[which, group] = jnp.where(seat_lane == 10, roll_lanes(up, 7), down)

    packed = []
    for f in range(4):
        planes = []
        for group in range(groups):
            low, high = sides(even_z, got_z, lambda ref: ref[group])
            parts = (ends[0, group], high, low, ends[1, group])
            plane = roll_lanes(parts[3], 3 * DEPTH - DEPTH * f)
            for seat in range(3):
                moved = roll_lanes(parts[seat], DEPTH * (seat - f))
                here = (seat_lane >= DEPTH * seat) & (seat_lane < DEPTH * (seat + 1))
                plane = jnp.where(here, moved, plane)
            planes.append(plane)
        packed.append(planes)
    coef, vx, vy, vz = packed
    for g in range(groups):
        here = coef[g]
        neighbours = (along(coef, g, 1), along(coef, g, -1), roll_rows(here, -1), roll_rows(here, 1))
        neighbours += (roll_lanes(here, -1), roll_lanes(here, 1))
        weights = [0.5 * (here + other) for other in neighbours]
        for which, weight in enumerate(weights):
            pw[which, g] = weight
        diag = (weights[0] + weights[1]) + (weights[2] + weights[3]) + (weights[4] + weights[5])
        fz = weights[4] * vz[g]
        spilled(0, g, weights[4], weights[4])
        spilled(1, g, fz, -fz)
        rhs = weights[0] * vx[g] - weights[1] * along(vx, g, -1)
        rhs = rhs + (weights[2] * vy[g] - weights[3] * roll_rows(vy[g], 1))
        rhs = rhs + (fz - weights[5] * roll_lanes(vz[g], 1))
        inside = here > 0
        scale = jnp.where(inside, 1.0 / jnp.where(inside, diag, 1.0), 0.0)
        pinv[g] = scale
        basis_z[0, g] = scale * rhs
        basis_z[3, g] = vz[g]
    for n in range(3):
        field = [basis_z[n, g] for g in range(groups)]
        for g in range(groups):
            here = field[g]
            fz = pw[4, g] * (roll_lanes(here, -1) - here)
            spilled(2 + n, g, -fz, fz)
            if n < 2:
                image = pw[0, g] * (here - along(field, g, 1)) + pw[1, g] * (here - along(field, g, -1))
                image = image + (pw[2, g] * (here - roll_rows(here, -1)) + pw[3, g] * (here - roll_rows(here, 1)))
                image = image + (pw[5, g] * (here - roll_lanes(here, 1)) - fz)
                basis_z[n + 1, g] = pinv[g] * image

    def inject(which, plane):
        group, seat = plane % groups, plane // groups
        return jnp.where(edge, roll_lanes(spill[which, group], LANES - 1 - 10 - GROUP * seat), 0.0)

    totals = [Totals() for _ in range(6)]

    def count(which, left, right):
        product = left[:ny] * right[:ny]
        totals[which].add(tree_sum([product[i : i + ROWS] for i in range(0, ny, ROWS)]))

    for x in range(-DEPTH + 1, nx + DEPTH - 1):
        e = x % total
        diag, rhs = diag_in[e], rhs_in[e] + inject(1, e)
        inside = diag > 0
        scale = jnp.where(inside, 1.0 / jnp.where(inside, diag + inject(0, e), 1.0), 0.0)
        inverse[e] = scale
        field = scale * rhs
        basis[0, e] = field
        if 0 <= x < nx:
            count(0, field, rhs)
    for n in range(3):
        reach = 2 - n
        old_flux = None
        here = basis[n, (-reach - 1) % total]
        for x in range(-reach - 1, nx + reach):
            e = x % total
            above = basis[n, (e + 1) % total]
            flux = wx[e] * (above - here)
            if x >= -reach:
                image = (old_flux - flux) + inject(2 + n, e)
                image = image + (
                    wy[0, e] * (here - roll_rows(here, -1)) + wy[1, e] * (here - roll_rows(here, 1))
                )
                image = image + (
                    wz[0, e] * (here - roll_lanes(here, -1)) + wz[1, e] * (here - roll_lanes(here, 1))
                )
                own = 0 <= x < nx
                if own:
                    count(2 * n + 1, here, image)
                if n < 2:
                    following = inverse[e] * image
                    basis[n + 1, e] = following
                    if own:
                        count(2 * n + 2, following, image)
            old_flux, here = flux, above
    lane = lane_index((1, LANES))
    row = jnp.zeros((1, LANES), jnp.float32)
    for which, total_ in enumerate(totals):
        value = jnp.sum(jnp.sum(total_.value(), 0, keepdims=True), 1, keepdims=True)
        row = jnp.where(lane == which, value, row)
    sums[...] = row


def finish(nx, ny, n_x, n_y, n_z, parity, gathered, press, vel, basis, basis_z, *refs):
    got_x, got_y, got_z = refs[:n_x], refs[n_x : n_x + n_y], refs[n_x + n_y : n_x + n_y + n_z]
    ustar, coef_cot = refs[n_x + n_y + n_z :]
    even_x, even_y, even_z = parity[0] == 0, parity[1] == 0, parity[2] == 0
    total, height = nx + 2 * DEPTH, ny + 2 * DEPTH
    groups = total // ROWS
    parts = gathered[...]
    while parts.shape[0] > ROWS:
        half = parts.shape[0] // 2
        parts = parts[:half] + parts[half:]
    sums = jnp.sum(parts, 0, keepdims=True)
    lane = lane_index((1, LANES))
    m0, m1, m2, m3, m4, m5 = [
        jnp.sum(jnp.where(lane == which, sums, 0.0), 1, keepdims=True) for which in range(6)
    ]
    l1, l2 = m2 / m1, m3 / m1
    d1, cross, d2 = m3 - l1 * m2, m4 - l1 * m3, m5 - l2 * m3
    l21 = cross / d1
    d2 = d2 - l21 * cross
    y1 = -l1 * m0 + m1
    y2 = m2 - l2 * m0 - l21 * y1
    c2 = y2 / d2
    c1 = y1 / d1 - l21 * c2
    c0 = (m0 / m1 - l1 * c1 - l2 * c2)[0, 0]
    c1, c2 = c1[0, 0], c2[0, 0]

    lanes = lane_index((height, LANES))
    seat_lane = lanes % GROUP
    spill = []
    for g in range(groups):
        cells = c0 * basis_z[0, g] + c1 * basis_z[1, g] + c2 * basis_z[2, g]
        spill.append(jnp.where(seat_lane == 10, roll_lanes(cells, 6), cells))
    lanes = lane_index((ny, LANES))
    at_low, at_high = lanes == 0, lanes == LANES - 1
    low_z, high_z = sides(even_z, got_z, lambda ref: ref[groups, :ny, :])
    press_z = jnp.where(lanes % 2 == 0, high_z, roll_lanes(low_z, 1))
    p_base, layer = 4 * DEPTH - 2, 2 * DEPTH - 1
    p_low, p_high = sides(even_x, got_x, lambda ref: ref[p_base])
    u_low, _ = sides(even_x, got_x, lambda ref: ref[layer])

    def solved(x):
        e = x % total
        return c0 * basis[0, e] + c1 * basis[1, e] + c2 * basis[2, e]

    rows = row_index((ROWS, LANES))
    below, here = solved(-1), solved(0)
    face_low = (p_low - press[0]) * (u_low + here[:ny] - below[:ny])
    for x in range(nx):
        above = solved(x + 1)
        group, seat = x % groups, x // groups
        own, p = here[:ny], press[x]
        out = vel[0, x] + (above[:ny] - own)
        ustar[0, x] = out
        face = (p - (press[x + 1] if x + 1 < nx else p_high)) * out
        answer = face_low + face
        face_low = face
        low, high = sides(even_y, got_y, lambda ref: ref[nx + 2 * DEPTH + x // GROUP, x % GROUP : x % GROUP + 1, :])
        shape = (ROWS, LANES)
        p_tile = jnp.where(rows == 0, jnp.broadcast_to(high, shape), jnp.broadcast_to(low, shape))
        p_tall = jnp.concatenate([p, p_tile], 0)
        u_row, _ = sides(even_y, got_y, lambda ref: ref[x, 3 * DEPTH - 1 : 3 * DEPTH, :])
        u_tall = jnp.concatenate([vel[1, x], jnp.broadcast_to(u_row, shape)], 0)
        out = vel[1, x] + (roll_rows(here, -1)[:ny] - own)
        ustar[1, x] = out
        back = roll_rows(u_tall, 1)[:ny] + (own - roll_rows(here, 1)[:ny])
        answer = answer + ((p - roll_rows(p_tall, -1)[:ny]) * out + (roll_rows(p_tall, 1)[:ny] - p) * back)
        shift = LANES - 1 - 10 - GROUP * seat
        lam_end = roll_lanes(spill[group][:ny], shift)
        u_end = roll_lanes(basis_z[3, group, :ny, :], shift)
        p_end = roll_lanes(press_z, LANES - 1 - 2 * x)
        out = vel[2, x] + (jnp.where(at_high, lam_end, roll_lanes(own, -1)) - own)
        ustar[2, x] = out
        answer = answer + (p - jnp.where(at_high, p_end, roll_lanes(p, -1))) * out
        back = jnp.where(at_low, u_end, roll_lanes(vel[2, x], 1))
        back = back + (own - jnp.where(at_low, lam_end, roll_lanes(own, 1)))
        answer = answer + (jnp.where(at_low, p_end, roll_lanes(p, 1)) - p) * back
        coef_cot[x] = 0.5 * answer
        here = above


def on_device(phase, press, vel):
    nx, ny, nz = phase.shape
    total, height = nx + 2 * DEPTH, ny + 2 * DEPTH
    groups = total // ROWS
    devices = lax.axis_size(AXES)
    n_x, n_y, n_z = (turns(axis) for axis in AXES)
    f32 = lambda *shape: jax.ShapeDtypeStruct(shape, jnp.float32)
    scratch = lambda *shape: pltpu.VMEM(shape, jnp.float32)
    parity = jnp.stack([lax.axis_index(axis) % 2 for axis in AXES]).astype(jnp.int32)
    inputs = [pltpu.with_memory_space_constraint(array, pltpu.HBM) for array in (phase, press, vel)]

    def call(kernel, args, in_specs, shapes, name, scratch_shapes=()):
        return pl.pallas_call(
            kernel,
            out_shape=shapes,
            in_specs=in_specs,
            out_specs=[VMEM] * len(shapes),
            scratch_shapes=list(scratch_shapes),
            compiler_params=PARAMS,
            cost_estimate=pl.CostEstimate(flops=3_000_000, bytes_accessed=3_000_000, transcendentals=0),
            name=name,
        )(*args)

    to_x = call(
        functools.partial(pack_x, nx),
        [parity] + inputs,
        [SMEM] + [HBM] * 3,
        [f32(4 * DEPTH - 1, ny, nz)] * n_x,
        "pack_x",
        [pltpu.VMEM((n_x, DEPTH, ny, nz), jnp.int32), pltpu.SemaphoreType.DMA((n_x, 5))],
    )
    got_x = exchange(to_x, "gx")
    coef, press, vel = call(
        load,
        inputs + [to_x[0]],
        [HBM] * 3 + [ANY],
        [f32(*press.shape), f32(*press.shape), f32(*vel.shape)],
        "load",
        [pltpu.VMEM(phase.shape, jnp.int32), pltpu.SemaphoreType.DMA((3,))],
    )
    to_y = call(
        functools.partial(pack_y, nx, ny, n_x),
        [parity, coef, press, vel, *got_x],
        [SMEM] + [VMEM] * (3 + n_x),
        [f32(total + -(-nx // GROUP), GROUP, nz)] * n_y,
        "pack_y",
    )
    got_y = exchange(to_y, "gy")
    to_z = call(
        functools.partial(pack_z, nx, ny, n_x, n_y),
        [parity, coef, press, vel, *got_x, *got_y],
        [SMEM] + [VMEM] * (3 + n_x + n_y),
        [f32(groups + 1, height, LANES)] * n_z,
        "pack_z",
    )
    got_z = exchange(to_z, "gz")
    cube = (total, height, nz)
    ready = call(
        functools.partial(prepare, nx, ny, n_x, n_y),
        [parity, coef, vel, to_z[0], *got_x, *got_y],
        [SMEM] + [VMEM] * 2 + [ANY] + [VMEM] * (n_x + n_y),
        [f32(*cube), f32(2, *cube), f32(2, *cube), f32(*cube), f32(*cube), f32(2, groups, height, LANES)],
        "prepare",
    )
    basis, basis_z, sums = call(
        functools.partial(krylov, nx, ny, n_z),
        [parity, *ready, *got_z],
        [SMEM] + [VMEM] * (6 + n_z),
        [f32(3, *cube), f32(4, groups, height, LANES), f32(1, LANES)],
        "krylov",
        [scratch(*cube)] + [scratch(n, groups, height, LANES) for n in (6,)] + [scratch(groups, height, LANES)]
        + [scratch(5, groups, height, LANES)],
    )
    spread = jnp.broadcast_to(sums[None], (devices, 1, LANES))
    gathered = lax.all_to_all(spread, AXES, 0, 0).reshape(devices, LANES)
    return call(
        functools.partial(finish, nx, ny, n_x, n_y, n_z),
        [parity, gathered, press, vel, basis, basis_z, *got_x, *got_y, *got_z],
        [SMEM] + [VMEM] * (5 + n_x + n_y + n_z),
        [f32(*vel.shape), f32(nx, ny, nz)],
        "finish",
    )


def solution(mesh):
    cells, faces = P(*AXES), P(None, *AXES)
    return jax.shard_map(
        on_device, mesh=mesh, in_specs=(cells, cells, faces), out_specs=(faces, cells), check_vma=False
    )
```

```python
import functools

import jax
import jax.numpy as jnp
from jax import lax
from jax.experimental import pallas as pl
from jax.experimental.pallas import tpu as pltpu
from jax.sharding import PartitionSpec as P

AXES = ("gx", "gy", "gz")
DEPTH = 4
GROUP = 4 * DEPTH
LANES = 128
ROWS = 8
VMEM = pl.BlockSpec(memory_space=pltpu.VMEM)
SMEM = pl.BlockSpec(memory_space=pltpu.SMEM)
HBM = pl.BlockSpec(memory_space=pltpu.HBM)
ANY = pl.BlockSpec(memory_space=pl.ANY)
PARAMS = pltpu.CompilerParams(vmem_limit_bytes=40 * 1024 * 1024)


def swaps(count, first):
    pairs = []
    for i in range(first, count - 1, 2):
        pairs += [(i, i + 1), (i + 1, i)]
    return pairs


def exchange(sends, axis):
    count = lax.axis_size(axis)
    return [lax.ppermute(send, axis, swaps(count, turn)) for turn, send in enumerate(sends)]


def turns(axis):
    return min(2, lax.axis_size(axis) - 1)


def coefficient(phase):
    return jnp.where(phase == 0, 8.0, jnp.where(phase == 1, 1.0, 2.0)).astype(jnp.float32)


def sides(even, got, load):
    one = load(got[0])
    two = load(got[1]) if len(got) > 1 else jnp.zeros_like(one)
    return jnp.where(even, two, one), jnp.where(even, one, two)


def lane_index(shape):
    return lax.broadcasted_iota(jnp.int32, shape, len(shape) - 1)


def row_index(shape):
    return lax.broadcasted_iota(jnp.int32, shape, len(shape) - 2)


def roll_rows(plane, shift):
    return pltpu.roll(plane, shift % plane.shape[0], 0)


def roll_lanes(plane, shift):
    return pltpu.roll(plane, shift % plane.shape[1], 1)


def inner_rhs(coef, vy, vz):
    rows, lanes = row_index(coef.shape), lane_index(coef.shape)
    up = jnp.where(rows == coef.shape[0] - 1, 0.0, 0.5 * (coef + roll_rows(coef, -1)))
    down = jnp.where(rows == 0, 0.0, 0.5 * (coef + roll_rows(coef, 1)))
    right = jnp.where(lanes == LANES - 1, 0.0, 0.5 * (coef + roll_lanes(coef, -1)))
    left = jnp.where(lanes == 0, 0.0, 0.5 * (coef + roll_lanes(coef, 1)))
    return (up * vy - down * roll_rows(vy, 1)) + (right * vz - left * roll_lanes(vz, 1))


RHS, VX, PRESS, VZ, VY = DEPTH, 2 * DEPTH - 1, 2 * DEPTH, 2 * DEPTH + 1, 2 * DEPTH + 2


def pack_x(nx, ny, parity, phase, press, vel, *refs):
    count = len(refs) - 5
    outs = refs[:count]
    held, held_x, held_y, held_z, sem = refs[count:]
    copies = []
    for turn, out in enumerate(outs):
        top = parity[0] == turn
        deep = jnp.where(top, nx - DEPTH, 0)
        less = jnp.where(top, nx - DEPTH + 1, 0)
        last = jnp.where(top, nx - 1, 0)
        parts = [
            (phase.at[pl.ds(deep, DEPTH)], held.at[turn]),
            (vel.at[0, pl.ds(deep, DEPTH)], held_x.at[turn]),
            (vel.at[1, pl.ds(less, DEPTH - 1)], held_y.at[turn]),
            (vel.at[2, pl.ds(less, DEPTH - 1)], held_z.at[turn]),
            (press.at[last], out.at[pl.ds(PRESS * ny, ny)]),
        ]
        for which, (src, dst) in enumerate(parts):
            copy = pltpu.make_async_copy(src, dst, sem.at[turn, which])
            copy.start()
            copies.append(copy)
    for copy in copies:
        copy.wait()
    lanes = lane_index((ny, LANES))
    rows = row_index((ROWS, LANES))
    for turn, out in enumerate(outs):
        top = parity[0] == turn
        coefs = [coefficient(held[turn, j]) for j in range(DEPTH)]
        flux = [0.5 * (coefs[j] + coefs[j + 1]) * held_x[turn, j] for j in range(DEPTH - 1)]
        columns = jnp.zeros((ny, LANES), jnp.float32)
        lines = jnp.zeros((ROWS, LANES), jnp.float32)
        for j in range(DEPTH):
            out[j * ny : (j + 1) * ny, :] = coefs[j]
        for j in range(DEPTH - 1):
            vy, vz = held_y[turn, j], held_z[turn, j]
            upper = (flux[j + 1] - flux[j]) if j + 1 < DEPTH - 1 else -flux[j]
            lower = (flux[j] - flux[j - 1]) if j else flux[j]
            inner = inner_rhs(jnp.where(top, coefs[j + 1], coefs[j]), vy, vz)
            out[(RHS + j) * ny : (RHS + j + 1) * ny, :] = jnp.where(top, upper, lower) + inner
            columns = jnp.where(lanes == j, roll_lanes(vz, j + 1), columns)
            lines = jnp.where(rows == j, roll_rows(vy[ny - ROWS :], j + 1), lines)
        out[VX * ny : (VX + 1) * ny, :] = held_x[turn, DEPTH - 1]
        out[VZ * ny : (VZ + 1) * ny, :] = columns
        out[VY * ny :, :] = lines


def load(phase, press, vel, after, coef, press_out, vel_out, rhs, held, sem):
    del after
    copies = []
    for which, (src, dst) in enumerate(((phase, held), (press, press_out), (vel, vel_out))):
        copies.append(pltpu.make_async_copy(src, dst, sem.at[which]))
        copies[-1].start()
    copies[0].wait()
    copies[1].wait()
    copies[2].wait()
    nx = coef.shape[0]
    here = coefficient(held[0])
    old_flux = None
    for x in range(nx):
        coef[x] = here
        answer = inner_rhs(here, vel_out[1, x], vel_out[2, x])
        if old_flux is not None:
            answer = answer - old_flux
        if x + 1 < nx:
            above = coefficient(held[x + 1])
            old_flux = 0.5 * (here + above) * vel_out[0, x]
            answer = answer + old_flux
            here = above
        rhs[x] = answer


class Block:
    def __init__(self, nx, ny, parity, coef, vel, rhs, got_x, row=0, height=None):
        self.nx, self.ny = nx, ny
        self.own_coef, self.vel, self.own_rhs, self.got_x = coef, vel, rhs, got_x
        self.even = parity[0] == 0
        self.row, self.height = row, height or ny
        self.low_face = 0.5 * (self.coef(nx + 2 * DEPTH - 1) + self.coef(0)) * self.halo(VX)[0]
        self.high_face = 0.5 * (self.coef(nx - 1) + self.coef(nx)) * self.take(vel, 0, nx - 1)

    def take(self, ref, *index):
        return ref[(*index, pl.ds(self.row, self.height), slice(None))]

    def halo(self, part):
        return sides(self.even, self.got_x, lambda ref: ref[pl.ds(part * self.ny + self.row, self.height), :])

    def coef(self, plane):
        if plane < self.nx:
            return self.take(self.own_coef, plane)
        above = plane < self.nx + DEPTH
        return self.halo((plane - self.nx) % DEPTH)[1 if above else 0]

    def rhs(self, plane):
        nx = self.nx
        if plane < nx:
            answer = self.take(self.own_rhs, plane)
        else:
            above = plane < nx + DEPTH
            layer = plane - nx if above else plane - nx - DEPTH - 1
            if layer < 0 or layer >= DEPTH - 1:
                return jnp.zeros((self.height, LANES), jnp.float32)
            answer = self.halo(RHS + layer)[1 if above else 0]
        if plane == 0:
            answer = answer - self.low_face
        if plane == nx + 2 * DEPTH - 1:
            answer = answer + self.low_face
        if plane == nx - 1:
            answer = answer + self.high_face
        if plane == nx:
            answer = answer - self.high_face
        return answer

    def layer(self, plane):
        if plane < self.nx + DEPTH:
            place = (1, plane - self.nx)
        else:
            place = (0, plane - self.nx - DEPTH - 1)
        return place if 0 <= place[1] < DEPTH - 1 else None

    def vz_end(self, plane):
        if plane < self.nx:
            return self.vel[2, plane], LANES - 1
        place = self.layer(plane)
        if place is None:
            return jnp.zeros((self.ny, LANES), jnp.float32), 0
        return self.halo(VZ)[place[0]], place[1]

    def vy_end(self, plane):
        if plane < self.nx:
            return self.vel[1, plane, self.ny - 1 :, :]
        place = self.layer(plane)
        if place is None:
            return jnp.zeros((1, LANES), jnp.float32)
        at = VY * self.ny + place[1]
        return sides(self.even, self.got_x, lambda ref: ref[at : at + 1, :])[place[0]]


def pack_y(nx, ny, n_x, parity, coef, press, vel, rhs, *refs):
    got_x, outs = refs[:n_x], refs[n_x:]
    total = nx + 2 * DEPTH
    rows, lanes = row_index((ROWS, LANES)), lane_index((ROWS, LANES))
    for turn, out in enumerate(outs):
        top = parity[1] == turn
        row = pl.multiple_of(jnp.where(top, ny - ROWS, 0), ROWS)
        block = Block(nx, ny, parity, coef, vel, rhs, got_x, row, ROWS)
        columns = jnp.zeros((ROWS, LANES), jnp.float32)
        low_end, high_end = block.halo(VZ)
        for plane in range(total):
            one, two = block.coef(plane), block.rhs(plane)
            one = jnp.where(top, roll_rows(one, DEPTH), one)
            two = jnp.where(top, roll_rows(two, -1), roll_rows(two, DEPTH))
            tile = jnp.where(rows < DEPTH, one, two)
            out[plane] = jnp.where(rows == ROWS - 1, block.vy_end(plane), tile)
            if plane < nx:
                source, lane = vel[2, plane, pl.ds(row, ROWS), :], LANES - 1
            elif block.layer(plane) is None:
                continue
            else:
                side, lane = block.layer(plane)
                source = (low_end, high_end)[side]
            columns = jnp.where(lanes == plane, roll_lanes(source, plane - lane), columns)
        out[total + nx // ROWS] = jnp.where(top, roll_rows(columns, DEPTH - 1), columns)
        for plane in range(nx):
            tile = press[plane, pl.ds(row, ROWS), :]
            edge = jnp.where(top, tile[ROWS - 1 : ROWS], tile[0:1])
            out[total + plane // ROWS, plane % ROWS : plane % ROWS + 1, :] = edge


def tall_end(block, tile_end, plane, lane):
    source, at = block.vz_end(plane)
    return jnp.concatenate([roll_lanes(source, lane - at), roll_lanes(tile_end, lane - plane)], 0)


def tile_of_ends(nx, even_y, got_y):
    rows = row_index((ROWS, LANES))
    low, high = sides(even_y, got_y, lambda ref: ref[nx + 2 * DEPTH + nx // ROWS])
    return jnp.where(rows < DEPTH, high, roll_rows(low, DEPTH + 1))


def press_lane(x):
    return GROUP * (x % ROWS) + ROWS + 2 * (x // ROWS)


def pack_z(nx, ny, n_x, n_y, n_z, parity, coef, press, vel, rhs, *refs):
    got_x, got_y = refs[:n_x], refs[n_x : n_x + n_y]
    full_coef, full_rhs, *sends = refs[n_x + n_y :]
    total, height = nx + 2 * DEPTH, ny + 2 * DEPTH
    groups = total // ROWS
    even_y = parity[1] == 0
    rows = row_index((ROWS, LANES))
    lanes = lane_index((height, LANES))
    block = Block(nx, ny, parity, coef, vel, rhs, got_x)
    tile_end = tile_of_ends(nx, even_y, got_y)
    parts = [jnp.zeros((height, LANES), jnp.float32) for _ in range(groups // 2 + 1)]
    made = [list(parts) for _ in sends]
    for plane in range(total):
        low, high = sides(even_y, got_y, lambda ref: ref[plane])
        c_own, c_tile = block.coef(plane), jnp.where(rows < DEPTH, high, roll_rows(low, DEPTH))
        r_own, r_tile = block.rhs(plane), jnp.where(rows < DEPTH, roll_rows(high, -DEPTH), roll_rows(low, 1))
        up = 0.5 * (c_own[ny - 1 :] + c_tile[:1]) * block.vy_end(plane)
        down = 0.5 * (c_tile[ROWS - 1 :] + c_own[:1]) * low[ROWS - 1 :]
        first, last = r_own[:ROWS], r_own[ny - ROWS :]
        r_tile = jnp.where(rows == 0, r_tile - up, jnp.where(rows == ROWS - 1, r_tile + down, r_tile))
        middle = [r_own[ROWS : ny - ROWS]] if ny > 2 * ROWS else []
        if ny > ROWS:
            first = jnp.where(rows == 0, first - down, first)
            last = jnp.where(rows == ROWS - 1, last + up, last)
            r_all = jnp.concatenate([first] + middle + [last, r_tile], 0)
        else:
            only = jnp.where(rows == 0, first - down, jnp.where(rows == ROWS - 1, first + up, first))
            r_all = jnp.concatenate([only, r_tile], 0)
        c_all = jnp.concatenate([c_own, c_tile], 0)
        full_coef[plane], full_rhs[plane] = c_all, r_all
        group, seat = plane % groups, plane // groups
        at = GROUP * seat + ROWS * (group % 2)
        end = tall_end(block, tile_end, plane, at + ROWS - 1)
        for turn in range(len(sends)):
            top = parity[2] == turn
            c_move = pltpu.roll(c_all, jnp.where(top, (at + DEPTH) % LANES, at), 1)
            r_move = pltpu.roll(r_all, jnp.where(top, (at + ROWS - 1) % LANES, at + DEPTH), 1)
            value = made[turn][group // 2]
            value = jnp.where((lanes >= at) & (lanes < at + DEPTH), c_move, value)
            value = jnp.where((lanes >= at + DEPTH) & (lanes < at + ROWS - 1), r_move, value)
            made[turn][group // 2] = jnp.where(lanes == at + ROWS - 1, end, value)
    for turn, send in enumerate(sends):
        top = parity[2] == turn
        value = made[turn][groups // 2][:ny]
        for plane in range(nx):
            at = press_lane(plane)
            moved = pltpu.roll(press[plane], jnp.where(top, (at + 1) % LANES, at), 1)
            value = jnp.where(lanes[:ny] == at, moved, value)
        made[turn][groups // 2] = jnp.concatenate([value, made[turn][groups // 2][ny:]], 0)
        for which, value in enumerate(made[turn]):
            send[which] = value


def prepare(nx, ny, n_x, n_y, parity, coef, vel, rhs, full_coef, full_rhs, *refs):
    got_x, got_y = refs[:n_x], refs[n_x : n_x + n_y]
    wx, wy, wz, diag_out, ends = refs[n_x + n_y :]
    total, height = nx + 2 * DEPTH, ny + 2 * DEPTH
    groups = total // ROWS
    lanes = lane_index((height, LANES))
    block = Block(nx, ny, parity, coef, vel, rhs, got_x)
    tile_end = tile_of_ends(nx, parity[1] == 0, got_y)
    for group in range(groups):
        made = [jnp.zeros((height, LANES), jnp.float32) for _ in range(3)]
        for seat in range(ROWS):
            plane = seat * groups + group
            at = GROUP * seat
            upper = (lanes >= at) & (lanes < at + DEPTH)
            lower = (lanes >= at + 3 * DEPTH) & (lanes < at + GROUP)
            for which, source in enumerate((full_coef[plane], full_rhs[plane])):
                value = jnp.where(upper, roll_lanes(source, at + DEPTH), made[which])
                made[which] = jnp.where(lower, roll_lanes(source, at + 3 * DEPTH), value)
            end = tall_end(block, tile_end, plane, at + DEPTH - 1)
            made[2] = jnp.where(lanes == at + DEPTH - 1, end, made[2])
        for which in range(3):
            ends[which, group] = made[which]
    old_weight = None
    here = full_coef[nx + DEPTH]
    for x in range(-DEPTH, nx + DEPTH - 1):
        e = x % total
        above = full_coef[(e + 1) % total]
        weight = 0.5 * (here + above)
        wx[e] = weight
        if x > -DEPTH:
            up, down = 0.5 * (here + roll_rows(here, -1)), 0.5 * (here + roll_rows(here, 1))
            right = jnp.where(lanes == LANES - 1, 0.0, 0.5 * (here + roll_lanes(here, -1)))
            left = jnp.where(lanes == 0, 0.0, 0.5 * (here + roll_lanes(here, 1)))
            wy[0, e], wy[1, e], wz[0, e], wz[1, e] = up, down, right, left
            diag_out[e] = jnp.where(here > 0, (weight + old_weight) + (up + down) + (right + left), 0.0)
        old_weight, here = weight, above


def tree_sum(parts):
    while len(parts) > 1:
        parts = [parts[i] + parts[i + 1] if i + 1 < len(parts) else parts[i] for i in range(0, len(parts), 2)]
    return parts[0]


class Totals:
    def __init__(self):
        self.stack = []

    def add(self, tile):
        level = 0
        while self.stack and self.stack[-1][0] == level:
            tile = self.stack.pop()[1] + tile
            level += 1
        self.stack.append((level, tile))

    def value(self):
        tiles = [tile for _, tile in self.stack]
        total = tiles.pop()
        while tiles:
            total = tiles.pop() + total
        return total


def krylov(nx, ny, n_z, parity, wx, wy, wz, diag_in, rhs_in, ends, *refs):
    got_z = refs[:n_z]
    basis, basis_z, sums = refs[n_z : n_z + 3]
    inverse, pw, pinv, spill = refs[n_z + 3 :]
    even_z = parity[2] == 0
    total, height = nx + 2 * DEPTH, ny + 2 * DEPTH
    groups = total // ROWS
    lanes = lane_index((height, LANES))
    seat_lane = lanes % GROUP
    edge = (lanes == 0) | (lanes == LANES - 1)

    def along(planes, group, step):
        if 0 <= group + step < groups:
            return planes[group + step]
        return roll_lanes(planes[(group + step) % groups], -GROUP * step)

    def spilled(which, group, up, down):
        spill[which, group] = jnp.where(seat_lane == 10, roll_lanes(up, 7), down)

    coef, rhs_z, vz = [], [], []
    for g in range(groups):
        low, high = sides(even_z, got_z, lambda ref: ref[g // 2])
        skip = ROWS * (g % 2)
        above = (seat_lane >= DEPTH) & (seat_lane < 2 * DEPTH)
        below = (seat_lane >= 2 * DEPTH) & (seat_lane < 3 * DEPTH)
        value = jnp.where(above, roll_lanes(high, DEPTH - skip), ends[0, g])
        coef.append(jnp.where(below, roll_lanes(low, 2 * DEPTH - skip), value))
        value = jnp.where(above, roll_lanes(high, -skip), ends[1, g])
        rhs_z.append(jnp.where(below, roll_lanes(low, DEPTH + 1 - skip), value))
        vz.append(jnp.where(below, roll_lanes(low, DEPTH - skip), ends[2, g]))
    for g in range(groups):
        here = coef[g]
        neighbours = (along(coef, g, 1), along(coef, g, -1), roll_rows(here, -1), roll_rows(here, 1))
        neighbours += (roll_lanes(here, -1), roll_lanes(here, 1))
        weights = [0.5 * (here + other) for other in neighbours]
        for which, weight in enumerate(weights):
            pw[which, g] = weight
        diag = (weights[0] + weights[1]) + (weights[2] + weights[3]) + (weights[4] + weights[5])
        face = (seat_lane == DEPTH - 1) | (seat_lane == 3 * DEPTH - 1)
        next_face = (seat_lane == DEPTH) | (seat_lane == 3 * DEPTH)
        fz = weights[4] * vz[g]
        spilled(0, g, weights[4], weights[4])
        spilled(1, g, fz, -fz)
        rhs = rhs_z[g] + jnp.where(face, fz, 0.0)
        rhs = rhs - jnp.where(next_face, weights[5] * roll_lanes(vz[g], 1), 0.0)
        inside = here > 0
        scale = jnp.where(inside, 1.0 / jnp.where(inside, diag, 1.0), 0.0)
        pinv[g] = scale
        basis_z[0, g] = scale * rhs
        basis_z[3, g] = vz[g]
    for n in range(3):
        field = [basis_z[n, g] for g in range(groups)]
        for g in range(groups):
            here = field[g]
            fz = pw[4, g] * (roll_lanes(here, -1) - here)
            spilled(2 + n, g, -fz, fz)
            if n < 2:
                image = pw[0, g] * (here - along(field, g, 1)) + pw[1, g] * (here - along(field, g, -1))
                image = image + (pw[2, g] * (here - roll_rows(here, -1)) + pw[3, g] * (here - roll_rows(here, 1)))
                image = image + (pw[5, g] * (here - roll_lanes(here, 1)) - fz)
                basis_z[n + 1, g] = pinv[g] * image

    def inject(which, plane):
        group, seat = plane % groups, plane // groups
        return jnp.where(edge, roll_lanes(spill[which, group], LANES - 1 - 10 - GROUP * seat), 0.0)

    totals = [Totals() for _ in range(6)]

    def count(which, left, right):
        product = left[:ny] * right[:ny]
        totals[which].add(tree_sum([product[i : i + ROWS] for i in range(0, ny, ROWS)]))

    for x in range(-DEPTH + 1, nx + DEPTH - 1):
        e = x % total
        diag, rhs = diag_in[e], rhs_in[e] + inject(1, e)
        inside = diag > 0
        scale = jnp.where(inside, 1.0 / jnp.where(inside, diag + inject(0, e), 1.0), 0.0)
        inverse[e] = scale
        field = scale * rhs
        basis[0, e] = field
        if 0 <= x < nx:
            count(0, field, rhs)
    for n in range(3):
        reach = 2 - n
        old_flux = None
        here = basis[n, (-reach - 1) % total]
        for x in range(-reach - 1, nx + reach):
            e = x % total
            above = basis[n, (e + 1) % total]
            flux = wx[e] * (above - here)
            if x >= -reach:
                image = (old_flux - flux) + inject(2 + n, e)
                image = image + (
                    wy[0, e] * (here - roll_rows(here, -1)) + wy[1, e] * (here - roll_rows(here, 1))
                )
                image = image + (
                    wz[0, e] * (here - roll_lanes(here, -1)) + wz[1, e] * (here - roll_lanes(here, 1))
                )
                own = 0 <= x < nx
                if own:
                    count(2 * n + 1, here, image)
                if n < 2:
                    following = inverse[e] * image
                    basis[n + 1, e] = following
                    if own:
                        count(2 * n + 2, following, image)
            old_flux, here = flux, above
    lane = lane_index((1, LANES))
    row = jnp.zeros((1, LANES), jnp.float32)
    for which, total_ in enumerate(totals):
        value = jnp.sum(jnp.sum(total_.value(), 0, keepdims=True), 1, keepdims=True)
        row = jnp.where(lane == which, value, row)
    sums[...] = row


def finish(nx, ny, n_x, n_y, n_z, parity, gathered, press, vel, basis, basis_z, *refs):
    got_x, got_y, got_z = refs[:n_x], refs[n_x : n_x + n_y], refs[n_x + n_y : n_x + n_y + n_z]
    ustar, coef_cot = refs[n_x + n_y + n_z :]
    even_x, even_y, even_z = parity[0] == 0, parity[1] == 0, parity[2] == 0
    total, height = nx + 2 * DEPTH, ny + 2 * DEPTH
    groups = total // ROWS
    parts = gathered[...]
    while parts.shape[0] > ROWS:
        half = parts.shape[0] // 2
        parts = parts[:half] + parts[half:]
    sums = jnp.sum(parts, 0, keepdims=True)
    lane = lane_index((1, LANES))
    m0, m1, m2, m3, m4, m5 = [
        jnp.sum(jnp.where(lane == which, sums, 0.0), 1, keepdims=True) for which in range(6)
    ]
    l1, l2 = m2 / m1, m3 / m1
    d1, cross, d2 = m3 - l1 * m2, m4 - l1 * m3, m5 - l2 * m3
    l21 = cross / d1
    d2 = d2 - l21 * cross
    y1 = -l1 * m0 + m1
    y2 = m2 - l2 * m0 - l21 * y1
    c2 = y2 / d2
    c1 = y1 / d1 - l21 * c2
    c0 = (m0 / m1 - l1 * c1 - l2 * c2)[0, 0]
    c1, c2 = c1[0, 0], c2[0, 0]

    lanes = lane_index((height, LANES))
    seat_lane = lanes % GROUP
    spill = []
    for g in range(groups):
        cells = c0 * basis_z[0, g] + c1 * basis_z[1, g] + c2 * basis_z[2, g]
        spill.append(jnp.where(seat_lane == 10, roll_lanes(cells, 6), cells))
    lanes = lane_index((ny, LANES))
    at_low, at_high = lanes == 0, lanes == LANES - 1
    low_z, high_z = sides(even_z, got_z, lambda ref: ref[groups // 2, :ny, :])
    press_z = jnp.where(lanes % 2 == 0, high_z, roll_lanes(low_z, 1))
    p_low, p_high = sides(even_x, got_x, lambda ref: ref[PRESS * ny : (PRESS + 1) * ny, :])
    u_low, _ = sides(even_x, got_x, lambda ref: ref[VX * ny : (VX + 1) * ny, :])

    def solved(x):
        e = x % total
        return c0 * basis[0, e] + c1 * basis[1, e] + c2 * basis[2, e]

    rows = row_index((ROWS, LANES))
    below, here = solved(-1), solved(0)
    face_low = (p_low - press[0]) * (u_low + here[:ny] - below[:ny])
    for x in range(nx):
        above = solved(x + 1)
        group, seat = x % groups, x // groups
        own, p = here[:ny], press[x]
        out = vel[0, x] + (above[:ny] - own)
        ustar[0, x] = out
        face = (p - (press[x + 1] if x + 1 < nx else p_high)) * out
        answer = face_low + face
        face_low = face
        low, high = sides(even_y, got_y, lambda ref: ref[total + x // ROWS, x % ROWS : x % ROWS + 1, :])
        shape = (ROWS, LANES)
        p_tile = jnp.where(rows == 0, jnp.broadcast_to(high, shape), jnp.broadcast_to(low, shape))
        p_tall = jnp.concatenate([p, p_tile], 0)
        u_row, _ = sides(even_y, got_y, lambda ref: ref[x, ROWS - 1 :, :])
        u_tall = jnp.concatenate([vel[1, x], jnp.broadcast_to(u_row, shape)], 0)
        out = vel[1, x] + (roll_rows(here, -1)[:ny] - own)
        ustar[1, x] = out
        back = roll_rows(u_tall, 1)[:ny] + (own - roll_rows(here, 1)[:ny])
        answer = answer + ((p - roll_rows(p_tall, -1)[:ny]) * out + (roll_rows(p_tall, 1)[:ny] - p) * back)
        shift = LANES - 1 - 10 - GROUP * seat
        lam_end = roll_lanes(spill[group][:ny], shift)
        u_end = roll_lanes(basis_z[3, group, :ny, :], shift)
        p_end = roll_lanes(press_z, LANES - 1 - press_lane(x))
        out = vel[2, x] + (jnp.where(at_high, lam_end, roll_lanes(own, -1)) - own)
        ustar[2, x] = out
        answer = answer + (p - jnp.where(at_high, p_end, roll_lanes(p, -1))) * out
        back = jnp.where(at_low, u_end, roll_lanes(vel[2, x], 1))
        back = back + (own - jnp.where(at_low, lam_end, roll_lanes(own, 1)))
        answer = answer + (jnp.where(at_low, p_end, roll_lanes(p, 1)) - p) * back
        coef_cot[x] = 0.5 * answer
        here = above


def on_device(phase, press, vel):
    nx, ny, nz = phase.shape
    total, height = nx + 2 * DEPTH, ny + 2 * DEPTH
    groups = total // ROWS
    devices = lax.axis_size(AXES)
    n_x, n_y, n_z = (turns(axis) for axis in AXES)
    f32 = lambda *shape: jax.ShapeDtypeStruct(shape, jnp.float32)
    scratch = lambda *shape: pltpu.VMEM(shape, jnp.float32)
    parity = jnp.stack([lax.axis_index(axis) % 2 for axis in AXES]).astype(jnp.int32)
    inputs = [pltpu.with_memory_space_constraint(array, pltpu.HBM) for array in (phase, press, vel)]

    def call(kernel, args, in_specs, shapes, name, scratch_shapes=()):
        return pl.pallas_call(
            kernel,
            out_shape=shapes,
            in_specs=in_specs,
            out_specs=[VMEM] * len(shapes),
            scratch_shapes=list(scratch_shapes),
            compiler_params=PARAMS,
            cost_estimate=pl.CostEstimate(flops=3_000_000, bytes_accessed=3_000_000, transcendentals=0),
            name=name,
        )(*args)

    to_x = call(
        functools.partial(pack_x, nx, ny),
        [parity] + inputs,
        [SMEM] + [HBM] * 3,
        [f32(VY * ny + ROWS, nz)] * n_x,
        "pack_x",
        [pltpu.VMEM((n_x, DEPTH, ny, nz), jnp.int32), scratch(n_x, DEPTH, ny, nz)]
        + [scratch(n_x, DEPTH - 1, ny, nz)] * 2
        + [pltpu.SemaphoreType.DMA((n_x, 5))],
    )
    got_x = exchange(to_x, "gx")
    coef, press, vel, rhs = call(
        load,
        inputs + [to_x[0]],
        [HBM] * 3 + [ANY],
        [f32(*press.shape), f32(*press.shape), f32(*vel.shape), f32(*press.shape)],
        "load",
        [pltpu.VMEM(phase.shape, jnp.int32), pltpu.SemaphoreType.DMA((3,))],
    )
    to_y = call(
        functools.partial(pack_y, nx, ny, n_x),
        [parity, coef, press, vel, rhs, *got_x],
        [SMEM] + [VMEM] * (4 + n_x),
        [f32(total + nx // ROWS + 1, ROWS, nz)] * n_y,
        "pack_y",
    )
    got_y = exchange(to_y, "gy")
    cube = (total, height, nz)
    full_coef, full_rhs, *to_z = call(
        functools.partial(pack_z, nx, ny, n_x, n_y, n_z),
        [parity, coef, press, vel, rhs, *got_x, *got_y],
        [SMEM] + [VMEM] * (4 + n_x + n_y),
        [f32(*cube)] * 2 + [f32(groups // 2 + 1, height, LANES)] * n_z,
        "pack_z",
    )
    got_z = exchange(to_z, "gz")
    wx, wy, wz, diag, ends = call(
        functools.partial(prepare, nx, ny, n_x, n_y),
        [parity, coef, vel, rhs, full_coef, full_rhs, *got_x, *got_y],
        [SMEM] + [VMEM] * (5 + n_x + n_y),
        [f32(*cube), f32(2, *cube), f32(2, *cube), f32(*cube), f32(3, groups, height, LANES)],
        "prepare",
    )
    basis, basis_z, sums = call(
        functools.partial(krylov, nx, ny, n_z),
        [parity, wx, wy, wz, diag, full_rhs, ends, *got_z],
        [SMEM] + [VMEM] * (6 + n_z),
        [f32(3, *cube), f32(4, groups, height, LANES), f32(1, LANES)],
        "krylov",
        [scratch(*cube), scratch(6, groups, height, LANES), scratch(groups, height, LANES)]
        + [scratch(5, groups, height, LANES)],
    )
    spread = jnp.broadcast_to(sums[None], (devices, 1, LANES))
    gathered = lax.all_to_all(spread, AXES, 0, 0).reshape(devices, LANES)
    return call(
        functools.partial(finish, nx, ny, n_x, n_y, n_z),
        [parity, gathered, press, vel, basis, basis_z, *got_x, *got_y, *got_z],
        [SMEM] + [VMEM] * (5 + n_x + n_y + n_z),
        [f32(*vel.shape), f32(nx, ny, nz)],
        "finish",
    )


def solution(mesh):
    cells, faces = P(*AXES), P(None, *AXES)
    return jax.shard_map(
        on_device, mesh=mesh, in_specs=(cells, cells, faces), out_specs=(faces, cells), check_vma=False
    )
```

```python
import functools

import jax
import jax.numpy as jnp
from jax import lax
from jax.experimental import pallas as pl
from jax.experimental.pallas import tpu as pltpu
from jax.sharding import PartitionSpec as P

AXES = ("gx", "gy", "gz")
DEPTH = 4
GROUP = 4 * DEPTH
LANES = 128
STRIDE = 4
ROWS = 8
VMEM = pl.BlockSpec(memory_space=pltpu.VMEM)
HBM = pl.BlockSpec(memory_space=pltpu.HBM)
ANY = pl.BlockSpec(memory_space=pl.ANY)
PARAMS = pltpu.CompilerParams(vmem_limit_bytes=40 * 1024 * 1024)


def swaps(count, first):
    pairs = []
    for i in range(first, count - 1, 2):
        pairs += [(i, i + 1), (i + 1, i)]
    return pairs


def exchange(sends, axis):
    count = lax.axis_size(axis)
    return [lax.ppermute(send, axis, swaps(count, turn)) for turn, send in enumerate(sends)]


def even(axis):
    return lax.axis_index(axis) % 2 == 0


def turns(axis):
    return min(2, lax.axis_size(axis) - 1)


def coefficient(phase):
    return jnp.where(phase == 0, 8.0, jnp.where(phase == 1, 1.0, 2.0)).astype(jnp.float32)


def sides(is_even, got, load):
    one = load(got[0])
    two = load(got[1]) if len(got) > 1 else jnp.zeros_like(one)
    return jnp.where(is_even, two, one), jnp.where(is_even, one, two)


def lane_index(shape):
    return lax.broadcasted_iota(jnp.int32, shape, len(shape) - 1)


def row_index(shape):
    return lax.broadcasted_iota(jnp.int32, shape, len(shape) - 2)


def roll_rows(plane, shift):
    return pltpu.roll(plane, shift % plane.shape[0], 0)


def roll_lanes(plane, shift):
    return pltpu.roll(plane, shift % plane.shape[1], 1)


def inner_rhs(coef, vy, vz):
    rows, lanes = row_index(coef.shape), lane_index(coef.shape)
    up = jnp.where(rows == coef.shape[0] - 1, 0.0, 0.5 * (coef + roll_rows(coef, -1)))
    down = jnp.where(rows == 0, 0.0, 0.5 * (coef + roll_rows(coef, 1)))
    right = jnp.where(lanes == LANES - 1, 0.0, 0.5 * (coef + roll_lanes(coef, -1)))
    left = jnp.where(lanes == 0, 0.0, 0.5 * (coef + roll_lanes(coef, 1)))
    return (up * vy - down * roll_rows(vy, 1)) + (right * vz - left * roll_lanes(vz, 1))


RHS, VX, PRESS, VZ, VY = DEPTH, 2 * DEPTH - 1, 2 * DEPTH, 2 * DEPTH + 1, 2 * DEPTH + 2


def pack_x(nx, ny, phase, press, vel, *refs):
    count = len(refs) - 3
    outs = refs[:count]
    held, held_vel, sem = refs[count:]
    copies = []
    for turn, out in enumerate(outs):
        top = even("gx") == (turn == 0)
        deep = jnp.where(top, nx - DEPTH, 0)
        last = jnp.where(top, nx - 1, 0)
        parts = [
            (vel.at[:, pl.ds(deep, DEPTH)], held_vel.at[turn]),
            (phase.at[pl.ds(deep, DEPTH)], held.at[turn]),
            (press.at[last], out.at[pl.ds(PRESS * ny, ny)]),
        ]
        for which, (src, dst) in enumerate(parts):
            copy = pltpu.make_async_copy(src, dst, sem.at[turn, which])
            copy.start()
            copies.append(copy)
    for copy in copies:
        copy.wait()
    lanes = lane_index((ny, LANES))
    rows = row_index((ROWS, LANES))
    for turn, out in enumerate(outs):
        top = even("gx") == (turn == 0)
        coefs = [coefficient(held[turn, j]) for j in range(DEPTH)]
        flux = [0.5 * (coefs[j] + coefs[j + 1]) * held_vel[turn, 0, j] for j in range(DEPTH - 1)]
        columns = jnp.zeros((ny, LANES), jnp.float32)
        lines = jnp.zeros((ROWS, LANES), jnp.float32)
        for j in range(DEPTH):
            out[j * ny : (j + 1) * ny, :] = coefs[j]
        for j in range(DEPTH - 1):
            vy = jnp.where(top, held_vel[turn, 1, j + 1], held_vel[turn, 1, j])
            vz = jnp.where(top, held_vel[turn, 2, j + 1], held_vel[turn, 2, j])
            upper = (flux[j + 1] - flux[j]) if j + 1 < DEPTH - 1 else -flux[j]
            lower = (flux[j] - flux[j - 1]) if j else flux[j]
            inner = inner_rhs(jnp.where(top, coefs[j + 1], coefs[j]), vy, vz)
            out[(RHS + j) * ny : (RHS + j + 1) * ny, :] = jnp.where(top, upper, lower) + inner
            columns = jnp.where(lanes == j, roll_lanes(vz, j + 1), columns)
            lines = jnp.where(rows == j, roll_rows(vy[ny - ROWS :], j + 1), lines)
        out[VX * ny : (VX + 1) * ny, :] = held_vel[turn, 0, DEPTH - 1]
        out[VZ * ny : (VZ + 1) * ny, :] = columns
        out[VY * ny :, :] = lines


def load(phase, press, vel, after, coef, press_out, vel_out, rhs, held, sem):
    del after
    copies = []
    for which, (src, dst) in enumerate(((phase, held), (press, press_out), (vel, vel_out))):
        copies.append(pltpu.make_async_copy(src, dst, sem.at[which]))
        copies[-1].start()
    copies[0].wait()
    copies[1].wait()
    copies[2].wait()
    nx = coef.shape[0]
    here = coefficient(held[0])
    old_flux = None
    for x in range(nx):
        coef[x] = here
        answer = inner_rhs(here, vel_out[1, x], vel_out[2, x])
        if old_flux is not None:
            answer = answer - old_flux
        if x + 1 < nx:
            above = coefficient(held[x + 1])
            old_flux = 0.5 * (here + above) * vel_out[0, x]
            answer = answer + old_flux
            here = above
        rhs[x] = answer


class Block:
    def __init__(self, nx, ny, coef, vel, rhs, got_x, row=0, height=None):
        self.nx, self.ny = nx, ny
        self.own_coef, self.vel, self.own_rhs, self.got_x = coef, vel, rhs, got_x
        self.even = even("gx")
        self.row, self.height = row, height or ny
        self.low_face = 0.5 * (self.coef(nx + 2 * DEPTH - 1) + self.coef(0)) * self.halo(VX)[0]
        self.high_face = 0.5 * (self.coef(nx - 1) + self.coef(nx)) * self.take(vel, 0, nx - 1)

    def take(self, ref, *index):
        return ref[(*index, pl.ds(self.row, self.height), slice(None))]

    def halo(self, part):
        return sides(self.even, self.got_x, lambda ref: ref[pl.ds(part * self.ny + self.row, self.height), :])

    def coef(self, plane):
        if plane < self.nx:
            return self.take(self.own_coef, plane)
        above = plane < self.nx + DEPTH
        return self.halo((plane - self.nx) % DEPTH)[1 if above else 0]

    def rhs(self, plane):
        nx = self.nx
        if plane < nx:
            answer = self.take(self.own_rhs, plane)
        else:
            above = plane < nx + DEPTH
            layer = plane - nx if above else plane - nx - DEPTH - 1
            if layer < 0 or layer >= DEPTH - 1:
                return jnp.zeros((self.height, LANES), jnp.float32)
            answer = self.halo(RHS + layer)[1 if above else 0]
        if plane == 0:
            answer = answer - self.low_face
        if plane == nx + 2 * DEPTH - 1:
            answer = answer + self.low_face
        if plane == nx - 1:
            answer = answer + self.high_face
        if plane == nx:
            answer = answer - self.high_face
        return answer

    def layer(self, plane):
        if plane < self.nx + DEPTH:
            place = (1, plane - self.nx)
        else:
            place = (0, plane - self.nx - DEPTH - 1)
        return place if 0 <= place[1] < DEPTH - 1 else None

    def vz_end(self, plane):
        if plane < self.nx:
            return self.vel[2, plane], LANES - 1
        place = self.layer(plane)
        if place is None:
            return jnp.zeros((self.ny, LANES), jnp.float32), 0
        return self.halo(VZ)[place[0]], place[1]

    def vy_end(self, plane):
        if plane < self.nx:
            return self.vel[1, plane, self.ny - 1 :, :]
        place = self.layer(plane)
        if place is None:
            return jnp.zeros((1, LANES), jnp.float32)
        at = VY * self.ny + place[1]
        return sides(self.even, self.got_x, lambda ref: ref[at : at + 1, :])[place[0]]


def pack_y(nx, ny, n_x, coef, press, vel, rhs, *refs):
    got_x, outs = refs[:n_x], refs[n_x:]
    total = nx + 2 * DEPTH
    rows, lanes = row_index((ROWS, LANES)), lane_index((ROWS, LANES))
    for turn, out in enumerate(outs):
        top = even("gy") == (turn == 0)
        row = pl.multiple_of(jnp.where(top, ny - ROWS, 0), ROWS)
        block = Block(nx, ny, coef, vel, rhs, got_x, row, ROWS)
        columns = jnp.zeros((ROWS, LANES), jnp.float32)
        low_end, high_end = block.halo(VZ)
        for plane in range(total):
            one, two = block.coef(plane), block.rhs(plane)
            one = jnp.where(top, roll_rows(one, DEPTH), one)
            two = jnp.where(top, roll_rows(two, -1), roll_rows(two, DEPTH))
            tile = jnp.where(rows < DEPTH, one, two)
            out[plane] = jnp.where(rows == ROWS - 1, block.vy_end(plane), tile)
            if plane < nx:
                source, lane = vel[2, plane, pl.ds(row, ROWS), :], LANES - 1
            elif block.layer(plane) is None:
                continue
            else:
                side, lane = block.layer(plane)
                source = (low_end, high_end)[side]
            columns = jnp.where(lanes == plane, roll_lanes(source, plane - lane), columns)
        out[total + nx // ROWS] = jnp.where(top, roll_rows(columns, DEPTH - 1), columns)
        for plane in range(nx):
            tile = press[plane, pl.ds(row, ROWS), :]
            edge = jnp.where(top, tile[ROWS - 1 : ROWS], tile[0:1])
            out[total + plane // ROWS, plane % ROWS : plane % ROWS + 1, :] = edge


def tall_end(block, tile_end, plane, lane):
    source, at = block.vz_end(plane)
    return jnp.concatenate([roll_lanes(source, lane - at), roll_lanes(tile_end, lane - plane)], 0)


def tile_of_ends(nx, even_y, got_y):
    rows = row_index((ROWS, LANES))
    low, high = sides(even_y, got_y, lambda ref: ref[nx + 2 * DEPTH + nx // ROWS])
    return jnp.where(rows < DEPTH, high, roll_rows(low, DEPTH + 1))


def press_lane(x):
    return GROUP * (x % ROWS) + ROWS + 2 * (x // ROWS)


def pack_z(nx, ny, n_x, n_y, n_z, coef, press, vel, rhs, *refs):
    got_x, got_y = refs[:n_x], refs[n_x : n_x + n_y]
    full_coef, full_rhs, *sends = refs[n_x + n_y :]
    total, height = nx + 2 * DEPTH, ny + 2 * DEPTH
    groups = total // ROWS
    even_y = even("gy")
    rows = row_index((ROWS, LANES))
    lanes = lane_index((height, LANES))
    block = Block(nx, ny, coef, vel, rhs, got_x)
    tile_end = tile_of_ends(nx, even_y, got_y)
    parts = [jnp.zeros((height, LANES), jnp.float32) for _ in range(groups // 2 + 1)]
    made = [list(parts) for _ in sends]
    for plane in range(total):
        low, high = sides(even_y, got_y, lambda ref: ref[plane])
        c_own, c_tile = block.coef(plane), jnp.where(rows < DEPTH, high, roll_rows(low, DEPTH))
        r_own, r_tile = block.rhs(plane), jnp.where(rows < DEPTH, roll_rows(high, -DEPTH), roll_rows(low, 1))
        up = 0.5 * (c_own[ny - 1 :] + c_tile[:1]) * block.vy_end(plane)
        down = 0.5 * (c_tile[ROWS - 1 :] + c_own[:1]) * low[ROWS - 1 :]
        first, last = r_own[:ROWS], r_own[ny - ROWS :]
        r_tile = jnp.where(rows == 0, r_tile - up, jnp.where(rows == ROWS - 1, r_tile + down, r_tile))
        middle = [r_own[ROWS : ny - ROWS]] if ny > 2 * ROWS else []
        if ny > ROWS:
            first = jnp.where(rows == 0, first - down, first)
            last = jnp.where(rows == ROWS - 1, last + up, last)
            r_all = jnp.concatenate([first] + middle + [last, r_tile], 0)
        else:
            only = jnp.where(rows == 0, first - down, jnp.where(rows == ROWS - 1, first + up, first))
            r_all = jnp.concatenate([only, r_tile], 0)
        c_all = jnp.concatenate([c_own, c_tile], 0)
        full_coef[plane], full_rhs[plane] = c_all, r_all
        group, seat = plane % groups, plane // groups
        at = GROUP * seat + ROWS * (group % 2)
        end = tall_end(block, tile_end, plane, at + ROWS - 1)
        for turn in range(len(sends)):
            top = even("gz") == (turn == 0)
            c_move = pltpu.roll(c_all, jnp.where(top, (at + DEPTH) % LANES, at), 1)
            r_move = pltpu.roll(r_all, jnp.where(top, (at + ROWS - 1) % LANES, at + DEPTH), 1)
            value = made[turn][group // 2]
            value = jnp.where((lanes >= at) & (lanes < at + DEPTH), c_move, value)
            value = jnp.where((lanes >= at + DEPTH) & (lanes < at + ROWS - 1), r_move, value)
            made[turn][group // 2] = jnp.where(lanes == at + ROWS - 1, end, value)
    for turn, send in enumerate(sends):
        top = even("gz") == (turn == 0)
        value = made[turn][groups // 2][:ny]
        for plane in range(nx):
            at = press_lane(plane)
            moved = pltpu.roll(press[plane], jnp.where(top, (at + 1) % LANES, at), 1)
            value = jnp.where(lanes[:ny] == at, moved, value)
        made[turn][groups // 2] = jnp.concatenate([value, made[turn][groups // 2][ny:]], 0)
        for which, value in enumerate(made[turn]):
            send[which] = value


def prepare(nx, ny, n_x, n_y, coef, vel, rhs, full_coef, full_rhs, *refs):
    got_x, got_y = refs[:n_x], refs[n_x : n_x + n_y]
    wx, wy, wz, diag_out, ends = refs[n_x + n_y :]
    total, height = nx + 2 * DEPTH, ny + 2 * DEPTH
    groups = total // ROWS
    lanes = lane_index((height, LANES))
    block = Block(nx, ny, coef, vel, rhs, got_x)
    tile_end = tile_of_ends(nx, even("gy"), got_y)
    for group in range(groups):
        made = [jnp.zeros((height, LANES), jnp.float32) for _ in range(3)]
        for seat in range(ROWS):
            plane = seat * groups + group
            at = GROUP * seat
            upper = (lanes >= at) & (lanes < at + DEPTH)
            lower = (lanes >= at + 3 * DEPTH) & (lanes < at + GROUP)
            for which, source in enumerate((full_coef[plane], full_rhs[plane])):
                value = jnp.where(upper, roll_lanes(source, at + DEPTH), made[which])
                made[which] = jnp.where(lower, roll_lanes(source, at + 3 * DEPTH), value)
            end = tall_end(block, tile_end, plane, at + DEPTH - 1)
            made[2] = jnp.where(lanes == at + DEPTH - 1, end, made[2])
        for which in range(3):
            ends[which, group] = made[which]
    old_weight = None
    here = full_coef[nx + DEPTH]
    for x in range(-DEPTH, nx + DEPTH - 1):
        e = x % total
        above = full_coef[(e + 1) % total]
        weight = 0.5 * (here + above)
        wx[e] = weight
        if x > -DEPTH:
            up, down = 0.5 * (here + roll_rows(here, -1)), 0.5 * (here + roll_rows(here, 1))
            right = jnp.where(lanes == LANES - 1, 0.0, 0.5 * (here + roll_lanes(here, -1)))
            left = jnp.where(lanes == 0, 0.0, 0.5 * (here + roll_lanes(here, 1)))
            wy[0, e], wy[1, e], wz[0, e], wz[1, e] = up, down, right, left
            diag_out[e] = jnp.where(here > 0, (weight + old_weight) + (up + down) + (right + left), 0.0)
        old_weight, here = weight, above


def tree_sum(parts):
    while len(parts) > 1:
        parts = [parts[i] + parts[i + 1] if i + 1 < len(parts) else parts[i] for i in range(0, len(parts), 2)]
    return parts[0]


class Totals:
    def __init__(self):
        self.stack = []

    def add(self, tile):
        level = 0
        while self.stack and self.stack[-1][0] == level:
            tile = self.stack.pop()[1] + tile
            level += 1
        self.stack.append((level, tile))

    def value(self):
        tiles = [tile for _, tile in self.stack]
        total = tiles.pop()
        while tiles:
            total = tiles.pop() + total
        return total


def krylov(nx, ny, n_z, wx, wy, wz, diag_in, rhs_in, ends, *refs):
    got_z = refs[:n_z]
    basis, basis_z, sums = refs[n_z : n_z + 3]
    inverse, pw, pinv, spill = refs[n_z + 3 :]
    even_z = even("gz")
    total, height = nx + 2 * DEPTH, ny + 2 * DEPTH
    groups = total // ROWS
    lanes = lane_index((height, LANES))
    seat_lane = lanes % GROUP
    edge = (lanes == 0) | (lanes == LANES - 1)

    def along(planes, group, step):
        if 0 <= group + step < groups:
            return planes[group + step]
        return roll_lanes(planes[(group + step) % groups], -GROUP * step)

    def spilled(which, group, up, down):
        spill[which, group] = jnp.where(seat_lane == 10, roll_lanes(up, 7), down)

    coef, rhs_z, vz = [], [], []
    for g in range(groups):
        low, high = sides(even_z, got_z, lambda ref: ref[g // 2])
        skip = ROWS * (g % 2)
        above = (seat_lane >= DEPTH) & (seat_lane < 2 * DEPTH)
        below = (seat_lane >= 2 * DEPTH) & (seat_lane < 3 * DEPTH)
        value = jnp.where(above, roll_lanes(high, DEPTH - skip), ends[0, g])
        coef.append(jnp.where(below, roll_lanes(low, 2 * DEPTH - skip), value))
        value = jnp.where(above, roll_lanes(high, -skip), ends[1, g])
        rhs_z.append(jnp.where(below, roll_lanes(low, DEPTH + 1 - skip), value))
        vz.append(jnp.where(below, roll_lanes(low, DEPTH - skip), ends[2, g]))
    for g in range(groups):
        here = coef[g]
        neighbours = (along(coef, g, 1), along(coef, g, -1), roll_rows(here, -1), roll_rows(here, 1))
        neighbours += (roll_lanes(here, -1), roll_lanes(here, 1))
        weights = [0.5 * (here + other) for other in neighbours]
        for which, weight in enumerate(weights):
            pw[which, g] = weight
        diag = (weights[0] + weights[1]) + (weights[2] + weights[3]) + (weights[4] + weights[5])
        face = (seat_lane == DEPTH - 1) | (seat_lane == 3 * DEPTH - 1)
        next_face = (seat_lane == DEPTH) | (seat_lane == 3 * DEPTH)
        fz = weights[4] * vz[g]
        spilled(0, g, weights[4], weights[4])
        spilled(1, g, fz, -fz)
        rhs = rhs_z[g] + jnp.where(face, fz, 0.0)
        rhs = rhs - jnp.where(next_face, weights[5] * roll_lanes(vz[g], 1), 0.0)
        inside = here > 0
        scale = jnp.where(inside, 1.0 / jnp.where(inside, diag, 1.0), 0.0)
        pinv[g] = scale
        basis_z[0, g] = scale * rhs
        basis_z[3, g] = vz[g]
    for n in range(3):
        field = [basis_z[n, g] for g in range(groups)]
        for g in range(groups):
            here = field[g]
            fz = pw[4, g] * (roll_lanes(here, -1) - here)
            spilled(2 + n, g, -fz, fz)
            if n < 2:
                image = pw[0, g] * (here - along(field, g, 1)) + pw[1, g] * (here - along(field, g, -1))
                image = image + (pw[2, g] * (here - roll_rows(here, -1)) + pw[3, g] * (here - roll_rows(here, 1)))
                image = image + (pw[5, g] * (here - roll_lanes(here, 1)) - fz)
                basis_z[n + 1, g] = pinv[g] * image

    def inject(which, plane):
        group, seat = plane % groups, plane // groups
        return jnp.where(edge, roll_lanes(spill[which, group], LANES - 1 - 10 - GROUP * seat), 0.0)

    totals = [Totals() for _ in range(6)]

    def count(which, left, right):
        product = left[:ny] * right[:ny]
        totals[which].add(tree_sum([product[i : i + ROWS] for i in range(0, ny, ROWS)]))

    for x in range(-DEPTH + 1, nx + DEPTH - 1):
        e = x % total
        diag, rhs = diag_in[e], rhs_in[e] + inject(1, e)
        inside = diag > 0
        scale = jnp.where(inside, 1.0 / jnp.where(inside, diag + inject(0, e), 1.0), 0.0)
        inverse[e] = scale
        field = scale * rhs
        basis[0, e] = field
        if 0 <= x < nx:
            count(0, field, rhs)
    for n in range(3):
        reach = 2 - n
        old_flux = None
        here = basis[n, (-reach - 1) % total]
        for x in range(-reach - 1, nx + reach):
            e = x % total
            above = basis[n, (e + 1) % total]
            flux = wx[e] * (above - here)
            if x >= -reach:
                image = (old_flux - flux) + inject(2 + n, e)
                image = image + (
                    wy[0, e] * (here - roll_rows(here, -1)) + wy[1, e] * (here - roll_rows(here, 1))
                )
                image = image + (
                    wz[0, e] * (here - roll_lanes(here, -1)) + wz[1, e] * (here - roll_lanes(here, 1))
                )
                own = 0 <= x < nx
                if own:
                    count(2 * n + 1, here, image)
                if n < 2:
                    following = inverse[e] * image
                    basis[n + 1, e] = following
                    if own:
                        count(2 * n + 2, following, image)
            old_flux, here = flux, above
    lane = lane_index((1, LANES))
    row = jnp.zeros((1, LANES), jnp.float32)
    for which, total_ in enumerate(totals):
        value = jnp.sum(jnp.sum(total_.value(), 0, keepdims=True), 1, keepdims=True)
        row = jnp.where(lane == which, value, row)
    sums[...] = row


def finish(nx, ny, n_x, n_y, n_z, gathered, press, vel, basis, basis_z, *refs):
    got_x, got_y, got_z = refs[:n_x], refs[n_x : n_x + n_y], refs[n_x + n_y : n_x + n_y + n_z]
    ustar_out, coef_out, ustar, coef_cot, sem = refs[n_x + n_y + n_z :]
    even_x, even_y, even_z = even("gx"), even("gy"), even("gz")
    total, height = nx + 2 * DEPTH, ny + 2 * DEPTH
    groups = total // ROWS
    parts = gathered[...]
    while parts.shape[0] > ROWS:
        half = parts.shape[0] // 2
        parts = parts[:half] + parts[half:]
    sums = jnp.sum(parts, 0, keepdims=True)
    lane = lane_index((1, LANES))
    m0, m1, m2, m3, m4, m5 = [
        jnp.sum(jnp.where(lane == which, sums, 0.0), 1, keepdims=True) for which in range(6)
    ]
    l1, l2 = m2 / m1, m3 / m1
    d1, cross, d2 = m3 - l1 * m2, m4 - l1 * m3, m5 - l2 * m3
    l21 = cross / d1
    d2 = d2 - l21 * cross
    y1 = -l1 * m0 + m1
    y2 = m2 - l2 * m0 - l21 * y1
    c2 = y2 / d2
    c1 = y1 / d1 - l21 * c2
    c0 = (m0 / m1 - l1 * c1 - l2 * c2)[0, 0]
    c1, c2 = c1[0, 0], c2[0, 0]

    lanes = lane_index((height, LANES))
    seat_lane = lanes % GROUP
    spill = []
    for g in range(groups):
        cells = c0 * basis_z[0, g] + c1 * basis_z[1, g] + c2 * basis_z[2, g]
        spill.append(jnp.where(seat_lane == 10, roll_lanes(cells, 6), cells))
    lanes = lane_index((ny, LANES))
    at_low, at_high = lanes == 0, lanes == LANES - 1
    low_z, high_z = sides(even_z, got_z, lambda ref: ref[groups // 2, :ny, :])
    press_z = jnp.where(lanes % 2 == 0, high_z, roll_lanes(low_z, 1))
    p_low, p_high = sides(even_x, got_x, lambda ref: ref[PRESS * ny : (PRESS + 1) * ny, :])
    u_low, _ = sides(even_x, got_x, lambda ref: ref[VX * ny : (VX + 1) * ny, :])

    def solved(x):
        e = x % total
        return c0 * basis[0, e] + c1 * basis[1, e] + c2 * basis[2, e]

    copies = []
    rows = row_index((ROWS, LANES))
    below, here = solved(-1), solved(0)
    face_low = (p_low - press[0]) * (u_low + here[:ny] - below[:ny])
    for x in range(nx):
        above = solved(x + 1)
        group, seat = x % groups, x // groups
        own, p = here[:ny], press[x]
        out = vel[0, x] + (above[:ny] - own)
        ustar[0, x] = out
        face = (p - (press[x + 1] if x + 1 < nx else p_high)) * out
        answer = face_low + face
        face_low = face
        low, high = sides(even_y, got_y, lambda ref: ref[total + x // ROWS, x % ROWS : x % ROWS + 1, :])
        shape = (ROWS, LANES)
        p_tile = jnp.where(rows == 0, jnp.broadcast_to(high, shape), jnp.broadcast_to(low, shape))
        p_tall = jnp.concatenate([p, p_tile], 0)
        u_row, _ = sides(even_y, got_y, lambda ref: ref[x, ROWS - 1 :, :])
        u_tall = jnp.concatenate([vel[1, x], jnp.broadcast_to(u_row, shape)], 0)
        out = vel[1, x] + (roll_rows(here, -1)[:ny] - own)
        ustar[1, x] = out
        back = roll_rows(u_tall, 1)[:ny] + (own - roll_rows(here, 1)[:ny])
        answer = answer + ((p - roll_rows(p_tall, -1)[:ny]) * out + (roll_rows(p_tall, 1)[:ny] - p) * back)
        shift = LANES - 1 - 10 - GROUP * seat
        lam_end = roll_lanes(spill[group][:ny], shift)
        u_end = roll_lanes(basis_z[3, group, :ny, :], shift)
        p_end = roll_lanes(press_z, LANES - 1 - press_lane(x))
        out = vel[2, x] + (jnp.where(at_high, lam_end, roll_lanes(own, -1)) - own)
        ustar[2, x] = out
        answer = answer + (p - jnp.where(at_high, p_end, roll_lanes(p, -1))) * out
        back = jnp.where(at_low, u_end, roll_lanes(vel[2, x], 1))
        back = back + (own - jnp.where(at_low, lam_end, roll_lanes(own, 1)))
        answer = answer + (jnp.where(at_low, p_end, roll_lanes(p, 1)) - p) * back
        coef_cot[x] = 0.5 * answer
        here = above
        if (x + 1) % STRIDE == 0:
            part = pl.ds(x + 1 - STRIDE, STRIDE)
            for which, (src, dst) in enumerate(
                ((ustar.at[:, part], ustar_out.at[:, part]), (coef_cot.at[part], coef_out.at[part]))
            ):
                copies.append(pltpu.make_async_copy(src, dst, sem.at[which, x // STRIDE]))
                copies[-1].start()
    for copy in copies:
        copy.wait()


def on_device(phase, press, vel):
    nx, ny, nz = phase.shape
    total, height = nx + 2 * DEPTH, ny + 2 * DEPTH
    groups = total // ROWS
    devices = lax.axis_size(AXES)
    n_x, n_y, n_z = (turns(axis) for axis in AXES)
    f32 = lambda *shape: jax.ShapeDtypeStruct(shape, jnp.float32)
    scratch = lambda *shape: pltpu.VMEM(shape, jnp.float32)
    inputs = [pltpu.with_memory_space_constraint(array, pltpu.HBM) for array in (phase, press, vel)]

    def call(kernel, args, in_specs, shapes, name, scratch_shapes=(), out_spec=VMEM):
        return pl.pallas_call(
            kernel,
            out_shape=shapes,
            in_specs=in_specs,
            out_specs=[out_spec] * len(shapes),
            scratch_shapes=list(scratch_shapes),
            compiler_params=PARAMS,
            cost_estimate=pl.CostEstimate(flops=3_000_000, bytes_accessed=3_000_000, transcendentals=0),
            name=name,
        )(*args)

    to_x = call(
        functools.partial(pack_x, nx, ny),
        inputs,
        [HBM] * 3,
        [f32(VY * ny + ROWS, nz)] * n_x,
        "pack_x",
        [pltpu.VMEM((n_x, DEPTH, ny, nz), jnp.int32), scratch(n_x, 3, DEPTH, ny, nz)]
        + [pltpu.SemaphoreType.DMA((n_x, 3))],
    )
    got_x = exchange(to_x, "gx")
    coef, press, vel, rhs = call(
        load,
        inputs + [to_x[0]],
        [HBM] * 3 + [ANY],
        [f32(*press.shape), f32(*press.shape), f32(*vel.shape), f32(*press.shape)],
        "load",
        [pltpu.VMEM(phase.shape, jnp.int32), pltpu.SemaphoreType.DMA((3,))],
    )
    to_y = call(
        functools.partial(pack_y, nx, ny, n_x),
        [coef, press, vel, rhs, *got_x],
        [VMEM] * (4 + n_x),
        [f32(total + nx // ROWS + 1, ROWS, nz)] * n_y,
        "pack_y",
    )
    got_y = exchange(to_y, "gy")
    cube = (total, height, nz)
    full_coef, full_rhs, *to_z = call(
        functools.partial(pack_z, nx, ny, n_x, n_y, n_z),
        [coef, press, vel, rhs, *got_x, *got_y],
        [VMEM] * (4 + n_x + n_y),
        [f32(*cube)] * 2 + [f32(groups // 2 + 1, height, LANES)] * n_z,
        "pack_z",
    )
    got_z = exchange(to_z, "gz")
    wx, wy, wz, diag, ends = call(
        functools.partial(prepare, nx, ny, n_x, n_y),
        [coef, vel, rhs, full_coef, full_rhs, *got_x, *got_y],
        [VMEM] * (5 + n_x + n_y),
        [f32(*cube), f32(2, *cube), f32(2, *cube), f32(*cube), f32(3, groups, height, LANES)],
        "prepare",
    )
    basis, basis_z, sums = call(
        functools.partial(krylov, nx, ny, n_z),
        [wx, wy, wz, diag, full_rhs, ends, *got_z],
        [VMEM] * (6 + n_z),
        [f32(3, *cube), f32(4, groups, height, LANES), f32(1, LANES)],
        "krylov",
        [scratch(*cube), scratch(6, groups, height, LANES), scratch(groups, height, LANES)]
        + [scratch(5, groups, height, LANES)],
    )
    spread = jnp.broadcast_to(sums[None], (devices, 1, LANES))
    gathered = lax.all_to_all(spread, AXES, 0, 0).reshape(devices, LANES)
    return call(
        functools.partial(finish, nx, ny, n_x, n_y, n_z),
        [gathered, press, vel, basis, basis_z, *got_x, *got_y, *got_z],
        [VMEM] * (5 + n_x + n_y + n_z),
        [f32(*vel.shape), f32(nx, ny, nz)],
        "finish",
        [scratch(*vel.shape), scratch(nx, ny, nz), pltpu.SemaphoreType.DMA((2, nx // STRIDE))],
        HBM,
    )


def solution(mesh):
    cells, faces = P(*AXES), P(None, *AXES)
    return jax.shard_map(
        on_device, mesh=mesh, in_specs=(cells, cells, faces), out_specs=(faces, cells), check_vma=False
    )
```

```python
import functools
import itertools

import jax
import jax.numpy as jnp
from jax import lax
from jax.experimental import pallas as pl
from jax.experimental.pallas import tpu as pltpu
from jax.sharding import PartitionSpec as P

AXES = ("gx", "gy", "gz")
SPARE = dict(gx="gy", gy="gz", gz="gx")
DEPTH = 4
GROUP = 4 * DEPTH
LANES = 128
STRIDE = 4
ROWS = 8
VMEM = pl.BlockSpec(memory_space=pltpu.VMEM)
HBM = pl.BlockSpec(memory_space=pltpu.HBM)
ANY = pl.BlockSpec(memory_space=pl.ANY)
PARAMS = pltpu.CompilerParams(vmem_limit_bytes=40 * 1024 * 1024)


def swaps(axis, turn):
    sizes = [lax.axis_size(name) for name in AXES]
    along, spare = AXES.index(axis), AXES.index(SPARE[axis])
    number = lambda place: (place[0] * sizes[1] + place[1]) * sizes[2] + place[2]
    pairs = []
    for place in itertools.product(*map(range, sizes)):
        partner = list(place)
        other = place[along] + (1 if (place[along] - turn) % 2 == 0 else -1)
        if 0 <= other < sizes[along]:
            partner[along] = other
        elif sizes[spare] % 2 == 0:
            partner[spare] ^= 1
        else:
            continue
        pairs.append((number(place), number(partner)))
    return pairs


def exchange(sends, axis):
    return [lax.ppermute(send, AXES, swaps(axis, turn)) for turn, send in enumerate(sends)]


def clear_if_alone(axis, turn, out):
    count, place = lax.axis_size(axis), lax.axis_index(axis)
    alone = []
    if turn == 1:
        alone.append(place == 0)
    if count % 2 != turn:
        alone.append(place == count - 1)
    for case in alone:

        @pl.when(case)
        def _():
            out[...] = jnp.zeros(out.shape, out.dtype)


def even(axis):
    return lax.axis_index(axis) % 2 == 0


def turns(axis):
    return min(2, lax.axis_size(axis) - 1)


def coefficient(phase):
    return jnp.where(phase == 0, 8.0, jnp.where(phase == 1, 1.0, 2.0)).astype(jnp.float32)


def sides(is_even, got, load):
    one = load(got[0])
    two = load(got[1]) if len(got) > 1 else jnp.zeros_like(one)
    return jnp.where(is_even, two, one), jnp.where(is_even, one, two)


def lane_index(shape):
    return lax.broadcasted_iota(jnp.int32, shape, len(shape) - 1)


def row_index(shape):
    return lax.broadcasted_iota(jnp.int32, shape, len(shape) - 2)


def roll_rows(plane, shift):
    return pltpu.roll(plane, shift % plane.shape[0], 0)


def roll_lanes(plane, shift):
    return pltpu.roll(plane, shift % plane.shape[1], 1)


def inner_rhs(coef, vy, vz):
    rows, lanes = row_index(coef.shape), lane_index(coef.shape)
    up = jnp.where(rows == coef.shape[0] - 1, 0.0, 0.5 * (coef + roll_rows(coef, -1)))
    down = jnp.where(rows == 0, 0.0, 0.5 * (coef + roll_rows(coef, 1)))
    right = jnp.where(lanes == LANES - 1, 0.0, 0.5 * (coef + roll_lanes(coef, -1)))
    left = jnp.where(lanes == 0, 0.0, 0.5 * (coef + roll_lanes(coef, 1)))
    return (up * vy - down * roll_rows(vy, 1)) + (right * vz - left * roll_lanes(vz, 1))


RHS, VX, PRESS, VY = DEPTH, 2 * DEPTH - 1, 2 * DEPTH, 2 * DEPTH + 1


def pack_x(nx, ny, phase, press, vel, *refs):
    count = len(refs) - 3
    outs = refs[:count]
    held, held_vel, sem = refs[count:]
    copies = []
    for turn, out in enumerate(outs):
        top = even("gx") == (turn == 0)
        deep = jnp.where(top, nx - DEPTH, 0)
        last = jnp.where(top, nx - 1, 0)
        parts = [
            (vel.at[:, pl.ds(deep, DEPTH)], held_vel.at[turn]),
            (phase.at[pl.ds(deep, DEPTH)], held.at[turn]),
            (press.at[last], out.at[pl.ds(PRESS * ny, ny)]),
        ]
        for which, (src, dst) in enumerate(parts):
            copy = pltpu.make_async_copy(src, dst, sem.at[turn, which])
            copy.start()
            copies.append(copy)
    for copy in copies:
        copy.wait()
    lanes = lane_index((ROWS, LANES))
    rows = row_index((ROWS, LANES))
    for turn, out in enumerate(outs):
        top = even("gx") == (turn == 0)
        coefs = [coefficient(held[turn, j]) for j in range(DEPTH)]
        flux = [0.5 * (coefs[j] + coefs[j + 1]) * held_vel[turn, 0, j] for j in range(DEPTH - 1)]
        columns = jnp.zeros((ROWS, LANES), jnp.float32)
        lines = jnp.zeros((ROWS, LANES), jnp.float32)
        for j in range(DEPTH):
            out[j * ny : (j + 1) * ny, :] = coefs[j]
        for j in range(DEPTH - 1):
            vy = jnp.where(top, held_vel[turn, 1, j + 1], held_vel[turn, 1, j])
            vz = jnp.where(top, held_vel[turn, 2, j + 1], held_vel[turn, 2, j])
            upper = (flux[j + 1] - flux[j]) if j + 1 < DEPTH - 1 else -flux[j]
            lower = (flux[j] - flux[j - 1]) if j else flux[j]
            inner = inner_rhs(jnp.where(top, coefs[j + 1], coefs[j]), vy, vz)
            out[(RHS + j) * ny : (RHS + j + 1) * ny, :] = jnp.where(top, upper, lower) + inner
            for t in range(ny // ROWS):
                lane = DEPTH * t + j
                columns = jnp.where(lanes == lane, roll_lanes(vz[t * ROWS : (t + 1) * ROWS], lane + 1), columns)
            lines = jnp.where(rows == j, roll_rows(vy[ny - ROWS :], j + 1), lines)
        out[VX * ny : (VX + 1) * ny, :] = held_vel[turn, 0, DEPTH - 1]
        out[VY * ny : VY * ny + ROWS, :] = lines
        out[VY * ny + ROWS :, :] = columns
        clear_if_alone("gx", turn, out)


def load(phase, press, vel, after, coef, press_out, vel_out, rhs, held, sem):
    del after
    copies = []
    for which, (src, dst) in enumerate(((phase, held), (press, press_out), (vel, vel_out))):
        copies.append(pltpu.make_async_copy(src, dst, sem.at[which]))
        copies[-1].start()
    copies[0].wait()
    copies[1].wait()
    copies[2].wait()
    nx = coef.shape[0]
    here = coefficient(held[0])
    old_flux = None
    for x in range(nx):
        coef[x] = here
        answer = inner_rhs(here, vel_out[1, x], vel_out[2, x])
        if old_flux is not None:
            answer = answer - old_flux
        if x + 1 < nx:
            above = coefficient(held[x + 1])
            old_flux = 0.5 * (here + above) * vel_out[0, x]
            answer = answer + old_flux
            here = above
        rhs[x] = answer


class Block:
    def __init__(self, nx, ny, coef, vel, rhs, got_x, row=0, height=None):
        self.nx, self.ny = nx, ny
        self.own_coef, self.vel, self.own_rhs, self.got_x = coef, vel, rhs, got_x
        self.even = even("gx")
        self.row, self.height = row, height or ny
        self.low_face = 0.5 * (self.coef(nx + 2 * DEPTH - 1) + self.coef(0)) * self.halo(VX)[0]
        self.high_face = 0.5 * (self.coef(nx - 1) + self.coef(nx)) * self.take(vel, 0, nx - 1)

    def take(self, ref, *index):
        return ref[(*index, pl.ds(self.row, self.height), slice(None))]

    def halo(self, part):
        return sides(self.even, self.got_x, lambda ref: ref[pl.ds(part * self.ny + self.row, self.height), :])

    def coef(self, plane):
        if plane < self.nx:
            return self.take(self.own_coef, plane)
        above = plane < self.nx + DEPTH
        return self.halo((plane - self.nx) % DEPTH)[1 if above else 0]

    def rhs(self, plane):
        nx = self.nx
        if plane < nx:
            answer = self.take(self.own_rhs, plane)
        else:
            above = plane < nx + DEPTH
            layer = plane - nx if above else plane - nx - DEPTH - 1
            if layer < 0 or layer >= DEPTH - 1:
                return jnp.zeros((self.height, LANES), jnp.float32)
            answer = self.halo(RHS + layer)[1 if above else 0]
        if plane == 0:
            answer = answer - self.low_face
        if plane == nx + 2 * DEPTH - 1:
            answer = answer + self.low_face
        if plane == nx - 1:
            answer = answer + self.high_face
        if plane == nx:
            answer = answer - self.high_face
        return answer

    def layer(self, plane):
        if plane < self.nx + DEPTH:
            place = (1, plane - self.nx)
        else:
            place = (0, plane - self.nx - DEPTH - 1)
        return place if 0 <= place[1] < DEPTH - 1 else None

    def columns(self):
        at = VY * self.ny + ROWS
        return sides(self.even, self.got_x, lambda ref: ref[at : at + ROWS, :])

    def vz_end(self, plane, lane):
        if plane < self.nx:
            return roll_lanes(self.vel[2, plane], lane + 1)
        place = self.layer(plane)
        if place is None:
            return jnp.zeros((self.ny, LANES), jnp.float32)
        source = self.columns()[place[0]]
        return jnp.concatenate(
            [roll_lanes(source, lane - DEPTH * t - place[1]) for t in range(self.ny // ROWS)], 0
        )

    def vy_end(self, plane):
        if plane < self.nx:
            return self.vel[1, plane, self.ny - 1 :, :]
        place = self.layer(plane)
        if place is None:
            return jnp.zeros((1, LANES), jnp.float32)
        at = VY * self.ny + place[1]
        return sides(self.even, self.got_x, lambda ref: ref[at : at + 1, :])[place[0]]


def pack_y(nx, ny, n_x, coef, press, vel, rhs, *refs):
    got_x, outs = refs[:n_x], refs[n_x:]
    total = nx + 2 * DEPTH
    rows, lanes = row_index((ROWS, LANES)), lane_index((ROWS, LANES))
    for turn, out in enumerate(outs):
        top = even("gy") == (turn == 0)
        row = pl.multiple_of(jnp.where(top, ny - ROWS, 0), ROWS)
        block = Block(nx, ny, coef, vel, rhs, got_x, row, ROWS)
        columns = jnp.zeros((ROWS, LANES), jnp.float32)
        ends = block.columns()
        for plane in range(total):
            one, two = block.coef(plane), block.rhs(plane)
            one = jnp.where(top, roll_rows(one, DEPTH), one)
            two = jnp.where(top, roll_rows(two, -1), roll_rows(two, DEPTH))
            tile = jnp.where(rows < DEPTH, one, two)
            out[plane] = jnp.where(rows == ROWS - 1, block.vy_end(plane), tile)
            if plane < nx:
                source = roll_lanes(vel[2, plane, pl.ds(row, ROWS), :], plane + 1)
            elif block.layer(plane) is None:
                continue
            else:
                side, layer = block.layer(plane)
                high = (plane - layer - DEPTH * (ny // ROWS - 1)) % LANES
                source = pltpu.roll(ends[side], jnp.where(top, high, (plane - layer) % LANES), 1)
            columns = jnp.where(lanes == plane, source, columns)
        out[total + nx // ROWS] = jnp.where(top, roll_rows(columns, DEPTH - 1), columns)
        for plane in range(nx):
            tile = press[plane, pl.ds(row, ROWS), :]
            edge = jnp.where(top, tile[ROWS - 1 : ROWS], tile[0:1])
            out[total + plane // ROWS, plane % ROWS : plane % ROWS + 1, :] = edge
        clear_if_alone("gy", turn, out)


def tall_end(block, tile_end, plane, lane):
    return jnp.concatenate([block.vz_end(plane, lane), roll_lanes(tile_end, lane - plane)], 0)


def tile_of_ends(nx, even_y, got_y):
    rows = row_index((ROWS, LANES))
    low, high = sides(even_y, got_y, lambda ref: ref[nx + 2 * DEPTH + nx // ROWS])
    return jnp.where(rows < DEPTH, high, roll_rows(low, DEPTH + 1))


def press_lane(x):
    return GROUP * (x % ROWS) + ROWS + 2 * (x // ROWS)


def pack_z(nx, ny, n_x, n_y, n_z, coef, press, vel, rhs, *refs):
    got_x, got_y = refs[:n_x], refs[n_x : n_x + n_y]
    full_coef, full_rhs, *sends = refs[n_x + n_y :]
    total, height = nx + 2 * DEPTH, ny + 2 * DEPTH
    groups = total // ROWS
    even_y = even("gy")
    rows = row_index((ROWS, LANES))
    lanes = lane_index((height, LANES))
    block = Block(nx, ny, coef, vel, rhs, got_x)
    tile_end = tile_of_ends(nx, even_y, got_y)
    parts = [jnp.zeros((height, LANES), jnp.float32) for _ in range(groups // 2 + 1)]
    made = [list(parts) for _ in sends]
    for plane in range(total):
        low, high = sides(even_y, got_y, lambda ref: ref[plane])
        c_own, c_tile = block.coef(plane), jnp.where(rows < DEPTH, high, roll_rows(low, DEPTH))
        r_own, r_tile = block.rhs(plane), jnp.where(rows < DEPTH, roll_rows(high, -DEPTH), roll_rows(low, 1))
        up = 0.5 * (c_own[ny - 1 :] + c_tile[:1]) * block.vy_end(plane)
        down = 0.5 * (c_tile[ROWS - 1 :] + c_own[:1]) * low[ROWS - 1 :]
        first, last = r_own[:ROWS], r_own[ny - ROWS :]
        r_tile = jnp.where(rows == 0, r_tile - up, jnp.where(rows == ROWS - 1, r_tile + down, r_tile))
        middle = [r_own[ROWS : ny - ROWS]] if ny > 2 * ROWS else []
        if ny > ROWS:
            first = jnp.where(rows == 0, first - down, first)
            last = jnp.where(rows == ROWS - 1, last + up, last)
            r_all = jnp.concatenate([first] + middle + [last, r_tile], 0)
        else:
            only = jnp.where(rows == 0, first - down, jnp.where(rows == ROWS - 1, first + up, first))
            r_all = jnp.concatenate([only, r_tile], 0)
        c_all = jnp.concatenate([c_own, c_tile], 0)
        full_coef[plane], full_rhs[plane] = c_all, r_all
        group, seat = plane % groups, plane // groups
        at = GROUP * seat + ROWS * (group % 2)
        end = tall_end(block, tile_end, plane, at + ROWS - 1)
        for turn in range(len(sends)):
            top = even("gz") == (turn == 0)
            c_move = pltpu.roll(c_all, jnp.where(top, (at + DEPTH) % LANES, at), 1)
            r_move = pltpu.roll(r_all, jnp.where(top, (at + ROWS - 1) % LANES, at + DEPTH), 1)
            value = made[turn][group // 2]
            value = jnp.where((lanes >= at) & (lanes < at + DEPTH), c_move, value)
            value = jnp.where((lanes >= at + DEPTH) & (lanes < at + ROWS - 1), r_move, value)
            made[turn][group // 2] = jnp.where(lanes == at + ROWS - 1, end, value)
    for turn, send in enumerate(sends):
        top = even("gz") == (turn == 0)
        value = made[turn][groups // 2][:ny]
        for plane in range(nx):
            at = press_lane(plane)
            moved = pltpu.roll(press[plane], jnp.where(top, (at + 1) % LANES, at), 1)
            value = jnp.where(lanes[:ny] == at, moved, value)
        made[turn][groups // 2] = jnp.concatenate([value, made[turn][groups // 2][ny:]], 0)
        for which, value in enumerate(made[turn]):
            send[which] = value
        clear_if_alone("gz", turn, send)


def prepare(nx, ny, n_x, n_y, coef, vel, rhs, full_coef, full_rhs, *refs):
    got_x, got_y = refs[:n_x], refs[n_x : n_x + n_y]
    wx, wy, wz, diag_out, ends = refs[n_x + n_y :]
    total, height = nx + 2 * DEPTH, ny + 2 * DEPTH
    groups = total // ROWS
    lanes = lane_index((height, LANES))
    block = Block(nx, ny, coef, vel, rhs, got_x)
    tile_end = tile_of_ends(nx, even("gy"), got_y)
    for group in range(groups):
        made = [jnp.zeros((height, LANES), jnp.float32) for _ in range(3)]
        for seat in range(ROWS):
            plane = seat * groups + group
            at = GROUP * seat
            upper = (lanes >= at) & (lanes < at + DEPTH)
            lower = (lanes >= at + 3 * DEPTH) & (lanes < at + GROUP)
            for which, source in enumerate((full_coef[plane], full_rhs[plane])):
                value = jnp.where(upper, roll_lanes(source, at + DEPTH), made[which])
                made[which] = jnp.where(lower, roll_lanes(source, at + 3 * DEPTH), value)
            end = tall_end(block, tile_end, plane, at + DEPTH - 1)
            made[2] = jnp.where(lanes == at + DEPTH - 1, end, made[2])
        for which in range(3):
            ends[which, group] = made[which]
    old_weight = None
    here = full_coef[nx + DEPTH]
    for x in range(-DEPTH, nx + DEPTH - 1):
        e = x % total
        above = full_coef[(e + 1) % total]
        weight = 0.5 * (here + above)
        wx[e] = weight
        if x > -DEPTH:
            up, down = 0.5 * (here + roll_rows(here, -1)), 0.5 * (here + roll_rows(here, 1))
            right = jnp.where(lanes == LANES - 1, 0.0, 0.5 * (here + roll_lanes(here, -1)))
            left = jnp.where(lanes == 0, 0.0, 0.5 * (here + roll_lanes(here, 1)))
            wy[0, e], wy[1, e], wz[0, e], wz[1, e] = up, down, right, left
            diag_out[e] = jnp.where(here > 0, (weight + old_weight) + (up + down) + (right + left), 0.0)
        old_weight, here = weight, above


def tree_sum(parts):
    while len(parts) > 1:
        parts = [parts[i] + parts[i + 1] if i + 1 < len(parts) else parts[i] for i in range(0, len(parts), 2)]
    return parts[0]


class Totals:
    def __init__(self):
        self.stack = []

    def add(self, tile):
        level = 0
        while self.stack and self.stack[-1][0] == level:
            tile = self.stack.pop()[1] + tile
            level += 1
        self.stack.append((level, tile))

    def value(self):
        tiles = [tile for _, tile in self.stack]
        total = tiles.pop()
        while tiles:
            total = tiles.pop() + total
        return total


def krylov(nx, ny, n_z, wx, wy, wz, diag_in, rhs_in, ends, *refs):
    got_z = refs[:n_z]
    basis, basis_z, sums = refs[n_z : n_z + 3]
    inverse, pw, pinv, spill = refs[n_z + 3 :]
    even_z = even("gz")
    total, height = nx + 2 * DEPTH, ny + 2 * DEPTH
    groups = total // ROWS
    lanes = lane_index((height, LANES))
    seat_lane = lanes % GROUP
    edge = (lanes == 0) | (lanes == LANES - 1)

    def along(planes, group, step):
        if 0 <= group + step < groups:
            return planes[group + step]
        return roll_lanes(planes[(group + step) % groups], -GROUP * step)

    def spilled(which, group, up, down):
        spill[which, group] = jnp.where(seat_lane == 10, roll_lanes(up, 7), down)

    coef, rhs_z, vz = [], [], []
    for g in range(groups):
        low, high = sides(even_z, got_z, lambda ref: ref[g // 2])
        skip = ROWS * (g % 2)
        above = (seat_lane >= DEPTH) & (seat_lane < 2 * DEPTH)
        below = (seat_lane >= 2 * DEPTH) & (seat_lane < 3 * DEPTH)
        value = jnp.where(above, roll_lanes(high, DEPTH - skip), ends[0, g])
        coef.append(jnp.where(below, roll_lanes(low, 2 * DEPTH - skip), value))
        value = jnp.where(above, roll_lanes(high, -skip), ends[1, g])
        rhs_z.append(jnp.where(below, roll_lanes(low, DEPTH + 1 - skip), value))
        vz.append(jnp.where(below, roll_lanes(low, DEPTH - skip), ends[2, g]))
    for g in range(groups):
        here = coef[g]
        neighbours = (along(coef, g, 1), along(coef, g, -1), roll_rows(here, -1), roll_rows(here, 1))
        neighbours += (roll_lanes(here, -1), roll_lanes(here, 1))
        weights = [0.5 * (here + other) for other in neighbours]
        for which, weight in enumerate(weights):
            pw[which, g] = weight
        diag = (weights[0] + weights[1]) + (weights[2] + weights[3]) + (weights[4] + weights[5])
        face = (seat_lane == DEPTH - 1) | (seat_lane == 3 * DEPTH - 1)
        next_face = (seat_lane == DEPTH) | (seat_lane == 3 * DEPTH)
        fz = weights[4] * vz[g]
        spilled(0, g, weights[4], weights[4])
        spilled(1, g, fz, -fz)
        rhs = rhs_z[g] + jnp.where(face, fz, 0.0)
        rhs = rhs - jnp.where(next_face, weights[5] * roll_lanes(vz[g], 1), 0.0)
        inside = here > 0
        scale = jnp.where(inside, 1.0 / jnp.where(inside, diag, 1.0), 0.0)
        pinv[g] = scale
        basis_z[0, g] = scale * rhs
        basis_z[3, g] = vz[g]
    for n in range(3):
        field = [basis_z[n, g] for g in range(groups)]
        for g in range(groups):
            here = field[g]
            fz = pw[4, g] * (roll_lanes(here, -1) - here)
            spilled(2 + n, g, -fz, fz)
            if n < 2:
                image = pw[0, g] * (here - along(field, g, 1)) + pw[1, g] * (here - along(field, g, -1))
                image = image + (pw[2, g] * (here - roll_rows(here, -1)) + pw[3, g] * (here - roll_rows(here, 1)))
                image = image + (pw[5, g] * (here - roll_lanes(here, 1)) - fz)
                basis_z[n + 1, g] = pinv[g] * image

    def inject(which, plane):
        group, seat = plane % groups, plane // groups
        return jnp.where(edge, roll_lanes(spill[which, group], LANES - 1 - 10 - GROUP * seat), 0.0)

    totals = [Totals() for _ in range(6)]

    def count(which, left, right):
        product = left[:ny] * right[:ny]
        totals[which].add(tree_sum([product[i : i + ROWS] for i in range(0, ny, ROWS)]))

    for x in range(-DEPTH + 1, nx + DEPTH - 1):
        e = x % total
        diag, rhs = diag_in[e], rhs_in[e] + inject(1, e)
        inside = diag > 0
        scale = jnp.where(inside, 1.0 / jnp.where(inside, diag + inject(0, e), 1.0), 0.0)
        inverse[e] = scale
        field = scale * rhs
        basis[0, e] = field
        if 0 <= x < nx:
            count(0, field, rhs)
    for n in range(3):
        reach = 2 - n
        old_flux = None
        here = basis[n, (-reach - 1) % total]
        for x in range(-reach - 1, nx + reach):
            e = x % total
            above = basis[n, (e + 1) % total]
            flux = wx[e] * (above - here)
            if x >= -reach:
                image = (old_flux - flux) + inject(2 + n, e)
                image = image + (
                    wy[0, e] * (here - roll_rows(here, -1)) + wy[1, e] * (here - roll_rows(here, 1))
                )
                image = image + (
                    wz[0, e] * (here - roll_lanes(here, -1)) + wz[1, e] * (here - roll_lanes(here, 1))
                )
                own = 0 <= x < nx
                if own:
                    count(2 * n + 1, here, image)
                if n < 2:
                    following = inverse[e] * image
                    basis[n + 1, e] = following
                    if own:
                        count(2 * n + 2, following, image)
            old_flux, here = flux, above
    lane = lane_index((1, LANES))
    row = jnp.zeros((1, LANES), jnp.float32)
    for which, total_ in enumerate(totals):
        value = jnp.sum(jnp.sum(total_.value(), 0, keepdims=True), 1, keepdims=True)
        row = jnp.where(lane == which, value, row)
    sums[...] = row


def finish(nx, ny, n_x, n_y, n_z, gathered, press, vel, basis, basis_z, *refs):
    got_x, got_y, got_z = refs[:n_x], refs[n_x : n_x + n_y], refs[n_x + n_y : n_x + n_y + n_z]
    ustar_out, coef_out, ustar, coef_cot, sem = refs[n_x + n_y + n_z :]
    even_x, even_y, even_z = even("gx"), even("gy"), even("gz")
    total, height = nx + 2 * DEPTH, ny + 2 * DEPTH
    groups = total // ROWS
    parts = gathered[...]
    while parts.shape[0] > ROWS:
        half = parts.shape[0] // 2
        parts = parts[:half] + parts[half:]
    sums = jnp.sum(parts, 0, keepdims=True)
    lane = lane_index((1, LANES))
    m0, m1, m2, m3, m4, m5 = [
        jnp.sum(jnp.where(lane == which, sums, 0.0), 1, keepdims=True) for which in range(6)
    ]
    l1, l2 = m2 / m1, m3 / m1
    d1, cross, d2 = m3 - l1 * m2, m4 - l1 * m3, m5 - l2 * m3
    l21 = cross / d1
    d2 = d2 - l21 * cross
    y1 = -l1 * m0 + m1
    y2 = m2 - l2 * m0 - l21 * y1
    c2 = y2 / d2
    c1 = y1 / d1 - l21 * c2
    c0 = (m0 / m1 - l1 * c1 - l2 * c2)[0, 0]
    c1, c2 = c1[0, 0], c2[0, 0]

    lanes = lane_index((height, LANES))
    seat_lane = lanes % GROUP
    spill = []
    for g in range(groups):
        cells = c0 * basis_z[0, g] + c1 * basis_z[1, g] + c2 * basis_z[2, g]
        spill.append(jnp.where(seat_lane == 10, roll_lanes(cells, 6), cells))
    lanes = lane_index((ny, LANES))
    at_low, at_high = lanes == 0, lanes == LANES - 1
    low_z, high_z = sides(even_z, got_z, lambda ref: ref[groups // 2, :ny, :])
    press_z = jnp.where(lanes % 2 == 0, high_z, roll_lanes(low_z, 1))
    p_low, p_high = sides(even_x, got_x, lambda ref: ref[PRESS * ny : (PRESS + 1) * ny, :])
    u_low, _ = sides(even_x, got_x, lambda ref: ref[VX * ny : (VX + 1) * ny, :])

    def solved(x):
        e = x % total
        return c0 * basis[0, e] + c1 * basis[1, e] + c2 * basis[2, e]

    copies = []
    rows = row_index((ROWS, LANES))
    below, here = solved(-1), solved(0)
    face_low = (p_low - press[0]) * (u_low + here[:ny] - below[:ny])
    for x in range(nx):
        above = solved(x + 1)
        group, seat = x % groups, x // groups
        own, p = here[:ny], press[x]
        out = vel[0, x] + (above[:ny] - own)
        ustar[0, x] = out
        face = (p - (press[x + 1] if x + 1 < nx else p_high)) * out
        answer = face_low + face
        face_low = face
        low, high = sides(even_y, got_y, lambda ref: ref[total + x // ROWS, x % ROWS : x % ROWS + 1, :])
        shape = (ROWS, LANES)
        p_tile = jnp.where(rows == 0, jnp.broadcast_to(high, shape), jnp.broadcast_to(low, shape))
        p_tall = jnp.concatenate([p, p_tile], 0)
        u_row, _ = sides(even_y, got_y, lambda ref: ref[x, ROWS - 1 :, :])
        u_tall = jnp.concatenate([vel[1, x], jnp.broadcast_to(u_row, shape)], 0)
        out = vel[1, x] + (roll_rows(here, -1)[:ny] - own)
        ustar[1, x] = out
        back = roll_rows(u_tall, 1)[:ny] + (own - roll_rows(here, 1)[:ny])
        answer = answer + ((p - roll_rows(p_tall, -1)[:ny]) * out + (roll_rows(p_tall, 1)[:ny] - p) * back)
        shift = LANES - 1 - 10 - GROUP * seat
        lam_end = roll_lanes(spill[group][:ny], shift)
        u_end = roll_lanes(basis_z[3, group, :ny, :], shift)
        p_end = roll_lanes(press_z, LANES - 1 - press_lane(x))
        out = vel[2, x] + (jnp.where(at_high, lam_end, roll_lanes(own, -1)) - own)
        ustar[2, x] = out
        answer = answer + (p - jnp.where(at_high, p_end, roll_lanes(p, -1))) * out
        back = jnp.where(at_low, u_end, roll_lanes(vel[2, x], 1))
        back = back + (own - jnp.where(at_low, lam_end, roll_lanes(own, 1)))
        answer = answer + (jnp.where(at_low, p_end, roll_lanes(p, 1)) - p) * back
        coef_cot[x] = 0.5 * answer
        here = above
        if (x + 1) % STRIDE == 0:
            part = pl.ds(x + 1 - STRIDE, STRIDE)
            for which, (src, dst) in enumerate(
                ((ustar.at[:, part], ustar_out.at[:, part]), (coef_cot.at[part], coef_out.at[part]))
            ):
                copies.append(pltpu.make_async_copy(src, dst, sem.at[which, x // STRIDE]))
                copies[-1].start()
    for copy in copies:
        copy.wait()


def on_device(phase, press, vel):
    nx, ny, nz = phase.shape
    total, height = nx + 2 * DEPTH, ny + 2 * DEPTH
    groups = total // ROWS
    devices = lax.axis_size(AXES)
    n_x, n_y, n_z = (turns(axis) for axis in AXES)
    f32 = lambda *shape: jax.ShapeDtypeStruct(shape, jnp.float32)
    scratch = lambda *shape: pltpu.VMEM(shape, jnp.float32)
    inputs = [pltpu.with_memory_space_constraint(array, pltpu.HBM) for array in (phase, press, vel)]

    def call(kernel, args, in_specs, shapes, name, scratch_shapes=(), out_spec=VMEM):
        return pl.pallas_call(
            kernel,
            out_shape=shapes,
            in_specs=in_specs,
            out_specs=[out_spec] * len(shapes),
            scratch_shapes=list(scratch_shapes),
            compiler_params=PARAMS,
            cost_estimate=pl.CostEstimate(flops=3_000_000, bytes_accessed=3_000_000, transcendentals=0),
            name=name,
        )(*args)

    to_x = call(
        functools.partial(pack_x, nx, ny),
        inputs,
        [HBM] * 3,
        [f32(VY * ny + 2 * ROWS, nz)] * n_x,
        "pack_x",
        [pltpu.VMEM((n_x, DEPTH, ny, nz), jnp.int32), scratch(n_x, 3, DEPTH, ny, nz)]
        + [pltpu.SemaphoreType.DMA((n_x, 3))],
    )
    got_x = exchange(to_x, "gx")
    coef, press, vel, rhs = call(
        load,
        inputs + [to_x[0]],
        [HBM] * 3 + [ANY],
        [f32(*press.shape), f32(*press.shape), f32(*vel.shape), f32(*press.shape)],
        "load",
        [pltpu.VMEM(phase.shape, jnp.int32), pltpu.SemaphoreType.DMA((3,))],
    )
    to_y = call(
        functools.partial(pack_y, nx, ny, n_x),
        [coef, press, vel, rhs, *got_x],
        [VMEM] * (4 + n_x),
        [f32(total + nx // ROWS + 1, ROWS, nz)] * n_y,
        "pack_y",
    )
    got_y = exchange(to_y, "gy")
    cube = (total, height, nz)
    full_coef, full_rhs, *to_z = call(
        functools.partial(pack_z, nx, ny, n_x, n_y, n_z),
        [coef, press, vel, rhs, *got_x, *got_y],
        [VMEM] * (4 + n_x + n_y),
        [f32(*cube)] * 2 + [f32(groups // 2 + 1, height, LANES)] * n_z,
        "pack_z",
    )
    got_z = exchange(to_z, "gz")
    wx, wy, wz, diag, ends = call(
        functools.partial(prepare, nx, ny, n_x, n_y),
        [coef, vel, rhs, full_coef, full_rhs, *got_x, *got_y],
        [VMEM] * (5 + n_x + n_y),
        [f32(*cube), f32(2, *cube), f32(2, *cube), f32(*cube), f32(3, groups, height, LANES)],
        "prepare",
    )
    basis, basis_z, sums = call(
        functools.partial(krylov, nx, ny, n_z),
        [wx, wy, wz, diag, full_rhs, ends, *got_z],
        [VMEM] * (6 + n_z),
        [f32(3, *cube), f32(4, groups, height, LANES), f32(1, LANES)],
        "krylov",
        [scratch(*cube), scratch(6, groups, height, LANES), scratch(groups, height, LANES)]
        + [scratch(5, groups, height, LANES)],
    )
    spread = jnp.broadcast_to(sums[None], (devices, 1, LANES))
    gathered = lax.all_to_all(spread, AXES, 0, 0).reshape(devices, LANES)
    return call(
        functools.partial(finish, nx, ny, n_x, n_y, n_z),
        [gathered, press, vel, basis, basis_z, *got_x, *got_y, *got_z],
        [VMEM] * (5 + n_x + n_y + n_z),
        [f32(*vel.shape), f32(nx, ny, nz)],
        "finish",
        [scratch(*vel.shape), scratch(nx, ny, nz), pltpu.SemaphoreType.DMA((2, nx // STRIDE))],
        HBM,
    )


def solution(mesh):
    cells, faces = P(*AXES), P(None, *AXES)
    return jax.shard_map(
        on_device, mesh=mesh, in_specs=(cells, cells, faces), out_specs=(faces, cells), check_vma=False
    )
```

```python
import functools
import itertools

import jax
import jax.numpy as jnp
from jax import lax
from jax.experimental import pallas as pl
from jax.experimental.pallas import tpu as pltpu
from jax.sharding import PartitionSpec as P

AXES = ("gx", "gy", "gz")
SPARE = dict(gx="gy", gy="gz", gz="gx")
DEPTH = 4
GROUP = 4 * DEPTH
LANES = 128
STRIDE = 4
ROWS = 8
VMEM = pl.BlockSpec(memory_space=pltpu.VMEM)
HBM = pl.BlockSpec(memory_space=pltpu.HBM)
ANY = pl.BlockSpec(memory_space=pl.ANY)
PARAMS = pltpu.CompilerParams(vmem_limit_bytes=40 * 1024 * 1024)


def swaps(axis, turn):
    sizes = [lax.axis_size(name) for name in AXES]
    along, spare = AXES.index(axis), AXES.index(SPARE[axis])
    number = lambda place: (place[0] * sizes[1] + place[1]) * sizes[2] + place[2]
    pairs = []
    for place in itertools.product(*map(range, sizes)):
        partner = list(place)
        other = place[along] + (1 if (place[along] - turn) % 2 == 0 else -1)
        if 0 <= other < sizes[along]:
            partner[along] = other
        elif sizes[spare] % 2 == 0:
            partner[spare] ^= 1
        else:
            continue
        pairs.append((number(place), number(partner)))
    return pairs


def exchange(sends, axis):
    return [lax.ppermute(send, AXES, swaps(axis, turn)) for turn, send in enumerate(sends)]


def clear_if_alone(axis, turn, out):
    count, place = lax.axis_size(axis), lax.axis_index(axis)
    alone = []
    if turn == 1:
        alone.append(place == 0)
    if count % 2 != turn:
        alone.append(place == count - 1)
    for case in alone:

        @pl.when(case)
        def _():
            out[...] = jnp.zeros(out.shape, out.dtype)


def even(axis):
    return lax.axis_index(axis) % 2 == 0


def turns(axis):
    return min(2, lax.axis_size(axis) - 1)


def coefficient(phase):
    return jnp.where(phase == 0, 8.0, jnp.where(phase == 1, 1.0, 2.0)).astype(jnp.float32)


def sides(is_even, got, load):
    one = load(got[0])
    two = load(got[1]) if len(got) > 1 else jnp.zeros_like(one)
    return jnp.where(is_even, two, one), jnp.where(is_even, one, two)


def lane_index(shape):
    return lax.broadcasted_iota(jnp.int32, shape, len(shape) - 1)


def row_index(shape):
    return lax.broadcasted_iota(jnp.int32, shape, len(shape) - 2)


def roll_rows(plane, shift):
    return pltpu.roll(plane, shift % plane.shape[0], 0)


def roll_lanes(plane, shift):
    return pltpu.roll(plane, shift % plane.shape[1], 1)


def inner_rhs(coef, vy, vz):
    rows, lanes = row_index(coef.shape), lane_index(coef.shape)
    up = jnp.where(rows == coef.shape[0] - 1, 0.0, 0.5 * (coef + roll_rows(coef, -1)))
    down = jnp.where(rows == 0, 0.0, 0.5 * (coef + roll_rows(coef, 1)))
    right = jnp.where(lanes == LANES - 1, 0.0, 0.5 * (coef + roll_lanes(coef, -1)))
    left = jnp.where(lanes == 0, 0.0, 0.5 * (coef + roll_lanes(coef, 1)))
    return (up * vy - down * roll_rows(vy, 1)) + (right * vz - left * roll_lanes(vz, 1))


RHS, VX, PRESS, VY = DEPTH, 2 * DEPTH - 1, 2 * DEPTH, 2 * DEPTH + 1


def pack_x(nx, ny, phase, press, vel, *refs):
    count = len(refs) - 3
    outs = refs[:count]
    held, held_vel, sem = refs[count:]
    copies = []
    for turn, out in enumerate(outs):
        top = even("gx") == (turn == 0)
        deep = jnp.where(top, nx - DEPTH, 0)
        last = jnp.where(top, nx - 1, 0)
        parts = [
            (vel.at[:, pl.ds(deep, DEPTH)], held_vel.at[turn]),
            (phase.at[pl.ds(deep, DEPTH)], held.at[turn]),
            (press.at[last], out.at[pl.ds(PRESS * ny, ny)]),
        ]
        for which, (src, dst) in enumerate(parts):
            copy = pltpu.make_async_copy(src, dst, sem.at[turn, which])
            copy.start()
            copies.append(copy)
    for copy in copies:
        copy.wait()
    lanes = lane_index((ROWS, LANES))
    rows = row_index((ROWS, LANES))
    for turn, out in enumerate(outs):
        top = even("gx") == (turn == 0)
        coefs = [coefficient(held[turn, j]) for j in range(DEPTH)]
        flux = [0.5 * (coefs[j] + coefs[j + 1]) * held_vel[turn, 0, j] for j in range(DEPTH - 1)]
        columns = jnp.zeros((ROWS, LANES), jnp.float32)
        lines = jnp.zeros((ROWS, LANES), jnp.float32)
        for j in range(DEPTH):
            out[j * ny : (j + 1) * ny, :] = coefs[j]
        for j in range(DEPTH - 1):
            vy = jnp.where(top, held_vel[turn, 1, j + 1], held_vel[turn, 1, j])
            vz = jnp.where(top, held_vel[turn, 2, j + 1], held_vel[turn, 2, j])
            upper = (flux[j + 1] - flux[j]) if j + 1 < DEPTH - 1 else -flux[j]
            lower = (flux[j] - flux[j - 1]) if j else flux[j]
            inner = inner_rhs(jnp.where(top, coefs[j + 1], coefs[j]), vy, vz)
            out[(RHS + j) * ny : (RHS + j + 1) * ny, :] = jnp.where(top, upper, lower) + inner
            for t in range(ny // ROWS):
                lane = DEPTH * t + j
                columns = jnp.where(lanes == lane, roll_lanes(vz[t * ROWS : (t + 1) * ROWS], lane + 1), columns)
            lines = jnp.where(rows == j, roll_rows(vy[ny - ROWS :], j + 1), lines)
        out[VX * ny : (VX + 1) * ny, :] = held_vel[turn, 0, DEPTH - 1]
        out[VY * ny : VY * ny + ROWS, :] = lines
        out[VY * ny + ROWS :, :] = columns
        clear_if_alone("gx", turn, out)


def load(phase, press, vel, after, coef, press_out, vel_out, rhs, held, sem):
    del after
    copies = []
    for which, (src, dst) in enumerate(((phase, held), (press, press_out), (vel, vel_out))):
        copies.append(pltpu.make_async_copy(src, dst, sem.at[which]))
        copies[-1].start()
    copies[0].wait()
    copies[1].wait()
    copies[2].wait()
    nx = coef.shape[0]
    here = coefficient(held[0])
    old_flux = None
    for x in range(nx):
        coef[x] = here
        answer = inner_rhs(here, vel_out[1, x], vel_out[2, x])
        if old_flux is not None:
            answer = answer - old_flux
        if x + 1 < nx:
            above = coefficient(held[x + 1])
            old_flux = 0.5 * (here + above) * vel_out[0, x]
            answer = answer + old_flux
            here = above
        rhs[x] = answer


class Block:
    def __init__(self, nx, ny, coef, vel, rhs, got_x, row=0, height=None):
        self.nx, self.ny = nx, ny
        self.own_coef, self.vel, self.own_rhs, self.got_x = coef, vel, rhs, got_x
        self.even = even("gx")
        self.row, self.height = row, height or ny
        self.low_face = 0.5 * (self.coef(nx + 2 * DEPTH - 1) + self.coef(0)) * self.halo(VX)[0]
        self.high_face = 0.5 * (self.coef(nx - 1) + self.coef(nx)) * self.take(vel, 0, nx - 1)

    def take(self, ref, *index):
        return ref[(*index, pl.ds(self.row, self.height), slice(None))]

    def halo(self, part):
        return sides(self.even, self.got_x, lambda ref: ref[pl.ds(part * self.ny + self.row, self.height), :])

    def coef(self, plane):
        if plane < self.nx:
            return self.take(self.own_coef, plane)
        above = plane < self.nx + DEPTH
        return self.halo((plane - self.nx) % DEPTH)[1 if above else 0]

    def rhs(self, plane):
        nx = self.nx
        if plane < nx:
            answer = self.take(self.own_rhs, plane)
        else:
            above = plane < nx + DEPTH
            layer = plane - nx if above else plane - nx - DEPTH - 1
            if layer < 0 or layer >= DEPTH - 1:
                return jnp.zeros((self.height, LANES), jnp.float32)
            answer = self.halo(RHS + layer)[1 if above else 0]
        if plane == 0:
            answer = answer - self.low_face
        if plane == nx + 2 * DEPTH - 1:
            answer = answer + self.low_face
        if plane == nx - 1:
            answer = answer + self.high_face
        if plane == nx:
            answer = answer - self.high_face
        return answer

    def layer(self, plane):
        if plane < self.nx + DEPTH:
            place = (1, plane - self.nx)
        else:
            place = (0, plane - self.nx - DEPTH - 1)
        return place if 0 <= place[1] < DEPTH - 1 else None

    def columns(self):
        at = VY * self.ny + ROWS
        return sides(self.even, self.got_x, lambda ref: ref[at : at + ROWS, :])

    def vz_end(self, plane, lane):
        if plane < self.nx:
            return roll_lanes(self.vel[2, plane], lane + 1)
        place = self.layer(plane)
        if place is None:
            return jnp.zeros((self.ny, LANES), jnp.float32)
        source = self.columns()[place[0]]
        return jnp.concatenate(
            [roll_lanes(source, lane - DEPTH * t - place[1]) for t in range(self.ny // ROWS)], 0
        )

    def vy_end(self, plane):
        if plane < self.nx:
            return self.vel[1, plane, self.ny - 1 :, :]
        place = self.layer(plane)
        if place is None:
            return jnp.zeros((1, LANES), jnp.float32)
        at = VY * self.ny + place[1]
        return sides(self.even, self.got_x, lambda ref: ref[at : at + 1, :])[place[0]]


def pack_y(nx, ny, n_x, coef, press, vel, rhs, *refs):
    got_x, outs = refs[:n_x], refs[n_x:]
    total = nx + 2 * DEPTH
    rows, lanes = row_index((ROWS, LANES)), lane_index((ROWS, LANES))
    for turn, out in enumerate(outs):
        top = even("gy") == (turn == 0)
        row = pl.multiple_of(jnp.where(top, ny - ROWS, 0), ROWS)
        block = Block(nx, ny, coef, vel, rhs, got_x, row, ROWS)
        columns = jnp.zeros((ROWS, LANES), jnp.float32)
        ends = block.columns()
        for plane in range(total):
            one, two = block.coef(plane), block.rhs(plane)
            one = jnp.where(top, roll_rows(one, DEPTH), one)
            two = jnp.where(top, roll_rows(two, -1), roll_rows(two, DEPTH))
            tile = jnp.where(rows < DEPTH, one, two)
            out[plane] = jnp.where(rows == ROWS - 1, block.vy_end(plane), tile)
            if plane < nx:
                source = roll_lanes(vel[2, plane, pl.ds(row, ROWS), :], plane + 1)
            elif block.layer(plane) is None:
                continue
            else:
                side, layer = block.layer(plane)
                high = (plane - layer - DEPTH * (ny // ROWS - 1)) % LANES
                source = pltpu.roll(ends[side], jnp.where(top, high, (plane - layer) % LANES), 1)
            columns = jnp.where(lanes == plane, source, columns)
        out[total + nx // ROWS] = jnp.where(top, roll_rows(columns, DEPTH - 1), columns)
        for plane in range(nx):
            tile = press[plane, pl.ds(row, ROWS), :]
            edge = jnp.where(top, tile[ROWS - 1 : ROWS], tile[0:1])
            out[total + plane // ROWS, plane % ROWS : plane % ROWS + 1, :] = edge
        clear_if_alone("gy", turn, out)


def tall_end(block, tile_end, plane, lane):
    return jnp.concatenate([block.vz_end(plane, lane), roll_lanes(tile_end, lane - plane)], 0)


def tile_of_ends(nx, even_y, got_y):
    rows = row_index((ROWS, LANES))
    low, high = sides(even_y, got_y, lambda ref: ref[nx + 2 * DEPTH + nx // ROWS])
    return jnp.where(rows < DEPTH, high, roll_rows(low, DEPTH + 1))


def press_lane(x):
    return GROUP * (x % ROWS) + ROWS + 2 * (x // ROWS)


def pack_z(nx, ny, n_x, n_y, n_z, coef, press, vel, rhs, *refs):
    got_x, got_y = refs[:n_x], refs[n_x : n_x + n_y]
    full_coef, full_rhs, *sends = refs[n_x + n_y :]
    total, height = nx + 2 * DEPTH, ny + 2 * DEPTH
    groups = total // ROWS
    even_y = even("gy")
    rows = row_index((ROWS, LANES))
    lanes = lane_index((height, LANES))
    block = Block(nx, ny, coef, vel, rhs, got_x)
    tile_end = tile_of_ends(nx, even_y, got_y)
    parts = [jnp.zeros((height, LANES), jnp.float32) for _ in range(groups // 2 + 1)]
    made = [list(parts) for _ in sends]
    for plane in range(total):
        low, high = sides(even_y, got_y, lambda ref: ref[plane])
        c_own, c_tile = block.coef(plane), jnp.where(rows < DEPTH, high, roll_rows(low, DEPTH))
        r_own, r_tile = block.rhs(plane), jnp.where(rows < DEPTH, roll_rows(high, -DEPTH), roll_rows(low, 1))
        up = 0.5 * (c_own[ny - 1 :] + c_tile[:1]) * block.vy_end(plane)
        down = 0.5 * (c_tile[ROWS - 1 :] + c_own[:1]) * low[ROWS - 1 :]
        first, last = r_own[:ROWS], r_own[ny - ROWS :]
        r_tile = jnp.where(rows == 0, r_tile - up, jnp.where(rows == ROWS - 1, r_tile + down, r_tile))
        middle = [r_own[ROWS : ny - ROWS]] if ny > 2 * ROWS else []
        if ny > ROWS:
            first = jnp.where(rows == 0, first - down, first)
            last = jnp.where(rows == ROWS - 1, last + up, last)
            r_all = jnp.concatenate([first] + middle + [last, r_tile], 0)
        else:
            only = jnp.where(rows == 0, first - down, jnp.where(rows == ROWS - 1, first + up, first))
            r_all = jnp.concatenate([only, r_tile], 0)
        c_all = jnp.concatenate([c_own, c_tile], 0)
        full_coef[plane], full_rhs[plane] = c_all, r_all
        group, seat = plane % groups, plane // groups
        at = GROUP * seat + ROWS * (group % 2)
        end = tall_end(block, tile_end, plane, at + ROWS - 1)
        for turn in range(len(sends)):
            top = even("gz") == (turn == 0)
            c_move = pltpu.roll(c_all, jnp.where(top, (at + DEPTH) % LANES, at), 1)
            r_move = pltpu.roll(r_all, jnp.where(top, (at + ROWS - 1) % LANES, at + DEPTH), 1)
            value = made[turn][group // 2]
            value = jnp.where((lanes >= at) & (lanes < at + DEPTH), c_move, value)
            value = jnp.where((lanes >= at + DEPTH) & (lanes < at + ROWS - 1), r_move, value)
            made[turn][group // 2] = jnp.where(lanes == at + ROWS - 1, end, value)
    for turn, send in enumerate(sends):
        top = even("gz") == (turn == 0)
        value = made[turn][groups // 2][:ny]
        for plane in range(nx):
            at = press_lane(plane)
            moved = pltpu.roll(press[plane], jnp.where(top, (at + 1) % LANES, at), 1)
            value = jnp.where(lanes[:ny] == at, moved, value)
        made[turn][groups // 2] = jnp.concatenate([value, made[turn][groups // 2][ny:]], 0)
        for which, value in enumerate(made[turn]):
            send[which] = value
        clear_if_alone("gz", turn, send)


def tree_sum(parts):
    while len(parts) > 1:
        parts = [parts[i] + parts[i + 1] if i + 1 < len(parts) else parts[i] for i in range(0, len(parts), 2)]
    return parts[0]


class Totals:
    def __init__(self):
        self.stack = []

    def add(self, tile):
        level = 0
        while self.stack and self.stack[-1][0] == level:
            tile = self.stack.pop()[1] + tile
            level += 1
        self.stack.append((level, tile))

    def value(self):
        tiles = [tile for _, tile in self.stack]
        total = tiles.pop()
        while tiles:
            total = tiles.pop() + total
        return total


def prepare(nx, ny, n_x, n_y, coef, vel, rhs, full_coef, full_rhs, *refs):
    got_x, got_y = refs[:n_x], refs[n_x : n_x + n_y]
    basis, ends, shares, wx, wy, wz, inverse = refs[n_x + n_y :]
    total, height = nx + 2 * DEPTH, ny + 2 * DEPTH
    groups = total // ROWS
    lanes = lane_index((height, LANES))
    block = Block(nx, ny, coef, vel, rhs, got_x)
    tile_end = tile_of_ends(nx, even("gy"), got_y)
    for group in range(groups):
        made = [jnp.zeros((height, LANES), jnp.float32) for _ in range(5)]
        for seat in range(ROWS):
            plane = seat * groups + group
            at = GROUP * seat
            for which, source in enumerate((full_coef[plane], full_rhs[plane])):
                here = (lanes >= at + DEPTH) & (lanes < at + GROUP)
                made[2 * which] = jnp.where(here, roll_lanes(source, at + DEPTH), made[2 * which])
                here = (lanes >= at) & (lanes < at + GROUP - DEPTH)
                made[2 * which + 1] = jnp.where(here, roll_lanes(source, at + GROUP - DEPTH), made[2 * which + 1])
            lane = at + GROUP - DEPTH - 1
            made[4] = jnp.where(lanes == lane, tall_end(block, tile_end, plane, lane), made[4])
        for which in range(5):
            ends[which, group] = made[which]
    totals = [Totals() for _ in range(6)]
    trusted = (lanes[:ROWS] >= DEPTH) & (lanes[:ROWS] < LANES - DEPTH)

    def count(which, left, right):
        product = left[:ny] * right[:ny]
        tile = tree_sum([product[i : i + ROWS] for i in range(0, ny, ROWS)])
        totals[which].add(jnp.where(trusted, tile, 0.0))

    old_weight = None
    here = full_coef[nx + DEPTH]
    for x in range(-DEPTH, nx + DEPTH - 1):
        e = x % total
        above = full_coef[(e + 1) % total]
        weight = 0.5 * (here + above)
        wx[e] = weight
        if x > -DEPTH:
            up, down = 0.5 * (here + roll_rows(here, -1)), 0.5 * (here + roll_rows(here, 1))
            right = jnp.where(lanes == LANES - 1, 0.0, 0.5 * (here + roll_lanes(here, -1)))
            left = jnp.where(lanes == 0, 0.0, 0.5 * (here + roll_lanes(here, 1)))
            wy[0, e], wy[1, e], wz[0, e], wz[1, e] = up, down, right, left
            diag = (weight + old_weight) + (up + down) + (right + left)
            inside = here > 0
            scale = jnp.where(inside, 1.0 / jnp.where(inside, diag, 1.0), 0.0)
            inverse[e] = scale
            source = full_rhs[e]
            field = scale * source
            basis[0, e] = field
            if 0 <= x < nx:
                count(0, field, source)
        old_weight, here = weight, above
    for n in range(3):
        reach = 2 - n
        old_flux = None
        here = basis[n, (-reach - 1) % total]
        for x in range(-reach - 1, nx + reach):
            e = x % total
            above = basis[n, (e + 1) % total]
            flux = wx[e] * (above - here)
            if x >= -reach:
                image = old_flux - flux
                image = image + (
                    wy[0, e] * (here - roll_rows(here, -1)) + wy[1, e] * (here - roll_rows(here, 1))
                )
                image = image + (
                    wz[0, e] * (here - roll_lanes(here, -1)) + wz[1, e] * (here - roll_lanes(here, 1))
                )
                own = 0 <= x < nx
                if own:
                    count(2 * n + 1, here, image)
                if n < 2:
                    following = inverse[e] * image
                    basis[n + 1, e] = following
                    if own:
                        count(2 * n + 2, following, image)
            old_flux, here = flux, above
    for which, total_ in enumerate(totals):
        shares[which] = total_.value()


def join(nx, ny, n_z, ends, shares, *refs):
    got_z = refs[:n_z]
    basis_z, vz_z, sums, weight_z, inverse_z = refs[n_z:]
    total, height = nx + 2 * DEPTH, ny + 2 * DEPTH
    groups = total // ROWS
    lanes = lane_index((height, LANES))
    seat_lane, seat = lanes % GROUP, lanes // GROUP
    coef, rhs, vz = [], [], []
    for side in range(2):
        for g in range(groups):
            got = sides(even("gz"), got_z, lambda ref: ref[g // 2])[side]
            skip = ROWS * (g % 2)
            if side == 0:
                outer = seat_lane < DEPTH
                coef.append(jnp.where(outer, roll_lanes(got, -skip), ends[0, g]))
                rhs.append(jnp.where(outer, roll_lanes(got, 1 - DEPTH - skip), ends[2, g]))
                vz.append(roll_lanes(got, -DEPTH - skip))
                vz_z[g] = vz[-1]
            else:
                outer = seat_lane >= GROUP - DEPTH
                coef.append(jnp.where(outer, roll_lanes(got, GROUP - DEPTH - skip), ends[1, g]))
                rhs.append(jnp.where(outer, roll_lanes(got, GROUP - 2 * DEPTH - skip), ends[3, g]))
                vz.append(ends[4, g])

    def along(planes, q, step):
        g = q % groups
        if 0 <= g + step < groups:
            return planes[q + step]
        return roll_lanes(planes[q - g + (g + step) % groups], -GROUP * step)

    totals = [Totals() for _ in range(6)]

    def count(which, q, left, right):
        first = DEPTH if q < groups else GROUP - 2 * DEPTH
        spot = seat_lane[:ROWS]
        mine = (spot >= first) & (spot < first + DEPTH) & (seat[:ROWS] * groups + q % groups < nx)
        product = left[:ny] * right[:ny]
        tile = tree_sum([product[i : i + ROWS] for i in range(0, ny, ROWS)])
        totals[which].add(jnp.where(mine, tile, 0.0))

    field = []
    for q in range(2 * groups):
        here = coef[q]
        neighbours = (along(coef, q, 1), along(coef, q, -1), roll_rows(here, -1), roll_rows(here, 1))
        neighbours += (roll_lanes(here, -1), roll_lanes(here, 1))
        weights = [0.5 * (here + other) for other in neighbours]
        for which, weight in enumerate(weights):
            weight_z[which, q] = weight
        diag = (weights[0] + weights[1]) + (weights[2] + weights[3]) + (weights[4] + weights[5])
        face = DEPTH - 1 if q < groups else GROUP - DEPTH - 1
        source = rhs[q] + jnp.where(seat_lane == face, weights[4] * vz[q], 0.0)
        source = source - jnp.where(seat_lane == face + 1, weights[5] * roll_lanes(vz[q], 1), 0.0)
        inside = here > 0
        scale = jnp.where(inside, 1.0 / jnp.where(inside, diag, 1.0), 0.0)
        inverse_z[q] = scale
        field.append(scale * source)
        basis_z[0, q] = field[q]
        count(0, q, field[q], source)
    for n in range(3):
        following = []
        for q in range(2 * groups):
            here = field[q]
            image = weight_z[0, q] * (here - along(field, q, 1)) + weight_z[1, q] * (here - along(field, q, -1))
            image = image + (
                weight_z[2, q] * (here - roll_rows(here, -1)) + weight_z[3, q] * (here - roll_rows(here, 1))
            )
            image = image + (
                weight_z[4, q] * (here - roll_lanes(here, -1)) + weight_z[5, q] * (here - roll_lanes(here, 1))
            )
            count(2 * n + 1, q, here, image)
            if n < 2:
                following.append(inverse_z[q] * image)
                basis_z[n + 1, q] = following[q]
                count(2 * n + 2, q, following[q], image)
        field = following
    lane = lane_index((1, LANES))
    row = jnp.zeros((1, LANES), jnp.float32)
    for which, total_ in enumerate(totals):
        value = total_.value() + shares[which]
        value = jnp.sum(jnp.sum(value, 0, keepdims=True), 1, keepdims=True)
        row = jnp.where(lane == which, value, row)
    sums[...] = row


def finish(nx, ny, n_x, n_y, n_z, gathered, press, vel, basis, basis_z, vz_z, *refs):
    got_x, got_y, got_z = refs[:n_x], refs[n_x : n_x + n_y], refs[n_x + n_y : n_x + n_y + n_z]
    ustar_out, coef_out, ustar, coef_cot, sem = refs[n_x + n_y + n_z :]
    even_x, even_y, even_z = even("gx"), even("gy"), even("gz")
    total, height = nx + 2 * DEPTH, ny + 2 * DEPTH
    groups = total // ROWS
    parts = gathered[...]
    while parts.shape[0] > ROWS:
        half = parts.shape[0] // 2
        parts = parts[:half] + parts[half:]
    sums = jnp.sum(parts, 0, keepdims=True)
    lane = lane_index((1, LANES))
    m0, m1, m2, m3, m4, m5 = [
        jnp.sum(jnp.where(lane == which, sums, 0.0), 1, keepdims=True) for which in range(6)
    ]
    l1, l2 = m2 / m1, m3 / m1
    d1, cross, d2 = m3 - l1 * m2, m4 - l1 * m3, m5 - l2 * m3
    l21 = cross / d1
    d2 = d2 - l21 * cross
    y1 = -l1 * m0 + m1
    y2 = m2 - l2 * m0 - l21 * y1
    c2 = y2 / d2
    c1 = y1 / d1 - l21 * c2
    c0 = (m0 / m1 - l1 * c1 - l2 * c2)[0, 0]
    c1, c2 = c1[0, 0], c2[0, 0]

    lanes = lane_index((height, LANES))
    seat_lane = lanes % GROUP
    spill = []
    for g in range(groups):
        low, high = [
            c0 * basis_z[0, q] + c1 * basis_z[1, q] + c2 * basis_z[2, q] for q in (g, groups + g)
        ]
        cells = jnp.where(seat_lane < DEPTH - 1, roll_lanes(high, DEPTH - GROUP + DEPTH - 1), roll_lanes(low, -1))
        cells = jnp.where(seat_lane == 2 * DEPTH - 2, roll_lanes(high, 2 * DEPTH - 2 - (GROUP - DEPTH)), cells)
        spill.append(jnp.where(seat_lane == 2 * DEPTH - 1, roll_lanes(low, DEPTH), cells))
    spoiled = (lanes < DEPTH - 1) | (lanes > LANES - DEPTH)
    lanes = lane_index((ny, LANES))
    at_low, at_high = lanes == 0, lanes == LANES - 1
    low_z, high_z = sides(even_z, got_z, lambda ref: ref[groups // 2, :ny, :])
    press_z = jnp.where(lanes % 2 == 0, high_z, roll_lanes(low_z, 1))
    p_low, p_high = sides(even_x, got_x, lambda ref: ref[PRESS * ny : (PRESS + 1) * ny, :])
    u_low, _ = sides(even_x, got_x, lambda ref: ref[VX * ny : (VX + 1) * ny, :])

    def solved(x):
        e = x % total
        cells = c0 * basis[0, e] + c1 * basis[1, e] + c2 * basis[2, e]
        return jnp.where(spoiled, roll_lanes(spill[e % groups], 1 - DEPTH - GROUP * (e // groups)), cells)

    copies = []
    rows = row_index((ROWS, LANES))
    below, here = solved(-1), solved(0)
    face_low = (p_low - press[0]) * (u_low + here[:ny] - below[:ny])
    for x in range(nx):
        above = solved(x + 1)
        group, seat = x % groups, x // groups
        own, p = here[:ny], press[x]
        out = vel[0, x] + (above[:ny] - own)
        ustar[0, x] = out
        face = (p - (press[x + 1] if x + 1 < nx else p_high)) * out
        answer = face_low + face
        face_low = face
        low, high = sides(even_y, got_y, lambda ref: ref[total + x // ROWS, x % ROWS : x % ROWS + 1, :])
        shape = (ROWS, LANES)
        p_tile = jnp.where(rows == 0, jnp.broadcast_to(high, shape), jnp.broadcast_to(low, shape))
        p_tall = jnp.concatenate([p, p_tile], 0)
        u_row, _ = sides(even_y, got_y, lambda ref: ref[x, ROWS - 1 :, :])
        u_tall = jnp.concatenate([vel[1, x], jnp.broadcast_to(u_row, shape)], 0)
        out = vel[1, x] + (roll_rows(here, -1)[:ny] - own)
        ustar[1, x] = out
        back = roll_rows(u_tall, 1)[:ny] + (own - roll_rows(here, 1)[:ny])
        answer = answer + ((p - roll_rows(p_tall, -1)[:ny]) * out + (roll_rows(p_tall, 1)[:ny] - p) * back)
        lam_end = roll_lanes(spill[group][:ny], 1 - 2 * DEPTH - GROUP * seat)
        u_end = roll_lanes(vz_z[group, :ny, :], 1 - DEPTH - GROUP * seat)
        p_end = roll_lanes(press_z, LANES - 1 - press_lane(x))
        out = vel[2, x] + (jnp.where(at_high, lam_end, roll_lanes(own, -1)) - own)
        ustar[2, x] = out
        answer = answer + (p - jnp.where(at_high, p_end, roll_lanes(p, -1))) * out
        back = jnp.where(at_low, u_end, roll_lanes(vel[2, x], 1))
        back = back + (own - jnp.where(at_low, lam_end, roll_lanes(own, 1)))
        answer = answer + (jnp.where(at_low, p_end, roll_lanes(p, 1)) - p) * back
        coef_cot[x] = 0.5 * answer
        here = above
        if (x + 1) % STRIDE == 0:
            part = pl.ds(x + 1 - STRIDE, STRIDE)
            for which, (src, dst) in enumerate(
                ((ustar.at[:, part], ustar_out.at[:, part]), (coef_cot.at[part], coef_out.at[part]))
            ):
                copies.append(pltpu.make_async_copy(src, dst, sem.at[which, x // STRIDE]))
                copies[-1].start()
    for copy in copies:
        copy.wait()


def on_device(phase, press, vel):
    nx, ny, nz = phase.shape
    total, height = nx + 2 * DEPTH, ny + 2 * DEPTH
    groups = total // ROWS
    devices = lax.axis_size(AXES)
    n_x, n_y, n_z = (turns(axis) for axis in AXES)
    f32 = lambda *shape: jax.ShapeDtypeStruct(shape, jnp.float32)
    scratch = lambda *shape: pltpu.VMEM(shape, jnp.float32)
    inputs = [pltpu.with_memory_space_constraint(array, pltpu.HBM) for array in (phase, press, vel)]

    def call(kernel, args, in_specs, shapes, name, scratch_shapes=(), out_spec=VMEM):
        return pl.pallas_call(
            kernel,
            out_shape=shapes,
            in_specs=in_specs,
            out_specs=[out_spec] * len(shapes),
            scratch_shapes=list(scratch_shapes),
            compiler_params=PARAMS,
            cost_estimate=pl.CostEstimate(flops=3_000_000, bytes_accessed=3_000_000, transcendentals=0),
            name=name,
        )(*args)

    to_x = call(
        functools.partial(pack_x, nx, ny),
        inputs,
        [HBM] * 3,
        [f32(VY * ny + 2 * ROWS, nz)] * n_x,
        "pack_x",
        [pltpu.VMEM((n_x, DEPTH, ny, nz), jnp.int32), scratch(n_x, 3, DEPTH, ny, nz)]
        + [pltpu.SemaphoreType.DMA((n_x, 3))],
    )
    got_x = exchange(to_x, "gx")
    coef, press, vel, rhs = call(
        load,
        inputs + [to_x[0]],
        [HBM] * 3 + [ANY],
        [f32(*press.shape), f32(*press.shape), f32(*vel.shape), f32(*press.shape)],
        "load",
        [pltpu.VMEM(phase.shape, jnp.int32), pltpu.SemaphoreType.DMA((3,))],
    )
    to_y = call(
        functools.partial(pack_y, nx, ny, n_x),
        [coef, press, vel, rhs, *got_x],
        [VMEM] * (4 + n_x),
        [f32(total + nx // ROWS + 1, ROWS, nz)] * n_y,
        "pack_y",
    )
    got_y = exchange(to_y, "gy")
    cube = (total, height, nz)
    full_coef, full_rhs, *to_z = call(
        functools.partial(pack_z, nx, ny, n_x, n_y, n_z),
        [coef, press, vel, rhs, *got_x, *got_y],
        [VMEM] * (4 + n_x + n_y),
        [f32(*cube)] * 2 + [f32(groups // 2 + 1, height, LANES)] * n_z,
        "pack_z",
    )
    got_z = exchange(to_z, "gz")
    basis, ends, shares = call(
        functools.partial(prepare, nx, ny, n_x, n_y),
        [coef, vel, rhs, full_coef, full_rhs, *got_x, *got_y],
        [VMEM] * (5 + n_x + n_y),
        [f32(3, *cube), f32(5, groups, height, LANES), f32(6, ROWS, LANES)],
        "prepare",
        [scratch(*cube), scratch(2, *cube), scratch(2, *cube), scratch(*cube)],
    )
    basis_z, vz_z, sums = call(
        functools.partial(join, nx, ny, n_z),
        [ends, shares, *got_z],
        [VMEM] * (2 + n_z),
        [f32(3, 2 * groups, height, LANES), f32(groups, height, LANES), f32(1, LANES)],
        "join",
        [scratch(6, 2 * groups, height, LANES), scratch(2 * groups, height, LANES)],
    )
    spread = jnp.broadcast_to(sums[None], (devices, 1, LANES))
    gathered = lax.all_to_all(spread, AXES, 0, 0).reshape(devices, LANES)
    return call(
        functools.partial(finish, nx, ny, n_x, n_y, n_z),
        [gathered, press, vel, basis, basis_z, vz_z, *got_x, *got_y, *got_z],
        [VMEM] * (6 + n_x + n_y + n_z),
        [f32(*vel.shape), f32(nx, ny, nz)],
        "finish",
        [scratch(*vel.shape), scratch(nx, ny, nz), pltpu.SemaphoreType.DMA((2, nx // STRIDE))],
        HBM,
    )


def solution(mesh):
    cells, faces = P(*AXES), P(None, *AXES)
    return jax.shard_map(
        on_device, mesh=mesh, in_specs=(cells, cells, faces), out_specs=(faces, cells), check_vma=False
    )
```

```python
import functools
import itertools

import jax
import jax.numpy as jnp
from jax import lax
from jax.experimental import pallas as pl
from jax.experimental.pallas import tpu as pltpu
from jax.sharding import PartitionSpec as P

AXES = ("gx", "gy", "gz")
SPARE = dict(gx="gy", gy="gz", gz="gx")
DEPTH = 4
GROUP = 4 * DEPTH
LANES = 128
STRIDE = 4
ROWS = 8
VMEM = pl.BlockSpec(memory_space=pltpu.VMEM)
HBM = pl.BlockSpec(memory_space=pltpu.HBM)
ANY = pl.BlockSpec(memory_space=pl.ANY)
PARAMS = pltpu.CompilerParams(vmem_limit_bytes=40 * 1024 * 1024)


def swaps(moves):
    sizes = [lax.axis_size(name) for name in AXES]
    number = lambda place: (place[0] * sizes[1] + place[1]) * sizes[2] + place[2]
    spare = AXES.index("gz" if len(moves) > 1 else SPARE[moves[0][0]])
    pairs = []
    for place in itertools.product(*map(range, sizes)):
        partner, met = list(place), True
        for axis, turn in moves:
            along = AXES.index(axis)
            partner[along] += 1 if (place[along] - turn) % 2 == 0 else -1
            met = met and 0 <= partner[along] < sizes[along]
        if not met:
            if sizes[spare] % 2:
                continue
            partner = list(place)
            partner[spare] ^= 1
        pairs.append((number(place), number(partner)))
    return pairs


def exchange(send, *moves):
    return lax.ppermute(send, AXES, swaps(moves))


def clear_if_alone(out, *moves):
    for axis, turn in moves:
        count, place = lax.axis_size(axis), lax.axis_index(axis)
        alone = []
        if turn == 1:
            alone.append(place == 0)
        if count % 2 != turn:
            alone.append(place == count - 1)
        for case in alone:

            @pl.when(case)
            def _():
                out[...] = jnp.zeros(out.shape, out.dtype)


def even(axis):
    return lax.axis_index(axis) % 2 == 0


def turns(axis):
    return min(2, lax.axis_size(axis) - 1)


def coefficient(phase):
    return jnp.where(phase == 0, 8.0, jnp.where(phase == 1, 1.0, 2.0)).astype(jnp.float32)


def sides(is_even, got, load):
    one = load(got[0])
    two = load(got[1]) if len(got) > 1 else jnp.zeros_like(one)
    return jnp.where(is_even, two, one), jnp.where(is_even, one, two)


def lane_index(shape):
    return lax.broadcasted_iota(jnp.int32, shape, len(shape) - 1)


def row_index(shape):
    return lax.broadcasted_iota(jnp.int32, shape, len(shape) - 2)


def roll_rows(plane, shift):
    return pltpu.roll(plane, shift % plane.shape[0], 0)


def roll_lanes(plane, shift):
    return pltpu.roll(plane, shift % plane.shape[1], 1)


def inner_rhs(coef, vy, vz):
    rows, lanes = row_index(coef.shape), lane_index(coef.shape)
    up = jnp.where(rows == coef.shape[0] - 1, 0.0, 0.5 * (coef + roll_rows(coef, -1)))
    down = jnp.where(rows == 0, 0.0, 0.5 * (coef + roll_rows(coef, 1)))
    right = jnp.where(lanes == LANES - 1, 0.0, 0.5 * (coef + roll_lanes(coef, -1)))
    left = jnp.where(lanes == 0, 0.0, 0.5 * (coef + roll_lanes(coef, 1)))
    return (up * vy - down * roll_rows(vy, 1)) + (right * vz - left * roll_lanes(vz, 1))


RHS, VX, PRESS, VY = DEPTH, 2 * DEPTH - 1, 2 * DEPTH, 2 * DEPTH + 1


def pack_first(nx, ny, n_x, n_y, phase, press, vel, *refs):
    outs, odd_outs, (held, held_vel, sem) = refs[:n_x], refs[n_x:-3], refs[-3:]
    if n_y > 1:
        *odd_outs, tile_phase, tile_vel, tile_press, tile_sem = odd_outs
    copies = []
    for turn, out in enumerate(outs):
        top = even("gx") == (turn == 0)
        deep = jnp.where(top, nx - DEPTH, 0)
        last = jnp.where(top, nx - 1, 0)
        parts = [
            (vel.at[:, pl.ds(deep, DEPTH)], held_vel.at[turn]),
            (phase.at[pl.ds(deep, DEPTH)], held.at[turn]),
            (press.at[last], out.at[pl.ds(PRESS * ny, ny)]),
        ]
        for which, (src, dst) in enumerate(parts):
            copy = pltpu.make_async_copy(src, dst, sem.at[turn, which])
            copy.start()
            copies.append(copy)
    if n_y > 1:
        row = pl.multiple_of(jnp.where(even("gy"), 0, ny - ROWS), ROWS)
        parts = [
            (phase.at[:, pl.ds(row, ROWS)], tile_phase),
            (vel.at[:, :, pl.ds(row, ROWS)], tile_vel),
            (press.at[:, pl.ds(row, ROWS)], tile_press),
        ]
        for which, (src, dst) in enumerate(parts):
            copy = pltpu.make_async_copy(src, dst, tile_sem.at[which])
            copy.start()
            copies.append(copy)
    for copy in copies:
        copy.wait()
    lanes = lane_index((ROWS, LANES))
    rows = row_index((ROWS, LANES))
    for turn, out in enumerate(outs):
        top = even("gx") == (turn == 0)
        coefs = [coefficient(held[turn, j]) for j in range(DEPTH)]
        flux = [0.5 * (coefs[j] + coefs[j + 1]) * held_vel[turn, 0, j] for j in range(DEPTH - 1)]
        columns = jnp.zeros((ROWS, LANES), jnp.float32)
        lines = jnp.zeros((ROWS, LANES), jnp.float32)
        for j in range(DEPTH):
            out[j * ny : (j + 1) * ny, :] = coefs[j]
        for j in range(DEPTH - 1):
            vy = jnp.where(top, held_vel[turn, 1, j + 1], held_vel[turn, 1, j])
            vz = jnp.where(top, held_vel[turn, 2, j + 1], held_vel[turn, 2, j])
            upper = (flux[j + 1] - flux[j]) if j + 1 < DEPTH - 1 else -flux[j]
            lower = (flux[j] - flux[j - 1]) if j else flux[j]
            inner = inner_rhs(jnp.where(top, coefs[j + 1], coefs[j]), vy, vz)
            out[(RHS + j) * ny : (RHS + j + 1) * ny, :] = jnp.where(top, upper, lower) + inner
            for t in range(ny // ROWS):
                lane = DEPTH * t + j
                columns = jnp.where(lanes == lane, roll_lanes(vz[t * ROWS : (t + 1) * ROWS], lane + 1), columns)
            lines = jnp.where(rows == j, roll_rows(vy[ny - ROWS :], j + 1), lines)
        out[VX * ny : (VX + 1) * ny, :] = held_vel[turn, 0, DEPTH - 1]
        out[VY * ny : VY * ny + ROWS, :] = lines
        out[VY * ny + ROWS :, :] = columns
        clear_if_alone(out, ("gx", turn))
    if n_y > 1:
        pack_odd(nx, tile_phase, tile_vel, tile_press, odd_outs)


def row_tile(coef, rhs, vy, top):
    rows = row_index((ROWS, LANES))
    coef = jnp.where(top, roll_rows(coef, DEPTH), coef)
    rhs = jnp.where(top, roll_rows(rhs, -1), roll_rows(rhs, DEPTH))
    return jnp.where(rows == ROWS - 1, vy, jnp.where(rows < DEPTH, coef, rhs))


def pack_odd(nx, tile_phase, tile_vel, tile_press, outs):
    out, *corners = outs
    top = jnp.logical_not(even("gy"))
    lanes = lane_index((ROWS, LANES))
    ends_at, vx_at = nx + nx // ROWS, nx + nx // ROWS + 1
    ends = jnp.zeros((ROWS, LANES), jnp.float32)
    here, old_flux = coefficient(tile_phase[0]), None
    for x in range(nx):
        vy, vz = tile_vel[1, x], tile_vel[2, x]
        answer = inner_rhs(here, vy, vz)
        if old_flux is not None:
            answer = answer - old_flux
        coef = here
        if x + 1 < nx:
            above = coefficient(tile_phase[x + 1])
            old_flux = 0.5 * (here + above) * tile_vel[0, x]
            answer = answer + old_flux
            here = above
        out[x] = row_tile(coef, answer, vy, top)
        ends = jnp.where(lanes == x, roll_lanes(vz, x + 1), ends)
        tile = tile_press[x]
        at = nx + x // ROWS
        out[at, x % ROWS : x % ROWS + 1, :] = jnp.where(top, tile[ROWS - 1 : ROWS], tile[0:1])
    shift = lambda tile: jnp.where(top, roll_rows(tile, -1), roll_rows(tile, DEPTH))
    ends = jnp.where(top, roll_rows(ends, DEPTH - 1), ends)
    out[ends_at] = ends
    out[vx_at] = shift(tile_vel[0, nx - 1])
    for turn, corner in enumerate(corners):
        first = jnp.where(even("gx") == (turn == 0), nx - DEPTH, 0)
        for j in range(DEPTH):
            corner[j] = out[first + j]
        corner[DEPTH] = pltpu.roll(ends, jnp.where(first == 0, 0, (DEPTH - nx) % LANES), 1)
        corner[DEPTH + 1] = out[vx_at]
        clear_if_alone(corner, ("gx", turn), ("gy", 1))
    clear_if_alone(out, ("gy", 1))


def merge_odd(nx, got, *refs):
    corners, out = refs[:-1], refs[-1]
    total = nx + 2 * DEPTH
    rows, lanes = row_index((ROWS, LANES)), lane_index((ROWS, LANES))
    ends_at, vx_at = nx + nx // ROWS, nx + nx // ROWS + 1
    low, high = zip(*[sides(even("gx"), corners, lambda ref: ref[j]) for j in range(DEPTH + 2)])
    tiles = [got[x] for x in range(nx)] + list(high[:DEPTH]) + list(low[:DEPTH])
    inner = (rows >= DEPTH) & (rows < ROWS - 1)

    def face(below, above, vx):
        weight = 0.5 * (tiles[below] + tiles[above])
        weight = jnp.where(even("gy"), roll_rows(weight, DEPTH - 1), roll_rows(weight, DEPTH))
        return jnp.where(inner, weight * vx, 0.0)

    low_face, high_face = face(total - 1, 0, low[DEPTH + 1]), face(nx - 1, nx, got[vx_at])
    for plane, tile in enumerate(tiles):
        if plane == 0:
            tile = tile - low_face
        if plane == total - 1:
            tile = tile + low_face
        if plane == nx - 1:
            tile = tile + high_face
        if plane == nx:
            tile = tile - high_face
        out[plane] = tile
    for at in range(nx // ROWS):
        out[total + at] = got[nx + at]
    ends = jnp.where(lanes < nx, got[ends_at], roll_lanes(high[DEPTH], nx))
    out[total + nx // ROWS] = jnp.where(lanes < nx + DEPTH, ends, roll_lanes(low[DEPTH], nx + DEPTH))


def load(phase, press, vel, after, coef, press_out, vel_out, rhs, held, sem):
    del after
    copies = []
    for which, (src, dst) in enumerate(((phase, held), (press, press_out), (vel, vel_out))):
        copies.append(pltpu.make_async_copy(src, dst, sem.at[which]))
        copies[-1].start()
    copies[0].wait()
    copies[1].wait()
    copies[2].wait()
    nx = coef.shape[0]
    here = coefficient(held[0])
    old_flux = None
    for x in range(nx):
        coef[x] = here
        answer = inner_rhs(here, vel_out[1, x], vel_out[2, x])
        if old_flux is not None:
            answer = answer - old_flux
        if x + 1 < nx:
            above = coefficient(held[x + 1])
            old_flux = 0.5 * (here + above) * vel_out[0, x]
            answer = answer + old_flux
            here = above
        rhs[x] = answer


class Block:
    def __init__(self, nx, ny, coef, vel, rhs, got_x, row=0, height=None):
        self.nx, self.ny = nx, ny
        self.own_coef, self.vel, self.own_rhs, self.got_x = coef, vel, rhs, got_x
        self.even = even("gx")
        self.row, self.height = row, height or ny
        self.low_face = 0.5 * (self.coef(nx + 2 * DEPTH - 1) + self.coef(0)) * self.halo(VX)[0]
        self.high_face = 0.5 * (self.coef(nx - 1) + self.coef(nx)) * self.take(vel, 0, nx - 1)

    def take(self, ref, *index):
        return ref[(*index, pl.ds(self.row, self.height), slice(None))]

    def halo(self, part):
        return sides(self.even, self.got_x, lambda ref: ref[pl.ds(part * self.ny + self.row, self.height), :])

    def coef(self, plane):
        if plane < self.nx:
            return self.take(self.own_coef, plane)
        above = plane < self.nx + DEPTH
        return self.halo((plane - self.nx) % DEPTH)[1 if above else 0]

    def rhs(self, plane):
        nx = self.nx
        if plane < nx:
            answer = self.take(self.own_rhs, plane)
        else:
            above = plane < nx + DEPTH
            layer = plane - nx if above else plane - nx - DEPTH - 1
            if layer < 0 or layer >= DEPTH - 1:
                return jnp.zeros((self.height, LANES), jnp.float32)
            answer = self.halo(RHS + layer)[1 if above else 0]
        if plane == 0:
            answer = answer - self.low_face
        if plane == nx + 2 * DEPTH - 1:
            answer = answer + self.low_face
        if plane == nx - 1:
            answer = answer + self.high_face
        if plane == nx:
            answer = answer - self.high_face
        return answer

    def layer(self, plane):
        if plane < self.nx + DEPTH:
            place = (1, plane - self.nx)
        else:
            place = (0, plane - self.nx - DEPTH - 1)
        return place if 0 <= place[1] < DEPTH - 1 else None

    def columns(self):
        at = VY * self.ny + ROWS
        return sides(self.even, self.got_x, lambda ref: ref[at : at + ROWS, :])

    def vz_end(self, plane, lane):
        if plane < self.nx:
            return roll_lanes(self.vel[2, plane], lane + 1)
        place = self.layer(plane)
        if place is None:
            return jnp.zeros((self.ny, LANES), jnp.float32)
        source = self.columns()[place[0]]
        return jnp.concatenate(
            [roll_lanes(source, lane - DEPTH * t - place[1]) for t in range(self.ny // ROWS)], 0
        )

    def vy_end(self, plane):
        if plane < self.nx:
            return self.vel[1, plane, self.ny - 1 :, :]
        place = self.layer(plane)
        if place is None:
            return jnp.zeros((1, LANES), jnp.float32)
        at = VY * self.ny + place[1]
        return sides(self.even, self.got_x, lambda ref: ref[at : at + 1, :])[place[0]]


def pack_y(nx, ny, n_x, coef, press, vel, rhs, *refs):
    got_x, out = refs[:n_x], refs[-1]
    total = nx + 2 * DEPTH
    lanes = lane_index((ROWS, LANES))
    top = even("gy")
    row = pl.multiple_of(jnp.where(top, ny - ROWS, 0), ROWS)
    block = Block(nx, ny, coef, vel, rhs, got_x, row, ROWS)
    columns = jnp.zeros((ROWS, LANES), jnp.float32)
    ends = block.columns()
    for plane in range(total):
        out[plane] = row_tile(block.coef(plane), block.rhs(plane), block.vy_end(plane), top)
        if plane < nx:
            source = roll_lanes(vel[2, plane, pl.ds(row, ROWS), :], plane + 1)
        elif block.layer(plane) is None:
            continue
        else:
            side, layer = block.layer(plane)
            high = (plane - layer - DEPTH * (ny // ROWS - 1)) % LANES
            source = pltpu.roll(ends[side], jnp.where(top, high, (plane - layer) % LANES), 1)
        columns = jnp.where(lanes == plane, source, columns)
    out[total + nx // ROWS] = jnp.where(top, roll_rows(columns, DEPTH - 1), columns)
    for plane in range(nx):
        tile = press[plane, pl.ds(row, ROWS), :]
        edge = jnp.where(top, tile[ROWS - 1 : ROWS], tile[0:1])
        out[total + plane // ROWS, plane % ROWS : plane % ROWS + 1, :] = edge
    clear_if_alone(out, ("gy", 0))


def tall_end(block, tile_end, plane, lane):
    return jnp.concatenate([block.vz_end(plane, lane), roll_lanes(tile_end, lane - plane)], 0)


def tile_of_ends(nx, even_y, got_y):
    rows = row_index((ROWS, LANES))
    low, high = sides(even_y, got_y, lambda ref: ref[nx + 2 * DEPTH + nx // ROWS])
    return jnp.where(rows < DEPTH, high, roll_rows(low, DEPTH + 1))


def press_lane(x):
    return GROUP * (x % ROWS) + ROWS + 2 * (x // ROWS)


def pack_z(nx, ny, n_x, n_y, n_z, coef, press, vel, rhs, *refs):
    got_x, got_y = refs[:n_x], refs[n_x : n_x + n_y]
    full_coef, full_rhs, *sends = refs[n_x + n_y :]
    total, height = nx + 2 * DEPTH, ny + 2 * DEPTH
    groups = total // ROWS
    even_y = even("gy")
    rows = row_index((ROWS, LANES))
    lanes = lane_index((height, LANES))
    block = Block(nx, ny, coef, vel, rhs, got_x)
    tile_end = tile_of_ends(nx, even_y, got_y)
    parts = [jnp.zeros((height, LANES), jnp.float32) for _ in range(groups // 2 + 1)]
    made = [list(parts) for _ in sends]
    for plane in range(total):
        low, high = sides(even_y, got_y, lambda ref: ref[plane])
        c_own, c_tile = block.coef(plane), jnp.where(rows < DEPTH, high, roll_rows(low, DEPTH))
        r_own, r_tile = block.rhs(plane), jnp.where(rows < DEPTH, roll_rows(high, -DEPTH), roll_rows(low, 1))
        up = 0.5 * (c_own[ny - 1 :] + c_tile[:1]) * block.vy_end(plane)
        down = 0.5 * (c_tile[ROWS - 1 :] + c_own[:1]) * low[ROWS - 1 :]
        first, last = r_own[:ROWS], r_own[ny - ROWS :]
        r_tile = jnp.where(rows == 0, r_tile - up, jnp.where(rows == ROWS - 1, r_tile + down, r_tile))
        middle = [r_own[ROWS : ny - ROWS]] if ny > 2 * ROWS else []
        if ny > ROWS:
            first = jnp.where(rows == 0, first - down, first)
            last = jnp.where(rows == ROWS - 1, last + up, last)
            r_all = jnp.concatenate([first] + middle + [last, r_tile], 0)
        else:
            only = jnp.where(rows == 0, first - down, jnp.where(rows == ROWS - 1, first + up, first))
            r_all = jnp.concatenate([only, r_tile], 0)
        c_all = jnp.concatenate([c_own, c_tile], 0)
        full_coef[plane], full_rhs[plane] = c_all, r_all
        group, seat = plane % groups, plane // groups
        at = GROUP * seat + ROWS * (group % 2)
        end = tall_end(block, tile_end, plane, at + ROWS - 1)
        for turn in range(len(sends)):
            top = even("gz") == (turn == 0)
            c_move = pltpu.roll(c_all, jnp.where(top, (at + DEPTH) % LANES, at), 1)
            r_move = pltpu.roll(r_all, jnp.where(top, (at + ROWS - 1) % LANES, at + DEPTH), 1)
            value = made[turn][group // 2]
            value = jnp.where((lanes >= at) & (lanes < at + DEPTH), c_move, value)
            value = jnp.where((lanes >= at + DEPTH) & (lanes < at + ROWS - 1), r_move, value)
            made[turn][group // 2] = jnp.where(lanes == at + ROWS - 1, end, value)
    for turn, send in enumerate(sends):
        top = even("gz") == (turn == 0)
        value = made[turn][groups // 2][:ny]
        for plane in range(nx):
            at = press_lane(plane)
            moved = pltpu.roll(press[plane], jnp.where(top, (at + 1) % LANES, at), 1)
            value = jnp.where(lanes[:ny] == at, moved, value)
        made[turn][groups // 2] = jnp.concatenate([value, made[turn][groups // 2][ny:]], 0)
        for which, value in enumerate(made[turn]):
            send[which] = value
        clear_if_alone(send, ("gz", turn))


def tree_sum(parts):
    while len(parts) > 1:
        parts = [parts[i] + parts[i + 1] if i + 1 < len(parts) else parts[i] for i in range(0, len(parts), 2)]
    return parts[0]


class Totals:
    def __init__(self):
        self.stack = []

    def add(self, tile):
        level = 0
        while self.stack and self.stack[-1][0] == level:
            tile = self.stack.pop()[1] + tile
            level += 1
        self.stack.append((level, tile))

    def value(self):
        tiles = [tile for _, tile in self.stack]
        total = tiles.pop()
        while tiles:
            total = tiles.pop() + total
        return total


def prepare(nx, ny, n_x, n_y, coef, vel, rhs, full_coef, full_rhs, *refs):
    got_x, got_y = refs[:n_x], refs[n_x : n_x + n_y]
    basis, ends, shares, wx, wy, wz, inverse = refs[n_x + n_y :]
    total, height = nx + 2 * DEPTH, ny + 2 * DEPTH
    groups = total // ROWS
    lanes = lane_index((height, LANES))
    block = Block(nx, ny, coef, vel, rhs, got_x)
    tile_end = tile_of_ends(nx, even("gy"), got_y)
    for group in range(groups):
        made = [jnp.zeros((height, LANES), jnp.float32) for _ in range(5)]
        for seat in range(ROWS):
            plane = seat * groups + group
            at = GROUP * seat
            for which, source in enumerate((full_coef[plane], full_rhs[plane])):
                here = (lanes >= at + DEPTH) & (lanes < at + GROUP)
                made[2 * which] = jnp.where(here, roll_lanes(source, at + DEPTH), made[2 * which])
                here = (lanes >= at) & (lanes < at + GROUP - DEPTH)
                made[2 * which + 1] = jnp.where(here, roll_lanes(source, at + GROUP - DEPTH), made[2 * which + 1])
            lane = at + GROUP - DEPTH - 1
            made[4] = jnp.where(lanes == lane, tall_end(block, tile_end, plane, lane), made[4])
        for which in range(5):
            ends[which, group] = made[which]
    totals = [Totals() for _ in range(6)]
    trusted = (lanes[:ROWS] >= DEPTH) & (lanes[:ROWS] < LANES - DEPTH)

    def count(which, left, right):
        product = left[:ny] * right[:ny]
        tile = tree_sum([product[i : i + ROWS] for i in range(0, ny, ROWS)])
        totals[which].add(jnp.where(trusted, tile, 0.0))

    old_weight = None
    here = full_coef[nx + DEPTH]
    for x in range(-DEPTH, nx + DEPTH - 1):
        e = x % total
        above = full_coef[(e + 1) % total]
        weight = 0.5 * (here + above)
        wx[e] = weight
        if x > -DEPTH:
            up, down = 0.5 * (here + roll_rows(here, -1)), 0.5 * (here + roll_rows(here, 1))
            right = jnp.where(lanes == LANES - 1, 0.0, 0.5 * (here + roll_lanes(here, -1)))
            left = jnp.where(lanes == 0, 0.0, 0.5 * (here + roll_lanes(here, 1)))
            wy[0, e], wy[1, e], wz[0, e], wz[1, e] = up, down, right, left
            diag = (weight + old_weight) + (up + down) + (right + left)
            inside = here > 0
            scale = jnp.where(inside, 1.0 / jnp.where(inside, diag, 1.0), 0.0)
            inverse[e] = scale
            source = full_rhs[e]
            field = scale * source
            basis[0, e] = field
            if 0 <= x < nx:
                count(0, field, source)
        old_weight, here = weight, above
    for n in range(3):
        reach = 2 - n
        old_flux = None
        here = basis[n, (-reach - 1) % total]
        for x in range(-reach - 1, nx + reach):
            e = x % total
            above = basis[n, (e + 1) % total]
            flux = wx[e] * (above - here)
            if x >= -reach:
                image = old_flux - flux
                image = image + (
                    wy[0, e] * (here - roll_rows(here, -1)) + wy[1, e] * (here - roll_rows(here, 1))
                )
                image = image + (
                    wz[0, e] * (here - roll_lanes(here, -1)) + wz[1, e] * (here - roll_lanes(here, 1))
                )
                own = 0 <= x < nx
                if own:
                    count(2 * n + 1, here, image)
                if n < 2:
                    following = inverse[e] * image
                    basis[n + 1, e] = following
                    if own:
                        count(2 * n + 2, following, image)
            old_flux, here = flux, above
    for which, total_ in enumerate(totals):
        shares[which] = total_.value()


def join(nx, ny, n_z, ends, shares, *refs):
    got_z = refs[:n_z]
    basis_z, vz_z, sums, weight_z, inverse_z = refs[n_z:]
    total, height = nx + 2 * DEPTH, ny + 2 * DEPTH
    groups = total // ROWS
    lanes = lane_index((height, LANES))
    seat_lane, seat = lanes % GROUP, lanes // GROUP
    coef, rhs, vz = [], [], []
    for side in range(2):
        for g in range(groups):
            got = sides(even("gz"), got_z, lambda ref: ref[g // 2])[side]
            skip = ROWS * (g % 2)
            if side == 0:
                outer = seat_lane < DEPTH
                coef.append(jnp.where(outer, roll_lanes(got, -skip), ends[0, g]))
                rhs.append(jnp.where(outer, roll_lanes(got, 1 - DEPTH - skip), ends[2, g]))
                vz.append(roll_lanes(got, -DEPTH - skip))
                vz_z[g] = vz[-1]
            else:
                outer = seat_lane >= GROUP - DEPTH
                coef.append(jnp.where(outer, roll_lanes(got, GROUP - DEPTH - skip), ends[1, g]))
                rhs.append(jnp.where(outer, roll_lanes(got, GROUP - 2 * DEPTH - skip), ends[3, g]))
                vz.append(ends[4, g])

    def along(planes, q, step):
        g = q % groups
        if 0 <= g + step < groups:
            return planes[q + step]
        return roll_lanes(planes[q - g + (g + step) % groups], -GROUP * step)

    totals = [Totals() for _ in range(6)]

    def count(which, q, left, right):
        first = DEPTH if q < groups else GROUP - 2 * DEPTH
        spot = seat_lane[:ROWS]
        mine = (spot >= first) & (spot < first + DEPTH) & (seat[:ROWS] * groups + q % groups < nx)
        product = left[:ny] * right[:ny]
        tile = tree_sum([product[i : i + ROWS] for i in range(0, ny, ROWS)])
        totals[which].add(jnp.where(mine, tile, 0.0))

    field = []
    for q in range(2 * groups):
        here = coef[q]
        neighbours = (along(coef, q, 1), along(coef, q, -1), roll_rows(here, -1), roll_rows(here, 1))
        neighbours += (roll_lanes(here, -1), roll_lanes(here, 1))
        weights = [0.5 * (here + other) for other in neighbours]
        for which, weight in enumerate(weights):
            weight_z[which, q] = weight
        diag = (weights[0] + weights[1]) + (weights[2] + weights[3]) + (weights[4] + weights[5])
        face = DEPTH - 1 if q < groups else GROUP - DEPTH - 1
        source = rhs[q] + jnp.where(seat_lane == face, weights[4] * vz[q], 0.0)
        source = source - jnp.where(seat_lane == face + 1, weights[5] * roll_lanes(vz[q], 1), 0.0)
        inside = here > 0
        scale = jnp.where(inside, 1.0 / jnp.where(inside, diag, 1.0), 0.0)
        inverse_z[q] = scale
        field.append(scale * source)
        basis_z[0, q] = field[q]
        count(0, q, field[q], source)
    for n in range(3):
        following = []
        for q in range(2 * groups):
            here = field[q]
            image = weight_z[0, q] * (here - along(field, q, 1)) + weight_z[1, q] * (here - along(field, q, -1))
            image = image + (
                weight_z[2, q] * (here - roll_rows(here, -1)) + weight_z[3, q] * (here - roll_rows(here, 1))
            )
            image = image + (
                weight_z[4, q] * (here - roll_lanes(here, -1)) + weight_z[5, q] * (here - roll_lanes(here, 1))
            )
            count(2 * n + 1, q, here, image)
            if n < 2:
                following.append(inverse_z[q] * image)
                basis_z[n + 1, q] = following[q]
                count(2 * n + 2, q, following[q], image)
        field = following
    lane = lane_index((1, LANES))
    row = jnp.zeros((1, LANES), jnp.float32)
    for which, total_ in enumerate(totals):
        value = total_.value() + shares[which]
        value = jnp.sum(jnp.sum(value, 0, keepdims=True), 1, keepdims=True)
        row = jnp.where(lane == which, value, row)
    sums[...] = row


def finish(nx, ny, n_x, n_y, n_z, gathered, press, vel, basis, basis_z, vz_z, *refs):
    got_x, got_y, got_z = refs[:n_x], refs[n_x : n_x + n_y], refs[n_x + n_y : n_x + n_y + n_z]
    ustar_out, coef_out, ustar, coef_cot, sem = refs[n_x + n_y + n_z :]
    even_x, even_y, even_z = even("gx"), even("gy"), even("gz")
    total, height = nx + 2 * DEPTH, ny + 2 * DEPTH
    groups = total // ROWS
    parts = gathered[...]
    while parts.shape[0] > ROWS:
        half = parts.shape[0] // 2
        parts = parts[:half] + parts[half:]
    sums = jnp.sum(parts, 0, keepdims=True)
    lane = lane_index((1, LANES))
    m0, m1, m2, m3, m4, m5 = [
        jnp.sum(jnp.where(lane == which, sums, 0.0), 1, keepdims=True) for which in range(6)
    ]
    l1, l2 = m2 / m1, m3 / m1
    d1, cross, d2 = m3 - l1 * m2, m4 - l1 * m3, m5 - l2 * m3
    l21 = cross / d1
    d2 = d2 - l21 * cross
    y1 = -l1 * m0 + m1
    y2 = m2 - l2 * m0 - l21 * y1
    c2 = y2 / d2
    c1 = y1 / d1 - l21 * c2
    c0 = (m0 / m1 - l1 * c1 - l2 * c2)[0, 0]
    c1, c2 = c1[0, 0], c2[0, 0]

    lanes = lane_index((height, LANES))
    seat_lane = lanes % GROUP
    spill = []
    for g in range(groups):
        low, high = [
            c0 * basis_z[0, q] + c1 * basis_z[1, q] + c2 * basis_z[2, q] for q in (g, groups + g)
        ]
        cells = jnp.where(seat_lane < DEPTH - 1, roll_lanes(high, DEPTH - GROUP + DEPTH - 1), roll_lanes(low, -1))
        cells = jnp.where(seat_lane == 2 * DEPTH - 2, roll_lanes(high, 2 * DEPTH - 2 - (GROUP - DEPTH)), cells)
        spill.append(jnp.where(seat_lane == 2 * DEPTH - 1, roll_lanes(low, DEPTH), cells))
    spoiled = (lanes < DEPTH - 1) | (lanes > LANES - DEPTH)
    lanes = lane_index((ny, LANES))
    at_low, at_high = lanes == 0, lanes == LANES - 1
    low_z, high_z = sides(even_z, got_z, lambda ref: ref[groups // 2, :ny, :])
    press_z = jnp.where(lanes % 2 == 0, high_z, roll_lanes(low_z, 1))
    p_low, p_high = sides(even_x, got_x, lambda ref: ref[PRESS * ny : (PRESS + 1) * ny, :])
    u_low, _ = sides(even_x, got_x, lambda ref: ref[VX * ny : (VX + 1) * ny, :])

    def solved(x):
        e = x % total
        cells = c0 * basis[0, e] + c1 * basis[1, e] + c2 * basis[2, e]
        return jnp.where(spoiled, roll_lanes(spill[e % groups], 1 - DEPTH - GROUP * (e // groups)), cells)

    copies = []
    rows = row_index((ROWS, LANES))
    below, here = solved(-1), solved(0)
    face_low = (p_low - press[0]) * (u_low + here[:ny] - below[:ny])
    for x in range(nx):
        above = solved(x + 1)
        group, seat = x % groups, x // groups
        own, p = here[:ny], press[x]
        out = vel[0, x] + (above[:ny] - own)
        ustar[0, x] = out
        face = (p - (press[x + 1] if x + 1 < nx else p_high)) * out
        answer = face_low + face
        face_low = face
        low, high = sides(even_y, got_y, lambda ref: ref[total + x // ROWS, x % ROWS : x % ROWS + 1, :])
        shape = (ROWS, LANES)
        p_tile = jnp.where(rows == 0, jnp.broadcast_to(high, shape), jnp.broadcast_to(low, shape))
        p_tall = jnp.concatenate([p, p_tile], 0)
        u_row, _ = sides(even_y, got_y, lambda ref: ref[x, ROWS - 1 :, :])
        u_tall = jnp.concatenate([vel[1, x], jnp.broadcast_to(u_row, shape)], 0)
        out = vel[1, x] + (roll_rows(here, -1)[:ny] - own)
        ustar[1, x] = out
        back = roll_rows(u_tall, 1)[:ny] + (own - roll_rows(here, 1)[:ny])
        answer = answer + ((p - roll_rows(p_tall, -1)[:ny]) * out + (roll_rows(p_tall, 1)[:ny] - p) * back)
        lam_end = roll_lanes(spill[group][:ny], 1 - 2 * DEPTH - GROUP * seat)
        u_end = roll_lanes(vz_z[group, :ny, :], 1 - DEPTH - GROUP * seat)
        p_end = roll_lanes(press_z, LANES - 1 - press_lane(x))
        out = vel[2, x] + (jnp.where(at_high, lam_end, roll_lanes(own, -1)) - own)
        ustar[2, x] = out
        answer = answer + (p - jnp.where(at_high, p_end, roll_lanes(p, -1))) * out
        back = jnp.where(at_low, u_end, roll_lanes(vel[2, x], 1))
        back = back + (own - jnp.where(at_low, lam_end, roll_lanes(own, 1)))
        answer = answer + (jnp.where(at_low, p_end, roll_lanes(p, 1)) - p) * back
        coef_cot[x] = 0.5 * answer
        here = above
        if (x + 1) % STRIDE == 0:
            part = pl.ds(x + 1 - STRIDE, STRIDE)
            for which, (src, dst) in enumerate(
                ((ustar.at[:, part], ustar_out.at[:, part]), (coef_cot.at[part], coef_out.at[part]))
            ):
                copies.append(pltpu.make_async_copy(src, dst, sem.at[which, x // STRIDE]))
                copies[-1].start()
    for copy in copies:
        copy.wait()


def on_device(phase, press, vel):
    nx, ny, nz = phase.shape
    total, height = nx + 2 * DEPTH, ny + 2 * DEPTH
    groups = total // ROWS
    devices = lax.axis_size(AXES)
    n_x, n_y, n_z = (turns(axis) for axis in AXES)
    f32 = lambda *shape: jax.ShapeDtypeStruct(shape, jnp.float32)
    scratch = lambda *shape: pltpu.VMEM(shape, jnp.float32)
    inputs = [pltpu.with_memory_space_constraint(array, pltpu.HBM) for array in (phase, press, vel)]

    def call(kernel, args, in_specs, shapes, name, scratch_shapes=(), out_spec=VMEM):
        return pl.pallas_call(
            kernel,
            out_shape=shapes,
            in_specs=in_specs,
            out_specs=[out_spec] * len(shapes),
            scratch_shapes=list(scratch_shapes),
            compiler_params=PARAMS,
            cost_estimate=pl.CostEstimate(flops=3_000_000, bytes_accessed=3_000_000, transcendentals=0),
            name=name,
        )(*args)

    odd = n_y > 1
    sent = call(
        functools.partial(pack_first, nx, ny, n_x, n_y),
        inputs,
        [HBM] * 3,
        [f32(VY * ny + 2 * ROWS, nz)] * n_x
        + ([f32(nx + nx // ROWS + 2, ROWS, nz)] + [f32(DEPTH + 2, ROWS, nz)] * n_x if odd else []),
        "pack_first",
        (
            [pltpu.VMEM((nx, ROWS, nz), jnp.int32), scratch(3, nx, ROWS, nz), scratch(nx, ROWS, nz)]
            + [pltpu.SemaphoreType.DMA((3,))]
            if odd
            else []
        )
        + [pltpu.VMEM((n_x, DEPTH, ny, nz), jnp.int32), scratch(n_x, 3, DEPTH, ny, nz)]
        + [pltpu.SemaphoreType.DMA((n_x, 3))],
    )
    to_x = sent[:n_x]
    got_x = [exchange(send, ("gx", turn)) for turn, send in enumerate(to_x)]
    if odd:
        got_odd = exchange(sent[n_x], ("gy", 1))
        corners = [exchange(send, ("gx", turn), ("gy", 1)) for turn, send in enumerate(sent[n_x + 1 :])]
    coef, press, vel, rhs = call(
        load,
        inputs + [to_x[0]],
        [HBM] * 3 + [ANY],
        [f32(*press.shape), f32(*press.shape), f32(*vel.shape), f32(*press.shape)],
        "load",
        [pltpu.VMEM(phase.shape, jnp.int32), pltpu.SemaphoreType.DMA((3,))],
    )
    rows_y = f32(total + nx // ROWS + 1, ROWS, nz)
    got_y, odd_rows = [], []
    if odd:
        odd_rows = call(
            functools.partial(merge_odd, nx),
            [got_odd, *corners],
            [VMEM] * (1 + n_x),
            [rows_y],
            "merge_odd",
        )
    if n_y:
        to_y = call(
            functools.partial(pack_y, nx, ny, n_x),
            [coef, press, vel, rhs, *got_x, *odd_rows],
            [VMEM] * (4 + n_x) + [ANY] * len(odd_rows),
            [rows_y],
            "pack_y",
        )
        got_y = [exchange(to_y[0], ("gy", 0)), *odd_rows]
    cube = (total, height, nz)
    full_coef, full_rhs, *to_z = call(
        functools.partial(pack_z, nx, ny, n_x, n_y, n_z),
        [coef, press, vel, rhs, *got_x, *got_y],
        [VMEM] * (4 + n_x + n_y),
        [f32(*cube)] * 2 + [f32(groups // 2 + 1, height, LANES)] * n_z,
        "pack_z",
    )
    got_z = [exchange(send, ("gz", turn)) for turn, send in enumerate(to_z)]
    basis, ends, shares = call(
        functools.partial(prepare, nx, ny, n_x, n_y),
        [coef, vel, rhs, full_coef, full_rhs, *got_x, *got_y],
        [VMEM] * (5 + n_x + n_y),
        [f32(3, *cube), f32(5, groups, height, LANES), f32(6, ROWS, LANES)],
        "prepare",
        [scratch(*cube), scratch(2, *cube), scratch(2, *cube), scratch(*cube)],
    )
    basis_z, vz_z, sums = call(
        functools.partial(join, nx, ny, n_z),
        [ends, shares, *got_z],
        [VMEM] * (2 + n_z),
        [f32(3, 2 * groups, height, LANES), f32(groups, height, LANES), f32(1, LANES)],
        "join",
        [scratch(6, 2 * groups, height, LANES), scratch(2 * groups, height, LANES)],
    )
    spread = jnp.broadcast_to(sums[None], (devices, 1, LANES))
    gathered = lax.all_to_all(spread, AXES, 0, 0).reshape(devices, LANES)
    return call(
        functools.partial(finish, nx, ny, n_x, n_y, n_z),
        [gathered, press, vel, basis, basis_z, vz_z, *got_x, *got_y, *got_z],
        [VMEM] * (6 + n_x + n_y + n_z),
        [f32(*vel.shape), f32(nx, ny, nz)],
        "finish",
        [scratch(*vel.shape), scratch(nx, ny, nz), pltpu.SemaphoreType.DMA((2, nx // STRIDE))],
        HBM,
    )


def solution(mesh):
    cells, faces = P(*AXES), P(None, *AXES)
    return jax.shard_map(
        on_device, mesh=mesh, in_specs=(cells, cells, faces), out_specs=(faces, cells), check_vma=False
    )
```

```python
import functools
import itertools

import jax
import jax.numpy as jnp
from jax import lax
from jax.experimental import pallas as pl
from jax.experimental.pallas import tpu as pltpu
from jax.sharding import PartitionSpec as P

AXES = ("gx", "gy", "gz")
SPARE = dict(gx="gy", gy="gz", gz="gx")
DEPTH = 4
GROUP = 4 * DEPTH
LANES = 128
STRIDE = 4
ROWS = 8
VMEM = pl.BlockSpec(memory_space=pltpu.VMEM)
HBM = pl.BlockSpec(memory_space=pltpu.HBM)
ANY = pl.BlockSpec(memory_space=pl.ANY)
PARAMS = pltpu.CompilerParams(vmem_limit_bytes=40 * 1024 * 1024)


def swaps(moves):
    sizes = [lax.axis_size(name) for name in AXES]
    number = lambda place: (place[0] * sizes[1] + place[1]) * sizes[2] + place[2]
    spare = AXES.index("gz" if len(moves) > 1 else SPARE[moves[0][0]])
    pairs = []
    for place in itertools.product(*map(range, sizes)):
        partner, met = list(place), True
        for axis, turn in moves:
            along = AXES.index(axis)
            partner[along] += 1 if (place[along] - turn) % 2 == 0 else -1
            met = met and 0 <= partner[along] < sizes[along]
        if not met:
            if sizes[spare] % 2:
                continue
            partner = list(place)
            partner[spare] ^= 1
        pairs.append((number(place), number(partner)))
    return pairs


def exchange(send, *moves):
    return lax.ppermute(send, AXES, swaps(moves))


def clear_if_alone(out, *moves):
    for axis, turn in moves:
        count, place = lax.axis_size(axis), lax.axis_index(axis)
        alone = []
        if turn == 1:
            alone.append(place == 0)
        if count % 2 != turn:
            alone.append(place == count - 1)
        for case in alone:

            @pl.when(case)
            def _():
                out[...] = jnp.zeros(out.shape, out.dtype)


def even(axis):
    return lax.axis_index(axis) % 2 == 0


def turns(axis):
    return min(2, lax.axis_size(axis) - 1)


def coefficient(phase):
    return jnp.where(phase == 0, 8.0, jnp.where(phase == 1, 1.0, 2.0)).astype(jnp.float32)


def sides(is_even, got, load):
    one = load(got[0])
    two = load(got[1]) if len(got) > 1 else jnp.zeros_like(one)
    return jnp.where(is_even, two, one), jnp.where(is_even, one, two)


def lane_index(shape):
    return lax.broadcasted_iota(jnp.int32, shape, len(shape) - 1)


def row_index(shape):
    return lax.broadcasted_iota(jnp.int32, shape, len(shape) - 2)


def roll_rows(plane, shift):
    return pltpu.roll(plane, shift % plane.shape[0], 0)


def roll_lanes(plane, shift):
    return pltpu.roll(plane, shift % plane.shape[1], 1)


def inner_rhs(coef, vy, vz):
    rows, lanes = row_index(coef.shape), lane_index(coef.shape)
    up = jnp.where(rows == coef.shape[0] - 1, 0.0, 0.5 * (coef + roll_rows(coef, -1)))
    down = jnp.where(rows == 0, 0.0, 0.5 * (coef + roll_rows(coef, 1)))
    right = jnp.where(lanes == LANES - 1, 0.0, 0.5 * (coef + roll_lanes(coef, -1)))
    left = jnp.where(lanes == 0, 0.0, 0.5 * (coef + roll_lanes(coef, 1)))
    return (up * vy - down * roll_rows(vy, 1)) + (right * vz - left * roll_lanes(vz, 1))


RHS, VX, PRESS, VY = DEPTH, 2 * DEPTH - 1, 2 * DEPTH, 2 * DEPTH + 1


def pack_first(nx, ny, n_x, n_y, phase, press, vel, *refs):
    outs, odd_outs, (held, held_vel, sem) = refs[:n_x], refs[n_x:-3], refs[-3:]
    if n_y > 1:
        *odd_outs, tile_phase, tile_vel, tile_press, tile_sem = odd_outs
    copies = []
    for turn, out in enumerate(outs):
        top = even("gx") == (turn == 0)
        deep = jnp.where(top, nx - DEPTH, 0)
        last = jnp.where(top, nx - 1, 0)
        parts = [
            (vel.at[:, pl.ds(deep, DEPTH)], held_vel.at[turn]),
            (phase.at[pl.ds(deep, DEPTH)], held.at[turn]),
            (press.at[last], out.at[pl.ds(PRESS * ny, ny)]),
        ]
        for which, (src, dst) in enumerate(parts):
            copy = pltpu.make_async_copy(src, dst, sem.at[turn, which])
            copy.start()
            copies.append(copy)
    if n_y > 1:
        row = pl.multiple_of(jnp.where(even("gy"), 0, ny - ROWS), ROWS)
        parts = [
            (phase.at[:, pl.ds(row, ROWS)], tile_phase),
            (vel.at[:, :, pl.ds(row, ROWS)], tile_vel),
            (press.at[:, pl.ds(row, ROWS)], tile_press),
        ]
        for which, (src, dst) in enumerate(parts):
            copy = pltpu.make_async_copy(src, dst, tile_sem.at[which])
            copy.start()
            copies.append(copy)
    for copy in copies:
        copy.wait()
    lanes = lane_index((ROWS, LANES))
    rows = row_index((ROWS, LANES))
    for turn, out in enumerate(outs):
        top = even("gx") == (turn == 0)
        coefs = [coefficient(held[turn, j]) for j in range(DEPTH)]
        flux = [0.5 * (coefs[j] + coefs[j + 1]) * held_vel[turn, 0, j] for j in range(DEPTH - 1)]
        columns = jnp.zeros((ROWS, LANES), jnp.float32)
        lines = jnp.zeros((ROWS, LANES), jnp.float32)
        for j in range(DEPTH):
            out[j * ny : (j + 1) * ny, :] = coefs[j]
        for j in range(DEPTH - 1):
            vy = jnp.where(top, held_vel[turn, 1, j + 1], held_vel[turn, 1, j])
            vz = jnp.where(top, held_vel[turn, 2, j + 1], held_vel[turn, 2, j])
            upper = (flux[j + 1] - flux[j]) if j + 1 < DEPTH - 1 else -flux[j]
            lower = (flux[j] - flux[j - 1]) if j else flux[j]
            inner = inner_rhs(jnp.where(top, coefs[j + 1], coefs[j]), vy, vz)
            out[(RHS + j) * ny : (RHS + j + 1) * ny, :] = jnp.where(top, upper, lower) + inner
            for t in range(ny // ROWS):
                lane = DEPTH * t + j
                columns = jnp.where(lanes == lane, roll_lanes(vz[t * ROWS : (t + 1) * ROWS], lane + 1), columns)
            lines = jnp.where(rows == j, roll_rows(vy[ny - ROWS :], j + 1), lines)
        out[VX * ny : (VX + 1) * ny, :] = held_vel[turn, 0, DEPTH - 1]
        out[VY * ny : VY * ny + ROWS, :] = lines
        out[VY * ny + ROWS :, :] = columns
        clear_if_alone(out, ("gx", turn))
    if n_y > 1:
        pack_odd(nx, tile_phase, tile_vel, tile_press, odd_outs)


def row_tile(coef, rhs, vy, top):
    rows = row_index((ROWS, LANES))
    coef = jnp.where(top, roll_rows(coef, DEPTH), coef)
    rhs = jnp.where(top, roll_rows(rhs, -1), roll_rows(rhs, DEPTH))
    return jnp.where(rows == ROWS - 1, vy, jnp.where(rows < DEPTH, coef, rhs))


def pack_odd(nx, tile_phase, tile_vel, tile_press, outs):
    out, *corners = outs
    top = jnp.logical_not(even("gy"))
    lanes = lane_index((ROWS, LANES))
    ends_at, vx_at = nx + nx // ROWS, nx + nx // ROWS + 1
    ends = jnp.zeros((ROWS, LANES), jnp.float32)
    here, old_flux = coefficient(tile_phase[0]), None
    for x in range(nx):
        vy, vz = tile_vel[1, x], tile_vel[2, x]
        answer = inner_rhs(here, vy, vz)
        if old_flux is not None:
            answer = answer - old_flux
        coef = here
        if x + 1 < nx:
            above = coefficient(tile_phase[x + 1])
            old_flux = 0.5 * (here + above) * tile_vel[0, x]
            answer = answer + old_flux
            here = above
        out[x] = row_tile(coef, answer, vy, top)
        ends = jnp.where(lanes == x, roll_lanes(vz, x + 1), ends)
        tile = tile_press[x]
        at = nx + x // ROWS
        out[at, x % ROWS : x % ROWS + 1, :] = jnp.where(top, tile[ROWS - 1 : ROWS], tile[0:1])
    shift = lambda tile: jnp.where(top, roll_rows(tile, -1), roll_rows(tile, DEPTH))
    ends = jnp.where(top, roll_rows(ends, DEPTH - 1), ends)
    out[ends_at] = ends
    out[vx_at] = shift(tile_vel[0, nx - 1])
    for turn, corner in enumerate(corners):
        first = jnp.where(even("gx") == (turn == 0), nx - DEPTH, 0)
        for j in range(DEPTH):
            corner[j] = out[first + j]
        corner[DEPTH] = pltpu.roll(ends, jnp.where(first == 0, 0, (DEPTH - nx) % LANES), 1)
        corner[DEPTH + 1] = out[vx_at]
        clear_if_alone(corner, ("gx", turn), ("gy", 1))
    clear_if_alone(out, ("gy", 1))


def merge_odd(nx, got, *refs):
    corners, out = refs[:-1], refs[-1]
    total = nx + 2 * DEPTH
    rows, lanes = row_index((ROWS, LANES)), lane_index((ROWS, LANES))
    ends_at, vx_at = nx + nx // ROWS, nx + nx // ROWS + 1
    low, high = zip(*[sides(even("gx"), corners, lambda ref: ref[j]) for j in range(DEPTH + 2)])
    tiles = [got[x] for x in range(nx)] + list(high[:DEPTH]) + list(low[:DEPTH])
    inner = (rows >= DEPTH) & (rows < ROWS - 1)

    def face(below, above, vx):
        weight = 0.5 * (tiles[below] + tiles[above])
        weight = jnp.where(even("gy"), roll_rows(weight, DEPTH - 1), roll_rows(weight, DEPTH))
        return jnp.where(inner, weight * vx, 0.0)

    low_face, high_face = face(total - 1, 0, low[DEPTH + 1]), face(nx - 1, nx, got[vx_at])
    for plane, tile in enumerate(tiles):
        if plane == 0:
            tile = tile - low_face
        if plane == total - 1:
            tile = tile + low_face
        if plane == nx - 1:
            tile = tile + high_face
        if plane == nx:
            tile = tile - high_face
        out[plane] = tile
    for at in range(nx // ROWS):
        out[total + at] = got[nx + at]
    ends = jnp.where(lanes < nx, got[ends_at], roll_lanes(high[DEPTH], nx))
    out[total + nx // ROWS] = jnp.where(lanes < nx + DEPTH, ends, roll_lanes(low[DEPTH], nx + DEPTH))


def load(phase, press, vel, after, coef, press_out, vel_out, rhs, held, sem):
    del after
    copies = []
    for which, (src, dst) in enumerate(((phase, held), (press, press_out), (vel, vel_out))):
        copies.append(pltpu.make_async_copy(src, dst, sem.at[which]))
        copies[-1].start()
    copies[0].wait()
    copies[1].wait()
    copies[2].wait()
    nx = coef.shape[0]
    here = coefficient(held[0])
    old_flux = None
    for x in range(nx):
        coef[x] = here
        answer = inner_rhs(here, vel_out[1, x], vel_out[2, x])
        if old_flux is not None:
            answer = answer - old_flux
        if x + 1 < nx:
            above = coefficient(held[x + 1])
            old_flux = 0.5 * (here + above) * vel_out[0, x]
            answer = answer + old_flux
            here = above
        rhs[x] = answer


class Block:
    def __init__(self, nx, ny, coef, vel, rhs, got_x, row=0, height=None, faces=True):
        self.nx, self.ny = nx, ny
        self.own_coef, self.vel, self.own_rhs, self.got_x = coef, vel, rhs, got_x
        self.even = even("gx")
        self.row, self.height = row, height or ny
        if not faces:
            return
        self.low_face = 0.5 * (self.coef(nx + 2 * DEPTH - 1) + self.coef(0)) * self.halo(VX)[0]
        self.high_face = 0.5 * (self.coef(nx - 1) + self.coef(nx)) * self.take(vel, 0, nx - 1)

    def take(self, ref, *index):
        return ref[(*index, pl.ds(self.row, self.height), slice(None))]

    def halo(self, part):
        return sides(self.even, self.got_x, lambda ref: ref[pl.ds(part * self.ny + self.row, self.height), :])

    def coef(self, plane):
        if plane < self.nx:
            return self.take(self.own_coef, plane)
        above = plane < self.nx + DEPTH
        return self.halo((plane - self.nx) % DEPTH)[1 if above else 0]

    def rhs(self, plane):
        nx = self.nx
        if plane < nx:
            answer = self.take(self.own_rhs, plane)
        else:
            above = plane < nx + DEPTH
            layer = plane - nx if above else plane - nx - DEPTH - 1
            if layer < 0 or layer >= DEPTH - 1:
                return jnp.zeros((self.height, LANES), jnp.float32)
            answer = self.halo(RHS + layer)[1 if above else 0]
        if plane == 0:
            answer = answer - self.low_face
        if plane == nx + 2 * DEPTH - 1:
            answer = answer + self.low_face
        if plane == nx - 1:
            answer = answer + self.high_face
        if plane == nx:
            answer = answer - self.high_face
        return answer

    def layer(self, plane):
        if plane < self.nx + DEPTH:
            place = (1, plane - self.nx)
        else:
            place = (0, plane - self.nx - DEPTH - 1)
        return place if 0 <= place[1] < DEPTH - 1 else None

    def columns(self):
        at = VY * self.ny + ROWS
        return sides(self.even, self.got_x, lambda ref: ref[at : at + ROWS, :])

    def vz_end(self, plane, lane):
        if plane < self.nx:
            return roll_lanes(self.vel[2, plane], lane + 1)
        place = self.layer(plane)
        if place is None:
            return jnp.zeros((self.ny, LANES), jnp.float32)
        source = self.columns()[place[0]]
        return jnp.concatenate(
            [roll_lanes(source, lane - DEPTH * t - place[1]) for t in range(self.ny // ROWS)], 0
        )

    def vy_end(self, plane):
        if plane < self.nx:
            return self.vel[1, plane, self.ny - 1 :, :]
        place = self.layer(plane)
        if place is None:
            return jnp.zeros((1, LANES), jnp.float32)
        at = VY * self.ny + place[1]
        return sides(self.even, self.got_x, lambda ref: ref[at : at + 1, :])[place[0]]


def pack_y(nx, ny, n_x, coef, press, vel, rhs, *refs):
    got_x, out = refs[:n_x], refs[-1]
    total = nx + 2 * DEPTH
    lanes = lane_index((ROWS, LANES))
    top = even("gy")
    row = pl.multiple_of(jnp.where(top, ny - ROWS, 0), ROWS)
    block = Block(nx, ny, coef, vel, rhs, got_x, row, ROWS)
    columns = jnp.zeros((ROWS, LANES), jnp.float32)
    ends = block.columns()
    for plane in range(total):
        out[plane] = row_tile(block.coef(plane), block.rhs(plane), block.vy_end(plane), top)
        if plane < nx:
            source = roll_lanes(vel[2, plane, pl.ds(row, ROWS), :], plane + 1)
        elif block.layer(plane) is None:
            continue
        else:
            side, layer = block.layer(plane)
            high = (plane - layer - DEPTH * (ny // ROWS - 1)) % LANES
            source = pltpu.roll(ends[side], jnp.where(top, high, (plane - layer) % LANES), 1)
        columns = jnp.where(lanes == plane, source, columns)
    out[total + nx // ROWS] = jnp.where(top, roll_rows(columns, DEPTH - 1), columns)
    for plane in range(nx):
        tile = press[plane, pl.ds(row, ROWS), :]
        edge = jnp.where(top, tile[ROWS - 1 : ROWS], tile[0:1])
        out[total + plane // ROWS, plane % ROWS : plane % ROWS + 1, :] = edge
    clear_if_alone(out, ("gy", 0))


def tall_end(block, tile_end, plane, lane):
    return jnp.concatenate([block.vz_end(plane, lane), roll_lanes(tile_end, lane - plane)], 0)


def tile_of_ends(nx, even_y, got_y):
    rows = row_index((ROWS, LANES))
    low, high = sides(even_y, got_y, lambda ref: ref[nx + 2 * DEPTH + nx // ROWS])
    return jnp.where(rows < DEPTH, high, roll_rows(low, DEPTH + 1))


def press_lane(x):
    return GROUP * (x % ROWS) + ROWS + 2 * (x // ROWS)


def pack_plane(lanes, at, top, coef, rhs, end):
    coef = pltpu.roll(coef, jnp.where(top, (at + DEPTH) % LANES, at), 1)
    rhs = pltpu.roll(rhs, jnp.where(top, (at + ROWS - 1) % LANES, at + DEPTH), 1)
    value = jnp.where(lanes == at + ROWS - 1, end, 0.0)
    value = jnp.where((lanes >= at + DEPTH) & (lanes < at + ROWS - 1), rhs, value)
    return jnp.where((lanes >= at) & (lanes < at + DEPTH), coef, value)


def half_tile(tile, below):
    rows = row_index((ROWS, LANES))
    coef = jnp.where(below, jnp.where(rows >= DEPTH, roll_rows(tile, DEPTH), 0.0), jnp.where(rows < DEPTH, tile, 0.0))
    rhs = jnp.where(
        below,
        jnp.where(rows > DEPTH, roll_rows(tile, 1), 0.0),
        jnp.where(rows < DEPTH - 1, roll_rows(tile, -DEPTH), 0.0),
    )
    return coef, rhs


def half_ends(tile, below):
    rows = row_index((ROWS, LANES))
    return jnp.where(
        below, jnp.where(rows > DEPTH, roll_rows(tile, DEPTH + 1), 0.0), jnp.where(rows < DEPTH - 1, tile, 0.0)
    )


def face_y(own_low, own_high, coef_tile, tile, vy_end, below):
    rows = row_index((ROWS, LANES))
    down = 0.5 * (coef_tile[ROWS - 1 :] + own_low) * tile[ROWS - 1 :]
    up = 0.5 * (own_high + coef_tile[:1]) * vy_end
    outside = jnp.where(below, jnp.where(rows == ROWS - 1, down, 0.0), jnp.where(rows == 0, -up, 0.0))
    inside = jnp.where(below, jnp.where(rows == 0, -down, 0.0), jnp.where(rows == ROWS - 1, up, 0.0))
    return outside, inside


def stage_z(nx, ny, n_x, n_z, coef, press, vel, rhs, *refs):
    got_x, (*got_odd, full_coef, full_rhs), sends = refs[:n_x], refs[n_x : len(refs) - n_z], refs[len(refs) - n_z :]
    total, height = nx + 2 * DEPTH, ny + 2 * DEPTH
    groups = total // ROWS
    below = even("gy")
    lanes = lane_index((height, LANES))
    block = Block(nx, ny, coef, vel, rhs, got_x)
    nothing = jnp.zeros((ROWS, LANES), jnp.float32)
    tile_end = half_ends(got_odd[0][total + nx // ROWS], below) if got_odd else nothing
    made = [[jnp.zeros((height, LANES), jnp.float32) for _ in range(groups // 2 + 1)] for _ in sends]
    row = pl.ds(pl.multiple_of(jnp.where(below, 0, ny - ROWS), ROWS), ROWS)
    for plane in range(total):
        c_own, r_own = block.coef(plane), block.rhs(plane)
        c_tile = r_tile = nothing
        full_rhs[plane, :ny, :] = r_own
        if got_odd:
            tile = got_odd[0][plane]
            c_tile, r_tile = half_tile(tile, below)
            outside, inside = face_y(c_own[:1], c_own[ny - 1 :], c_tile, tile, block.vy_end(plane), below)
            r_tile = r_tile + outside
            full_rhs[plane, row, :] = full_rhs[plane, row, :] + inside
        c_all = jnp.concatenate([c_own, c_tile], 0)
        full_coef[plane] = c_all
        full_rhs[plane, ny:, :] = r_tile
        r_all = full_rhs[plane]
        group, seat = plane % groups, plane // groups
        at = GROUP * seat + ROWS * (group % 2)
        end = tall_end(block, tile_end, plane, at + ROWS - 1)
        for turn in range(n_z):
            value = pack_plane(lanes, at, even("gz") == (turn == 0), c_all, r_all, end)
            made[turn][group // 2] = made[turn][group // 2] + value
    for turn, send in enumerate(sends):
        top = even("gz") == (turn == 0)
        value = made[turn][groups // 2][:ny]
        for plane in range(nx):
            at = press_lane(plane)
            moved = pltpu.roll(press[plane], jnp.where(top, (at + 1) % LANES, at), 1)
            value = jnp.where(lanes[:ny] == at, moved, value)
        made[turn][groups // 2] = jnp.concatenate([value, made[turn][groups // 2][ny:]], 0)
        for which, value in enumerate(made[turn]):
            send[which] = value


def pack_z(nx, ny, n_x, n_z, vel, *refs):
    got_x, got, (full_coef, full_rhs, *sends) = refs[:n_x], refs[n_x], refs[-2 - n_z :]
    total = nx + 2 * DEPTH
    groups = total // ROWS
    below = jnp.logical_not(even("gy"))
    lanes = lane_index((ROWS, LANES))
    block = Block(nx, ny, full_coef, vel, full_rhs, got_x, faces=False)
    tile_end = half_ends(got[total + nx // ROWS], below)
    row = pl.ds(pl.multiple_of(jnp.where(below, 0, ny - ROWS), ROWS), ROWS)
    added = [[[jnp.zeros((ROWS, LANES), jnp.float32) for _ in range(2)] for _ in range(groups // 2 + 1)] for _ in sends]
    for plane in range(total):
        tile = got[plane]
        c_tile, r_tile = half_tile(tile, below)
        low, high = full_coef[plane, :1, :], full_coef[plane, ny - 1 : ny, :]
        outside, inside = face_y(low, high, c_tile, tile, block.vy_end(plane), below)
        r_tile = r_tile + outside
        full_coef[plane, ny:, :] = full_coef[plane, ny:, :] + c_tile
        full_rhs[plane, ny:, :] = full_rhs[plane, ny:, :] + r_tile
        full_rhs[plane, row, :] = full_rhs[plane, row, :] + inside
        group, seat = plane % groups, plane // groups
        at = GROUP * seat + ROWS * (group % 2)
        end = roll_lanes(tile_end, at + ROWS - 1 - plane)
        for turn in range(n_z):
            top = even("gz") == (turn == 0)
            inside_move = pltpu.roll(inside, jnp.where(top, (at + ROWS - 1) % LANES, at + DEPTH), 1)
            inside_move = jnp.where((lanes >= at + DEPTH) & (lanes < at + ROWS - 1), inside_move, 0.0)
            slot = added[turn][group // 2]
            slot[0] = slot[0] + pack_plane(lanes, at, top, c_tile, r_tile, end)
            slot[1] = slot[1] + inside_move
    for turn, send in enumerate(sends):
        for which, (tile, inside) in enumerate(added[turn]):
            send[which, ny:, :] = send[which, ny:, :] + tile
            send[which, row, :] = send[which, row, :] + inside
        clear_if_alone(send, ("gz", turn))


def tree_sum(parts):
    while len(parts) > 1:
        parts = [parts[i] + parts[i + 1] if i + 1 < len(parts) else parts[i] for i in range(0, len(parts), 2)]
    return parts[0]


class Totals:
    def __init__(self):
        self.stack = []

    def add(self, tile):
        level = 0
        while self.stack and self.stack[-1][0] == level:
            tile = self.stack.pop()[1] + tile
            level += 1
        self.stack.append((level, tile))

    def value(self):
        tiles = [tile for _, tile in self.stack]
        total = tiles.pop()
        while tiles:
            total = tiles.pop() + total
        return total


def prepare(nx, ny, n_x, n_y, coef, vel, rhs, full_coef, full_rhs, *refs):
    got_x, got_y = refs[:n_x], refs[n_x : n_x + n_y]
    basis, ends, shares, wx, wy, wz, inverse = refs[n_x + n_y :]
    total, height = nx + 2 * DEPTH, ny + 2 * DEPTH
    groups = total // ROWS
    lanes = lane_index((height, LANES))
    block = Block(nx, ny, coef, vel, rhs, got_x)
    tile_end = tile_of_ends(nx, even("gy"), got_y)
    for group in range(groups):
        made = [jnp.zeros((height, LANES), jnp.float32) for _ in range(5)]
        for seat in range(ROWS):
            plane = seat * groups + group
            at = GROUP * seat
            for which, source in enumerate((full_coef[plane], full_rhs[plane])):
                here = (lanes >= at + DEPTH) & (lanes < at + GROUP)
                made[2 * which] = jnp.where(here, roll_lanes(source, at + DEPTH), made[2 * which])
                here = (lanes >= at) & (lanes < at + GROUP - DEPTH)
                made[2 * which + 1] = jnp.where(here, roll_lanes(source, at + GROUP - DEPTH), made[2 * which + 1])
            lane = at + GROUP - DEPTH - 1
            made[4] = jnp.where(lanes == lane, tall_end(block, tile_end, plane, lane), made[4])
        for which in range(5):
            ends[which, group] = made[which]
    totals = [Totals() for _ in range(6)]
    trusted = (lanes[:ROWS] >= DEPTH) & (lanes[:ROWS] < LANES - DEPTH)

    def count(which, left, right):
        product = left[:ny] * right[:ny]
        tile = tree_sum([product[i : i + ROWS] for i in range(0, ny, ROWS)])
        totals[which].add(jnp.where(trusted, tile, 0.0))

    old_weight = None
    here = full_coef[nx + DEPTH]
    for x in range(-DEPTH, nx + DEPTH - 1):
        e = x % total
        above = full_coef[(e + 1) % total]
        weight = 0.5 * (here + above)
        wx[e] = weight
        if x > -DEPTH:
            up, down = 0.5 * (here + roll_rows(here, -1)), 0.5 * (here + roll_rows(here, 1))
            right = jnp.where(lanes == LANES - 1, 0.0, 0.5 * (here + roll_lanes(here, -1)))
            left = jnp.where(lanes == 0, 0.0, 0.5 * (here + roll_lanes(here, 1)))
            wy[0, e], wy[1, e], wz[0, e], wz[1, e] = up, down, right, left
            diag = (weight + old_weight) + (up + down) + (right + left)
            inside = here > 0
            scale = jnp.where(inside, 1.0 / jnp.where(inside, diag, 1.0), 0.0)
            inverse[e] = scale
            source = full_rhs[e]
            field = scale * source
            basis[0, e] = field
            if 0 <= x < nx:
                count(0, field, source)
        old_weight, here = weight, above
    for n in range(3):
        reach = 2 - n
        old_flux = None
        here = basis[n, (-reach - 1) % total]
        for x in range(-reach - 1, nx + reach):
            e = x % total
            above = basis[n, (e + 1) % total]
            flux = wx[e] * (above - here)
            if x >= -reach:
                image = old_flux - flux
                image = image + (
                    wy[0, e] * (here - roll_rows(here, -1)) + wy[1, e] * (here - roll_rows(here, 1))
                )
                image = image + (
                    wz[0, e] * (here - roll_lanes(here, -1)) + wz[1, e] * (here - roll_lanes(here, 1))
                )
                own = 0 <= x < nx
                if own:
                    count(2 * n + 1, here, image)
                if n < 2:
                    following = inverse[e] * image
                    basis[n + 1, e] = following
                    if own:
                        count(2 * n + 2, following, image)
            old_flux, here = flux, above
    for which, total_ in enumerate(totals):
        shares[which] = total_.value()


def join(nx, ny, n_z, ends, shares, *refs):
    got_z = refs[:n_z]
    basis_z, vz_z, sums, weight_z, inverse_z = refs[n_z:]
    total, height = nx + 2 * DEPTH, ny + 2 * DEPTH
    groups = total // ROWS
    lanes = lane_index((height, LANES))
    seat_lane, seat = lanes % GROUP, lanes // GROUP
    coef, rhs, vz = [], [], []
    for side in range(2):
        for g in range(groups):
            got = sides(even("gz"), got_z, lambda ref: ref[g // 2])[side]
            skip = ROWS * (g % 2)
            if side == 0:
                outer = seat_lane < DEPTH
                coef.append(jnp.where(outer, roll_lanes(got, -skip), ends[0, g]))
                rhs.append(jnp.where(outer, roll_lanes(got, 1 - DEPTH - skip), ends[2, g]))
                vz.append(roll_lanes(got, -DEPTH - skip))
                vz_z[g] = vz[-1]
            else:
                outer = seat_lane >= GROUP - DEPTH
                coef.append(jnp.where(outer, roll_lanes(got, GROUP - DEPTH - skip), ends[1, g]))
                rhs.append(jnp.where(outer, roll_lanes(got, GROUP - 2 * DEPTH - skip), ends[3, g]))
                vz.append(ends[4, g])

    def along(planes, q, step):
        g = q % groups
        if 0 <= g + step < groups:
            return planes[q + step]
        return roll_lanes(planes[q - g + (g + step) % groups], -GROUP * step)

    totals = [Totals() for _ in range(6)]

    def count(which, q, left, right):
        first = DEPTH if q < groups else GROUP - 2 * DEPTH
        spot = seat_lane[:ROWS]
        mine = (spot >= first) & (spot < first + DEPTH) & (seat[:ROWS] * groups + q % groups < nx)
        product = left[:ny] * right[:ny]
        tile = tree_sum([product[i : i + ROWS] for i in range(0, ny, ROWS)])
        totals[which].add(jnp.where(mine, tile, 0.0))

    field = []
    for q in range(2 * groups):
        here = coef[q]
        neighbours = (along(coef, q, 1), along(coef, q, -1), roll_rows(here, -1), roll_rows(here, 1))
        neighbours += (roll_lanes(here, -1), roll_lanes(here, 1))
        weights = [0.5 * (here + other) for other in neighbours]
        for which, weight in enumerate(weights):
            weight_z[which, q] = weight
        diag = (weights[0] + weights[1]) + (weights[2] + weights[3]) + (weights[4] + weights[5])
        face = DEPTH - 1 if q < groups else GROUP - DEPTH - 1
        source = rhs[q] + jnp.where(seat_lane == face, weights[4] * vz[q], 0.0)
        source = source - jnp.where(seat_lane == face + 1, weights[5] * roll_lanes(vz[q], 1), 0.0)
        inside = here > 0
        scale = jnp.where(inside, 1.0 / jnp.where(inside, diag, 1.0), 0.0)
        inverse_z[q] = scale
        field.append(scale * source)
        basis_z[0, q] = field[q]
        count(0, q, field[q], source)
    for n in range(3):
        following = []
        for q in range(2 * groups):
            here = field[q]
            image = weight_z[0, q] * (here - along(field, q, 1)) + weight_z[1, q] * (here - along(field, q, -1))
            image = image + (
                weight_z[2, q] * (here - roll_rows(here, -1)) + weight_z[3, q] * (here - roll_rows(here, 1))
            )
            image = image + (
                weight_z[4, q] * (here - roll_lanes(here, -1)) + weight_z[5, q] * (here - roll_lanes(here, 1))
            )
            count(2 * n + 1, q, here, image)
            if n < 2:
                following.append(inverse_z[q] * image)
                basis_z[n + 1, q] = following[q]
                count(2 * n + 2, q, following[q], image)
        field = following
    lane = lane_index((1, LANES))
    row = jnp.zeros((1, LANES), jnp.float32)
    for which, total_ in enumerate(totals):
        value = total_.value() + shares[which]
        value = jnp.sum(jnp.sum(value, 0, keepdims=True), 1, keepdims=True)
        row = jnp.where(lane == which, value, row)
    sums[...] = row


def finish(nx, ny, n_x, n_y, n_z, gathered, press, vel, basis, basis_z, vz_z, *refs):
    got_x, got_y, got_z = refs[:n_x], refs[n_x : n_x + n_y], refs[n_x + n_y : n_x + n_y + n_z]
    ustar_out, coef_out, ustar, coef_cot, sem = refs[n_x + n_y + n_z :]
    even_x, even_y, even_z = even("gx"), even("gy"), even("gz")
    total, height = nx + 2 * DEPTH, ny + 2 * DEPTH
    groups = total // ROWS
    parts = gathered[...]
    while parts.shape[0] > ROWS:
        half = parts.shape[0] // 2
        parts = parts[:half] + parts[half:]
    sums = jnp.sum(parts, 0, keepdims=True)
    lane = lane_index((1, LANES))
    m0, m1, m2, m3, m4, m5 = [
        jnp.sum(jnp.where(lane == which, sums, 0.0), 1, keepdims=True) for which in range(6)
    ]
    l1, l2 = m2 / m1, m3 / m1
    d1, cross, d2 = m3 - l1 * m2, m4 - l1 * m3, m5 - l2 * m3
    l21 = cross / d1
    d2 = d2 - l21 * cross
    y1 = -l1 * m0 + m1
    y2 = m2 - l2 * m0 - l21 * y1
    c2 = y2 / d2
    c1 = y1 / d1 - l21 * c2
    c0 = (m0 / m1 - l1 * c1 - l2 * c2)[0, 0]
    c1, c2 = c1[0, 0], c2[0, 0]

    lanes = lane_index((height, LANES))
    seat_lane = lanes % GROUP
    spill = []
    for g in range(groups):
        low, high = [
            c0 * basis_z[0, q] + c1 * basis_z[1, q] + c2 * basis_z[2, q] for q in (g, groups + g)
        ]
        cells = jnp.where(seat_lane < DEPTH - 1, roll_lanes(high, DEPTH - GROUP + DEPTH - 1), roll_lanes(low, -1))
        cells = jnp.where(seat_lane == 2 * DEPTH - 2, roll_lanes(high, 2 * DEPTH - 2 - (GROUP - DEPTH)), cells)
        spill.append(jnp.where(seat_lane == 2 * DEPTH - 1, roll_lanes(low, DEPTH), cells))
    spoiled = (lanes < DEPTH - 1) | (lanes > LANES - DEPTH)
    lanes = lane_index((ny, LANES))
    at_low, at_high = lanes == 0, lanes == LANES - 1
    low_z, high_z = sides(even_z, got_z, lambda ref: ref[groups // 2, :ny, :])
    press_z = jnp.where(lanes % 2 == 0, high_z, roll_lanes(low_z, 1))
    p_low, p_high = sides(even_x, got_x, lambda ref: ref[PRESS * ny : (PRESS + 1) * ny, :])
    u_low, _ = sides(even_x, got_x, lambda ref: ref[VX * ny : (VX + 1) * ny, :])

    def solved(x):
        e = x % total
        cells = c0 * basis[0, e] + c1 * basis[1, e] + c2 * basis[2, e]
        return jnp.where(spoiled, roll_lanes(spill[e % groups], 1 - DEPTH - GROUP * (e // groups)), cells)

    copies = []
    rows = row_index((ROWS, LANES))
    below, here = solved(-1), solved(0)
    face_low = (p_low - press[0]) * (u_low + here[:ny] - below[:ny])
    for x in range(nx):
        above = solved(x + 1)
        group, seat = x % groups, x // groups
        own, p = here[:ny], press[x]
        out = vel[0, x] + (above[:ny] - own)
        ustar[0, x] = out
        face = (p - (press[x + 1] if x + 1 < nx else p_high)) * out
        answer = face_low + face
        face_low = face
        low, high = sides(even_y, got_y, lambda ref: ref[total + x // ROWS, x % ROWS : x % ROWS + 1, :])
        shape = (ROWS, LANES)
        p_tile = jnp.where(rows == 0, jnp.broadcast_to(high, shape), jnp.broadcast_to(low, shape))
        p_tall = jnp.concatenate([p, p_tile], 0)
        u_row, _ = sides(even_y, got_y, lambda ref: ref[x, ROWS - 1 :, :])
        u_tall = jnp.concatenate([vel[1, x], jnp.broadcast_to(u_row, shape)], 0)
        out = vel[1, x] + (roll_rows(here, -1)[:ny] - own)
        ustar[1, x] = out
        back = roll_rows(u_tall, 1)[:ny] + (own - roll_rows(here, 1)[:ny])
        answer = answer + ((p - roll_rows(p_tall, -1)[:ny]) * out + (roll_rows(p_tall, 1)[:ny] - p) * back)
        lam_end = roll_lanes(spill[group][:ny], 1 - 2 * DEPTH - GROUP * seat)
        u_end = roll_lanes(vz_z[group, :ny, :], 1 - DEPTH - GROUP * seat)
        p_end = roll_lanes(press_z, LANES - 1 - press_lane(x))
        out = vel[2, x] + (jnp.where(at_high, lam_end, roll_lanes(own, -1)) - own)
        ustar[2, x] = out
        answer = answer + (p - jnp.where(at_high, p_end, roll_lanes(p, -1))) * out
        back = jnp.where(at_low, u_end, roll_lanes(vel[2, x], 1))
        back = back + (own - jnp.where(at_low, lam_end, roll_lanes(own, 1)))
        answer = answer + (jnp.where(at_low, p_end, roll_lanes(p, 1)) - p) * back
        coef_cot[x] = 0.5 * answer
        here = above
        if (x + 1) % STRIDE == 0:
            part = pl.ds(x + 1 - STRIDE, STRIDE)
            for which, (src, dst) in enumerate(
                ((ustar.at[:, part], ustar_out.at[:, part]), (coef_cot.at[part], coef_out.at[part]))
            ):
                copies.append(pltpu.make_async_copy(src, dst, sem.at[which, x // STRIDE]))
                copies[-1].start()
    for copy in copies:
        copy.wait()


def on_device(phase, press, vel):
    nx, ny, nz = phase.shape
    total, height = nx + 2 * DEPTH, ny + 2 * DEPTH
    groups = total // ROWS
    devices = lax.axis_size(AXES)
    n_x, n_y, n_z = (turns(axis) for axis in AXES)
    f32 = lambda *shape: jax.ShapeDtypeStruct(shape, jnp.float32)
    scratch = lambda *shape: pltpu.VMEM(shape, jnp.float32)
    inputs = [pltpu.with_memory_space_constraint(array, pltpu.HBM) for array in (phase, press, vel)]

    def call(kernel, args, in_specs, shapes, name, scratch_shapes=(), out_spec=VMEM, aliases={}):
        return pl.pallas_call(
            kernel,
            out_shape=shapes,
            in_specs=in_specs,
            out_specs=[out_spec] * len(shapes),
            scratch_shapes=list(scratch_shapes),
            input_output_aliases=aliases,
            compiler_params=PARAMS,
            cost_estimate=pl.CostEstimate(flops=3_000_000, bytes_accessed=3_000_000, transcendentals=0),
            name=name,
        )(*args)

    odd = n_y > 1
    sent = call(
        functools.partial(pack_first, nx, ny, n_x, n_y),
        inputs,
        [HBM] * 3,
        [f32(VY * ny + 2 * ROWS, nz)] * n_x
        + ([f32(nx + nx // ROWS + 2, ROWS, nz)] + [f32(DEPTH + 2, ROWS, nz)] * n_x if odd else []),
        "pack_first",
        (
            [pltpu.VMEM((nx, ROWS, nz), jnp.int32), scratch(3, nx, ROWS, nz), scratch(nx, ROWS, nz)]
            + [pltpu.SemaphoreType.DMA((3,))]
            if odd
            else []
        )
        + [pltpu.VMEM((n_x, DEPTH, ny, nz), jnp.int32), scratch(n_x, 3, DEPTH, ny, nz)]
        + [pltpu.SemaphoreType.DMA((n_x, 3))],
    )
    to_x = sent[:n_x]
    got_x = [exchange(send, ("gx", turn)) for turn, send in enumerate(to_x)]
    if odd:
        got_odd = exchange(sent[n_x], ("gy", 1))
        corners = [exchange(send, ("gx", turn), ("gy", 1)) for turn, send in enumerate(sent[n_x + 1 :])]
    coef, press, vel, rhs = call(
        load,
        inputs + [to_x[0]],
        [HBM] * 3 + [ANY],
        [f32(*press.shape), f32(*press.shape), f32(*vel.shape), f32(*press.shape)],
        "load",
        [pltpu.VMEM(phase.shape, jnp.int32), pltpu.SemaphoreType.DMA((3,))],
    )
    rows_y = f32(total + nx // ROWS + 1, ROWS, nz)
    got_y, odd_rows = [], []
    if odd:
        odd_rows = call(
            functools.partial(merge_odd, nx),
            [got_odd, *corners],
            [VMEM] * (1 + n_x),
            [rows_y],
            "merge_odd",
        )
    if n_y:
        to_y = call(
            functools.partial(pack_y, nx, ny, n_x),
            [coef, press, vel, rhs, *got_x, *odd_rows],
            [VMEM] * (4 + n_x) + [ANY] * len(odd_rows),
            [rows_y],
            "pack_y",
        )
        got_y = [exchange(to_y[0], ("gy", 0)), *odd_rows]
    cube = (total, height, nz)
    packs = [f32(groups // 2 + 1, height, LANES)] * n_z
    staged = call(
        functools.partial(stage_z, nx, ny, n_x, n_z),
        [coef, press, vel, rhs, *got_x, *odd_rows],
        [VMEM] * (4 + n_x + len(odd_rows)),
        [f32(*cube)] * 2 + packs,
        "stage_z",
    )
    full_coef, full_rhs, *to_z = call(
        functools.partial(pack_z, nx, ny, n_x, n_z),
        [vel, *got_x, got_y[0], *staged],
        [VMEM] * (4 + n_x + n_z),
        [f32(*cube)] * 2 + packs,
        "pack_z",
        aliases={2 + n_x + which: which for which in range(2 + n_z)},
    )
    got_z = [exchange(send, ("gz", turn)) for turn, send in enumerate(to_z)]
    basis, ends, shares = call(
        functools.partial(prepare, nx, ny, n_x, n_y),
        [coef, vel, rhs, full_coef, full_rhs, *got_x, *got_y],
        [VMEM] * (5 + n_x + n_y),
        [f32(3, *cube), f32(5, groups, height, LANES), f32(6, ROWS, LANES)],
        "prepare",
        [scratch(*cube), scratch(2, *cube), scratch(2, *cube), scratch(*cube)],
    )
    basis_z, vz_z, sums = call(
        functools.partial(join, nx, ny, n_z),
        [ends, shares, *got_z],
        [VMEM] * (2 + n_z),
        [f32(3, 2 * groups, height, LANES), f32(groups, height, LANES), f32(1, LANES)],
        "join",
        [scratch(6, 2 * groups, height, LANES), scratch(2 * groups, height, LANES)],
    )
    spread = jnp.broadcast_to(sums[None], (devices, 1, LANES))
    gathered = lax.all_to_all(spread, AXES, 0, 0).reshape(devices, LANES)
    return call(
        functools.partial(finish, nx, ny, n_x, n_y, n_z),
        [gathered, press, vel, basis, basis_z, vz_z, *got_x, *got_y, *got_z],
        [VMEM] * (6 + n_x + n_y + n_z),
        [f32(*vel.shape), f32(nx, ny, nz)],
        "finish",
        [scratch(*vel.shape), scratch(nx, ny, nz), pltpu.SemaphoreType.DMA((2, nx // STRIDE))],
        HBM,
    )


def solution(mesh):
    cells, faces = P(*AXES), P(None, *AXES)
    return jax.shard_map(
        on_device, mesh=mesh, in_specs=(cells, cells, faces), out_specs=(faces, cells), check_vma=False
    )
```

```python
import functools
import itertools

import jax
import jax.numpy as jnp
from jax import lax
from jax.experimental import pallas as pl
from jax.experimental.pallas import tpu as pltpu
from jax.sharding import PartitionSpec as P

AXES = ("gx", "gy", "gz")
SPARE = dict(gx="gy", gy="gz", gz="gx")
DEPTH = 4
GROUP = 4 * DEPTH
LANES = 128
STRIDE = 4
ROWS = 8
VMEM = pl.BlockSpec(memory_space=pltpu.VMEM)
HBM = pl.BlockSpec(memory_space=pltpu.HBM)
ANY = pl.BlockSpec(memory_space=pl.ANY)
PARAMS = pltpu.CompilerParams(vmem_limit_bytes=40 * 1024 * 1024)


def swaps(moves):
    sizes = [lax.axis_size(name) for name in AXES]
    number = lambda place: (place[0] * sizes[1] + place[1]) * sizes[2] + place[2]
    spare = AXES.index("gz" if len(moves) > 1 else SPARE[moves[0][0]])
    pairs = []
    for place in itertools.product(*map(range, sizes)):
        partner, met = list(place), True
        for axis, turn in moves:
            along = AXES.index(axis)
            partner[along] += 1 if (place[along] - turn) % 2 == 0 else -1
            met = met and 0 <= partner[along] < sizes[along]
        if not met:
            if sizes[spare] % 2:
                continue
            partner = list(place)
            partner[spare] ^= 1
        pairs.append((number(place), number(partner)))
    return pairs


def exchange(send, *moves):
    return lax.ppermute(send, AXES, swaps(moves))


def clear_if_alone(out, *moves):
    for axis, turn in moves:
        count, place = lax.axis_size(axis), lax.axis_index(axis)
        alone = []
        if turn == 1:
            alone.append(place == 0)
        if count % 2 != turn:
            alone.append(place == count - 1)
        for case in alone:

            @pl.when(case)
            def _():
                out[...] = jnp.zeros(out.shape, out.dtype)


def even(axis):
    return lax.axis_index(axis) % 2 == 0


def turns(axis):
    return min(2, lax.axis_size(axis) - 1)


def coefficient(phase):
    return jnp.where(phase == 0, 8.0, jnp.where(phase == 1, 1.0, 2.0)).astype(jnp.float32)


def sides(is_even, got, load):
    one = load(got[0])
    two = load(got[1]) if len(got) > 1 else jnp.zeros_like(one)
    return jnp.where(is_even, two, one), jnp.where(is_even, one, two)


def lane_index(shape):
    return lax.broadcasted_iota(jnp.int32, shape, len(shape) - 1)


def row_index(shape):
    return lax.broadcasted_iota(jnp.int32, shape, len(shape) - 2)


def roll_rows(plane, shift):
    return pltpu.roll(plane, shift % plane.shape[0], 0)


def roll_lanes(plane, shift):
    return pltpu.roll(plane, shift % plane.shape[1], 1)


def inner_rhs(coef, vy, vz):
    rows, lanes = row_index(coef.shape), lane_index(coef.shape)
    up = jnp.where(rows == coef.shape[0] - 1, 0.0, 0.5 * (coef + roll_rows(coef, -1)))
    down = jnp.where(rows == 0, 0.0, 0.5 * (coef + roll_rows(coef, 1)))
    right = jnp.where(lanes == LANES - 1, 0.0, 0.5 * (coef + roll_lanes(coef, -1)))
    left = jnp.where(lanes == 0, 0.0, 0.5 * (coef + roll_lanes(coef, 1)))
    return (up * vy - down * roll_rows(vy, 1)) + (right * vz - left * roll_lanes(vz, 1))


RHS, VX, PRESS, VY = DEPTH, 2 * DEPTH - 1, 2 * DEPTH, 2 * DEPTH + 1


def pack_first(nx, ny, n_x, n_y, phase, press, vel, *refs):
    outs, odd_outs, (held, held_vel, sem) = refs[:n_x], refs[n_x:-3], refs[-3:]
    if n_y > 1:
        *odd_outs, tile_phase, tile_vel, tile_press, tile_sem = odd_outs
    copies = []
    for turn, out in enumerate(outs):
        top = even("gx") == (turn == 0)
        deep = jnp.where(top, nx - DEPTH, 0)
        last = jnp.where(top, nx - 1, 0)
        parts = [
            (vel.at[:, pl.ds(deep, DEPTH)], held_vel.at[turn]),
            (phase.at[pl.ds(deep, DEPTH)], held.at[turn]),
            (press.at[last], out.at[pl.ds(PRESS * ny, ny)]),
        ]
        for which, (src, dst) in enumerate(parts):
            copy = pltpu.make_async_copy(src, dst, sem.at[turn, which])
            copy.start()
            copies.append(copy)
    if n_y > 1:
        row = pl.multiple_of(jnp.where(even("gy"), 0, ny - ROWS), ROWS)
        parts = [
            (phase.at[:, pl.ds(row, ROWS)], tile_phase),
            (vel.at[:, :, pl.ds(row, ROWS)], tile_vel),
            (press.at[:, pl.ds(row, ROWS)], tile_press),
        ]
        for which, (src, dst) in enumerate(parts):
            copy = pltpu.make_async_copy(src, dst, tile_sem.at[which])
            copy.start()
            copies.append(copy)
    for copy in copies:
        copy.wait()
    lanes = lane_index((ROWS, LANES))
    rows = row_index((ROWS, LANES))
    for turn, out in enumerate(outs):
        top = even("gx") == (turn == 0)
        coefs = [coefficient(held[turn, j]) for j in range(DEPTH)]
        flux = [0.5 * (coefs[j] + coefs[j + 1]) * held_vel[turn, 0, j] for j in range(DEPTH - 1)]
        columns = jnp.zeros((ROWS, LANES), jnp.float32)
        lines = jnp.zeros((ROWS, LANES), jnp.float32)
        for j in range(DEPTH):
            out[j * ny : (j + 1) * ny, :] = coefs[j]
        for j in range(DEPTH - 1):
            vy = jnp.where(top, held_vel[turn, 1, j + 1], held_vel[turn, 1, j])
            vz = jnp.where(top, held_vel[turn, 2, j + 1], held_vel[turn, 2, j])
            upper = (flux[j + 1] - flux[j]) if j + 1 < DEPTH - 1 else -flux[j]
            lower = (flux[j] - flux[j - 1]) if j else flux[j]
            inner = inner_rhs(jnp.where(top, coefs[j + 1], coefs[j]), vy, vz)
            out[(RHS + j) * ny : (RHS + j + 1) * ny, :] = jnp.where(top, upper, lower) + inner
            for t in range(ny // ROWS):
                lane = DEPTH * t + j
                columns = jnp.where(lanes == lane, roll_lanes(vz[t * ROWS : (t + 1) * ROWS], lane + 1), columns)
            lines = jnp.where(rows == j, roll_rows(vy[ny - ROWS :], j + 1), lines)
        out[VX * ny : (VX + 1) * ny, :] = held_vel[turn, 0, DEPTH - 1]
        out[VY * ny : VY * ny + ROWS, :] = lines
        out[VY * ny + ROWS :, :] = columns
        clear_if_alone(out, ("gx", turn))
    if n_y > 1:
        pack_odd(nx, tile_phase, tile_vel, tile_press, odd_outs)


def row_tile(coef, rhs, vy, top):
    rows = row_index((ROWS, LANES))
    coef = jnp.where(top, roll_rows(coef, DEPTH), coef)
    rhs = jnp.where(top, roll_rows(rhs, -1), roll_rows(rhs, DEPTH))
    return jnp.where(rows == ROWS - 1, vy, jnp.where(rows < DEPTH, coef, rhs))


def pack_odd(nx, tile_phase, tile_vel, tile_press, outs):
    out, *corners = outs
    top = jnp.logical_not(even("gy"))
    lanes = lane_index((ROWS, LANES))
    ends_at, vx_at = nx + nx // ROWS, nx + nx // ROWS + 1
    ends = jnp.zeros((ROWS, LANES), jnp.float32)
    here, old_flux = coefficient(tile_phase[0]), None
    for x in range(nx):
        vy, vz = tile_vel[1, x], tile_vel[2, x]
        answer = inner_rhs(here, vy, vz)
        if old_flux is not None:
            answer = answer - old_flux
        coef = here
        if x + 1 < nx:
            above = coefficient(tile_phase[x + 1])
            old_flux = 0.5 * (here + above) * tile_vel[0, x]
            answer = answer + old_flux
            here = above
        out[x] = row_tile(coef, answer, vy, top)
        ends = jnp.where(lanes == x, roll_lanes(vz, x + 1), ends)
        tile = tile_press[x]
        at = nx + x // ROWS
        out[at, x % ROWS : x % ROWS + 1, :] = jnp.where(top, tile[ROWS - 1 : ROWS], tile[0:1])
    shift = lambda tile: jnp.where(top, roll_rows(tile, -1), roll_rows(tile, DEPTH))
    ends = jnp.where(top, roll_rows(ends, DEPTH - 1), ends)
    out[ends_at] = ends
    out[vx_at] = shift(tile_vel[0, nx - 1])
    for turn, corner in enumerate(corners):
        first = jnp.where(even("gx") == (turn == 0), nx - DEPTH, 0)
        for j in range(DEPTH):
            corner[j] = out[first + j]
        corner[DEPTH] = pltpu.roll(ends, jnp.where(first == 0, 0, (DEPTH - nx) % LANES), 1)
        corner[DEPTH + 1] = out[vx_at]
        clear_if_alone(corner, ("gx", turn), ("gy", 1))
    clear_if_alone(out, ("gy", 1))


def merge_odd(nx, got, *refs):
    corners, out = refs[:-1], refs[-1]
    total = nx + 2 * DEPTH
    rows, lanes = row_index((ROWS, LANES)), lane_index((ROWS, LANES))
    ends_at, vx_at = nx + nx // ROWS, nx + nx // ROWS + 1
    low, high = zip(*[sides(even("gx"), corners, lambda ref: ref[j]) for j in range(DEPTH + 2)])
    tiles = [got[x] for x in range(nx)] + list(high[:DEPTH]) + list(low[:DEPTH])
    inner = (rows >= DEPTH) & (rows < ROWS - 1)

    def face(below, above, vx):
        weight = 0.5 * (tiles[below] + tiles[above])
        weight = jnp.where(even("gy"), roll_rows(weight, DEPTH - 1), roll_rows(weight, DEPTH))
        return jnp.where(inner, weight * vx, 0.0)

    low_face, high_face = face(total - 1, 0, low[DEPTH + 1]), face(nx - 1, nx, got[vx_at])
    for plane, tile in enumerate(tiles):
        if plane == 0:
            tile = tile - low_face
        if plane == total - 1:
            tile = tile + low_face
        if plane == nx - 1:
            tile = tile + high_face
        if plane == nx:
            tile = tile - high_face
        out[plane] = tile
    for at in range(nx // ROWS):
        out[total + at] = got[nx + at]
    ends = jnp.where(lanes < nx, got[ends_at], roll_lanes(high[DEPTH], nx))
    out[total + nx // ROWS] = jnp.where(lanes < nx + DEPTH, ends, roll_lanes(low[DEPTH], nx + DEPTH))


def load(phase, press, vel, after, coef, press_out, vel_out, rhs, held, sem):
    del after
    copies = []
    for which, (src, dst) in enumerate(((phase, held), (press, press_out), (vel, vel_out))):
        copies.append(pltpu.make_async_copy(src, dst, sem.at[which]))
        copies[-1].start()
    copies[0].wait()
    copies[1].wait()
    copies[2].wait()
    nx = coef.shape[0]
    here = coefficient(held[0])
    old_flux = None
    for x in range(nx):
        coef[x] = here
        answer = inner_rhs(here, vel_out[1, x], vel_out[2, x])
        if old_flux is not None:
            answer = answer - old_flux
        if x + 1 < nx:
            above = coefficient(held[x + 1])
            old_flux = 0.5 * (here + above) * vel_out[0, x]
            answer = answer + old_flux
            here = above
        rhs[x] = answer


class Block:
    def __init__(self, nx, ny, coef, vel, rhs, got_x, row=0, height=None, faces=True):
        self.nx, self.ny = nx, ny
        self.own_coef, self.vel, self.own_rhs, self.got_x = coef, vel, rhs, got_x
        self.even = even("gx")
        self.row, self.height = row, height or ny
        if not faces:
            return
        self.low_face = 0.5 * (self.coef(nx + 2 * DEPTH - 1) + self.coef(0)) * self.halo(VX)[0]
        self.high_face = 0.5 * (self.coef(nx - 1) + self.coef(nx)) * self.take(vel, 0, nx - 1)

    def take(self, ref, *index):
        return ref[(*index, pl.ds(self.row, self.height), slice(None))]

    def halo(self, part):
        return sides(self.even, self.got_x, lambda ref: ref[pl.ds(part * self.ny + self.row, self.height), :])

    def coef(self, plane):
        if plane < self.nx:
            return self.take(self.own_coef, plane)
        above = plane < self.nx + DEPTH
        return self.halo((plane - self.nx) % DEPTH)[1 if above else 0]

    def rhs(self, plane):
        nx = self.nx
        if plane < nx:
            answer = self.take(self.own_rhs, plane)
        else:
            above = plane < nx + DEPTH
            layer = plane - nx if above else plane - nx - DEPTH - 1
            if layer < 0 or layer >= DEPTH - 1:
                return jnp.zeros((self.height, LANES), jnp.float32)
            answer = self.halo(RHS + layer)[1 if above else 0]
        if plane == 0:
            answer = answer - self.low_face
        if plane == nx + 2 * DEPTH - 1:
            answer = answer + self.low_face
        if plane == nx - 1:
            answer = answer + self.high_face
        if plane == nx:
            answer = answer - self.high_face
        return answer

    def layer(self, plane):
        if plane < self.nx + DEPTH:
            place = (1, plane - self.nx)
        else:
            place = (0, plane - self.nx - DEPTH - 1)
        return place if 0 <= place[1] < DEPTH - 1 else None

    def columns(self):
        at = VY * self.ny + ROWS
        return sides(self.even, self.got_x, lambda ref: ref[at : at + ROWS, :])

    def vz_end(self, plane, lane):
        if plane < self.nx:
            return roll_lanes(self.vel[2, plane], lane + 1)
        place = self.layer(plane)
        if place is None:
            return jnp.zeros((self.ny, LANES), jnp.float32)
        source = self.columns()[place[0]]
        return jnp.concatenate(
            [roll_lanes(source, lane - DEPTH * t - place[1]) for t in range(self.ny // ROWS)], 0
        )

    def vy_end(self, plane):
        if plane < self.nx:
            return self.vel[1, plane, self.ny - 1 :, :]
        place = self.layer(plane)
        if place is None:
            return jnp.zeros((1, LANES), jnp.float32)
        at = VY * self.ny + place[1]
        return sides(self.even, self.got_x, lambda ref: ref[at : at + 1, :])[place[0]]


def pack_y(nx, ny, n_x, coef, press, vel, rhs, *refs):
    got_x, out = refs[:n_x], refs[-1]
    total = nx + 2 * DEPTH
    lanes = lane_index((ROWS, LANES))
    top = even("gy")
    row = pl.multiple_of(jnp.where(top, ny - ROWS, 0), ROWS)
    block = Block(nx, ny, coef, vel, rhs, got_x, row, ROWS)
    columns = jnp.zeros((ROWS, LANES), jnp.float32)
    ends = block.columns()
    for plane in range(total):
        out[plane] = row_tile(block.coef(plane), block.rhs(plane), block.vy_end(plane), top)
        if plane < nx:
            source = roll_lanes(vel[2, plane, pl.ds(row, ROWS), :], plane + 1)
        elif block.layer(plane) is None:
            continue
        else:
            side, layer = block.layer(plane)
            high = (plane - layer - DEPTH * (ny // ROWS - 1)) % LANES
            source = pltpu.roll(ends[side], jnp.where(top, high, (plane - layer) % LANES), 1)
        columns = jnp.where(lanes == plane, source, columns)
    out[total + nx // ROWS] = jnp.where(top, roll_rows(columns, DEPTH - 1), columns)
    for plane in range(nx):
        tile = press[plane, pl.ds(row, ROWS), :]
        edge = jnp.where(top, tile[ROWS - 1 : ROWS], tile[0:1])
        out[total + plane // ROWS, plane % ROWS : plane % ROWS + 1, :] = edge
    clear_if_alone(out, ("gy", 0))


def tall_end(block, tile_end, plane, lane):
    return jnp.concatenate([block.vz_end(plane, lane), roll_lanes(tile_end, lane - plane)], 0)


def tile_of_ends(nx, even_y, got_y):
    rows = row_index((ROWS, LANES))
    low, high = sides(even_y, got_y, lambda ref: ref[nx + 2 * DEPTH + nx // ROWS])
    return jnp.where(rows < DEPTH, high, roll_rows(low, DEPTH + 1))


def press_lane(x):
    return GROUP * (x % ROWS) + ROWS + 2 * (x // ROWS)


def pack_plane(lanes, at, top, coef, rhs, end):
    coef = pltpu.roll(coef, jnp.where(top, (at + DEPTH) % LANES, at), 1)
    rhs = pltpu.roll(rhs, jnp.where(top, (at + ROWS - 1) % LANES, at + DEPTH), 1)
    value = jnp.where(lanes == at + ROWS - 1, end, 0.0)
    value = jnp.where((lanes >= at + DEPTH) & (lanes < at + ROWS - 1), rhs, value)
    return jnp.where((lanes >= at) & (lanes < at + DEPTH), coef, value)


def half_tile(tile, below):
    rows = row_index((ROWS, LANES))
    coef = jnp.where(below, jnp.where(rows >= DEPTH, roll_rows(tile, DEPTH), 0.0), jnp.where(rows < DEPTH, tile, 0.0))
    rhs = jnp.where(
        below,
        jnp.where(rows > DEPTH, roll_rows(tile, 1), 0.0),
        jnp.where(rows < DEPTH - 1, roll_rows(tile, -DEPTH), 0.0),
    )
    return coef, rhs


def half_ends(tile, below):
    rows = row_index((ROWS, LANES))
    return jnp.where(
        below, jnp.where(rows > DEPTH, roll_rows(tile, DEPTH + 1), 0.0), jnp.where(rows < DEPTH - 1, tile, 0.0)
    )


def face_y(own_low, own_high, coef_tile, tile, vy_end, below):
    rows = row_index((ROWS, LANES))
    down = 0.5 * (coef_tile[ROWS - 1 :] + own_low) * tile[ROWS - 1 :]
    up = 0.5 * (own_high + coef_tile[:1]) * vy_end
    outside = jnp.where(below, jnp.where(rows == ROWS - 1, down, 0.0), jnp.where(rows == 0, -up, 0.0))
    inside = jnp.where(below, jnp.where(rows == 0, -down, 0.0), jnp.where(rows == ROWS - 1, up, 0.0))
    return outside, inside


def stage_z(nx, ny, n_x, n_z, coef, press, vel, rhs, *refs):
    got_x, (*got_odd, full_coef, full_rhs), sends = refs[:n_x], refs[n_x : len(refs) - n_z], refs[len(refs) - n_z :]
    total, height = nx + 2 * DEPTH, ny + 2 * DEPTH
    groups = total // ROWS
    below = even("gy")
    lanes = lane_index((height, LANES))
    block = Block(nx, ny, coef, vel, rhs, got_x)
    nothing = jnp.zeros((ROWS, LANES), jnp.float32)
    tile_end = half_ends(got_odd[0][total + nx // ROWS], below) if got_odd else nothing
    made = [[jnp.zeros((height, LANES), jnp.float32) for _ in range(groups // 2 + 1)] for _ in sends]
    row = pl.ds(pl.multiple_of(jnp.where(below, 0, ny - ROWS), ROWS), ROWS)
    for plane in range(total):
        c_own, r_own = block.coef(plane), block.rhs(plane)
        c_tile = r_tile = nothing
        full_rhs[plane, :ny, :] = r_own
        if got_odd:
            tile = got_odd[0][plane]
            c_tile, r_tile = half_tile(tile, below)
            outside, inside = face_y(c_own[:1], c_own[ny - 1 :], c_tile, tile, block.vy_end(plane), below)
            r_tile = r_tile + outside
            full_rhs[plane, row, :] = full_rhs[plane, row, :] + inside
        c_all = jnp.concatenate([c_own, c_tile], 0)
        full_coef[plane] = c_all
        full_rhs[plane, ny:, :] = r_tile
        r_all = full_rhs[plane]
        group, seat = plane % groups, plane // groups
        at = GROUP * seat + ROWS * (group % 2)
        end = tall_end(block, tile_end, plane, at + ROWS - 1)
        for turn in range(n_z):
            value = pack_plane(lanes, at, even("gz") == (turn == 0), c_all, r_all, end)
            made[turn][group // 2] = made[turn][group // 2] + value
    for turn, send in enumerate(sends):
        top = even("gz") == (turn == 0)
        value = made[turn][groups // 2][:ny]
        for plane in range(nx):
            at = press_lane(plane)
            moved = pltpu.roll(press[plane], jnp.where(top, (at + 1) % LANES, at), 1)
            value = jnp.where(lanes[:ny] == at, moved, value)
        made[turn][groups // 2] = jnp.concatenate([value, made[turn][groups // 2][ny:]], 0)
        for which, value in enumerate(made[turn]):
            send[which] = value


def pack_z(nx, ny, n_x, n_z, vel, *refs):
    got_x, got, (full_coef, full_rhs, *sends) = refs[:n_x], refs[n_x], refs[-2 - n_z :]
    total = nx + 2 * DEPTH
    groups = total // ROWS
    below = jnp.logical_not(even("gy"))
    lanes = lane_index((ROWS, LANES))
    block = Block(nx, ny, full_coef, vel, full_rhs, got_x, faces=False)
    tile_end = half_ends(got[total + nx // ROWS], below)
    row = pl.ds(pl.multiple_of(jnp.where(below, 0, ny - ROWS), ROWS), ROWS)
    added = [[[jnp.zeros((ROWS, LANES), jnp.float32) for _ in range(2)] for _ in range(groups // 2 + 1)] for _ in sends]
    for plane in range(total):
        tile = got[plane]
        c_tile, r_tile = half_tile(tile, below)
        low, high = full_coef[plane, :1, :], full_coef[plane, ny - 1 : ny, :]
        outside, inside = face_y(low, high, c_tile, tile, block.vy_end(plane), below)
        r_tile = r_tile + outside
        full_coef[plane, ny:, :] = full_coef[plane, ny:, :] + c_tile
        full_rhs[plane, ny:, :] = full_rhs[plane, ny:, :] + r_tile
        full_rhs[plane, row, :] = full_rhs[plane, row, :] + inside
        group, seat = plane % groups, plane // groups
        at = GROUP * seat + ROWS * (group % 2)
        end = roll_lanes(tile_end, at + ROWS - 1 - plane)
        for turn in range(n_z):
            top = even("gz") == (turn == 0)
            inside_move = pltpu.roll(inside, jnp.where(top, (at + ROWS - 1) % LANES, at + DEPTH), 1)
            inside_move = jnp.where((lanes >= at + DEPTH) & (lanes < at + ROWS - 1), inside_move, 0.0)
            slot = added[turn][group // 2]
            slot[0] = slot[0] + pack_plane(lanes, at, top, c_tile, r_tile, end)
            slot[1] = slot[1] + inside_move
    for turn, send in enumerate(sends):
        for which, (tile, inside) in enumerate(added[turn]):
            send[which, ny:, :] = send[which, ny:, :] + tile
            send[which, row, :] = send[which, row, :] + inside
        clear_if_alone(send, ("gz", turn))


def tree_sum(parts):
    while len(parts) > 1:
        parts = [parts[i] + parts[i + 1] if i + 1 < len(parts) else parts[i] for i in range(0, len(parts), 2)]
    return parts[0]


class Totals:
    def __init__(self):
        self.stack = []

    def add(self, tile):
        level = 0
        while self.stack and self.stack[-1][0] == level:
            tile = self.stack.pop()[1] + tile
            level += 1
        self.stack.append((level, tile))

    def value(self):
        tiles = [tile for _, tile in self.stack]
        total = tiles.pop()
        while tiles:
            total = tiles.pop() + total
        return total


def prepare(nx, ny, n_x, n_y, coef, vel, rhs, full_coef, full_rhs, *refs):
    got_x, got_y = refs[:n_x], refs[n_x : n_x + n_y]
    basis, ends, shares, wx, wy, wz, inverse = refs[n_x + n_y :]
    total, height = nx + 2 * DEPTH, ny + 2 * DEPTH
    groups = total // ROWS
    lanes = lane_index((height, LANES))
    block = Block(nx, ny, coef, vel, rhs, got_x)
    tile_end = tile_of_ends(nx, even("gy"), got_y)
    for group in range(groups):
        made = [jnp.zeros((height, LANES), jnp.float32) for _ in range(5)]
        for seat in range(ROWS):
            plane = seat * groups + group
            at = GROUP * seat
            for which, source in enumerate((full_coef[plane], full_rhs[plane])):
                here = (lanes >= at + DEPTH) & (lanes < at + GROUP)
                made[2 * which] = jnp.where(here, roll_lanes(source, at + DEPTH), made[2 * which])
                here = (lanes >= at) & (lanes < at + GROUP - DEPTH)
                made[2 * which + 1] = jnp.where(here, roll_lanes(source, at + GROUP - DEPTH), made[2 * which + 1])
            lane = at + GROUP - DEPTH - 1
            made[4] = jnp.where(lanes == lane, tall_end(block, tile_end, plane, lane), made[4])
        for which in range(5):
            ends[which, group] = made[which]
    totals = [Totals() for _ in range(6)]
    trusted = (lanes[:ROWS] >= DEPTH) & (lanes[:ROWS] < LANES - DEPTH)

    def count(which, left, right):
        product = left[:ny] * right[:ny]
        tile = tree_sum([product[i : i + ROWS] for i in range(0, ny, ROWS)])
        totals[which].add(jnp.where(trusted, tile, 0.0))

    old_weight = None
    here = full_coef[nx + DEPTH]
    for x in range(-DEPTH, nx + DEPTH - 1):
        e = x % total
        above = full_coef[(e + 1) % total]
        weight = 0.5 * (here + above)
        wx[e] = weight
        if x > -DEPTH:
            up, down = 0.5 * (here + roll_rows(here, -1)), 0.5 * (here + roll_rows(here, 1))
            right = jnp.where(lanes == LANES - 1, 0.0, 0.5 * (here + roll_lanes(here, -1)))
            left = jnp.where(lanes == 0, 0.0, 0.5 * (here + roll_lanes(here, 1)))
            wy[0, e], wy[1, e], wz[0, e], wz[1, e] = up, down, right, left
            diag = (weight + old_weight) + (up + down) + (right + left)
            inside = here > 0
            scale = jnp.where(inside, 1.0 / jnp.where(inside, diag, 1.0), 0.0)
            inverse[e] = scale
            source = full_rhs[e]
            field = scale * source
            basis[0, e] = field
            if 0 <= x < nx:
                count(0, field, source)
        old_weight, here = weight, above
    for n in range(3):
        reach = 2 - n
        old_flux = None
        here = basis[n, (-reach - 1) % total]
        for x in range(-reach - 1, nx + reach):
            e = x % total
            above = basis[n, (e + 1) % total]
            flux = wx[e] * (above - here)
            if x >= -reach:
                image = old_flux - flux
                image = image + (
                    wy[0, e] * (here - roll_rows(here, -1)) + wy[1, e] * (here - roll_rows(here, 1))
                )
                image = image + (
                    wz[0, e] * (here - roll_lanes(here, -1)) + wz[1, e] * (here - roll_lanes(here, 1))
                )
                own = 0 <= x < nx
                if own:
                    count(2 * n + 1, here, image)
                if n < 2:
                    following = inverse[e] * image
                    basis[n + 1, e] = following
                    if own:
                        count(2 * n + 2, following, image)
            old_flux, here = flux, above
    for which, total_ in enumerate(totals):
        shares[which] = total_.value()


def join(nx, ny, n_z, after, ends, shares, *refs):
    del after
    got_z = refs[:n_z]
    basis_z, vz_z, sums, weight_z, inverse_z = refs[n_z:]
    total, height = nx + 2 * DEPTH, ny + 2 * DEPTH
    groups = total // ROWS
    lanes = lane_index((height, LANES))
    seat_lane, seat = lanes % GROUP, lanes // GROUP
    coef, rhs, vz = [], [], []
    for side in range(2):
        for g in range(groups):
            got = sides(even("gz"), got_z, lambda ref: ref[g // 2])[side]
            skip = ROWS * (g % 2)
            if side == 0:
                outer = seat_lane < DEPTH
                coef.append(jnp.where(outer, roll_lanes(got, -skip), ends[0, g]))
                rhs.append(jnp.where(outer, roll_lanes(got, 1 - DEPTH - skip), ends[2, g]))
                vz.append(roll_lanes(got, -DEPTH - skip))
                vz_z[g] = vz[-1]
            else:
                outer = seat_lane >= GROUP - DEPTH
                coef.append(jnp.where(outer, roll_lanes(got, GROUP - DEPTH - skip), ends[1, g]))
                rhs.append(jnp.where(outer, roll_lanes(got, GROUP - 2 * DEPTH - skip), ends[3, g]))
                vz.append(ends[4, g])

    def along(planes, q, step):
        g = q % groups
        if 0 <= g + step < groups:
            return planes[q + step]
        return roll_lanes(planes[q - g + (g + step) % groups], -GROUP * step)

    totals = [Totals() for _ in range(6)]

    def count(which, q, left, right):
        first = DEPTH if q < groups else GROUP - 2 * DEPTH
        spot = seat_lane[:ROWS]
        mine = (spot >= first) & (spot < first + DEPTH) & (seat[:ROWS] * groups + q % groups < nx)
        product = left[:ny] * right[:ny]
        tile = tree_sum([product[i : i + ROWS] for i in range(0, ny, ROWS)])
        totals[which].add(jnp.where(mine, tile, 0.0))

    field = []
    for q in range(2 * groups):
        here = coef[q]
        neighbours = (along(coef, q, 1), along(coef, q, -1), roll_rows(here, -1), roll_rows(here, 1))
        neighbours += (roll_lanes(here, -1), roll_lanes(here, 1))
        weights = [0.5 * (here + other) for other in neighbours]
        for which, weight in enumerate(weights):
            weight_z[which, q] = weight
        diag = (weights[0] + weights[1]) + (weights[2] + weights[3]) + (weights[4] + weights[5])
        face = DEPTH - 1 if q < groups else GROUP - DEPTH - 1
        source = rhs[q] + jnp.where(seat_lane == face, weights[4] * vz[q], 0.0)
        source = source - jnp.where(seat_lane == face + 1, weights[5] * roll_lanes(vz[q], 1), 0.0)
        inside = here > 0
        scale = jnp.where(inside, 1.0 / jnp.where(inside, diag, 1.0), 0.0)
        inverse_z[q] = scale
        field.append(scale * source)
        basis_z[0, q] = field[q]
        count(0, q, field[q], source)
    for n in range(3):
        following = []
        for q in range(2 * groups):
            here = field[q]
            image = weight_z[0, q] * (here - along(field, q, 1)) + weight_z[1, q] * (here - along(field, q, -1))
            image = image + (
                weight_z[2, q] * (here - roll_rows(here, -1)) + weight_z[3, q] * (here - roll_rows(here, 1))
            )
            image = image + (
                weight_z[4, q] * (here - roll_lanes(here, -1)) + weight_z[5, q] * (here - roll_lanes(here, 1))
            )
            count(2 * n + 1, q, here, image)
            if n < 2:
                following.append(inverse_z[q] * image)
                basis_z[n + 1, q] = following[q]
                count(2 * n + 2, q, following[q], image)
        field = following
    lane = lane_index((1, LANES))
    row = jnp.zeros((1, LANES), jnp.float32)
    for which, total_ in enumerate(totals):
        value = total_.value() + shares[which]
        value = jnp.sum(jnp.sum(value, 0, keepdims=True), 1, keepdims=True)
        row = jnp.where(lane == which, value, row)
    sums[...] = row


def slopes(nx, ny, n_x, n_y, press, vel, *refs):
    got_x, got_y, (slope_x, slope_y, slope_z, base) = refs[:n_x], refs[n_x : n_x + n_y], refs[n_x + n_y :]
    total = nx + 2 * DEPTH
    rows, shape = row_index((ROWS, LANES)), (ROWS, LANES)
    lanes = lane_index((ny, LANES))
    at_low, at_high = lanes == 0, lanes == LANES - 1
    p_low, p_high = sides(even("gx"), got_x, lambda ref: ref[PRESS * ny : (PRESS + 1) * ny, :])
    u_low, _ = sides(even("gx"), got_x, lambda ref: ref[VX * ny : (VX + 1) * ny, :])
    old = p_low - press[0]
    slope_x[0] = old
    old = old * u_low
    for x in range(nx):
        p = press[x]
        slope = p - (press[x + 1] if x + 1 < nx else p_high)
        slope_x[x + 1] = slope
        new = slope * vel[0, x]
        answer, old = old + new, new
        low, high = sides(even("gy"), got_y, lambda ref: ref[total + x // ROWS, x % ROWS : x % ROWS + 1, :])
        p_tile = jnp.where(rows == 0, jnp.broadcast_to(high, shape), jnp.broadcast_to(low, shape))
        p_tall = jnp.concatenate([p, p_tile], 0)
        u_row, _ = sides(even("gy"), got_y, lambda ref: ref[x, ROWS - 1 :, :])
        u_tall = jnp.concatenate([vel[1, x], jnp.broadcast_to(u_row, shape)], 0)
        up, down = p - roll_rows(p_tall, -1)[:ny], roll_rows(p_tall, 1)[:ny] - p
        slope_y[0, x], slope_y[1, x] = up, down
        answer = answer + (up * vel[1, x] + down * roll_rows(u_tall, 1)[:ny])
        up = p - jnp.where(at_high, 0.0, roll_lanes(p, -1))
        down = jnp.where(at_low, 0.0, roll_lanes(p, 1)) - p
        slope_z[0, x], slope_z[1, x] = up, down
        base[x] = answer + (up * vel[2, x] + down * jnp.where(at_low, 0.0, roll_lanes(vel[2, x], 1)))


def finish(nx, ny, n_z, gathered, vel, basis, basis_z, vz_z, slope_x, slope_y, slope_z, base, *refs):
    got_z, (ustar_out, coef_out, ustar, coef_cot, sem) = refs[:n_z], refs[n_z:]
    total, height = nx + 2 * DEPTH, ny + 2 * DEPTH
    groups = total // ROWS
    parts = gathered[...]
    while parts.shape[0] > ROWS:
        half = parts.shape[0] // 2
        parts = parts[:half] + parts[half:]
    sums = jnp.sum(parts, 0, keepdims=True)
    lane = lane_index((1, LANES))
    m0, m1, m2, m3, m4, m5 = [
        jnp.sum(jnp.where(lane == which, sums, 0.0), 1, keepdims=True) for which in range(6)
    ]
    l1, l2 = m2 / m1, m3 / m1
    d1, cross, d2 = m3 - l1 * m2, m4 - l1 * m3, m5 - l2 * m3
    l21 = cross / d1
    d2 = d2 - l21 * cross
    y1 = -l1 * m0 + m1
    y2 = m2 - l2 * m0 - l21 * y1
    c2 = y2 / d2
    c1 = y1 / d1 - l21 * c2
    c0 = (m0 / m1 - l1 * c1 - l2 * c2)[0, 0]
    c1, c2 = c1[0, 0], c2[0, 0]

    lanes = lane_index((height, LANES))
    seat_lane = lanes % GROUP
    spill = []
    for g in range(groups):
        low, high = [
            c0 * basis_z[0, q] + c1 * basis_z[1, q] + c2 * basis_z[2, q] for q in (g, groups + g)
        ]
        cells = jnp.where(seat_lane < DEPTH - 1, roll_lanes(high, DEPTH - GROUP + DEPTH - 1), roll_lanes(low, -1))
        cells = jnp.where(seat_lane == 2 * DEPTH - 2, roll_lanes(high, 2 * DEPTH - 2 - (GROUP - DEPTH)), cells)
        spill.append(jnp.where(seat_lane == 2 * DEPTH - 1, roll_lanes(low, DEPTH), cells))
    spoiled = (lanes < DEPTH - 1) | (lanes > LANES - DEPTH)
    lanes = lane_index((ny, LANES))
    at_low, at_high = lanes == 0, lanes == LANES - 1
    low_z, high_z = sides(even("gz"), got_z, lambda ref: ref[groups // 2, :ny, :])
    press_z = jnp.where(lanes % 2 == 0, high_z, roll_lanes(low_z, 1))

    def solved(x):
        e = x % total
        cells = c0 * basis[0, e] + c1 * basis[1, e] + c2 * basis[2, e]
        return jnp.where(spoiled, roll_lanes(spill[e % groups], 1 - DEPTH - GROUP * (e // groups)), cells)

    copies = []
    below, here = solved(-1), solved(0)
    down = here[:ny] - below[:ny]
    for x in range(nx):
        above = solved(x + 1)
        group, seat = x % groups, x // groups
        own = here[:ny]
        up = above[:ny] - own
        ustar[0, x] = vel[0, x] + up
        answer = base[x] + (slope_x[x + 1] * up + slope_x[x] * down)
        next_down = up
        up, down = roll_rows(here, -1)[:ny] - own, own - roll_rows(here, 1)[:ny]
        ustar[1, x] = vel[1, x] + up
        answer = answer + (slope_y[0, x] * up + slope_y[1, x] * down)
        lam_end = roll_lanes(spill[group][:ny], 1 - 2 * DEPTH - GROUP * seat)
        u_end = roll_lanes(vz_z[group, :ny, :], 1 - DEPTH - GROUP * seat)
        p_end = roll_lanes(press_z, LANES - 1 - press_lane(x))
        up = jnp.where(at_high, lam_end, roll_lanes(own, -1)) - own
        down = own - jnp.where(at_low, lam_end, roll_lanes(own, 1))
        out = vel[2, x] + up
        ustar[2, x] = out
        answer = answer + (slope_z[0, x] * up + slope_z[1, x] * down)
        beyond = jnp.where(at_low, p_end * (u_end + down) + slope_z[1, x] * u_end, 0.0)
        answer = answer + jnp.where(at_high, -p_end * out, beyond)
        down = next_down
        coef_cot[x] = 0.5 * answer
        here = above
        if (x + 1) % STRIDE == 0:
            part = pl.ds(x + 1 - STRIDE, STRIDE)
            for which, (src, dst) in enumerate(
                ((ustar.at[:, part], ustar_out.at[:, part]), (coef_cot.at[part], coef_out.at[part]))
            ):
                copies.append(pltpu.make_async_copy(src, dst, sem.at[which, x // STRIDE]))
                copies[-1].start()
    for copy in copies:
        copy.wait()


def on_device(phase, press, vel):
    nx, ny, nz = phase.shape
    total, height = nx + 2 * DEPTH, ny + 2 * DEPTH
    groups = total // ROWS
    devices = lax.axis_size(AXES)
    n_x, n_y, n_z = (turns(axis) for axis in AXES)
    f32 = lambda *shape: jax.ShapeDtypeStruct(shape, jnp.float32)
    scratch = lambda *shape: pltpu.VMEM(shape, jnp.float32)
    inputs = [pltpu.with_memory_space_constraint(array, pltpu.HBM) for array in (phase, press, vel)]

    def call(kernel, args, in_specs, shapes, name, scratch_shapes=(), out_spec=VMEM, aliases={}):
        return pl.pallas_call(
            kernel,
            out_shape=shapes,
            in_specs=in_specs,
            out_specs=[out_spec] * len(shapes),
            scratch_shapes=list(scratch_shapes),
            input_output_aliases=aliases,
            compiler_params=PARAMS,
            cost_estimate=pl.CostEstimate(flops=3_000_000, bytes_accessed=3_000_000, transcendentals=0),
            name=name,
        )(*args)

    odd = n_y > 1
    sent = call(
        functools.partial(pack_first, nx, ny, n_x, n_y),
        inputs,
        [HBM] * 3,
        [f32(VY * ny + 2 * ROWS, nz)] * n_x
        + ([f32(nx + nx // ROWS + 2, ROWS, nz)] + [f32(DEPTH + 2, ROWS, nz)] * n_x if odd else []),
        "pack_first",
        (
            [pltpu.VMEM((nx, ROWS, nz), jnp.int32), scratch(3, nx, ROWS, nz), scratch(nx, ROWS, nz)]
            + [pltpu.SemaphoreType.DMA((3,))]
            if odd
            else []
        )
        + [pltpu.VMEM((n_x, DEPTH, ny, nz), jnp.int32), scratch(n_x, 3, DEPTH, ny, nz)]
        + [pltpu.SemaphoreType.DMA((n_x, 3))],
    )
    to_x = sent[:n_x]
    got_x = [exchange(send, ("gx", turn)) for turn, send in enumerate(to_x)]
    if odd:
        got_odd = exchange(sent[n_x], ("gy", 1))
        corners = [exchange(send, ("gx", turn), ("gy", 1)) for turn, send in enumerate(sent[n_x + 1 :])]
    coef, press, vel, rhs = call(
        load,
        inputs + [to_x[0]],
        [HBM] * 3 + [ANY],
        [f32(*press.shape), f32(*press.shape), f32(*vel.shape), f32(*press.shape)],
        "load",
        [pltpu.VMEM(phase.shape, jnp.int32), pltpu.SemaphoreType.DMA((3,))],
    )
    rows_y = f32(total + nx // ROWS + 1, ROWS, nz)
    got_y, odd_rows = [], []
    if odd:
        odd_rows = call(
            functools.partial(merge_odd, nx),
            [got_odd, *corners],
            [VMEM] * (1 + n_x),
            [rows_y],
            "merge_odd",
        )
    if n_y:
        to_y = call(
            functools.partial(pack_y, nx, ny, n_x),
            [coef, press, vel, rhs, *got_x, *odd_rows],
            [VMEM] * (4 + n_x) + [ANY] * len(odd_rows),
            [rows_y],
            "pack_y",
        )
        got_y = [exchange(to_y[0], ("gy", 0)), *odd_rows]
    cube = (total, height, nz)
    packs = [f32(groups // 2 + 1, height, LANES)] * n_z
    staged = call(
        functools.partial(stage_z, nx, ny, n_x, n_z),
        [coef, press, vel, rhs, *got_x, *odd_rows],
        [VMEM] * (4 + n_x + len(odd_rows)),
        [f32(*cube)] * 2 + packs,
        "stage_z",
    )
    full_coef, full_rhs, *to_z = call(
        functools.partial(pack_z, nx, ny, n_x, n_z),
        [vel, *got_x, got_y[0], *staged],
        [VMEM] * (4 + n_x + n_z),
        [f32(*cube)] * 2 + packs,
        "pack_z",
        aliases={2 + n_x + which: which for which in range(2 + n_z)},
    )
    got_z = [exchange(send, ("gz", turn)) for turn, send in enumerate(to_z)]
    basis, ends, shares = call(
        functools.partial(prepare, nx, ny, n_x, n_y),
        [coef, vel, rhs, full_coef, full_rhs, *got_x, *got_y],
        [VMEM] * (5 + n_x + n_y),
        [f32(3, *cube), f32(5, groups, height, LANES), f32(6, ROWS, LANES)],
        "prepare",
        [scratch(*cube), scratch(2, *cube), scratch(2, *cube), scratch(*cube)],
    )
    slope = call(
        functools.partial(slopes, nx, ny, n_x, n_y),
        [press, vel, *got_x, *got_y],
        [VMEM] * (2 + n_x + n_y),
        [f32(nx + 1, ny, nz), f32(2, nx, ny, nz), f32(2, nx, ny, nz), f32(nx, ny, nz)],
        "slopes",
    )
    basis_z, vz_z, sums = call(
        functools.partial(join, nx, ny, n_z),
        [slope[-1], ends, shares, *got_z],
        [ANY] + [VMEM] * (2 + n_z),
        [f32(3, 2 * groups, height, LANES), f32(groups, height, LANES), f32(1, LANES)],
        "join",
        [scratch(6, 2 * groups, height, LANES), scratch(2 * groups, height, LANES)],
    )
    spread = jnp.broadcast_to(sums[None], (devices, 1, LANES))
    gathered = lax.all_to_all(spread, AXES, 0, 0).reshape(devices, LANES)
    return call(
        functools.partial(finish, nx, ny, n_z),
        [gathered, vel, basis, basis_z, vz_z, *slope, *got_z],
        [VMEM] * (9 + n_z),
        [f32(*vel.shape), f32(nx, ny, nz)],
        "finish",
        [scratch(*vel.shape), scratch(nx, ny, nz), pltpu.SemaphoreType.DMA((2, nx // STRIDE))],
        HBM,
    )


def solution(mesh):
    cells, faces = P(*AXES), P(None, *AXES)
    return jax.shard_map(
        on_device, mesh=mesh, in_specs=(cells, cells, faces), out_specs=(faces, cells), check_vma=False
    )
```

```python
import functools
import itertools

import jax
import jax.numpy as jnp
from jax import lax
from jax.experimental import pallas as pl
from jax.experimental.pallas import tpu as pltpu
from jax.sharding import PartitionSpec as P

AXES = ("gx", "gy", "gz")
SPARE = dict(gx="gy", gy="gz", gz="gx")
DEPTH = 4
GROUP = 4 * DEPTH
LANES = 128
STRIDE = 4
ROWS = 8
VMEM = pl.BlockSpec(memory_space=pltpu.VMEM)
HBM = pl.BlockSpec(memory_space=pltpu.HBM)
ANY = pl.BlockSpec(memory_space=pl.ANY)
PARAMS = pltpu.CompilerParams(vmem_limit_bytes=40 * 1024 * 1024)


def swaps(moves):
    sizes = [lax.axis_size(name) for name in AXES]
    number = lambda place: (place[0] * sizes[1] + place[1]) * sizes[2] + place[2]
    spare = AXES.index("gz" if len(moves) > 1 else SPARE[moves[0][0]])
    pairs = []
    for place in itertools.product(*map(range, sizes)):
        partner, met = list(place), True
        for axis, turn in moves:
            along = AXES.index(axis)
            partner[along] += 1 if (place[along] - turn) % 2 == 0 else -1
            met = met and 0 <= partner[along] < sizes[along]
        if not met:
            if sizes[spare] % 2:
                continue
            partner = list(place)
            partner[spare] ^= 1
        pairs.append((number(place), number(partner)))
    return pairs


def exchange(send, *moves):
    return lax.ppermute(send, AXES, swaps(moves))


def clear_if_alone(out, *moves):
    for axis, turn in moves:
        count, place = lax.axis_size(axis), lax.axis_index(axis)
        alone = []
        if turn == 1:
            alone.append(place == 0)
        if count % 2 != turn:
            alone.append(place == count - 1)
        for case in alone:

            @pl.when(case)
            def _():
                out[...] = jnp.zeros(out.shape, out.dtype)


def even(axis):
    return lax.axis_index(axis) % 2 == 0


def turns(axis):
    return min(2, lax.axis_size(axis) - 1)


def coefficient(phase):
    return jnp.where(phase == 0, 8.0, jnp.where(phase == 1, 1.0, 2.0)).astype(jnp.float32)


def sides(is_even, got, load):
    one = load(got[0])
    two = load(got[1]) if len(got) > 1 else jnp.zeros_like(one)
    return jnp.where(is_even, two, one), jnp.where(is_even, one, two)


def lane_index(shape):
    return lax.broadcasted_iota(jnp.int32, shape, len(shape) - 1)


def row_index(shape):
    return lax.broadcasted_iota(jnp.int32, shape, len(shape) - 2)


def roll_rows(plane, shift):
    return pltpu.roll(plane, shift % plane.shape[0], 0)


def roll_lanes(plane, shift):
    return pltpu.roll(plane, shift % plane.shape[1], 1)


def inner_rhs(coef, vy, vz):
    rows, lanes = row_index(coef.shape), lane_index(coef.shape)
    up = jnp.where(rows == coef.shape[0] - 1, 0.0, 0.5 * (coef + roll_rows(coef, -1)))
    down = jnp.where(rows == 0, 0.0, 0.5 * (coef + roll_rows(coef, 1)))
    right = jnp.where(lanes == LANES - 1, 0.0, 0.5 * (coef + roll_lanes(coef, -1)))
    left = jnp.where(lanes == 0, 0.0, 0.5 * (coef + roll_lanes(coef, 1)))
    return (up * vy - down * roll_rows(vy, 1)) + (right * vz - left * roll_lanes(vz, 1))


RHS, VX, PRESS, VY = DEPTH, 2 * DEPTH - 1, 2 * DEPTH, 2 * DEPTH + 1


def pack_first(nx, ny, n_x, n_y, phase, press, vel, *refs):
    outs, odd_outs, (held, held_vel, sem) = refs[:n_x], refs[n_x:-3], refs[-3:]
    if n_y > 1:
        *odd_outs, tile_phase, tile_vel, tile_press, tile_sem = odd_outs
    copies, late = [], []
    for turn, out in enumerate(outs):
        top = even("gx") == (turn == 0)
        deep = jnp.where(top, nx - DEPTH, 0)
        last = jnp.where(top, nx - 1, 0)
        parts = [
            (vel.at[:, pl.ds(deep, DEPTH)], held_vel.at[turn]),
            (phase.at[pl.ds(deep, DEPTH)], held.at[turn]),
            (press.at[last], out.at[pl.ds(PRESS * ny, ny)]),
        ]
        for which, (src, dst) in enumerate(parts):
            copy = pltpu.make_async_copy(src, dst, sem.at[turn, which])
            copy.start()
            copies.append(copy)
    if n_y > 1:
        row = pl.multiple_of(jnp.where(even("gy"), 0, ny - ROWS), ROWS)
        parts = [
            (phase.at[:, pl.ds(row, ROWS)], tile_phase),
            (vel.at[:, :, pl.ds(row, ROWS)], tile_vel),
            (press.at[:, pl.ds(row, ROWS)], tile_press),
        ]
        for which, (src, dst) in enumerate(parts):
            copy = pltpu.make_async_copy(src, dst, tile_sem.at[which])
            copy.start()
            late.append(copy)
    lanes = lane_index((ROWS, LANES))
    rows = row_index((ROWS, LANES))
    for turn, out in enumerate(outs):
        for copy in copies[3 * turn : 3 * turn + 3]:
            copy.wait()
        top = even("gx") == (turn == 0)
        coefs = [coefficient(held[turn, j]) for j in range(DEPTH)]
        flux = [0.5 * (coefs[j] + coefs[j + 1]) * held_vel[turn, 0, j] for j in range(DEPTH - 1)]
        columns = jnp.zeros((ROWS, LANES), jnp.float32)
        lines = jnp.zeros((ROWS, LANES), jnp.float32)
        for j in range(DEPTH):
            out[j * ny : (j + 1) * ny, :] = coefs[j]
        for j in range(DEPTH - 1):
            vy = jnp.where(top, held_vel[turn, 1, j + 1], held_vel[turn, 1, j])
            vz = jnp.where(top, held_vel[turn, 2, j + 1], held_vel[turn, 2, j])
            upper = (flux[j + 1] - flux[j]) if j + 1 < DEPTH - 1 else -flux[j]
            lower = (flux[j] - flux[j - 1]) if j else flux[j]
            inner = inner_rhs(jnp.where(top, coefs[j + 1], coefs[j]), vy, vz)
            out[(RHS + j) * ny : (RHS + j + 1) * ny, :] = jnp.where(top, upper, lower) + inner
            for t in range(ny // ROWS):
                lane = DEPTH * t + j
                columns = jnp.where(lanes == lane, roll_lanes(vz[t * ROWS : (t + 1) * ROWS], lane + 1), columns)
            lines = jnp.where(rows == j, roll_rows(vy[ny - ROWS :], j + 1), lines)
        out[VX * ny : (VX + 1) * ny, :] = held_vel[turn, 0, DEPTH - 1]
        out[VY * ny : VY * ny + ROWS, :] = lines
        out[VY * ny + ROWS :, :] = columns
        clear_if_alone(out, ("gx", turn))
    for copy in late:
        copy.wait()
    if n_y > 1:
        pack_odd(nx, tile_phase, tile_vel, tile_press, odd_outs)


def row_tile(coef, rhs, vy, top):
    rows = row_index((ROWS, LANES))
    coef = jnp.where(top, roll_rows(coef, DEPTH), coef)
    rhs = jnp.where(top, roll_rows(rhs, -1), roll_rows(rhs, DEPTH))
    return jnp.where(rows == ROWS - 1, vy, jnp.where(rows < DEPTH, coef, rhs))


def pack_odd(nx, tile_phase, tile_vel, tile_press, outs):
    out, *corners = outs
    top = jnp.logical_not(even("gy"))
    lanes = lane_index((ROWS, LANES))
    ends_at, vx_at = nx + nx // ROWS, nx + nx // ROWS + 1
    ends = jnp.zeros((ROWS, LANES), jnp.float32)
    here, old_flux = coefficient(tile_phase[0]), None
    for x in range(nx):
        vy, vz = tile_vel[1, x], tile_vel[2, x]
        answer = inner_rhs(here, vy, vz)
        if old_flux is not None:
            answer = answer - old_flux
        coef = here
        if x + 1 < nx:
            above = coefficient(tile_phase[x + 1])
            old_flux = 0.5 * (here + above) * tile_vel[0, x]
            answer = answer + old_flux
            here = above
        out[x] = row_tile(coef, answer, vy, top)
        ends = jnp.where(lanes == x, roll_lanes(vz, x + 1), ends)
        tile = tile_press[x]
        at = nx + x // ROWS
        out[at, x % ROWS : x % ROWS + 1, :] = jnp.where(top, tile[ROWS - 1 : ROWS], tile[0:1])
    shift = lambda tile: jnp.where(top, roll_rows(tile, -1), roll_rows(tile, DEPTH))
    ends = jnp.where(top, roll_rows(ends, DEPTH - 1), ends)
    out[ends_at] = ends
    out[vx_at] = shift(tile_vel[0, nx - 1])
    for turn, corner in enumerate(corners):
        first = jnp.where(even("gx") == (turn == 0), nx - DEPTH, 0)
        for j in range(DEPTH):
            corner[j] = out[first + j]
        corner[DEPTH] = pltpu.roll(ends, jnp.where(first == 0, 0, (DEPTH - nx) % LANES), 1)
        corner[DEPTH + 1] = out[vx_at]
        clear_if_alone(corner, ("gx", turn), ("gy", 1))
    clear_if_alone(out, ("gy", 1))


def merge_odd(nx, got, *refs):
    corners, out = refs[:-1], refs[-1]
    total = nx + 2 * DEPTH
    rows, lanes = row_index((ROWS, LANES)), lane_index((ROWS, LANES))
    ends_at, vx_at = nx + nx // ROWS, nx + nx // ROWS + 1
    low, high = zip(*[sides(even("gx"), corners, lambda ref: ref[j]) for j in range(DEPTH + 2)])
    tiles = [got[x] for x in range(nx)] + list(high[:DEPTH]) + list(low[:DEPTH])
    inner = (rows >= DEPTH) & (rows < ROWS - 1)

    def face(below, above, vx):
        weight = 0.5 * (tiles[below] + tiles[above])
        weight = jnp.where(even("gy"), roll_rows(weight, DEPTH - 1), roll_rows(weight, DEPTH))
        return jnp.where(inner, weight * vx, 0.0)

    low_face, high_face = face(total - 1, 0, low[DEPTH + 1]), face(nx - 1, nx, got[vx_at])
    for plane, tile in enumerate(tiles):
        if plane == 0:
            tile = tile - low_face
        if plane == total - 1:
            tile = tile + low_face
        if plane == nx - 1:
            tile = tile + high_face
        if plane == nx:
            tile = tile - high_face
        out[plane] = tile
    for at in range(nx // ROWS):
        out[total + at] = got[nx + at]
    ends = jnp.where(lanes < nx, got[ends_at], roll_lanes(high[DEPTH], nx))
    out[total + nx // ROWS] = jnp.where(lanes < nx + DEPTH, ends, roll_lanes(low[DEPTH], nx + DEPTH))


def load(phase, press, vel, after, coef, press_out, vel_out, rhs, held, sem):
    del after
    copies = []
    for which, (src, dst) in enumerate(((phase, held), (press, press_out), (vel, vel_out))):
        copies.append(pltpu.make_async_copy(src, dst, sem.at[which]))
        copies[-1].start()
    copies[0].wait()
    copies[1].wait()
    copies[2].wait()
    nx = coef.shape[0]
    here = coefficient(held[0])
    old_flux = None
    for x in range(nx):
        coef[x] = here
        answer = inner_rhs(here, vel_out[1, x], vel_out[2, x])
        if old_flux is not None:
            answer = answer - old_flux
        if x + 1 < nx:
            above = coefficient(held[x + 1])
            old_flux = 0.5 * (here + above) * vel_out[0, x]
            answer = answer + old_flux
            here = above
        rhs[x] = answer


class Block:
    def __init__(self, nx, ny, coef, vel, rhs, got_x, row=0, height=None, faces=True):
        self.nx, self.ny = nx, ny
        self.own_coef, self.vel, self.own_rhs, self.got_x = coef, vel, rhs, got_x
        self.even = even("gx")
        self.row, self.height = row, height or ny
        if not faces:
            return
        self.low_face = 0.5 * (self.coef(nx + 2 * DEPTH - 1) + self.coef(0)) * self.halo(VX)[0]
        self.high_face = 0.5 * (self.coef(nx - 1) + self.coef(nx)) * self.take(vel, 0, nx - 1)

    def take(self, ref, *index):
        return ref[(*index, pl.ds(self.row, self.height), slice(None))]

    def halo(self, part):
        return sides(self.even, self.got_x, lambda ref: ref[pl.ds(part * self.ny + self.row, self.height), :])

    def coef(self, plane):
        if plane < self.nx:
            return self.take(self.own_coef, plane)
        above = plane < self.nx + DEPTH
        return self.halo((plane - self.nx) % DEPTH)[1 if above else 0]

    def rhs(self, plane):
        nx = self.nx
        if plane < nx:
            answer = self.take(self.own_rhs, plane)
        else:
            above = plane < nx + DEPTH
            layer = plane - nx if above else plane - nx - DEPTH - 1
            if layer < 0 or layer >= DEPTH - 1:
                return jnp.zeros((self.height, LANES), jnp.float32)
            answer = self.halo(RHS + layer)[1 if above else 0]
        if plane == 0:
            answer = answer - self.low_face
        if plane == nx + 2 * DEPTH - 1:
            answer = answer + self.low_face
        if plane == nx - 1:
            answer = answer + self.high_face
        if plane == nx:
            answer = answer - self.high_face
        return answer

    def layer(self, plane):
        if plane < self.nx + DEPTH:
            place = (1, plane - self.nx)
        else:
            place = (0, plane - self.nx - DEPTH - 1)
        return place if 0 <= place[1] < DEPTH - 1 else None

    def columns(self):
        at = VY * self.ny + ROWS
        return sides(self.even, self.got_x, lambda ref: ref[at : at + ROWS, :])

    def vz_end(self, plane, lane):
        if plane < self.nx:
            return roll_lanes(self.vel[2, plane], lane + 1)
        place = self.layer(plane)
        if place is None:
            return jnp.zeros((self.ny, LANES), jnp.float32)
        source = self.columns()[place[0]]
        return jnp.concatenate(
            [roll_lanes(source, lane - DEPTH * t - place[1]) for t in range(self.ny // ROWS)], 0
        )

    def vy_end(self, plane):
        if plane < self.nx:
            return self.vel[1, plane, self.ny - 1 :, :]
        place = self.layer(plane)
        if place is None:
            return jnp.zeros((1, LANES), jnp.float32)
        at = VY * self.ny + place[1]
        return sides(self.even, self.got_x, lambda ref: ref[at : at + 1, :])[place[0]]


def pack_y(nx, ny, n_x, coef, press, vel, rhs, *refs):
    got_x, out = refs[:n_x], refs[-1]
    total = nx + 2 * DEPTH
    lanes = lane_index((ROWS, LANES))
    top = even("gy")
    row = pl.multiple_of(jnp.where(top, ny - ROWS, 0), ROWS)
    block = Block(nx, ny, coef, vel, rhs, got_x, row, ROWS)
    columns = jnp.zeros((ROWS, LANES), jnp.float32)
    ends = block.columns()
    for plane in range(total):
        out[plane] = row_tile(block.coef(plane), block.rhs(plane), block.vy_end(plane), top)
        if plane < nx:
            source = roll_lanes(vel[2, plane, pl.ds(row, ROWS), :], plane + 1)
        elif block.layer(plane) is None:
            continue
        else:
            side, layer = block.layer(plane)
            high = (plane - layer - DEPTH * (ny // ROWS - 1)) % LANES
            source = pltpu.roll(ends[side], jnp.where(top, high, (plane - layer) % LANES), 1)
        columns = jnp.where(lanes == plane, source, columns)
    out[total + nx // ROWS] = jnp.where(top, roll_rows(columns, DEPTH - 1), columns)
    for plane in range(nx):
        tile = press[plane, pl.ds(row, ROWS), :]
        edge = jnp.where(top, tile[ROWS - 1 : ROWS], tile[0:1])
        out[total + plane // ROWS, plane % ROWS : plane % ROWS + 1, :] = edge
    clear_if_alone(out, ("gy", 0))


def tall_end(block, tile_end, plane, lane):
    return jnp.concatenate([block.vz_end(plane, lane), roll_lanes(tile_end, lane - plane)], 0)


def tile_of_ends(nx, even_y, got_y):
    rows = row_index((ROWS, LANES))
    low, high = sides(even_y, got_y, lambda ref: ref[nx + 2 * DEPTH + nx // ROWS])
    return jnp.where(rows < DEPTH, high, roll_rows(low, DEPTH + 1))


def press_lane(x):
    return GROUP * (x % ROWS) + ROWS + 2 * (x // ROWS)


def pack_plane(lanes, at, top, coef, rhs, end):
    coef = pltpu.roll(coef, jnp.where(top, (at + DEPTH) % LANES, at), 1)
    rhs = pltpu.roll(rhs, jnp.where(top, (at + ROWS - 1) % LANES, at + DEPTH), 1)
    value = jnp.where(lanes == at + ROWS - 1, end, 0.0)
    value = jnp.where((lanes >= at + DEPTH) & (lanes < at + ROWS - 1), rhs, value)
    return jnp.where((lanes >= at) & (lanes < at + DEPTH), coef, value)


def half_tile(tile, below):
    rows = row_index((ROWS, LANES))
    coef = jnp.where(below, jnp.where(rows >= DEPTH, roll_rows(tile, DEPTH), 0.0), jnp.where(rows < DEPTH, tile, 0.0))
    rhs = jnp.where(
        below,
        jnp.where(rows > DEPTH, roll_rows(tile, 1), 0.0),
        jnp.where(rows < DEPTH - 1, roll_rows(tile, -DEPTH), 0.0),
    )
    return coef, rhs


def half_ends(tile, below):
    rows = row_index((ROWS, LANES))
    return jnp.where(
        below, jnp.where(rows > DEPTH, roll_rows(tile, DEPTH + 1), 0.0), jnp.where(rows < DEPTH - 1, tile, 0.0)
    )


def face_y(own_low, own_high, coef_tile, tile, vy_end, below):
    rows = row_index((ROWS, LANES))
    down = 0.5 * (coef_tile[ROWS - 1 :] + own_low) * tile[ROWS - 1 :]
    up = 0.5 * (own_high + coef_tile[:1]) * vy_end
    outside = jnp.where(below, jnp.where(rows == ROWS - 1, down, 0.0), jnp.where(rows == 0, -up, 0.0))
    inside = jnp.where(below, jnp.where(rows == 0, -down, 0.0), jnp.where(rows == ROWS - 1, up, 0.0))
    return outside, inside


def stage_z(nx, ny, n_x, n_z, coef, press, vel, rhs, *refs):
    got_x, (*got_odd, full_coef, full_rhs), sends = refs[:n_x], refs[n_x : len(refs) - n_z], refs[len(refs) - n_z :]
    total, height = nx + 2 * DEPTH, ny + 2 * DEPTH
    groups = total // ROWS
    below = even("gy")
    lanes = lane_index((height, LANES))
    block = Block(nx, ny, coef, vel, rhs, got_x)
    nothing = jnp.zeros((ROWS, LANES), jnp.float32)
    tile_end = half_ends(got_odd[0][total + nx // ROWS], below) if got_odd else nothing
    made = [[jnp.zeros((height, LANES), jnp.float32) for _ in range(groups // 2 + 1)] for _ in sends]
    row = pl.ds(pl.multiple_of(jnp.where(below, 0, ny - ROWS), ROWS), ROWS)
    for plane in range(total):
        c_own, r_own = block.coef(plane), block.rhs(plane)
        c_tile = r_tile = nothing
        full_rhs[plane, :ny, :] = r_own
        if got_odd:
            tile = got_odd[0][plane]
            c_tile, r_tile = half_tile(tile, below)
            outside, inside = face_y(c_own[:1], c_own[ny - 1 :], c_tile, tile, block.vy_end(plane), below)
            r_tile = r_tile + outside
            full_rhs[plane, row, :] = full_rhs[plane, row, :] + inside
        c_all = jnp.concatenate([c_own, c_tile], 0)
        full_coef[plane] = c_all
        full_rhs[plane, ny:, :] = r_tile
        r_all = full_rhs[plane]
        group, seat = plane % groups, plane // groups
        at = GROUP * seat + ROWS * (group % 2)
        end = tall_end(block, tile_end, plane, at + ROWS - 1)
        for turn in range(n_z):
            value = pack_plane(lanes, at, even("gz") == (turn == 0), c_all, r_all, end)
            made[turn][group // 2] = made[turn][group // 2] + value
    for turn, send in enumerate(sends):
        top = even("gz") == (turn == 0)
        value = made[turn][groups // 2][:ny]
        for plane in range(nx):
            at = press_lane(plane)
            moved = pltpu.roll(press[plane], jnp.where(top, (at + 1) % LANES, at), 1)
            value = jnp.where(lanes[:ny] == at, moved, value)
        made[turn][groups // 2] = jnp.concatenate([value, made[turn][groups // 2][ny:]], 0)
        for which, value in enumerate(made[turn]):
            send[which] = value


def pack_z(nx, ny, n_x, n_z, vel, *refs):
    got_x, got, (full_coef, full_rhs, *sends) = refs[:n_x], refs[n_x], refs[-2 - n_z :]
    total = nx + 2 * DEPTH
    groups = total // ROWS
    below = jnp.logical_not(even("gy"))
    lanes = lane_index((ROWS, LANES))
    block = Block(nx, ny, full_coef, vel, full_rhs, got_x, faces=False)
    tile_end = half_ends(got[total + nx // ROWS], below)
    row = pl.ds(pl.multiple_of(jnp.where(below, 0, ny - ROWS), ROWS), ROWS)
    added = [[[jnp.zeros((ROWS, LANES), jnp.float32) for _ in range(2)] for _ in range(groups // 2 + 1)] for _ in sends]
    for plane in range(total):
        tile = got[plane]
        c_tile, r_tile = half_tile(tile, below)
        low, high = full_coef[plane, :1, :], full_coef[plane, ny - 1 : ny, :]
        outside, inside = face_y(low, high, c_tile, tile, block.vy_end(plane), below)
        r_tile = r_tile + outside
        full_coef[plane, ny:, :] = full_coef[plane, ny:, :] + c_tile
        full_rhs[plane, ny:, :] = full_rhs[plane, ny:, :] + r_tile
        full_rhs[plane, row, :] = full_rhs[plane, row, :] + inside
        group, seat = plane % groups, plane // groups
        at = GROUP * seat + ROWS * (group % 2)
        end = roll_lanes(tile_end, at + ROWS - 1 - plane)
        for turn in range(n_z):
            top = even("gz") == (turn == 0)
            inside_move = pltpu.roll(inside, jnp.where(top, (at + ROWS - 1) % LANES, at + DEPTH), 1)
            inside_move = jnp.where((lanes >= at + DEPTH) & (lanes < at + ROWS - 1), inside_move, 0.0)
            slot = added[turn][group // 2]
            slot[0] = slot[0] + pack_plane(lanes, at, top, c_tile, r_tile, end)
            slot[1] = slot[1] + inside_move
    for turn, send in enumerate(sends):
        for which, (tile, inside) in enumerate(added[turn]):
            send[which, ny:, :] = send[which, ny:, :] + tile
            send[which, row, :] = send[which, row, :] + inside
        clear_if_alone(send, ("gz", turn))


def tree_sum(parts):
    while len(parts) > 1:
        parts = [parts[i] + parts[i + 1] if i + 1 < len(parts) else parts[i] for i in range(0, len(parts), 2)]
    return parts[0]


class Totals:
    def __init__(self):
        self.stack = []

    def add(self, tile):
        level = 0
        while self.stack and self.stack[-1][0] == level:
            tile = self.stack.pop()[1] + tile
            level += 1
        self.stack.append((level, tile))

    def value(self):
        tiles = [tile for _, tile in self.stack]
        total = tiles.pop()
        while tiles:
            total = tiles.pop() + total
        return total


def prepare(nx, ny, n_x, n_y, coef, vel, rhs, full_coef, full_rhs, *refs):
    got_x, got_y = refs[:n_x], refs[n_x : n_x + n_y]
    basis, ends, shares, wx, wy, wz, inverse = refs[n_x + n_y :]
    total, height = nx + 2 * DEPTH, ny + 2 * DEPTH
    groups = total // ROWS
    lanes = lane_index((height, LANES))
    block = Block(nx, ny, coef, vel, rhs, got_x)
    tile_end = tile_of_ends(nx, even("gy"), got_y)
    for group in range(groups):
        made = [jnp.zeros((height, LANES), jnp.float32) for _ in range(5)]
        for seat in range(ROWS):
            plane = seat * groups + group
            at = GROUP * seat
            for which, source in enumerate((full_coef[plane], full_rhs[plane])):
                here = (lanes >= at + DEPTH) & (lanes < at + GROUP)
                made[2 * which] = jnp.where(here, roll_lanes(source, at + DEPTH), made[2 * which])
                here = (lanes >= at) & (lanes < at + GROUP - DEPTH)
                made[2 * which + 1] = jnp.where(here, roll_lanes(source, at + GROUP - DEPTH), made[2 * which + 1])
            lane = at + GROUP - DEPTH - 1
            made[4] = jnp.where(lanes == lane, tall_end(block, tile_end, plane, lane), made[4])
        for which in range(5):
            ends[which, group] = made[which]
    totals = [Totals() for _ in range(6)]
    trusted = (lanes[:ROWS] >= DEPTH) & (lanes[:ROWS] < LANES - DEPTH)

    def count(which, left, right):
        product = left[:ny] * right[:ny]
        tile = tree_sum([product[i : i + ROWS] for i in range(0, ny, ROWS)])
        totals[which].add(jnp.where(trusted, tile, 0.0))

    old_weight = None
    here = full_coef[nx + DEPTH]
    for x in range(-DEPTH, nx + DEPTH - 1):
        e = x % total
        above = full_coef[(e + 1) % total]
        weight = 0.5 * (here + above)
        wx[e] = weight
        if x > -DEPTH:
            up, down = 0.5 * (here + roll_rows(here, -1)), 0.5 * (here + roll_rows(here, 1))
            right = jnp.where(lanes == LANES - 1, 0.0, 0.5 * (here + roll_lanes(here, -1)))
            left = jnp.where(lanes == 0, 0.0, 0.5 * (here + roll_lanes(here, 1)))
            wy[0, e], wy[1, e], wz[0, e], wz[1, e] = up, down, right, left
            diag = (weight + old_weight) + (up + down) + (right + left)
            inside = here > 0
            scale = jnp.where(inside, 1.0 / jnp.where(inside, diag, 1.0), 0.0)
            inverse[e] = scale
            source = full_rhs[e]
            field = scale * source
            basis[0, e] = field
            if 0 <= x < nx:
                count(0, field, source)
        old_weight, here = weight, above
    for n in range(3):
        reach = 2 - n
        old_flux = None
        here = basis[n, (-reach - 1) % total]
        for x in range(-reach - 1, nx + reach):
            e = x % total
            above = basis[n, (e + 1) % total]
            flux = wx[e] * (above - here)
            if x >= -reach:
                image = old_flux - flux
                image = image + (
                    wy[0, e] * (here - roll_rows(here, -1)) + wy[1, e] * (here - roll_rows(here, 1))
                )
                image = image + (
                    wz[0, e] * (here - roll_lanes(here, -1)) + wz[1, e] * (here - roll_lanes(here, 1))
                )
                own = 0 <= x < nx
                if own:
                    count(2 * n + 1, here, image)
                if n < 2:
                    following = inverse[e] * image
                    basis[n + 1, e] = following
                    if own:
                        count(2 * n + 2, following, image)
            old_flux, here = flux, above
    for which, total_ in enumerate(totals):
        shares[which] = total_.value()


def beside_z(side):
    place = lax.axis_index("gz")
    return place > 0 if side == 0 else place < lax.axis_size("gz") - 1


def solve_end(nx, ny, side, received, ends, basis_z, vz_z, shares, weight_z, inverse_z):
    total, height = nx + 2 * DEPTH, ny + 2 * DEPTH
    groups = total // ROWS
    lanes = lane_index((height, LANES))
    seat_lane, seat = lanes % GROUP, lanes // GROUP
    outer = seat_lane < DEPTH if side == 0 else seat_lane >= GROUP - DEPTH
    coef, rhs, vz = [], [], []
    for g in range(groups):
        got, skip = received(g // 2), ROWS * (g % 2)
        start = 0 if side == 0 else GROUP - DEPTH
        less = 1 if side == 0 else 0
        coef.append(jnp.where(outer, roll_lanes(got, start - skip), ends[side, g]))
        rhs.append(jnp.where(outer, roll_lanes(got, start + less - DEPTH - skip), ends[2 + side, g]))
        if side == 0:
            vz.append(roll_lanes(got, -DEPTH - skip))
            vz_z[g] = vz[-1]
        else:
            vz.append(ends[4, g])

    def along(planes, g, step):
        if 0 <= g + step < groups:
            return planes[g + step]
        return roll_lanes(planes[(g + step) % groups], -GROUP * step)

    totals = [Totals() for _ in range(6)]

    def count(which, g, left, right):
        first = DEPTH if side == 0 else GROUP - 2 * DEPTH
        spot = seat_lane[:ROWS]
        mine = (spot >= first) & (spot < first + DEPTH) & (seat[:ROWS] * groups + g < nx)
        product = left[:ny] * right[:ny]
        tile = tree_sum([product[i : i + ROWS] for i in range(0, ny, ROWS)])
        totals[which].add(jnp.where(mine, tile, 0.0))

    field = []
    for g in range(groups):
        here, q = coef[g], side * groups + g
        neighbours = (along(coef, g, 1), along(coef, g, -1), roll_rows(here, -1), roll_rows(here, 1))
        neighbours += (roll_lanes(here, -1), roll_lanes(here, 1))
        weights = [0.5 * (here + other) for other in neighbours]
        for which, weight in enumerate(weights):
            weight_z[which, g] = weight
        diag = (weights[0] + weights[1]) + (weights[2] + weights[3]) + (weights[4] + weights[5])
        face = DEPTH - 1 if side == 0 else GROUP - DEPTH - 1
        source = rhs[g] + jnp.where(seat_lane == face, weights[4] * vz[g], 0.0)
        source = source - jnp.where(seat_lane == face + 1, weights[5] * roll_lanes(vz[g], 1), 0.0)
        inside = here > 0
        scale = jnp.where(inside, 1.0 / jnp.where(inside, diag, 1.0), 0.0)
        inverse_z[g] = scale
        field.append(scale * source)
        basis_z[0, q] = field[g]
        count(0, g, field[g], source)
    for n in range(3):
        following = []
        for g in range(groups):
            here, q = field[g], side * groups + g
            image = weight_z[0, g] * (here - along(field, g, 1)) + weight_z[1, g] * (here - along(field, g, -1))
            image = image + (
                weight_z[2, g] * (here - roll_rows(here, -1)) + weight_z[3, g] * (here - roll_rows(here, 1))
            )
            image = image + (
                weight_z[4, g] * (here - roll_lanes(here, -1)) + weight_z[5, g] * (here - roll_lanes(here, 1))
            )
            count(2 * n + 1, g, here, image)
            if n < 2:
                following.append(inverse_z[g] * image)
                basis_z[n + 1, q] = following[g]
                count(2 * n + 2, g, following[g], image)
        field = following
    for which, total_ in enumerate(totals):
        shares[which] = shares[which] + total_.value()


def outer_ends(nx, ny, ends, shares_in, basis_z, vz_z, shares, *scratch):
    shares[...] = shares_in[...]
    nothing = jnp.zeros((ny + 2 * DEPTH, LANES), jnp.float32)
    for side in range(2):

        @pl.when(jnp.logical_not(beside_z(side)))
        def _():
            solve_end(nx, ny, side, lambda i: nothing, ends, basis_z, vz_z, shares, *scratch)


def join(nx, ny, n_z, after, ends, *refs):
    del after
    got_z, (basis_z, vz_z, shares, sums, *scratch) = refs[:n_z], refs[n_z + 3 :]
    for side in range(2):

        @pl.when(beside_z(side))
        def _():
            received = lambda i: sides(even("gz"), got_z, lambda ref: ref[i])[side]
            solve_end(nx, ny, side, received, ends, basis_z, vz_z, shares, *scratch)

    lane = lane_index((1, LANES))
    row = jnp.zeros((1, LANES), jnp.float32)
    for which in range(6):
        value = jnp.sum(jnp.sum(shares[which], 0, keepdims=True), 1, keepdims=True)
        row = jnp.where(lane == which, value, row)
    sums[...] = row


def slopes(nx, ny, n_x, n_y, press, vel, *refs):
    got_x, got_y, (slope_x, slope_y, slope_z, base) = refs[:n_x], refs[n_x : n_x + n_y], refs[n_x + n_y :]
    total = nx + 2 * DEPTH
    rows, shape = row_index((ROWS, LANES)), (ROWS, LANES)
    lanes = lane_index((ny, LANES))
    at_low, at_high = lanes == 0, lanes == LANES - 1
    p_low, p_high = sides(even("gx"), got_x, lambda ref: ref[PRESS * ny : (PRESS + 1) * ny, :])
    u_low, _ = sides(even("gx"), got_x, lambda ref: ref[VX * ny : (VX + 1) * ny, :])
    old = p_low - press[0]
    slope_x[0] = old
    old = old * u_low
    for x in range(nx):
        p = press[x]
        slope = p - (press[x + 1] if x + 1 < nx else p_high)
        slope_x[x + 1] = slope
        new = slope * vel[0, x]
        answer, old = old + new, new
        low, high = sides(even("gy"), got_y, lambda ref: ref[total + x // ROWS, x % ROWS : x % ROWS + 1, :])
        p_tile = jnp.where(rows == 0, jnp.broadcast_to(high, shape), jnp.broadcast_to(low, shape))
        p_tall = jnp.concatenate([p, p_tile], 0)
        u_row, _ = sides(even("gy"), got_y, lambda ref: ref[x, ROWS - 1 :, :])
        u_tall = jnp.concatenate([vel[1, x], jnp.broadcast_to(u_row, shape)], 0)
        up, down = p - roll_rows(p_tall, -1)[:ny], roll_rows(p_tall, 1)[:ny] - p
        slope_y[0, x], slope_y[1, x] = up, down
        answer = answer + (up * vel[1, x] + down * roll_rows(u_tall, 1)[:ny])
        up = p - jnp.where(at_high, 0.0, roll_lanes(p, -1))
        down = jnp.where(at_low, 0.0, roll_lanes(p, 1)) - p
        slope_z[0, x], slope_z[1, x] = up, down
        base[x] = answer + (up * vel[2, x] + down * jnp.where(at_low, 0.0, roll_lanes(vel[2, x], 1)))


def finish(nx, ny, n_z, gathered, vel, basis, basis_z, vz_z, slope_x, slope_y, slope_z, base, *refs):
    got_z, (ustar_out, coef_out, ustar, coef_cot, sem) = refs[:n_z], refs[n_z:]
    total, height = nx + 2 * DEPTH, ny + 2 * DEPTH
    groups = total // ROWS
    parts = gathered[...]
    while parts.shape[0] > ROWS:
        half = parts.shape[0] // 2
        parts = parts[:half] + parts[half:]
    sums = jnp.sum(parts, 0, keepdims=True)
    lane = lane_index((1, LANES))
    m0, m1, m2, m3, m4, m5 = [
        jnp.sum(jnp.where(lane == which, sums, 0.0), 1, keepdims=True) for which in range(6)
    ]
    l1, l2 = m2 / m1, m3 / m1
    d1, cross, d2 = m3 - l1 * m2, m4 - l1 * m3, m5 - l2 * m3
    l21 = cross / d1
    d2 = d2 - l21 * cross
    y1 = -l1 * m0 + m1
    y2 = m2 - l2 * m0 - l21 * y1
    c2 = y2 / d2
    c1 = y1 / d1 - l21 * c2
    c0 = (m0 / m1 - l1 * c1 - l2 * c2)[0, 0]
    c1, c2 = c1[0, 0], c2[0, 0]

    lanes = lane_index((height, LANES))
    seat_lane = lanes % GROUP
    spill = []
    for g in range(groups):
        low, high = [
            c0 * basis_z[0, q] + c1 * basis_z[1, q] + c2 * basis_z[2, q] for q in (g, groups + g)
        ]
        cells = jnp.where(seat_lane < DEPTH - 1, roll_lanes(high, DEPTH - GROUP + DEPTH - 1), roll_lanes(low, -1))
        cells = jnp.where(seat_lane == 2 * DEPTH - 2, roll_lanes(high, 2 * DEPTH - 2 - (GROUP - DEPTH)), cells)
        spill.append(jnp.where(seat_lane == 2 * DEPTH - 1, roll_lanes(low, DEPTH), cells))
    spoiled = (lanes < DEPTH - 1) | (lanes > LANES - DEPTH)
    lanes = lane_index((ny, LANES))
    at_low, at_high = lanes == 0, lanes == LANES - 1
    low_z, high_z = sides(even("gz"), got_z, lambda ref: ref[groups // 2, :ny, :])
    press_z = jnp.where(lanes % 2 == 0, high_z, roll_lanes(low_z, 1))

    def solved(x):
        e = x % total
        cells = c0 * basis[0, e] + c1 * basis[1, e] + c2 * basis[2, e]
        return jnp.where(spoiled, roll_lanes(spill[e % groups], 1 - DEPTH - GROUP * (e // groups)), cells)

    copies = []
    below, here = solved(-1), solved(0)
    down = here[:ny] - below[:ny]
    for x in range(nx):
        above = solved(x + 1)
        group, seat = x % groups, x // groups
        own = here[:ny]
        up = above[:ny] - own
        ustar[0, x] = vel[0, x] + up
        answer = base[x] + (slope_x[x + 1] * up + slope_x[x] * down)
        next_down = up
        up, down = roll_rows(here, -1)[:ny] - own, own - roll_rows(here, 1)[:ny]
        ustar[1, x] = vel[1, x] + up
        answer = answer + (slope_y[0, x] * up + slope_y[1, x] * down)
        lam_end = roll_lanes(spill[group][:ny], 1 - 2 * DEPTH - GROUP * seat)
        u_end = roll_lanes(vz_z[group, :ny, :], 1 - DEPTH - GROUP * seat)
        p_end = roll_lanes(press_z, LANES - 1 - press_lane(x))
        up = jnp.where(at_high, lam_end, roll_lanes(own, -1)) - own
        down = own - jnp.where(at_low, lam_end, roll_lanes(own, 1))
        out = vel[2, x] + up
        ustar[2, x] = out
        answer = answer + (slope_z[0, x] * up + slope_z[1, x] * down)
        beyond = jnp.where(at_low, p_end * (u_end + down) + slope_z[1, x] * u_end, 0.0)
        answer = answer + jnp.where(at_high, -p_end * out, beyond)
        down = next_down
        coef_cot[x] = 0.5 * answer
        here = above
        if (x + 1) % STRIDE == 0:
            part = pl.ds(x + 1 - STRIDE, STRIDE)
            for which, (src, dst) in enumerate(
                ((ustar.at[:, part], ustar_out.at[:, part]), (coef_cot.at[part], coef_out.at[part]))
            ):
                copies.append(pltpu.make_async_copy(src, dst, sem.at[which, x // STRIDE]))
                copies[-1].start()
    for copy in copies:
        copy.wait()


def on_device(phase, press, vel):
    nx, ny, nz = phase.shape
    total, height = nx + 2 * DEPTH, ny + 2 * DEPTH
    groups = total // ROWS
    devices = lax.axis_size(AXES)
    n_x, n_y, n_z = (turns(axis) for axis in AXES)
    f32 = lambda *shape: jax.ShapeDtypeStruct(shape, jnp.float32)
    scratch = lambda *shape: pltpu.VMEM(shape, jnp.float32)
    inputs = [pltpu.with_memory_space_constraint(array, pltpu.HBM) for array in (phase, press, vel)]

    def call(kernel, args, in_specs, shapes, name, scratch_shapes=(), out_spec=VMEM, aliases={}):
        return pl.pallas_call(
            kernel,
            out_shape=shapes,
            in_specs=in_specs,
            out_specs=[out_spec] * len(shapes),
            scratch_shapes=list(scratch_shapes),
            input_output_aliases=aliases,
            compiler_params=PARAMS,
            cost_estimate=pl.CostEstimate(flops=3_000_000, bytes_accessed=3_000_000, transcendentals=0),
            name=name,
        )(*args)

    odd = n_y > 1
    sent = call(
        functools.partial(pack_first, nx, ny, n_x, n_y),
        inputs,
        [HBM] * 3,
        [f32(VY * ny + 2 * ROWS, nz)] * n_x
        + ([f32(nx + nx // ROWS + 2, ROWS, nz)] + [f32(DEPTH + 2, ROWS, nz)] * n_x if odd else []),
        "pack_first",
        (
            [pltpu.VMEM((nx, ROWS, nz), jnp.int32), scratch(3, nx, ROWS, nz), scratch(nx, ROWS, nz)]
            + [pltpu.SemaphoreType.DMA((3,))]
            if odd
            else []
        )
        + [pltpu.VMEM((n_x, DEPTH, ny, nz), jnp.int32), scratch(n_x, 3, DEPTH, ny, nz)]
        + [pltpu.SemaphoreType.DMA((n_x, 3))],
    )
    to_x = sent[:n_x]
    got_x = [exchange(send, ("gx", turn)) for turn, send in enumerate(to_x)]
    if odd:
        got_odd = exchange(sent[n_x], ("gy", 1))
        corners = [exchange(send, ("gx", turn), ("gy", 1)) for turn, send in enumerate(sent[n_x + 1 :])]
    coef, press, vel, rhs = call(
        load,
        inputs + [to_x[0]],
        [HBM] * 3 + [ANY],
        [f32(*press.shape), f32(*press.shape), f32(*vel.shape), f32(*press.shape)],
        "load",
        [pltpu.VMEM(phase.shape, jnp.int32), pltpu.SemaphoreType.DMA((3,))],
    )
    rows_y = f32(total + nx // ROWS + 1, ROWS, nz)
    got_y, odd_rows = [], []
    if odd:
        odd_rows = call(
            functools.partial(merge_odd, nx),
            [got_odd, *corners],
            [VMEM] * (1 + n_x),
            [rows_y],
            "merge_odd",
        )
    if n_y:
        to_y = call(
            functools.partial(pack_y, nx, ny, n_x),
            [coef, press, vel, rhs, *got_x, *odd_rows],
            [VMEM] * (4 + n_x) + [ANY] * len(odd_rows),
            [rows_y],
            "pack_y",
        )
        got_y = [exchange(to_y[0], ("gy", 0)), *odd_rows]
    cube = (total, height, nz)
    packs = [f32(groups // 2 + 1, height, LANES)] * n_z
    staged = call(
        functools.partial(stage_z, nx, ny, n_x, n_z),
        [coef, press, vel, rhs, *got_x, *odd_rows],
        [VMEM] * (4 + n_x + len(odd_rows)),
        [f32(*cube)] * 2 + packs,
        "stage_z",
    )
    full_coef, full_rhs, *to_z = call(
        functools.partial(pack_z, nx, ny, n_x, n_z),
        [vel, *got_x, got_y[0], *staged],
        [VMEM] * (4 + n_x + n_z),
        [f32(*cube)] * 2 + packs,
        "pack_z",
        aliases={2 + n_x + which: which for which in range(2 + n_z)},
    )
    got_z = [exchange(send, ("gz", turn)) for turn, send in enumerate(to_z)]
    basis, ends, shares = call(
        functools.partial(prepare, nx, ny, n_x, n_y),
        [coef, vel, rhs, full_coef, full_rhs, *got_x, *got_y],
        [VMEM] * (5 + n_x + n_y),
        [f32(3, *cube), f32(5, groups, height, LANES), f32(6, ROWS, LANES)],
        "prepare",
        [scratch(*cube), scratch(2, *cube), scratch(2, *cube), scratch(*cube)],
    )
    slope = call(
        functools.partial(slopes, nx, ny, n_x, n_y),
        [press, vel, *got_x, *got_y],
        [VMEM] * (2 + n_x + n_y),
        [f32(nx + 1, ny, nz), f32(2, nx, ny, nz), f32(2, nx, ny, nz), f32(nx, ny, nz)],
        "slopes",
    )
    shapes_z = [f32(3, 2 * groups, height, LANES), f32(groups, height, LANES), f32(6, ROWS, LANES)]
    scratch_z = [scratch(6, groups, height, LANES), scratch(groups, height, LANES)]
    outer = call(
        functools.partial(outer_ends, nx, ny),
        [ends, shares],
        [VMEM] * 2,
        shapes_z,
        "outer_ends",
        scratch_z,
    )
    basis_z, vz_z, _, sums = call(
        functools.partial(join, nx, ny, n_z),
        [slope[-1], ends, *got_z, *outer],
        [ANY] + [VMEM] * (4 + n_z),
        shapes_z + [f32(1, LANES)],
        "join",
        scratch_z,
        aliases={2 + n_z + which: which for which in range(3)},
    )
    spread = jnp.broadcast_to(sums[None], (devices, 1, LANES))
    gathered = lax.all_to_all(spread, AXES, 0, 0).reshape(devices, LANES)
    return call(
        functools.partial(finish, nx, ny, n_z),
        [gathered, vel, basis, basis_z, vz_z, *slope, *got_z],
        [VMEM] * (9 + n_z),
        [f32(*vel.shape), f32(nx, ny, nz)],
        "finish",
        [scratch(*vel.shape), scratch(nx, ny, nz), pltpu.SemaphoreType.DMA((2, nx // STRIDE))],
        HBM,
    )


def solution(mesh):
    cells, faces = P(*AXES), P(None, *AXES)
    return jax.shard_map(
        on_device, mesh=mesh, in_specs=(cells, cells, faces), out_specs=(faces, cells), check_vma=False
    )
```

```python
import functools
import itertools

import jax
import jax.numpy as jnp
from jax import lax
from jax.experimental import pallas as pl
from jax.experimental.pallas import tpu as pltpu
from jax.sharding import PartitionSpec as P

AXES = ("gx", "gy", "gz")
SPARE = dict(gx="gy", gy="gz", gz="gx")
DEPTH = 4
GROUP = 4 * DEPTH
LANES = 128
STRIDE = 4
ROWS = 8
VMEM = pl.BlockSpec(memory_space=pltpu.VMEM)
HBM = pl.BlockSpec(memory_space=pltpu.HBM)
ANY = pl.BlockSpec(memory_space=pl.ANY)
PARAMS = pltpu.CompilerParams(vmem_limit_bytes=40 * 1024 * 1024)


def swaps(moves):
    sizes = [lax.axis_size(name) for name in AXES]
    number = lambda place: (place[0] * sizes[1] + place[1]) * sizes[2] + place[2]
    spare = AXES.index("gz" if len(moves) > 1 else SPARE[moves[0][0]])
    pairs = []
    for place in itertools.product(*map(range, sizes)):
        partner, met = list(place), True
        for axis, turn in moves:
            along = AXES.index(axis)
            partner[along] += 1 if (place[along] - turn) % 2 == 0 else -1
            met = met and 0 <= partner[along] < sizes[along]
        if not met:
            if sizes[spare] % 2:
                continue
            partner = list(place)
            partner[spare] ^= 1
        pairs.append((number(place), number(partner)))
    return pairs


def exchange(send, *moves):
    return lax.ppermute(send, AXES, swaps(moves))


def clear_if_alone(out, *moves):
    for axis, turn in moves:
        count, place = lax.axis_size(axis), lax.axis_index(axis)
        alone = []
        if turn == 1:
            alone.append(place == 0)
        if count % 2 != turn:
            alone.append(place == count - 1)
        for case in alone:

            @pl.when(case)
            def _():
                out[...] = jnp.zeros(out.shape, out.dtype)


def even(axis):
    return lax.axis_index(axis) % 2 == 0


def turns(axis):
    return min(2, lax.axis_size(axis) - 1)


def coefficient(phase):
    return jnp.where(phase == 0, 8.0, jnp.where(phase == 1, 1.0, 2.0)).astype(jnp.float32)


def sides(is_even, got, load):
    one = load(got[0])
    two = load(got[1]) if len(got) > 1 else jnp.zeros_like(one)
    return jnp.where(is_even, two, one), jnp.where(is_even, one, two)


def lane_index(shape):
    return lax.broadcasted_iota(jnp.int32, shape, len(shape) - 1)


def row_index(shape):
    return lax.broadcasted_iota(jnp.int32, shape, len(shape) - 2)


def roll_rows(plane, shift):
    return pltpu.roll(plane, shift % plane.shape[0], 0)


def roll_lanes(plane, shift):
    return pltpu.roll(plane, shift % plane.shape[1], 1)


def inner_rhs(coef, vy, vz):
    rows, lanes = row_index(coef.shape), lane_index(coef.shape)
    up = jnp.where(rows == coef.shape[0] - 1, 0.0, 0.5 * (coef + roll_rows(coef, -1)))
    down = jnp.where(rows == 0, 0.0, 0.5 * (coef + roll_rows(coef, 1)))
    right = jnp.where(lanes == LANES - 1, 0.0, 0.5 * (coef + roll_lanes(coef, -1)))
    left = jnp.where(lanes == 0, 0.0, 0.5 * (coef + roll_lanes(coef, 1)))
    return (up * vy - down * roll_rows(vy, 1)) + (right * vz - left * roll_lanes(vz, 1))


RHS, VX, PRESS, VY = DEPTH, 2 * DEPTH - 1, 2 * DEPTH, 2 * DEPTH + 1


def pack_first(nx, ny, n_x, n_y, phase, press, vel, *refs):
    outs, odd_outs, (held, held_vel, sem) = refs[:n_x], refs[n_x:-3], refs[-3:]
    if n_y > 1:
        *odd_outs, tile_phase, tile_vel, tile_press, tile_sem = odd_outs
    copies, late = [], []
    for turn, out in enumerate(outs):
        top = even("gx") == (turn == 0)
        deep = jnp.where(top, nx - DEPTH, 0)
        last = jnp.where(top, nx - 1, 0)
        parts = [
            (vel.at[:, pl.ds(deep, DEPTH)], held_vel.at[turn]),
            (phase.at[pl.ds(deep, DEPTH)], held.at[turn]),
            (press.at[last], out.at[pl.ds(PRESS * ny, ny)]),
        ]
        for which, (src, dst) in enumerate(parts):
            copy = pltpu.make_async_copy(src, dst, sem.at[turn, which])
            copy.start()
            copies.append(copy)
    if n_y > 1:
        row = pl.multiple_of(jnp.where(even("gy"), 0, ny - ROWS), ROWS)
        parts = [
            (phase.at[:, pl.ds(row, ROWS)], tile_phase),
            (vel.at[:, :, pl.ds(row, ROWS)], tile_vel),
            (press.at[:, pl.ds(row, ROWS)], tile_press),
        ]
        for which, (src, dst) in enumerate(parts):
            copy = pltpu.make_async_copy(src, dst, tile_sem.at[which])
            copy.start()
            late.append(copy)
    lanes = lane_index((ROWS, LANES))
    rows = row_index((ROWS, LANES))
    for turn, out in enumerate(outs):
        for copy in copies[3 * turn : 3 * turn + 3]:
            copy.wait()
        top = even("gx") == (turn == 0)
        coefs = [coefficient(held[turn, j]) for j in range(DEPTH)]
        flux = [0.5 * (coefs[j] + coefs[j + 1]) * held_vel[turn, 0, j] for j in range(DEPTH - 1)]
        columns = jnp.zeros((ROWS, LANES), jnp.float32)
        lines = jnp.zeros((ROWS, LANES), jnp.float32)
        for j in range(DEPTH):
            out[j * ny : (j + 1) * ny, :] = coefs[j]
        for j in range(DEPTH - 1):
            vy = jnp.where(top, held_vel[turn, 1, j + 1], held_vel[turn, 1, j])
            vz = jnp.where(top, held_vel[turn, 2, j + 1], held_vel[turn, 2, j])
            upper = (flux[j + 1] - flux[j]) if j + 1 < DEPTH - 1 else -flux[j]
            lower = (flux[j] - flux[j - 1]) if j else flux[j]
            inner = inner_rhs(jnp.where(top, coefs[j + 1], coefs[j]), vy, vz)
            out[(RHS + j) * ny : (RHS + j + 1) * ny, :] = jnp.where(top, upper, lower) + inner
            for t in range(ny // ROWS):
                lane = DEPTH * t + j
                columns = jnp.where(lanes == lane, roll_lanes(vz[t * ROWS : (t + 1) * ROWS], lane + 1), columns)
            lines = jnp.where(rows == j, roll_rows(vy[ny - ROWS :], j + 1), lines)
        out[VX * ny : (VX + 1) * ny, :] = held_vel[turn, 0, DEPTH - 1]
        out[VY * ny : VY * ny + ROWS, :] = lines
        out[VY * ny + ROWS :, :] = columns
        clear_if_alone(out, ("gx", turn))
    for copy in late:
        copy.wait()
    if n_y > 1:
        pack_odd(nx, tile_phase, tile_vel, tile_press, odd_outs)


def row_tile(coef, rhs, vy, top):
    rows = row_index((ROWS, LANES))
    coef = jnp.where(top, roll_rows(coef, DEPTH), coef)
    rhs = jnp.where(top, roll_rows(rhs, -1), roll_rows(rhs, DEPTH))
    return jnp.where(rows == ROWS - 1, vy, jnp.where(rows < DEPTH, coef, rhs))


def pack_odd(nx, tile_phase, tile_vel, tile_press, outs):
    out, *corners = outs
    top = jnp.logical_not(even("gy"))
    lanes = lane_index((ROWS, LANES))
    ends_at, vx_at = nx + nx // ROWS, nx + nx // ROWS + 1
    ends = jnp.zeros((ROWS, LANES), jnp.float32)
    here, old_flux = coefficient(tile_phase[0]), None
    for x in range(nx):
        vy, vz = tile_vel[1, x], tile_vel[2, x]
        answer = inner_rhs(here, vy, vz)
        if old_flux is not None:
            answer = answer - old_flux
        coef = here
        if x + 1 < nx:
            above = coefficient(tile_phase[x + 1])
            old_flux = 0.5 * (here + above) * tile_vel[0, x]
            answer = answer + old_flux
            here = above
        out[x] = row_tile(coef, answer, vy, top)
        ends = jnp.where(lanes == x, roll_lanes(vz, x + 1), ends)
        tile = tile_press[x]
        at = nx + x // ROWS
        out[at, x % ROWS : x % ROWS + 1, :] = jnp.where(top, tile[ROWS - 1 : ROWS], tile[0:1])
    shift = lambda tile: jnp.where(top, roll_rows(tile, -1), roll_rows(tile, DEPTH))
    ends = jnp.where(top, roll_rows(ends, DEPTH - 1), ends)
    out[ends_at] = ends
    out[vx_at] = shift(tile_vel[0, nx - 1])
    for turn, corner in enumerate(corners):
        first = jnp.where(even("gx") == (turn == 0), nx - DEPTH, 0)
        for j in range(DEPTH):
            corner[j] = out[first + j]
        corner[DEPTH] = pltpu.roll(ends, jnp.where(first == 0, 0, (DEPTH - nx) % LANES), 1)
        corner[DEPTH + 1] = out[vx_at]
        clear_if_alone(corner, ("gx", turn), ("gy", 1))
    clear_if_alone(out, ("gy", 1))


def merge_odd(nx, got, *refs):
    corners, out = refs[:-1][::-1], refs[-1]
    total = nx + 2 * DEPTH
    rows, lanes = row_index((ROWS, LANES)), lane_index((ROWS, LANES))
    ends_at, vx_at = nx + nx // ROWS, nx + nx // ROWS + 1
    low, high = zip(*[sides(even("gx"), corners, lambda ref: ref[j]) for j in range(DEPTH + 2)])
    tiles = [got[x] for x in range(nx)] + list(high[:DEPTH]) + list(low[:DEPTH])
    inner = (rows >= DEPTH) & (rows < ROWS - 1)

    def face(below, above, vx):
        weight = 0.5 * (tiles[below] + tiles[above])
        weight = jnp.where(even("gy"), roll_rows(weight, DEPTH - 1), roll_rows(weight, DEPTH))
        return jnp.where(inner, weight * vx, 0.0)

    low_face, high_face = face(total - 1, 0, low[DEPTH + 1]), face(nx - 1, nx, got[vx_at])
    for plane, tile in enumerate(tiles):
        if plane == 0:
            tile = tile - low_face
        if plane == total - 1:
            tile = tile + low_face
        if plane == nx - 1:
            tile = tile + high_face
        if plane == nx:
            tile = tile - high_face
        out[plane] = tile
    for at in range(nx // ROWS):
        out[total + at] = got[nx + at]
    ends = jnp.where(lanes < nx, got[ends_at], roll_lanes(high[DEPTH], nx))
    out[total + nx // ROWS] = jnp.where(lanes < nx + DEPTH, ends, roll_lanes(low[DEPTH], nx + DEPTH))


def load(phase, press, vel, after, coef, press_out, vel_out, rhs, held, sem):
    del after
    copies = []
    for which, (src, dst) in enumerate(((phase, held), (press, press_out), (vel, vel_out))):
        copies.append(pltpu.make_async_copy(src, dst, sem.at[which]))
        copies[-1].start()
    copies[0].wait()
    copies[1].wait()
    copies[2].wait()
    nx = coef.shape[0]
    here = coefficient(held[0])
    old_flux = None
    for x in range(nx):
        coef[x] = here
        answer = inner_rhs(here, vel_out[1, x], vel_out[2, x])
        if old_flux is not None:
            answer = answer - old_flux
        if x + 1 < nx:
            above = coefficient(held[x + 1])
            old_flux = 0.5 * (here + above) * vel_out[0, x]
            answer = answer + old_flux
            here = above
        rhs[x] = answer


class Block:
    def __init__(self, nx, ny, coef, vel, rhs, got_x, row=0, height=None, faces=True):
        self.nx, self.ny = nx, ny
        self.own_coef, self.vel, self.own_rhs, self.got_x = coef, vel, rhs, got_x
        self.even = even("gx")
        self.row, self.height = row, height or ny
        if not faces:
            return
        self.low_face = 0.5 * (self.coef(nx + 2 * DEPTH - 1) + self.coef(0)) * self.halo(VX)[0]
        self.high_face = 0.5 * (self.coef(nx - 1) + self.coef(nx)) * self.take(vel, 0, nx - 1)

    def take(self, ref, *index):
        return ref[(*index, pl.ds(self.row, self.height), slice(None))]

    def halo(self, part):
        return sides(self.even, self.got_x, lambda ref: ref[pl.ds(part * self.ny + self.row, self.height), :])

    def coef(self, plane):
        if plane < self.nx:
            return self.take(self.own_coef, plane)
        above = plane < self.nx + DEPTH
        return self.halo((plane - self.nx) % DEPTH)[1 if above else 0]

    def rhs(self, plane):
        nx = self.nx
        if plane < nx:
            answer = self.take(self.own_rhs, plane)
        else:
            above = plane < nx + DEPTH
            layer = plane - nx if above else plane - nx - DEPTH - 1
            if layer < 0 or layer >= DEPTH - 1:
                return jnp.zeros((self.height, LANES), jnp.float32)
            answer = self.halo(RHS + layer)[1 if above else 0]
        if plane == 0:
            answer = answer - self.low_face
        if plane == nx + 2 * DEPTH - 1:
            answer = answer + self.low_face
        if plane == nx - 1:
            answer = answer + self.high_face
        if plane == nx:
            answer = answer - self.high_face
        return answer

    def layer(self, plane):
        if plane < self.nx + DEPTH:
            place = (1, plane - self.nx)
        else:
            place = (0, plane - self.nx - DEPTH - 1)
        return place if 0 <= place[1] < DEPTH - 1 else None

    def columns(self):
        at = VY * self.ny + ROWS
        return sides(self.even, self.got_x, lambda ref: ref[at : at + ROWS, :])

    def vz_end(self, plane, lane):
        if plane < self.nx:
            return roll_lanes(self.vel[2, plane], lane + 1)
        place = self.layer(plane)
        if place is None:
            return jnp.zeros((self.ny, LANES), jnp.float32)
        source = self.columns()[place[0]]
        return jnp.concatenate(
            [roll_lanes(source, lane - DEPTH * t - place[1]) for t in range(self.ny // ROWS)], 0
        )

    def vy_end(self, plane):
        if plane < self.nx:
            return self.vel[1, plane, self.ny - 1 :, :]
        place = self.layer(plane)
        if place is None:
            return jnp.zeros((1, LANES), jnp.float32)
        at = VY * self.ny + place[1]
        return sides(self.even, self.got_x, lambda ref: ref[at : at + 1, :])[place[0]]


def pack_y(nx, ny, n_x, coef, press, vel, rhs, *refs):
    got_x, out = refs[:n_x], refs[-1]
    total = nx + 2 * DEPTH
    lanes = lane_index((ROWS, LANES))
    top = even("gy")
    row = pl.multiple_of(jnp.where(top, ny - ROWS, 0), ROWS)
    block = Block(nx, ny, coef, vel, rhs, got_x, row, ROWS)
    columns = jnp.zeros((ROWS, LANES), jnp.float32)
    ends = block.columns()
    for plane in range(total):
        out[plane] = row_tile(block.coef(plane), block.rhs(plane), block.vy_end(plane), top)
        if plane < nx:
            source = roll_lanes(vel[2, plane, pl.ds(row, ROWS), :], plane + 1)
        elif block.layer(plane) is None:
            continue
        else:
            side, layer = block.layer(plane)
            high = (plane - layer - DEPTH * (ny // ROWS - 1)) % LANES
            source = pltpu.roll(ends[side], jnp.where(top, high, (plane - layer) % LANES), 1)
        columns = jnp.where(lanes == plane, source, columns)
    out[total + nx // ROWS] = jnp.where(top, roll_rows(columns, DEPTH - 1), columns)
    for plane in range(nx):
        tile = press[plane, pl.ds(row, ROWS), :]
        edge = jnp.where(top, tile[ROWS - 1 : ROWS], tile[0:1])
        out[total + plane // ROWS, plane % ROWS : plane % ROWS + 1, :] = edge
    clear_if_alone(out, ("gy", 0))


def tall_end(block, tile_end, plane, lane):
    return jnp.concatenate([block.vz_end(plane, lane), roll_lanes(tile_end, lane - plane)], 0)


def tile_of_ends(nx, even_y, got_y):
    rows = row_index((ROWS, LANES))
    low, high = sides(even_y, got_y, lambda ref: ref[nx + 2 * DEPTH + nx // ROWS])
    return jnp.where(rows < DEPTH, high, roll_rows(low, DEPTH + 1))


def press_lane(x):
    return GROUP * (x % ROWS) + ROWS + 2 * (x // ROWS)


def pack_plane(lanes, at, top, coef, rhs, end):
    coef = pltpu.roll(coef, jnp.where(top, (at + DEPTH) % LANES, at), 1)
    rhs = pltpu.roll(rhs, jnp.where(top, (at + ROWS - 1) % LANES, at + DEPTH), 1)
    value = jnp.where(lanes == at + ROWS - 1, end, 0.0)
    value = jnp.where((lanes >= at + DEPTH) & (lanes < at + ROWS - 1), rhs, value)
    return jnp.where((lanes >= at) & (lanes < at + DEPTH), coef, value)


def half_tile(tile, below):
    rows = row_index((ROWS, LANES))
    coef = jnp.where(below, jnp.where(rows >= DEPTH, roll_rows(tile, DEPTH), 0.0), jnp.where(rows < DEPTH, tile, 0.0))
    rhs = jnp.where(
        below,
        jnp.where(rows > DEPTH, roll_rows(tile, 1), 0.0),
        jnp.where(rows < DEPTH - 1, roll_rows(tile, -DEPTH), 0.0),
    )
    return coef, rhs


def half_ends(tile, below):
    rows = row_index((ROWS, LANES))
    return jnp.where(
        below, jnp.where(rows > DEPTH, roll_rows(tile, DEPTH + 1), 0.0), jnp.where(rows < DEPTH - 1, tile, 0.0)
    )


def face_y(own_low, own_high, coef_tile, tile, vy_end, below):
    rows = row_index((ROWS, LANES))
    down = 0.5 * (coef_tile[ROWS - 1 :] + own_low) * tile[ROWS - 1 :]
    up = 0.5 * (own_high + coef_tile[:1]) * vy_end
    outside = jnp.where(below, jnp.where(rows == ROWS - 1, down, 0.0), jnp.where(rows == 0, -up, 0.0))
    inside = jnp.where(below, jnp.where(rows == 0, -down, 0.0), jnp.where(rows == ROWS - 1, up, 0.0))
    return outside, inside


def stage_z(nx, ny, n_x, n_z, coef, press, vel, rhs, *refs):
    got_x, (*got_odd, full_coef, full_rhs), sends = refs[:n_x], refs[n_x : len(refs) - n_z], refs[len(refs) - n_z :]
    total, height = nx + 2 * DEPTH, ny + 2 * DEPTH
    groups = total // ROWS
    below = even("gy")
    lanes = lane_index((height, LANES))
    block = Block(nx, ny, coef, vel, rhs, got_x)
    nothing = jnp.zeros((ROWS, LANES), jnp.float32)
    tile_end = half_ends(got_odd[0][total + nx // ROWS], below) if got_odd else nothing
    made = [[jnp.zeros((height, LANES), jnp.float32) for _ in range(groups // 2 + 1)] for _ in sends]
    row = pl.ds(pl.multiple_of(jnp.where(below, 0, ny - ROWS), ROWS), ROWS)
    for plane in range(total):
        c_own, r_own = block.coef(plane), block.rhs(plane)
        c_tile = r_tile = nothing
        full_rhs[plane, :ny, :] = r_own
        if got_odd:
            tile = got_odd[0][plane]
            c_tile, r_tile = half_tile(tile, below)
            outside, inside = face_y(c_own[:1], c_own[ny - 1 :], c_tile, tile, block.vy_end(plane), below)
            r_tile = r_tile + outside
            full_rhs[plane, row, :] = full_rhs[plane, row, :] + inside
        c_all = jnp.concatenate([c_own, c_tile], 0)
        full_coef[plane] = c_all
        full_rhs[plane, ny:, :] = r_tile
        r_all = full_rhs[plane]
        group, seat = plane % groups, plane // groups
        at = GROUP * seat + ROWS * (group % 2)
        end = tall_end(block, tile_end, plane, at + ROWS - 1)
        for turn in range(n_z):
            value = pack_plane(lanes, at, even("gz") == (turn == 0), c_all, r_all, end)
            made[turn][group // 2] = made[turn][group // 2] + value
    for turn, send in enumerate(sends):
        top = even("gz") == (turn == 0)
        value = made[turn][groups // 2][:ny]
        for plane in range(nx):
            at = press_lane(plane)
            moved = pltpu.roll(press[plane], jnp.where(top, (at + 1) % LANES, at), 1)
            value = jnp.where(lanes[:ny] == at, moved, value)
        made[turn][groups // 2] = jnp.concatenate([value, made[turn][groups // 2][ny:]], 0)
        for which, value in enumerate(made[turn]):
            send[which] = value


def pack_z(nx, ny, n_x, n_z, vel, *refs):
    got_x, got, (full_coef, full_rhs, *sends) = refs[:n_x], refs[n_x], refs[-2 - n_z :]
    total = nx + 2 * DEPTH
    groups = total // ROWS
    below = jnp.logical_not(even("gy"))
    lanes = lane_index((ROWS, LANES))
    block = Block(nx, ny, full_coef, vel, full_rhs, got_x, faces=False)
    tile_end = half_ends(got[total + nx // ROWS], below)
    row = pl.ds(pl.multiple_of(jnp.where(below, 0, ny - ROWS), ROWS), ROWS)
    added = [[[jnp.zeros((ROWS, LANES), jnp.float32) for _ in range(2)] for _ in range(groups // 2 + 1)] for _ in sends]
    for plane in range(total):
        tile = got[plane]
        c_tile, r_tile = half_tile(tile, below)
        low, high = full_coef[plane, :1, :], full_coef[plane, ny - 1 : ny, :]
        outside, inside = face_y(low, high, c_tile, tile, block.vy_end(plane), below)
        r_tile = r_tile + outside
        full_coef[plane, ny:, :] = full_coef[plane, ny:, :] + c_tile
        full_rhs[plane, ny:, :] = full_rhs[plane, ny:, :] + r_tile
        full_rhs[plane, row, :] = full_rhs[plane, row, :] + inside
        group, seat = plane % groups, plane // groups
        at = GROUP * seat + ROWS * (group % 2)
        end = roll_lanes(tile_end, at + ROWS - 1 - plane)
        for turn in range(n_z):
            top = even("gz") == (turn == 0)
            inside_move = pltpu.roll(inside, jnp.where(top, (at + ROWS - 1) % LANES, at + DEPTH), 1)
            inside_move = jnp.where((lanes >= at + DEPTH) & (lanes < at + ROWS - 1), inside_move, 0.0)
            slot = added[turn][group // 2]
            slot[0] = slot[0] + pack_plane(lanes, at, top, c_tile, r_tile, end)
            slot[1] = slot[1] + inside_move
    for turn, send in enumerate(sends):
        for which, (tile, inside) in enumerate(added[turn]):
            send[which, ny:, :] = send[which, ny:, :] + tile
            send[which, row, :] = send[which, row, :] + inside
        clear_if_alone(send, ("gz", turn))


def tree_sum(parts):
    while len(parts) > 1:
        parts = [parts[i] + parts[i + 1] if i + 1 < len(parts) else parts[i] for i in range(0, len(parts), 2)]
    return parts[0]


class Totals:
    def __init__(self):
        self.stack = []

    def add(self, tile):
        level = 0
        while self.stack and self.stack[-1][0] == level:
            tile = self.stack.pop()[1] + tile
            level += 1
        self.stack.append((level, tile))

    def value(self):
        tiles = [tile for _, tile in self.stack]
        total = tiles.pop()
        while tiles:
            total = tiles.pop() + total
        return total


def prepare(nx, ny, n_x, n_y, coef, vel, rhs, full_coef, full_rhs, *refs):
    got_x, got_y = refs[:n_x], refs[n_x : n_x + n_y]
    basis, ends, shares, wx, wy, wz, inverse = refs[n_x + n_y :]
    total, height = nx + 2 * DEPTH, ny + 2 * DEPTH
    groups = total // ROWS
    lanes = lane_index((height, LANES))
    block = Block(nx, ny, coef, vel, rhs, got_x)
    tile_end = tile_of_ends(nx, even("gy"), got_y)
    for group in range(groups):
        made = [jnp.zeros((height, LANES), jnp.float32) for _ in range(5)]
        for seat in range(ROWS):
            plane = seat * groups + group
            at = GROUP * seat
            for which, source in enumerate((full_coef[plane], full_rhs[plane])):
                here = (lanes >= at + DEPTH) & (lanes < at + GROUP)
                made[2 * which] = jnp.where(here, roll_lanes(source, at + DEPTH), made[2 * which])
                here = (lanes >= at) & (lanes < at + GROUP - DEPTH)
                made[2 * which + 1] = jnp.where(here, roll_lanes(source, at + GROUP - DEPTH), made[2 * which + 1])
            lane = at + GROUP - DEPTH - 1
            made[4] = jnp.where(lanes == lane, tall_end(block, tile_end, plane, lane), made[4])
        for which in range(5):
            ends[which, group] = made[which]
    totals = [Totals() for _ in range(6)]
    trusted = (lanes[:ROWS] >= DEPTH) & (lanes[:ROWS] < LANES - DEPTH)

    def count(which, left, right):
        product = left[:ny] * right[:ny]
        tile = tree_sum([product[i : i + ROWS] for i in range(0, ny, ROWS)])
        totals[which].add(jnp.where(trusted, tile, 0.0))

    old_weight = None
    here = full_coef[nx + DEPTH]
    for x in range(-DEPTH, nx + DEPTH - 1):
        e = x % total
        above = full_coef[(e + 1) % total]
        weight = 0.5 * (here + above)
        wx[e] = weight
        if x > -DEPTH:
            up, down = 0.5 * (here + roll_rows(here, -1)), 0.5 * (here + roll_rows(here, 1))
            right = jnp.where(lanes == LANES - 1, 0.0, 0.5 * (here + roll_lanes(here, -1)))
            left = jnp.where(lanes == 0, 0.0, 0.5 * (here + roll_lanes(here, 1)))
            wy[0, e], wy[1, e], wz[0, e], wz[1, e] = up, down, right, left
            diag = (weight + old_weight) + (up + down) + (right + left)
            inside = here > 0
            scale = jnp.where(inside, 1.0 / jnp.where(inside, diag, 1.0), 0.0)
            inverse[e] = scale
            source = full_rhs[e]
            field = scale * source
            basis[0, e] = field
            if 0 <= x < nx:
                count(0, field, source)
        old_weight, here = weight, above
    for n in range(3):
        reach = 2 - n
        old_flux = None
        here = basis[n, (-reach - 1) % total]
        for x in range(-reach - 1, nx + reach):
            e = x % total
            above = basis[n, (e + 1) % total]
            flux = wx[e] * (above - here)
            if x >= -reach:
                image = old_flux - flux
                image = image + (
                    wy[0, e] * (here - roll_rows(here, -1)) + wy[1, e] * (here - roll_rows(here, 1))
                )
                image = image + (
                    wz[0, e] * (here - roll_lanes(here, -1)) + wz[1, e] * (here - roll_lanes(here, 1))
                )
                own = 0 <= x < nx
                if own:
                    count(2 * n + 1, here, image)
                if n < 2:
                    following = inverse[e] * image
                    basis[n + 1, e] = following
                    if own:
                        count(2 * n + 2, following, image)
            old_flux, here = flux, above
    for which, total_ in enumerate(totals):
        shares[which] = total_.value()


def beside_z(side):
    place = lax.axis_index("gz")
    return place > 0 if side == 0 else place < lax.axis_size("gz") - 1


def solve_end(nx, ny, side, received, ends, basis_z, vz_z, shares, weight_z, inverse_z):
    total, height = nx + 2 * DEPTH, ny + 2 * DEPTH
    groups = total // ROWS
    lanes = lane_index((height, LANES))
    seat_lane, seat = lanes % GROUP, lanes // GROUP
    outer = seat_lane < DEPTH if side == 0 else seat_lane >= GROUP - DEPTH
    coef, rhs, vz = [], [], []
    for g in range(groups):
        got, skip = received(g // 2), ROWS * (g % 2)
        start = 0 if side == 0 else GROUP - DEPTH
        less = 1 if side == 0 else 0
        coef.append(jnp.where(outer, roll_lanes(got, start - skip), ends[side, g]))
        rhs.append(jnp.where(outer, roll_lanes(got, start + less - DEPTH - skip), ends[2 + side, g]))
        if side == 0:
            vz.append(roll_lanes(got, -DEPTH - skip))
            vz_z[g] = vz[-1]
        else:
            vz.append(ends[4, g])

    def along(planes, g, step):
        if 0 <= g + step < groups:
            return planes[g + step]
        return roll_lanes(planes[(g + step) % groups], -GROUP * step)

    totals = [Totals() for _ in range(6)]

    def count(which, g, left, right):
        first = DEPTH if side == 0 else GROUP - 2 * DEPTH
        spot = seat_lane[:ROWS]
        mine = (spot >= first) & (spot < first + DEPTH) & (seat[:ROWS] * groups + g < nx)
        product = left[:ny] * right[:ny]
        tile = tree_sum([product[i : i + ROWS] for i in range(0, ny, ROWS)])
        totals[which].add(jnp.where(mine, tile, 0.0))

    field = []
    for g in range(groups):
        here, q = coef[g], side * groups + g
        neighbours = (along(coef, g, 1), along(coef, g, -1), roll_rows(here, -1), roll_rows(here, 1))
        neighbours += (roll_lanes(here, -1), roll_lanes(here, 1))
        weights = [0.5 * (here + other) for other in neighbours]
        for which, weight in enumerate(weights):
            weight_z[which, g] = weight
        diag = (weights[0] + weights[1]) + (weights[2] + weights[3]) + (weights[4] + weights[5])
        face = DEPTH - 1 if side == 0 else GROUP - DEPTH - 1
        source = rhs[g] + jnp.where(seat_lane == face, weights[4] * vz[g], 0.0)
        source = source - jnp.where(seat_lane == face + 1, weights[5] * roll_lanes(vz[g], 1), 0.0)
        inside = here > 0
        scale = jnp.where(inside, 1.0 / jnp.where(inside, diag, 1.0), 0.0)
        inverse_z[g] = scale
        field.append(scale * source)
        basis_z[0, q] = field[g]
        count(0, g, field[g], source)
    for n in range(3):
        following = []
        for g in range(groups):
            here, q = field[g], side * groups + g
            image = weight_z[0, g] * (here - along(field, g, 1)) + weight_z[1, g] * (here - along(field, g, -1))
            image = image + (
                weight_z[2, g] * (here - roll_rows(here, -1)) + weight_z[3, g] * (here - roll_rows(here, 1))
            )
            image = image + (
                weight_z[4, g] * (here - roll_lanes(here, -1)) + weight_z[5, g] * (here - roll_lanes(here, 1))
            )
            count(2 * n + 1, g, here, image)
            if n < 2:
                following.append(inverse_z[g] * image)
                basis_z[n + 1, q] = following[g]
                count(2 * n + 2, g, following[g], image)
        field = following
    for which, total_ in enumerate(totals):
        shares[which] = shares[which] + total_.value()


def outer_ends(nx, ny, ends, shares_in, basis_z, vz_z, shares, *scratch):
    shares[...] = shares_in[...]
    nothing = jnp.zeros((ny + 2 * DEPTH, LANES), jnp.float32)
    for side in range(2):

        @pl.when(jnp.logical_not(beside_z(side)))
        def _():
            solve_end(nx, ny, side, lambda i: nothing, ends, basis_z, vz_z, shares, *scratch)


def join(nx, ny, n_z, after, ends, *refs):
    del after
    got_z, (basis_z, vz_z, shares, sums, *scratch) = refs[:n_z], refs[n_z + 3 :]
    for side in range(2):

        @pl.when(beside_z(side))
        def _():
            received = lambda i: sides(even("gz"), got_z, lambda ref: ref[i])[side]
            solve_end(nx, ny, side, received, ends, basis_z, vz_z, shares, *scratch)

    lane = lane_index((1, LANES))
    row = jnp.zeros((1, LANES), jnp.float32)
    for which in range(6):
        value = jnp.sum(jnp.sum(shares[which], 0, keepdims=True), 1, keepdims=True)
        row = jnp.where(lane == which, value, row)
    sums[...] = row


def slopes(nx, ny, n_x, n_y, press, vel, *refs):
    got_x, got_y, (slope_x, slope_y, slope_z, base) = refs[:n_x], refs[n_x : n_x + n_y], refs[n_x + n_y :]
    total = nx + 2 * DEPTH
    rows, shape = row_index((ROWS, LANES)), (ROWS, LANES)
    lanes = lane_index((ny, LANES))
    at_low, at_high = lanes == 0, lanes == LANES - 1
    p_low, p_high = sides(even("gx"), got_x, lambda ref: ref[PRESS * ny : (PRESS + 1) * ny, :])
    u_low, _ = sides(even("gx"), got_x, lambda ref: ref[VX * ny : (VX + 1) * ny, :])
    old = p_low - press[0]
    slope_x[0] = old
    old = old * u_low
    for x in range(nx):
        p = press[x]
        slope = p - (press[x + 1] if x + 1 < nx else p_high)
        slope_x[x + 1] = slope
        new = slope * vel[0, x]
        answer, old = old + new, new
        low, high = sides(even("gy"), got_y, lambda ref: ref[total + x // ROWS, x % ROWS : x % ROWS + 1, :])
        p_tile = jnp.where(rows == 0, jnp.broadcast_to(high, shape), jnp.broadcast_to(low, shape))
        p_tall = jnp.concatenate([p, p_tile], 0)
        u_row, _ = sides(even("gy"), got_y, lambda ref: ref[x, ROWS - 1 :, :])
        u_tall = jnp.concatenate([vel[1, x], jnp.broadcast_to(u_row, shape)], 0)
        up, down = p - roll_rows(p_tall, -1)[:ny], roll_rows(p_tall, 1)[:ny] - p
        slope_y[0, x], slope_y[1, x] = up, down
        answer = answer + (up * vel[1, x] + down * roll_rows(u_tall, 1)[:ny])
        up = p - jnp.where(at_high, 0.0, roll_lanes(p, -1))
        down = jnp.where(at_low, 0.0, roll_lanes(p, 1)) - p
        slope_z[0, x], slope_z[1, x] = up, down
        base[x] = answer + (up * vel[2, x] + down * jnp.where(at_low, 0.0, roll_lanes(vel[2, x], 1)))


def finish(nx, ny, n_z, gathered, vel, basis, basis_z, vz_z, slope_x, slope_y, slope_z, base, *refs):
    got_z, (ustar_out, coef_out, ustar, coef_cot, sem) = refs[:n_z], refs[n_z:]
    total, height = nx + 2 * DEPTH, ny + 2 * DEPTH
    groups = total // ROWS
    parts = gathered[...]
    while parts.shape[0] > ROWS:
        half = parts.shape[0] // 2
        parts = parts[:half] + parts[half:]
    sums = jnp.sum(parts, 0, keepdims=True)
    lane = lane_index((1, LANES))
    m0, m1, m2, m3, m4, m5 = [
        jnp.sum(jnp.where(lane == which, sums, 0.0), 1, keepdims=True) for which in range(6)
    ]
    l1, l2 = m2 / m1, m3 / m1
    d1, cross, d2 = m3 - l1 * m2, m4 - l1 * m3, m5 - l2 * m3
    l21 = cross / d1
    d2 = d2 - l21 * cross
    y1 = -l1 * m0 + m1
    y2 = m2 - l2 * m0 - l21 * y1
    c2 = y2 / d2
    c1 = y1 / d1 - l21 * c2
    c0 = (m0 / m1 - l1 * c1 - l2 * c2)[0, 0]
    c1, c2 = c1[0, 0], c2[0, 0]

    lanes = lane_index((height, LANES))
    seat_lane = lanes % GROUP
    spill = []
    for g in range(groups):
        low, high = [
            c0 * basis_z[0, q] + c1 * basis_z[1, q] + c2 * basis_z[2, q] for q in (g, groups + g)
        ]
        cells = jnp.where(seat_lane < DEPTH - 1, roll_lanes(high, DEPTH - GROUP + DEPTH - 1), roll_lanes(low, -1))
        cells = jnp.where(seat_lane == 2 * DEPTH - 2, roll_lanes(high, 2 * DEPTH - 2 - (GROUP - DEPTH)), cells)
        spill.append(jnp.where(seat_lane == 2 * DEPTH - 1, roll_lanes(low, DEPTH), cells))
    spoiled = (lanes < DEPTH - 1) | (lanes > LANES - DEPTH)
    lanes = lane_index((ny, LANES))
    at_low, at_high = lanes == 0, lanes == LANES - 1
    low_z, high_z = sides(even("gz"), got_z, lambda ref: ref[groups // 2, :ny, :])
    press_z = jnp.where(lanes % 2 == 0, high_z, roll_lanes(low_z, 1))

    def solved(x):
        e = x % total
        cells = c0 * basis[0, e] + c1 * basis[1, e] + c2 * basis[2, e]
        return jnp.where(spoiled, roll_lanes(spill[e % groups], 1 - DEPTH - GROUP * (e // groups)), cells)

    copies = []
    below, here = solved(-1), solved(0)
    down = here[:ny] - below[:ny]
    for x in range(nx):
        above = solved(x + 1)
        group, seat = x % groups, x // groups
        own = here[:ny]
        up = above[:ny] - own
        ustar[0, x] = vel[0, x] + up
        answer = base[x] + (slope_x[x + 1] * up + slope_x[x] * down)
        next_down = up
        up, down = roll_rows(here, -1)[:ny] - own, own - roll_rows(here, 1)[:ny]
        ustar[1, x] = vel[1, x] + up
        answer = answer + (slope_y[0, x] * up + slope_y[1, x] * down)
        lam_end = roll_lanes(spill[group][:ny], 1 - 2 * DEPTH - GROUP * seat)
        u_end = roll_lanes(vz_z[group, :ny, :], 1 - DEPTH - GROUP * seat)
        p_end = roll_lanes(press_z, LANES - 1 - press_lane(x))
        up = jnp.where(at_high, lam_end, roll_lanes(own, -1)) - own
        down = own - jnp.where(at_low, lam_end, roll_lanes(own, 1))
        out = vel[2, x] + up
        ustar[2, x] = out
        answer = answer + (slope_z[0, x] * up + slope_z[1, x] * down)
        beyond = jnp.where(at_low, p_end * (u_end + down) + slope_z[1, x] * u_end, 0.0)
        answer = answer + jnp.where(at_high, -p_end * out, beyond)
        down = next_down
        coef_cot[x] = 0.5 * answer
        here = above
        if (x + 1) % STRIDE == 0:
            part = pl.ds(x + 1 - STRIDE, STRIDE)
            for which, (src, dst) in enumerate(
                ((ustar.at[:, part], ustar_out.at[:, part]), (coef_cot.at[part], coef_out.at[part]))
            ):
                copies.append(pltpu.make_async_copy(src, dst, sem.at[which, x // STRIDE]))
                copies[-1].start()
    for copy in copies:
        copy.wait()


def on_device(phase, press, vel):
    nx, ny, nz = phase.shape
    total, height = nx + 2 * DEPTH, ny + 2 * DEPTH
    groups = total // ROWS
    devices = lax.axis_size(AXES)
    n_x, n_y, n_z = (turns(axis) for axis in AXES)
    f32 = lambda *shape: jax.ShapeDtypeStruct(shape, jnp.float32)
    scratch = lambda *shape: pltpu.VMEM(shape, jnp.float32)
    inputs = [pltpu.with_memory_space_constraint(array, pltpu.HBM) for array in (phase, press, vel)]

    def call(kernel, args, in_specs, shapes, name, scratch_shapes=(), out_spec=VMEM, aliases={}):
        return pl.pallas_call(
            kernel,
            out_shape=shapes,
            in_specs=in_specs,
            out_specs=[out_spec] * len(shapes),
            scratch_shapes=list(scratch_shapes),
            input_output_aliases=aliases,
            compiler_params=PARAMS,
            cost_estimate=pl.CostEstimate(flops=3_000_000, bytes_accessed=3_000_000, transcendentals=0),
            name=name,
        )(*args)

    odd = n_y > 1
    sent = call(
        functools.partial(pack_first, nx, ny, n_x, n_y),
        inputs,
        [HBM] * 3,
        [f32(VY * ny + 2 * ROWS, nz)] * n_x
        + ([f32(nx + nx // ROWS + 2, ROWS, nz)] + [f32(DEPTH + 2, ROWS, nz)] * n_x if odd else []),
        "pack_first",
        (
            [pltpu.VMEM((nx, ROWS, nz), jnp.int32), scratch(3, nx, ROWS, nz), scratch(nx, ROWS, nz)]
            + [pltpu.SemaphoreType.DMA((3,))]
            if odd
            else []
        )
        + [pltpu.VMEM((n_x, DEPTH, ny, nz), jnp.int32), scratch(n_x, 3, DEPTH, ny, nz)]
        + [pltpu.SemaphoreType.DMA((n_x, 3))],
    )
    to_x = sent[:n_x]
    got_x = [exchange(send, ("gx", turn)) for turn, send in enumerate(to_x)]
    if odd:
        got_odd = exchange(sent[n_x], ("gy", 1))
        corners = [exchange(send, ("gx", turn), ("gy", 1)) for turn, send in enumerate(sent[n_x + 1 :])]
    coef, press, vel, rhs = call(
        load,
        inputs + [to_x[0]],
        [HBM] * 3 + [ANY],
        [f32(*press.shape), f32(*press.shape), f32(*vel.shape), f32(*press.shape)],
        "load",
        [pltpu.VMEM(phase.shape, jnp.int32), pltpu.SemaphoreType.DMA((3,))],
    )
    rows_y = f32(total + nx // ROWS + 1, ROWS, nz)
    got_y, odd_rows = [], []
    if odd:
        odd_rows = call(
            functools.partial(merge_odd, nx),
            [got_odd, *corners[::-1]],
            [VMEM] * (1 + n_x),
            [rows_y],
            "merge_odd",
        )
    if n_y:
        to_y = call(
            functools.partial(pack_y, nx, ny, n_x),
            [coef, press, vel, rhs, *got_x, *odd_rows],
            [VMEM] * (4 + n_x) + [ANY] * len(odd_rows),
            [rows_y],
            "pack_y",
        )
        got_y = [exchange(to_y[0], ("gy", 0)), *odd_rows]
    cube = (total, height, nz)
    packs = [f32(groups // 2 + 1, height, LANES)] * n_z
    staged = call(
        functools.partial(stage_z, nx, ny, n_x, n_z),
        [coef, press, vel, rhs, *got_x, *odd_rows],
        [VMEM] * (4 + n_x + len(odd_rows)),
        [f32(*cube)] * 2 + packs,
        "stage_z",
    )
    full_coef, full_rhs, *to_z = call(
        functools.partial(pack_z, nx, ny, n_x, n_z),
        [vel, *got_x, got_y[0], *staged],
        [VMEM] * (4 + n_x + n_z),
        [f32(*cube)] * 2 + packs,
        "pack_z",
        aliases={2 + n_x + which: which for which in range(2 + n_z)},
    )
    got_z = [exchange(send, ("gz", turn)) for turn, send in enumerate(to_z)]
    basis, ends, shares = call(
        functools.partial(prepare, nx, ny, n_x, n_y),
        [coef, vel, rhs, full_coef, full_rhs, *got_x, *got_y],
        [VMEM] * (5 + n_x + n_y),
        [f32(3, *cube), f32(5, groups, height, LANES), f32(6, ROWS, LANES)],
        "prepare",
        [scratch(*cube), scratch(2, *cube), scratch(2, *cube), scratch(*cube)],
    )
    slope = call(
        functools.partial(slopes, nx, ny, n_x, n_y),
        [press, vel, *got_x, *got_y],
        [VMEM] * (2 + n_x + n_y),
        [f32(nx + 1, ny, nz), f32(2, nx, ny, nz), f32(2, nx, ny, nz), f32(nx, ny, nz)],
        "slopes",
    )
    shapes_z = [f32(3, 2 * groups, height, LANES), f32(groups, height, LANES), f32(6, ROWS, LANES)]
    scratch_z = [scratch(6, groups, height, LANES), scratch(groups, height, LANES)]
    outer = call(
        functools.partial(outer_ends, nx, ny),
        [ends, shares],
        [VMEM] * 2,
        shapes_z,
        "outer_ends",
        scratch_z,
    )
    basis_z, vz_z, _, sums = call(
        functools.partial(join, nx, ny, n_z),
        [slope[-1], ends, *got_z, *outer],
        [ANY] + [VMEM] * (4 + n_z),
        shapes_z + [f32(1, LANES)],
        "join",
        scratch_z,
        aliases={2 + n_z + which: which for which in range(3)},
    )
    spread = jnp.broadcast_to(sums[None], (devices, 1, LANES))
    gathered = lax.all_to_all(spread, AXES, 0, 0).reshape(devices, LANES)
    return call(
        functools.partial(finish, nx, ny, n_z),
        [gathered, vel, basis, basis_z, vz_z, *slope, *got_z],
        [VMEM] * (9 + n_z),
        [f32(*vel.shape), f32(nx, ny, nz)],
        "finish",
        [scratch(*vel.shape), scratch(nx, ny, nz), pltpu.SemaphoreType.DMA((2, nx // STRIDE))],
        HBM,
    )


def solution(mesh):
    cells, faces = P(*AXES), P(None, *AXES)
    return jax.shard_map(
        on_device, mesh=mesh, in_specs=(cells, cells, faces), out_specs=(faces, cells), check_vma=False
    )
```

```python
import functools
import itertools

import jax
import jax.numpy as jnp
from jax import lax
from jax.experimental import pallas as pl
from jax.experimental.pallas import tpu as pltpu
from jax.sharding import PartitionSpec as P

AXES = ("gx", "gy", "gz")
SPARE = dict(gx="gy", gy="gz", gz="gx")
DEPTH = 4
GROUP = 4 * DEPTH
LANES = 128
STRIDE = 4
ROWS = 8
VMEM = pl.BlockSpec(memory_space=pltpu.VMEM)
HBM = pl.BlockSpec(memory_space=pltpu.HBM)
ANY = pl.BlockSpec(memory_space=pl.ANY)
PARAMS = pltpu.CompilerParams(vmem_limit_bytes=40 * 1024 * 1024)


def swaps(moves):
    sizes = [lax.axis_size(name) for name in AXES]
    number = lambda place: (place[0] * sizes[1] + place[1]) * sizes[2] + place[2]
    spare = AXES.index("gz" if len(moves) > 1 else SPARE[moves[0][0]])
    pairs = []
    for place in itertools.product(*map(range, sizes)):
        partner, met = list(place), True
        for axis, turn in moves:
            along = AXES.index(axis)
            partner[along] += 1 if (place[along] - turn) % 2 == 0 else -1
            met = met and 0 <= partner[along] < sizes[along]
        if not met:
            if sizes[spare] % 2:
                continue
            partner = list(place)
            partner[spare] ^= 1
        pairs.append((number(place), number(partner)))
    return pairs


def exchange(send, *moves):
    return lax.ppermute(send, AXES, swaps(moves))


def clear_if_alone(out, *moves):
    for axis, turn in moves:
        count, place = lax.axis_size(axis), lax.axis_index(axis)
        alone = []
        if turn == 1:
            alone.append(place == 0)
        if count % 2 != turn:
            alone.append(place == count - 1)
        for case in alone:

            @pl.when(case)
            def _():
                out[...] = jnp.zeros(out.shape, out.dtype)


def even(axis):
    return lax.axis_index(axis) % 2 == 0


def turns(axis):
    return min(2, lax.axis_size(axis) - 1)


def coefficient(phase):
    return jnp.where(phase == 0, 8.0, jnp.where(phase == 1, 1.0, 2.0)).astype(jnp.float32)


def sides(is_even, got, load):
    one = load(got[0])
    two = load(got[1]) if len(got) > 1 else jnp.zeros_like(one)
    return jnp.where(is_even, two, one), jnp.where(is_even, one, two)


def lane_index(shape):
    return lax.broadcasted_iota(jnp.int32, shape, len(shape) - 1)


def row_index(shape):
    return lax.broadcasted_iota(jnp.int32, shape, len(shape) - 2)


def roll_rows(plane, shift):
    return pltpu.roll(plane, shift % plane.shape[0], 0)


def roll_lanes(plane, shift):
    return pltpu.roll(plane, shift % plane.shape[1], 1)


def inner_rhs(coef, vy, vz):
    rows, lanes = row_index(coef.shape), lane_index(coef.shape)
    up = jnp.where(rows == coef.shape[0] - 1, 0.0, 0.5 * (coef + roll_rows(coef, -1)))
    down = jnp.where(rows == 0, 0.0, 0.5 * (coef + roll_rows(coef, 1)))
    right = jnp.where(lanes == LANES - 1, 0.0, 0.5 * (coef + roll_lanes(coef, -1)))
    left = jnp.where(lanes == 0, 0.0, 0.5 * (coef + roll_lanes(coef, 1)))
    return (up * vy - down * roll_rows(vy, 1)) + (right * vz - left * roll_lanes(vz, 1))


RHS, VX, PRESS, VY = DEPTH, 2 * DEPTH - 1, 2 * DEPTH, 2 * DEPTH + 1


def pack_first(nx, ny, n_x, n_y, phase, press, vel, *refs):
    outs, odd_outs, (held, held_vel, sem) = refs[:n_x], refs[n_x:-3], refs[-3:]
    if n_y > 1:
        *odd_outs, tile_phase, tile_vel, tile_press, tile_sem = odd_outs
    copies, late = [], []
    for turn, out in enumerate(outs):
        top = even("gx") == (turn == 0)
        deep = jnp.where(top, nx - DEPTH, 0)
        last = jnp.where(top, nx - 1, 0)
        parts = [
            (vel.at[:, pl.ds(deep, DEPTH)], held_vel.at[turn]),
            (phase.at[pl.ds(deep, DEPTH)], held.at[turn]),
            (press.at[last], out.at[pl.ds(PRESS * ny, ny)]),
        ]
        for which, (src, dst) in enumerate(parts):
            copy = pltpu.make_async_copy(src, dst, sem.at[turn, which])
            copy.start()
            copies.append(copy)
    if n_y > 1:
        row = pl.multiple_of(jnp.where(even("gy"), 0, ny - ROWS), ROWS)
        parts = [
            (phase.at[:, pl.ds(row, ROWS)], tile_phase),
            (vel.at[:, :, pl.ds(row, ROWS)], tile_vel),
            (press.at[:, pl.ds(row, ROWS)], tile_press),
        ]
        for which, (src, dst) in enumerate(parts):
            copy = pltpu.make_async_copy(src, dst, tile_sem.at[which])
            copy.start()
            late.append(copy)
    lanes = lane_index((ROWS, LANES))
    rows = row_index((ROWS, LANES))
    for turn, out in enumerate(outs):
        for copy in copies[3 * turn : 3 * turn + 3]:
            copy.wait()
        top = even("gx") == (turn == 0)
        coefs = [coefficient(held[turn, j]) for j in range(DEPTH)]
        flux = [0.5 * (coefs[j] + coefs[j + 1]) * held_vel[turn, 0, j] for j in range(DEPTH - 1)]
        columns = jnp.zeros((ROWS, LANES), jnp.float32)
        lines = jnp.zeros((ROWS, LANES), jnp.float32)
        for j in range(DEPTH):
            out[j * ny : (j + 1) * ny, :] = coefs[j]
        for j in range(DEPTH - 1):
            vy = jnp.where(top, held_vel[turn, 1, j + 1], held_vel[turn, 1, j])
            vz = jnp.where(top, held_vel[turn, 2, j + 1], held_vel[turn, 2, j])
            upper = (flux[j + 1] - flux[j]) if j + 1 < DEPTH - 1 else -flux[j]
            lower = (flux[j] - flux[j - 1]) if j else flux[j]
            inner = inner_rhs(jnp.where(top, coefs[j + 1], coefs[j]), vy, vz)
            out[(RHS + j) * ny : (RHS + j + 1) * ny, :] = jnp.where(top, upper, lower) + inner
            for t in range(ny // ROWS):
                lane = DEPTH * t + j
                columns = jnp.where(lanes == lane, roll_lanes(vz[t * ROWS : (t + 1) * ROWS], lane + 1), columns)
            lines = jnp.where(rows == j, roll_rows(vy[ny - ROWS :], j + 1), lines)
        out[VX * ny : (VX + 1) * ny, :] = held_vel[turn, 0, DEPTH - 1]
        out[VY * ny : VY * ny + ROWS, :] = lines
        out[VY * ny + ROWS :, :] = columns
        clear_if_alone(out, ("gx", turn))
    for copy in late:
        copy.wait()
    if n_y > 1:
        pack_odd(nx, tile_phase, tile_vel, tile_press, odd_outs)


def row_tile(coef, rhs, vy, top):
    rows = row_index((ROWS, LANES))
    coef = jnp.where(top, roll_rows(coef, DEPTH), coef)
    rhs = jnp.where(top, roll_rows(rhs, -1), roll_rows(rhs, DEPTH))
    return jnp.where(rows == ROWS - 1, vy, jnp.where(rows < DEPTH, coef, rhs))


def pack_odd(nx, tile_phase, tile_vel, tile_press, outs):
    out, *corners = outs
    top = jnp.logical_not(even("gy"))
    lanes = lane_index((ROWS, LANES))
    ends_at, vx_at = nx + nx // ROWS, nx + nx // ROWS + 1
    ends = jnp.zeros((ROWS, LANES), jnp.float32)
    here, old_flux = coefficient(tile_phase[0]), None
    for x in range(nx):
        vy, vz = tile_vel[1, x], tile_vel[2, x]
        answer = inner_rhs(here, vy, vz)
        if old_flux is not None:
            answer = answer - old_flux
        coef = here
        if x + 1 < nx:
            above = coefficient(tile_phase[x + 1])
            old_flux = 0.5 * (here + above) * tile_vel[0, x]
            answer = answer + old_flux
            here = above
        out[x] = row_tile(coef, answer, vy, top)
        ends = jnp.where(lanes == x, roll_lanes(vz, x + 1), ends)
        tile = tile_press[x]
        at = nx + x // ROWS
        out[at, x % ROWS : x % ROWS + 1, :] = jnp.where(top, tile[ROWS - 1 : ROWS], tile[0:1])
    shift = lambda tile: jnp.where(top, roll_rows(tile, -1), roll_rows(tile, DEPTH))
    ends = jnp.where(top, roll_rows(ends, DEPTH - 1), ends)
    out[ends_at] = ends
    out[vx_at] = shift(tile_vel[0, nx - 1])
    for turn, corner in enumerate(corners):
        first = jnp.where(even("gx") == (turn == 0), nx - DEPTH, 0)
        for j in range(DEPTH):
            corner[j] = out[first + j]
        corner[DEPTH] = pltpu.roll(ends, jnp.where(first == 0, 0, (DEPTH - nx) % LANES), 1)
        corner[DEPTH + 1] = out[vx_at]
        clear_if_alone(corner, ("gx", turn), ("gy", 1))
    clear_if_alone(out, ("gy", 1))


def merge_odd(nx, got, *refs):
    corners, out = refs[:-1][::-1], refs[-1]
    total = nx + 2 * DEPTH
    rows, lanes = row_index((ROWS, LANES)), lane_index((ROWS, LANES))
    ends_at, vx_at = nx + nx // ROWS, nx + nx // ROWS + 1
    low, high = zip(*[sides(even("gx"), corners, lambda ref: ref[j]) for j in range(DEPTH + 2)])
    tiles = [got[x] for x in range(nx)] + list(high[:DEPTH]) + list(low[:DEPTH])
    inner = (rows >= DEPTH) & (rows < ROWS - 1)

    def face(below, above, vx):
        weight = 0.5 * (tiles[below] + tiles[above])
        weight = jnp.where(even("gy"), roll_rows(weight, DEPTH - 1), roll_rows(weight, DEPTH))
        return jnp.where(inner, weight * vx, 0.0)

    low_face, high_face = face(total - 1, 0, low[DEPTH + 1]), face(nx - 1, nx, got[vx_at])
    for plane, tile in enumerate(tiles):
        if plane == 0:
            tile = tile - low_face
        if plane == total - 1:
            tile = tile + low_face
        if plane == nx - 1:
            tile = tile + high_face
        if plane == nx:
            tile = tile - high_face
        out[plane] = tile
    for at in range(nx // ROWS):
        out[total + at] = got[nx + at]
    ends = jnp.where(lanes < nx, got[ends_at], roll_lanes(high[DEPTH], nx))
    out[total + nx // ROWS] = jnp.where(lanes < nx + DEPTH, ends, roll_lanes(low[DEPTH], nx + DEPTH))


def load(phase, press, vel, after, coef, press_out, vel_out, rhs, held, sem):
    del after
    copies = []
    for which, (src, dst) in enumerate(((phase, held), (press, press_out), (vel, vel_out))):
        copies.append(pltpu.make_async_copy(src, dst, sem.at[which]))
        copies[-1].start()
    copies[0].wait()
    copies[1].wait()
    copies[2].wait()
    nx = coef.shape[0]
    here = coefficient(held[0])
    old_flux = None
    for x in range(nx):
        coef[x] = here
        answer = inner_rhs(here, vel_out[1, x], vel_out[2, x])
        if old_flux is not None:
            answer = answer - old_flux
        if x + 1 < nx:
            above = coefficient(held[x + 1])
            old_flux = 0.5 * (here + above) * vel_out[0, x]
            answer = answer + old_flux
            here = above
        rhs[x] = answer


class Block:
    def __init__(self, nx, ny, coef, vel, rhs, got_x, row=0, height=None, faces=True):
        self.nx, self.ny = nx, ny
        self.own_coef, self.vel, self.own_rhs, self.got_x = coef, vel, rhs, got_x
        self.even = even("gx")
        self.row, self.height = row, height or ny
        if not faces:
            return
        self.low_face = 0.5 * (self.coef(nx + 2 * DEPTH - 1) + self.coef(0)) * self.halo(VX)[0]
        self.high_face = 0.5 * (self.coef(nx - 1) + self.coef(nx)) * self.take(vel, 0, nx - 1)

    def take(self, ref, *index):
        return ref[(*index, pl.ds(self.row, self.height), slice(None))]

    def halo(self, part):
        return sides(self.even, self.got_x, lambda ref: ref[pl.ds(part * self.ny + self.row, self.height), :])

    def coef(self, plane):
        if plane < self.nx:
            return self.take(self.own_coef, plane)
        above = plane < self.nx + DEPTH
        return self.halo((plane - self.nx) % DEPTH)[1 if above else 0]

    def rhs(self, plane):
        nx = self.nx
        if plane < nx:
            answer = self.take(self.own_rhs, plane)
        else:
            above = plane < nx + DEPTH
            layer = plane - nx if above else plane - nx - DEPTH - 1
            if layer < 0 or layer >= DEPTH - 1:
                return jnp.zeros((self.height, LANES), jnp.float32)
            answer = self.halo(RHS + layer)[1 if above else 0]
        if plane == 0:
            answer = answer - self.low_face
        if plane == nx + 2 * DEPTH - 1:
            answer = answer + self.low_face
        if plane == nx - 1:
            answer = answer + self.high_face
        if plane == nx:
            answer = answer - self.high_face
        return answer

    def layer(self, plane):
        if plane < self.nx + DEPTH:
            place = (1, plane - self.nx)
        else:
            place = (0, plane - self.nx - DEPTH - 1)
        return place if 0 <= place[1] < DEPTH - 1 else None

    def columns(self):
        at = VY * self.ny + ROWS
        return sides(self.even, self.got_x, lambda ref: ref[at : at + ROWS, :])

    def vz_end(self, plane, lane):
        if plane < self.nx:
            return roll_lanes(self.vel[2, plane], lane + 1)
        place = self.layer(plane)
        if place is None:
            return jnp.zeros((self.ny, LANES), jnp.float32)
        source = self.columns()[place[0]]
        return jnp.concatenate(
            [roll_lanes(source, lane - DEPTH * t - place[1]) for t in range(self.ny // ROWS)], 0
        )

    def vy_end(self, plane):
        if plane < self.nx:
            return self.vel[1, plane, self.ny - 1 :, :]
        place = self.layer(plane)
        if place is None:
            return jnp.zeros((1, LANES), jnp.float32)
        at = VY * self.ny + place[1]
        return sides(self.even, self.got_x, lambda ref: ref[at : at + 1, :])[place[0]]


def pack_y(nx, ny, n_x, coef, press, vel, rhs, *refs):
    got_x, out = refs[:n_x], refs[-1]
    total = nx + 2 * DEPTH
    lanes = lane_index((ROWS, LANES))
    top = even("gy")
    row = pl.multiple_of(jnp.where(top, ny - ROWS, 0), ROWS)
    block = Block(nx, ny, coef, vel, rhs, got_x, row, ROWS)
    columns = jnp.zeros((ROWS, LANES), jnp.float32)
    ends = block.columns()
    for plane in range(total):
        out[plane] = row_tile(block.coef(plane), block.rhs(plane), block.vy_end(plane), top)
        if plane < nx:
            source = roll_lanes(vel[2, plane, pl.ds(row, ROWS), :], plane + 1)
        elif block.layer(plane) is None:
            continue
        else:
            side, layer = block.layer(plane)
            high = (plane - layer - DEPTH * (ny // ROWS - 1)) % LANES
            source = pltpu.roll(ends[side], jnp.where(top, high, (plane - layer) % LANES), 1)
        columns = jnp.where(lanes == plane, source, columns)
    out[total + nx // ROWS] = jnp.where(top, roll_rows(columns, DEPTH - 1), columns)
    for plane in range(nx):
        tile = press[plane, pl.ds(row, ROWS), :]
        edge = jnp.where(top, tile[ROWS - 1 : ROWS], tile[0:1])
        out[total + plane // ROWS, plane % ROWS : plane % ROWS + 1, :] = edge
    clear_if_alone(out, ("gy", 0))


def tall_end(block, tile_end, plane, lane):
    return jnp.concatenate([block.vz_end(plane, lane), roll_lanes(tile_end, lane - plane)], 0)


def tile_of_ends(nx, even_y, got_y):
    rows = row_index((ROWS, LANES))
    low, high = sides(even_y, got_y, lambda ref: ref[nx + 2 * DEPTH + nx // ROWS])
    return jnp.where(rows < DEPTH, high, roll_rows(low, DEPTH + 1))


def press_lane(x):
    return GROUP * (x % ROWS) + ROWS + 2 * (x // ROWS)


def pack_plane(lanes, at, top, coef, rhs, end):
    coef = pltpu.roll(coef, jnp.where(top, (at + DEPTH) % LANES, at), 1)
    rhs = pltpu.roll(rhs, jnp.where(top, (at + ROWS - 1) % LANES, at + DEPTH), 1)
    value = jnp.where(lanes == at + ROWS - 1, end, 0.0)
    value = jnp.where((lanes >= at + DEPTH) & (lanes < at + ROWS - 1), rhs, value)
    return jnp.where((lanes >= at) & (lanes < at + DEPTH), coef, value)


def half_tile(tile, below):
    rows = row_index((ROWS, LANES))
    coef = jnp.where(below, jnp.where(rows >= DEPTH, roll_rows(tile, DEPTH), 0.0), jnp.where(rows < DEPTH, tile, 0.0))
    rhs = jnp.where(
        below,
        jnp.where(rows > DEPTH, roll_rows(tile, 1), 0.0),
        jnp.where(rows < DEPTH - 1, roll_rows(tile, -DEPTH), 0.0),
    )
    return coef, rhs


def half_ends(tile, below):
    rows = row_index((ROWS, LANES))
    return jnp.where(
        below, jnp.where(rows > DEPTH, roll_rows(tile, DEPTH + 1), 0.0), jnp.where(rows < DEPTH - 1, tile, 0.0)
    )


def face_y(own_low, own_high, coef_tile, tile, vy_end, below):
    rows = row_index((ROWS, LANES))
    down = 0.5 * (coef_tile[ROWS - 1 :] + own_low) * tile[ROWS - 1 :]
    up = 0.5 * (own_high + coef_tile[:1]) * vy_end
    outside = jnp.where(below, jnp.where(rows == ROWS - 1, down, 0.0), jnp.where(rows == 0, -up, 0.0))
    inside = jnp.where(below, jnp.where(rows == 0, -down, 0.0), jnp.where(rows == ROWS - 1, up, 0.0))
    return outside, inside


def stage_z(nx, ny, n_x, n_z, coef, press, vel, rhs, *refs):
    got_x, (*got_odd, full_coef, full_rhs), sends = refs[:n_x], refs[n_x : len(refs) - n_z], refs[len(refs) - n_z :]
    total, height = nx + 2 * DEPTH, ny + 2 * DEPTH
    groups = total // ROWS
    below = even("gy")
    lanes = lane_index((height, LANES))
    block = Block(nx, ny, coef, vel, rhs, got_x)
    nothing = jnp.zeros((ROWS, LANES), jnp.float32)
    tile_end = half_ends(got_odd[0][total + nx // ROWS], below) if got_odd else nothing
    made = [[jnp.zeros((height, LANES), jnp.float32) for _ in range(groups // 2 + 1)] for _ in sends]
    row = pl.ds(pl.multiple_of(jnp.where(below, 0, ny - ROWS), ROWS), ROWS)
    for plane in range(total):
        c_own, r_own = block.coef(plane), block.rhs(plane)
        c_tile = r_tile = nothing
        full_rhs[plane, :ny, :] = r_own
        if got_odd:
            tile = got_odd[0][plane]
            c_tile, r_tile = half_tile(tile, below)
            outside, inside = face_y(c_own[:1], c_own[ny - 1 :], c_tile, tile, block.vy_end(plane), below)
            r_tile = r_tile + outside
            full_rhs[plane, row, :] = full_rhs[plane, row, :] + inside
        c_all = jnp.concatenate([c_own, c_tile], 0)
        full_coef[plane] = c_all
        full_rhs[plane, ny:, :] = r_tile
        r_all = full_rhs[plane]
        group, seat = plane % groups, plane // groups
        at = GROUP * seat + ROWS * (group % 2)
        end = tall_end(block, tile_end, plane, at + ROWS - 1)
        for turn in range(n_z):
            value = pack_plane(lanes, at, even("gz") == (turn == 0), c_all, r_all, end)
            made[turn][group // 2] = made[turn][group // 2] + value
    for turn, send in enumerate(sends):
        top = even("gz") == (turn == 0)
        value = made[turn][groups // 2][:ny]
        for plane in range(nx):
            at = press_lane(plane)
            moved = pltpu.roll(press[plane], jnp.where(top, (at + 1) % LANES, at), 1)
            value = jnp.where(lanes[:ny] == at, moved, value)
        made[turn][groups // 2] = jnp.concatenate([value, made[turn][groups // 2][ny:]], 0)
        for which, value in enumerate(made[turn]):
            send[which] = value


def pack_z(nx, ny, n_x, n_z, vel, *refs):
    got_x, got, (full_coef, full_rhs, *sends) = refs[:n_x], refs[n_x], refs[-2 - n_z :]
    total = nx + 2 * DEPTH
    groups = total // ROWS
    below = jnp.logical_not(even("gy"))
    lanes = lane_index((ROWS, LANES))
    block = Block(nx, ny, full_coef, vel, full_rhs, got_x, faces=False)
    tile_end = half_ends(got[total + nx // ROWS], below)
    row = pl.ds(pl.multiple_of(jnp.where(below, 0, ny - ROWS), ROWS), ROWS)
    added = [[[jnp.zeros((ROWS, LANES), jnp.float32) for _ in range(2)] for _ in range(groups // 2 + 1)] for _ in sends]
    for plane in range(total):
        tile = got[plane]
        c_tile, r_tile = half_tile(tile, below)
        low, high = full_coef[plane, :1, :], full_coef[plane, ny - 1 : ny, :]
        outside, inside = face_y(low, high, c_tile, tile, block.vy_end(plane), below)
        r_tile = r_tile + outside
        full_coef[plane, ny:, :] = full_coef[plane, ny:, :] + c_tile
        full_rhs[plane, ny:, :] = full_rhs[plane, ny:, :] + r_tile
        full_rhs[plane, row, :] = full_rhs[plane, row, :] + inside
        group, seat = plane % groups, plane // groups
        at = GROUP * seat + ROWS * (group % 2)
        end = roll_lanes(tile_end, at + ROWS - 1 - plane)
        for turn in range(n_z):
            top = even("gz") == (turn == 0)
            inside_move = pltpu.roll(inside, jnp.where(top, (at + ROWS - 1) % LANES, at + DEPTH), 1)
            inside_move = jnp.where((lanes >= at + DEPTH) & (lanes < at + ROWS - 1), inside_move, 0.0)
            slot = added[turn][group // 2]
            slot[0] = slot[0] + pack_plane(lanes, at, top, c_tile, r_tile, end)
            slot[1] = slot[1] + inside_move
    for turn, send in enumerate(sends):
        for which, (tile, inside) in enumerate(added[turn]):
            send[which, ny:, :] = send[which, ny:, :] + tile
            send[which, row, :] = send[which, row, :] + inside
        clear_if_alone(send, ("gz", turn))


def tree_sum(parts):
    while len(parts) > 1:
        parts = [parts[i] + parts[i + 1] if i + 1 < len(parts) else parts[i] for i in range(0, len(parts), 2)]
    return parts[0]


class Totals:
    def __init__(self):
        self.stack = []

    def add(self, tile):
        level = 0
        while self.stack and self.stack[-1][0] == level:
            tile = self.stack.pop()[1] + tile
            level += 1
        self.stack.append((level, tile))

    def value(self):
        tiles = [tile for _, tile in self.stack]
        total = tiles.pop()
        while tiles:
            total = tiles.pop() + total
        return total


def prepare(nx, ny, n_x, n_y, coef, vel, rhs, full_coef, full_rhs, *refs):
    got_x, got_y = refs[:n_x], refs[n_x : n_x + n_y]
    basis, ends, shares, wx, wy, wz, inverse = refs[n_x + n_y :]
    total, height = nx + 2 * DEPTH, ny + 2 * DEPTH
    groups = total // ROWS
    lanes = lane_index((height, LANES))
    block = Block(nx, ny, coef, vel, rhs, got_x)
    tile_end = tile_of_ends(nx, even("gy"), got_y)
    for group in range(groups):
        made = [jnp.zeros((height, LANES), jnp.float32) for _ in range(5)]
        for seat in range(ROWS):
            plane = seat * groups + group
            at = GROUP * seat
            for which, source in enumerate((full_coef[plane], full_rhs[plane])):
                here = (lanes >= at + DEPTH) & (lanes < at + GROUP)
                made[2 * which] = jnp.where(here, roll_lanes(source, at + DEPTH), made[2 * which])
                here = (lanes >= at) & (lanes < at + GROUP - DEPTH)
                made[2 * which + 1] = jnp.where(here, roll_lanes(source, at + GROUP - DEPTH), made[2 * which + 1])
            lane = at + GROUP - DEPTH - 1
            made[4] = jnp.where(lanes == lane, tall_end(block, tile_end, plane, lane), made[4])
        for which in range(5):
            ends[which, group] = made[which]
    totals = [Totals() for _ in range(6)]
    trusted = (lanes[:ROWS] >= DEPTH) & (lanes[:ROWS] < LANES - DEPTH)

    def count(which, left, right):
        product = left[:ny] * right[:ny]
        tile = tree_sum([product[i : i + ROWS] for i in range(0, ny, ROWS)])
        totals[which].add(jnp.where(trusted, tile, 0.0))

    old_weight = None
    here = full_coef[nx + DEPTH]
    for x in range(-DEPTH, nx + DEPTH - 1):
        e = x % total
        above = full_coef[(e + 1) % total]
        weight = 0.5 * (here + above)
        wx[e] = weight
        if x > -DEPTH:
            up, down = 0.5 * (here + roll_rows(here, -1)), 0.5 * (here + roll_rows(here, 1))
            right = jnp.where(lanes == LANES - 1, 0.0, 0.5 * (here + roll_lanes(here, -1)))
            left = jnp.where(lanes == 0, 0.0, 0.5 * (here + roll_lanes(here, 1)))
            wy[0, e], wy[1, e], wz[0, e], wz[1, e] = up, down, right, left
            diag = (weight + old_weight) + (up + down) + (right + left)
            inside = here > 0
            scale = jnp.where(inside, 1.0 / jnp.where(inside, diag, 1.0), 0.0)
            inverse[e] = scale
            source = full_rhs[e]
            field = scale * source
            basis[0, e] = field
            if 0 <= x < nx:
                count(0, field, source)
        old_weight, here = weight, above
    for n in range(3):
        reach = 2 - n
        old_flux = None
        here = basis[n, (-reach - 1) % total]
        for x in range(-reach - 1, nx + reach):
            e = x % total
            above = basis[n, (e + 1) % total]
            flux = wx[e] * (above - here)
            if x >= -reach:
                image = old_flux - flux
                image = image + (
                    wy[0, e] * (here - roll_rows(here, -1)) + wy[1, e] * (here - roll_rows(here, 1))
                )
                image = image + (
                    wz[0, e] * (here - roll_lanes(here, -1)) + wz[1, e] * (here - roll_lanes(here, 1))
                )
                own = 0 <= x < nx
                if own:
                    count(2 * n + 1, here, image)
                if n < 2:
                    following = inverse[e] * image
                    basis[n + 1, e] = following
                    if own:
                        count(2 * n + 2, following, image)
            old_flux, here = flux, above
    for which, total_ in enumerate(totals):
        shares[which] = total_.value()


def beside_z(side):
    place = lax.axis_index("gz")
    return place > 0 if side == 0 else place < lax.axis_size("gz") - 1


def solve_end(nx, ny, side, received, ends, basis_z, vz_z, shares, weight_z, inverse_z):
    total, height = nx + 2 * DEPTH, ny + 2 * DEPTH
    groups = total // ROWS
    lanes = lane_index((height, LANES))
    seat_lane, seat = lanes % GROUP, lanes // GROUP
    outer = seat_lane < DEPTH if side == 0 else seat_lane >= GROUP - DEPTH
    coef, rhs, vz = [], [], []
    for g in range(groups):
        got, skip = received(g // 2), ROWS * (g % 2)
        start = 0 if side == 0 else GROUP - DEPTH
        less = 1 if side == 0 else 0
        coef.append(jnp.where(outer, roll_lanes(got, start - skip), ends[side, g]))
        rhs.append(jnp.where(outer, roll_lanes(got, start + less - DEPTH - skip), ends[2 + side, g]))
        if side == 0:
            vz.append(roll_lanes(got, -DEPTH - skip))
            vz_z[g] = vz[-1]
        else:
            vz.append(ends[4, g])

    def along(planes, g, step):
        if 0 <= g + step < groups:
            return planes[g + step]
        return roll_lanes(planes[(g + step) % groups], -GROUP * step)

    totals = [Totals() for _ in range(6)]

    def count(which, g, left, right):
        first = DEPTH if side == 0 else GROUP - 2 * DEPTH
        spot = seat_lane[:ROWS]
        mine = (spot >= first) & (spot < first + DEPTH) & (seat[:ROWS] * groups + g < nx)
        product = left[:ny] * right[:ny]
        tile = tree_sum([product[i : i + ROWS] for i in range(0, ny, ROWS)])
        totals[which].add(jnp.where(mine, tile, 0.0))

    field = []
    for g in range(groups):
        here, q = coef[g], side * groups + g
        neighbours = (along(coef, g, 1), along(coef, g, -1), roll_rows(here, -1), roll_rows(here, 1))
        neighbours += (roll_lanes(here, -1), roll_lanes(here, 1))
        weights = [0.5 * (here + other) for other in neighbours]
        for which, weight in enumerate(weights):
            weight_z[which, g] = weight
        diag = (weights[0] + weights[1]) + (weights[2] + weights[3]) + (weights[4] + weights[5])
        face = DEPTH - 1 if side == 0 else GROUP - DEPTH - 1
        source = rhs[g] + jnp.where(seat_lane == face, weights[4] * vz[g], 0.0)
        source = source - jnp.where(seat_lane == face + 1, weights[5] * roll_lanes(vz[g], 1), 0.0)
        inside = here > 0
        scale = jnp.where(inside, 1.0 / jnp.where(inside, diag, 1.0), 0.0)
        inverse_z[g] = scale
        field.append(scale * source)
        basis_z[0, q] = field[g]
        count(0, g, field[g], source)
    for n in range(3):
        following = []
        for g in range(groups):
            here, q = field[g], side * groups + g
            image = weight_z[0, g] * (here - along(field, g, 1)) + weight_z[1, g] * (here - along(field, g, -1))
            image = image + (
                weight_z[2, g] * (here - roll_rows(here, -1)) + weight_z[3, g] * (here - roll_rows(here, 1))
            )
            image = image + (
                weight_z[4, g] * (here - roll_lanes(here, -1)) + weight_z[5, g] * (here - roll_lanes(here, 1))
            )
            count(2 * n + 1, g, here, image)
            if n < 2:
                following.append(inverse_z[g] * image)
                basis_z[n + 1, q] = following[g]
                count(2 * n + 2, g, following[g], image)
        field = following
    for which, total_ in enumerate(totals):
        shares[which] = shares[which] + total_.value()


def outer_ends(nx, ny, ends, shares_in, basis_z, vz_z, shares, *scratch):
    shares[...] = shares_in[...]
    nothing = jnp.zeros((ny + 2 * DEPTH, LANES), jnp.float32)
    for side in range(2):

        @pl.when(jnp.logical_not(beside_z(side)))
        def _():
            solve_end(nx, ny, side, lambda i: nothing, ends, basis_z, vz_z, shares, *scratch)


def join(nx, ny, n_z, after, ends, *refs):
    del after
    got_z, (basis_z, vz_z, shares, sums, *scratch) = refs[:n_z], refs[n_z + 3 :]
    for side in range(2):

        @pl.when(beside_z(side))
        def _():
            received = lambda i: sides(even("gz"), got_z, lambda ref: ref[i])[side]
            solve_end(nx, ny, side, received, ends, basis_z, vz_z, shares, *scratch)

    lane = lane_index((1, LANES))
    row = jnp.zeros((1, LANES), jnp.float32)
    for which in range(6):
        value = jnp.sum(jnp.sum(shares[which], 0, keepdims=True), 1, keepdims=True)
        row = jnp.where(lane == which, value, row)
    sums[...] = row


def slopes(nx, ny, n_x, n_y, press, vel, *refs):
    got_x, got_y, (slope_x, slope_y, slope_z, base) = refs[:n_x], refs[n_x : n_x + n_y], refs[n_x + n_y :]
    total = nx + 2 * DEPTH
    rows, shape = row_index((ROWS, LANES)), (ROWS, LANES)
    lanes = lane_index((ny, LANES))
    at_low, at_high = lanes == 0, lanes == LANES - 1
    p_low, p_high = sides(even("gx"), got_x, lambda ref: ref[PRESS * ny : (PRESS + 1) * ny, :])
    u_low, _ = sides(even("gx"), got_x, lambda ref: ref[VX * ny : (VX + 1) * ny, :])
    old = p_low - press[0]
    slope_x[0] = old
    old = old * u_low
    for x in range(nx):
        p = press[x]
        slope = p - (press[x + 1] if x + 1 < nx else p_high)
        slope_x[x + 1] = slope
        new = slope * vel[0, x]
        answer, old = old + new, new
        low, high = sides(even("gy"), got_y, lambda ref: ref[total + x // ROWS, x % ROWS : x % ROWS + 1, :])
        p_tile = jnp.where(rows == 0, jnp.broadcast_to(high, shape), jnp.broadcast_to(low, shape))
        p_tall = jnp.concatenate([p, p_tile], 0)
        u_row, _ = sides(even("gy"), got_y, lambda ref: ref[x, ROWS - 1 :, :])
        u_tall = jnp.concatenate([vel[1, x], jnp.broadcast_to(u_row, shape)], 0)
        up, down = p - roll_rows(p_tall, -1)[:ny], roll_rows(p_tall, 1)[:ny] - p
        slope_y[0, x], slope_y[1, x] = up, down
        answer = answer + (up * vel[1, x] + down * roll_rows(u_tall, 1)[:ny])
        up = p - jnp.where(at_high, 0.0, roll_lanes(p, -1))
        down = jnp.where(at_low, 0.0, roll_lanes(p, 1)) - p
        slope_z[0, x], slope_z[1, x] = up, down
        base[x] = answer + (up * vel[2, x] + down * jnp.where(at_low, 0.0, roll_lanes(vel[2, x], 1)))


def finish(nx, ny, n_z, gathered, vel, basis, basis_z, vz_z, slope_x, slope_y, slope_z, base, *refs):
    got_z, (ustar_out, coef_out, ustar, coef_cot, sem) = refs[:n_z], refs[n_z:]
    total, height = nx + 2 * DEPTH, ny + 2 * DEPTH
    groups = total // ROWS
    parts = gathered[...]
    while parts.shape[0] > ROWS:
        half = parts.shape[0] // 2
        parts = parts[:half] + parts[half:]
    sums = jnp.sum(parts, 0, keepdims=True)
    lane = lane_index((1, LANES))
    m0, m1, m2, m3, m4, m5 = [
        jnp.sum(jnp.where(lane == which, sums, 0.0), 1, keepdims=True) for which in range(6)
    ]
    l1, l2 = m2 / m1, m3 / m1
    d1, cross, d2 = m3 - l1 * m2, m4 - l1 * m3, m5 - l2 * m3
    l21 = cross / d1
    d2 = d2 - l21 * cross
    y1 = -l1 * m0 + m1
    y2 = m2 - l2 * m0 - l21 * y1
    c2 = y2 / d2
    c1 = y1 / d1 - l21 * c2
    c0 = (m0 / m1 - l1 * c1 - l2 * c2)[0, 0]
    c1, c2 = c1[0, 0], c2[0, 0]

    lanes = lane_index((height, LANES))
    seat_lane = lanes % GROUP
    spill = []
    for g in range(groups):
        low, high = [
            c0 * basis_z[0, q] + c1 * basis_z[1, q] + c2 * basis_z[2, q] for q in (g, groups + g)
        ]
        cells = jnp.where(seat_lane < DEPTH - 1, roll_lanes(high, DEPTH - GROUP + DEPTH - 1), roll_lanes(low, -1))
        cells = jnp.where(seat_lane == 2 * DEPTH - 2, roll_lanes(high, 2 * DEPTH - 2 - (GROUP - DEPTH)), cells)
        spill.append(jnp.where(seat_lane == 2 * DEPTH - 1, roll_lanes(low, DEPTH), cells))
    spoiled = (lanes < DEPTH - 1) | (lanes > LANES - DEPTH)
    lanes = lane_index((ny, LANES))
    at_low, at_high = lanes == 0, lanes == LANES - 1
    low_z, high_z = sides(even("gz"), got_z, lambda ref: ref[groups // 2, :ny, :])
    press_z = jnp.where(lanes % 2 == 0, high_z, roll_lanes(low_z, 1))

    def solved(x):
        e = x % total
        cells = c0 * basis[0, e] + c1 * basis[1, e] + c2 * basis[2, e]
        return jnp.where(spoiled, roll_lanes(spill[e % groups], 1 - DEPTH - GROUP * (e // groups)), cells)

    copies = []
    below, here = solved(-1), solved(0)
    down = here[:ny] - below[:ny]
    for x in range(nx):
        above = solved(x + 1)
        group, seat = x % groups, x // groups
        own = here[:ny]
        up = above[:ny] - own
        ustar[0, x] = vel[0, x] + up
        answer = base[x] + (slope_x[x + 1] * up + slope_x[x] * down)
        next_down = up
        up, down = roll_rows(here, -1)[:ny] - own, own - roll_rows(here, 1)[:ny]
        ustar[1, x] = vel[1, x] + up
        answer = answer + (slope_y[0, x] * up + slope_y[1, x] * down)
        lam_end = roll_lanes(spill[group][:ny], 1 - 2 * DEPTH - GROUP * seat)
        u_end = roll_lanes(vz_z[group, :ny, :], 1 - DEPTH - GROUP * seat)
        p_end = roll_lanes(press_z, LANES - 1 - press_lane(x))
        up = jnp.where(at_high, lam_end, roll_lanes(own, -1)) - own
        down = own - jnp.where(at_low, lam_end, roll_lanes(own, 1))
        out = vel[2, x] + up
        ustar[2, x] = out
        answer = answer + (slope_z[0, x] * up + slope_z[1, x] * down)
        beyond = jnp.where(at_low, p_end * (u_end + down) + slope_z[1, x] * u_end, 0.0)
        answer = answer + jnp.where(at_high, -p_end * out, beyond)
        down = next_down
        coef_cot[x] = 0.5 * answer
        here = above
        if (x + 1) % STRIDE == 0:
            part = pl.ds(x + 1 - STRIDE, STRIDE)
            for which, (src, dst) in enumerate(
                ((ustar.at[:, part], ustar_out.at[:, part]), (coef_cot.at[part], coef_out.at[part]))
            ):
                copies.append(pltpu.make_async_copy(src, dst, sem.at[which, x // STRIDE]))
                copies[-1].start()
    for copy in copies:
        copy.wait()


def on_device(phase, press, vel):
    nx, ny, nz = phase.shape
    total, height = nx + 2 * DEPTH, ny + 2 * DEPTH
    groups = total // ROWS
    devices = lax.axis_size(AXES)
    n_x, n_y, n_z = (turns(axis) for axis in AXES)
    f32 = lambda *shape: jax.ShapeDtypeStruct(shape, jnp.float32)
    scratch = lambda *shape: pltpu.VMEM(shape, jnp.float32)
    inputs = [pltpu.with_memory_space_constraint(array, pltpu.HBM) for array in (phase, press, vel)]

    def call(kernel, args, in_specs, shapes, name, scratch_shapes=(), out_spec=VMEM, aliases={}):
        return pl.pallas_call(
            kernel,
            out_shape=shapes,
            in_specs=in_specs,
            out_specs=[out_spec] * len(shapes),
            scratch_shapes=list(scratch_shapes),
            input_output_aliases=aliases,
            compiler_params=PARAMS,
            cost_estimate=pl.CostEstimate(flops=3_000_000, bytes_accessed=3_000_000, transcendentals=0),
            name=name,
        )(*args)

    odd = n_y > 1
    sent = call(
        functools.partial(pack_first, nx, ny, n_x, n_y),
        inputs,
        [HBM] * 3,
        [f32(VY * ny + 2 * ROWS, nz)] * n_x
        + ([f32(nx + nx // ROWS + 2, ROWS, nz)] + [f32(DEPTH + 2, ROWS, nz)] * n_x if odd else []),
        "pack_first",
        (
            [pltpu.VMEM((nx, ROWS, nz), jnp.int32), scratch(3, nx, ROWS, nz), scratch(nx, ROWS, nz)]
            + [pltpu.SemaphoreType.DMA((3,))]
            if odd
            else []
        )
        + [pltpu.VMEM((n_x, DEPTH, ny, nz), jnp.int32), scratch(n_x, 3, DEPTH, ny, nz)]
        + [pltpu.SemaphoreType.DMA((n_x, 3))],
    )
    to_x = sent[:n_x]
    got_x = [exchange(send, ("gx", turn)) for turn, send in enumerate(to_x)]
    if odd:
        got_odd = exchange(sent[n_x], ("gy", 1))
        corners = [exchange(send, ("gx", turn), ("gy", 1)) for turn, send in enumerate(sent[n_x + 1 :])]
    coef, press, vel, rhs = call(
        load,
        inputs + [to_x[0]],
        [HBM] * 3 + [ANY],
        [f32(*press.shape), f32(*press.shape), f32(*vel.shape), f32(*press.shape)],
        "load",
        [pltpu.VMEM(phase.shape, jnp.int32), pltpu.SemaphoreType.DMA((3,))],
    )
    rows_y = f32(total + nx // ROWS + 1, ROWS, nz)
    got_y, odd_rows, from_odd = [], [], []
    if odd:
        from_odd = [got_odd, *corners[::-1]]
        odd_rows = call(
            functools.partial(merge_odd, nx),
            from_odd,
            [VMEM] * (1 + n_x),
            [rows_y],
            "merge_odd",
        )
    if n_y:
        to_y = call(
            functools.partial(pack_y, nx, ny, n_x),
            [coef, press, vel, rhs, *got_x, *from_odd],
            [VMEM] * (4 + n_x) + [ANY] * len(from_odd),
            [rows_y],
            "pack_y",
        )
        got_y = [exchange(to_y[0], ("gy", 0)), *odd_rows]
    cube = (total, height, nz)
    packs = [f32(groups // 2 + 1, height, LANES)] * n_z
    staged = call(
        functools.partial(stage_z, nx, ny, n_x, n_z),
        [coef, press, vel, rhs, *got_x, *odd_rows],
        [VMEM] * (4 + n_x + len(odd_rows)),
        [f32(*cube)] * 2 + packs,
        "stage_z",
    )
    full_coef, full_rhs, *to_z = call(
        functools.partial(pack_z, nx, ny, n_x, n_z),
        [vel, *got_x, got_y[0], *staged],
        [VMEM] * (4 + n_x + n_z),
        [f32(*cube)] * 2 + packs,
        "pack_z",
        aliases={2 + n_x + which: which for which in range(2 + n_z)},
    )
    got_z = [exchange(send, ("gz", turn)) for turn, send in enumerate(to_z)]
    basis, ends, shares = call(
        functools.partial(prepare, nx, ny, n_x, n_y),
        [coef, vel, rhs, full_coef, full_rhs, *got_x, *got_y],
        [VMEM] * (5 + n_x + n_y),
        [f32(3, *cube), f32(5, groups, height, LANES), f32(6, ROWS, LANES)],
        "prepare",
        [scratch(*cube), scratch(2, *cube), scratch(2, *cube), scratch(*cube)],
    )
    slope = call(
        functools.partial(slopes, nx, ny, n_x, n_y),
        [press, vel, *got_x, *got_y],
        [VMEM] * (2 + n_x + n_y),
        [f32(nx + 1, ny, nz), f32(2, nx, ny, nz), f32(2, nx, ny, nz), f32(nx, ny, nz)],
        "slopes",
    )
    shapes_z = [f32(3, 2 * groups, height, LANES), f32(groups, height, LANES), f32(6, ROWS, LANES)]
    scratch_z = [scratch(6, groups, height, LANES), scratch(groups, height, LANES)]
    outer = call(
        functools.partial(outer_ends, nx, ny),
        [ends, shares],
        [VMEM] * 2,
        shapes_z,
        "outer_ends",
        scratch_z,
    )
    basis_z, vz_z, _, sums = call(
        functools.partial(join, nx, ny, n_z),
        [slope[-1], ends, *got_z, *outer],
        [ANY] + [VMEM] * (4 + n_z),
        shapes_z + [f32(1, LANES)],
        "join",
        scratch_z,
        aliases={2 + n_z + which: which for which in range(3)},
    )
    spread = jnp.broadcast_to(sums[None], (devices, 1, LANES))
    gathered = lax.all_to_all(spread, AXES, 0, 0).reshape(devices, LANES)
    return call(
        functools.partial(finish, nx, ny, n_z),
        [gathered, vel, basis, basis_z, vz_z, *slope, *got_z],
        [VMEM] * (9 + n_z),
        [f32(*vel.shape), f32(nx, ny, nz)],
        "finish",
        [scratch(*vel.shape), scratch(nx, ny, nz), pltpu.SemaphoreType.DMA((2, nx // STRIDE))],
        HBM,
    )


def solution(mesh):
    cells, faces = P(*AXES), P(None, *AXES)
    return jax.shard_map(
        on_device, mesh=mesh, in_specs=(cells, cells, faces), out_specs=(faces, cells), check_vma=False
    )
```

```python
import functools
import itertools

import jax
import jax.numpy as jnp
from jax import lax
from jax.experimental import pallas as pl
from jax.experimental.pallas import tpu as pltpu
from jax.sharding import PartitionSpec as P

AXES = ("gx", "gy", "gz")
SPARE = dict(gx="gy", gy="gz", gz="gx")
DEPTH = 4
GROUP = 4 * DEPTH
LANES = 128
STRIDE = 4
ROWS = 8
VMEM = pl.BlockSpec(memory_space=pltpu.VMEM)
HBM = pl.BlockSpec(memory_space=pltpu.HBM)
ANY = pl.BlockSpec(memory_space=pl.ANY)
PARAMS = pltpu.CompilerParams(vmem_limit_bytes=40 * 1024 * 1024)


def swaps(moves):
    sizes = [lax.axis_size(name) for name in AXES]
    number = lambda place: (place[0] * sizes[1] + place[1]) * sizes[2] + place[2]
    spare = AXES.index("gz" if len(moves) > 1 else SPARE[moves[0][0]])
    pairs = []
    for place in itertools.product(*map(range, sizes)):
        partner, met = list(place), True
        for axis, turn in moves:
            along = AXES.index(axis)
            partner[along] += 1 if (place[along] - turn) % 2 == 0 else -1
            met = met and 0 <= partner[along] < sizes[along]
        if not met:
            if sizes[spare] % 2:
                continue
            partner = list(place)
            partner[spare] ^= 1
        pairs.append((number(place), number(partner)))
    return pairs


def exchange(send, *moves):
    return lax.ppermute(send, AXES, swaps(moves))


def clear_if_alone(out, *moves):
    for axis, turn in moves:
        count, place = lax.axis_size(axis), lax.axis_index(axis)
        alone = []
        if turn == 1:
            alone.append(place == 0)
        if count % 2 != turn:
            alone.append(place == count - 1)
        for case in alone:

            @pl.when(case)
            def _():
                out[...] = jnp.zeros(out.shape, out.dtype)


def even(axis):
    return lax.axis_index(axis) % 2 == 0


def turns(axis):
    return min(2, lax.axis_size(axis) - 1)


def coefficient(phase):
    return jnp.where(phase == 0, 8.0, jnp.where(phase == 1, 1.0, 2.0)).astype(jnp.float32)


def sides(is_even, got, load):
    one = load(got[0])
    two = load(got[1]) if len(got) > 1 else jnp.zeros_like(one)
    return jnp.where(is_even, two, one), jnp.where(is_even, one, two)


def lane_index(shape):
    return lax.broadcasted_iota(jnp.int32, shape, len(shape) - 1)


def row_index(shape):
    return lax.broadcasted_iota(jnp.int32, shape, len(shape) - 2)


def roll_rows(plane, shift):
    return pltpu.roll(plane, shift % plane.shape[0], 0)


def roll_lanes(plane, shift):
    return pltpu.roll(plane, shift % plane.shape[1], 1)


def inner_rhs(coef, vy, vz):
    rows, lanes = row_index(coef.shape), lane_index(coef.shape)
    up = jnp.where(rows == coef.shape[0] - 1, 0.0, 0.5 * (coef + roll_rows(coef, -1)))
    down = jnp.where(rows == 0, 0.0, 0.5 * (coef + roll_rows(coef, 1)))
    right = jnp.where(lanes == LANES - 1, 0.0, 0.5 * (coef + roll_lanes(coef, -1)))
    left = jnp.where(lanes == 0, 0.0, 0.5 * (coef + roll_lanes(coef, 1)))
    return (up * vy - down * roll_rows(vy, 1)) + (right * vz - left * roll_lanes(vz, 1))


RHS, VX, PRESS, VY = DEPTH, 2 * DEPTH - 1, 2 * DEPTH, 2 * DEPTH + 1


def pack_first(nx, ny, n_x, n_y, phase, press, vel, *refs):
    outs, odd_outs, (held, held_vel, sem) = refs[:n_x], refs[n_x:-3], refs[-3:]
    if n_y > 1:
        *odd_outs, tile_phase, tile_vel, tile_press, tile_sem = odd_outs
    copies, late = [], []
    for turn, out in enumerate(outs):
        top = even("gx") == (turn == 0)
        deep = jnp.where(top, nx - DEPTH, 0)
        last = jnp.where(top, nx - 1, 0)
        parts = [
            (vel.at[:, pl.ds(deep, DEPTH)], held_vel.at[turn]),
            (phase.at[pl.ds(deep, DEPTH)], held.at[turn]),
            (press.at[last], out.at[pl.ds(PRESS * ny, ny)]),
        ]
        for which, (src, dst) in enumerate(parts):
            copy = pltpu.make_async_copy(src, dst, sem.at[turn, which])
            copy.start()
            copies.append(copy)
    if n_y > 1:
        row = pl.multiple_of(jnp.where(even("gy"), 0, ny - ROWS), ROWS)
        parts = [
            (phase.at[:, pl.ds(row, ROWS)], tile_phase),
            (vel.at[:, :, pl.ds(row, ROWS)], tile_vel),
            (press.at[:, pl.ds(row, ROWS)], tile_press),
        ]
        for which, (src, dst) in enumerate(parts):
            copy = pltpu.make_async_copy(src, dst, tile_sem.at[which])
            copy.start()
            late.append(copy)
    lanes = lane_index((ROWS, LANES))
    rows = row_index((ROWS, LANES))
    for turn, out in enumerate(outs):
        for copy in copies[3 * turn : 3 * turn + 3]:
            copy.wait()
        top = even("gx") == (turn == 0)
        coefs = [coefficient(held[turn, j]) for j in range(DEPTH)]
        flux = [0.5 * (coefs[j] + coefs[j + 1]) * held_vel[turn, 0, j] for j in range(DEPTH - 1)]
        columns = jnp.zeros((ROWS, LANES), jnp.float32)
        lines = jnp.zeros((ROWS, LANES), jnp.float32)
        for j in range(DEPTH):
            out[j * ny : (j + 1) * ny, :] = coefs[j]
        for j in range(DEPTH - 1):
            vy = jnp.where(top, held_vel[turn, 1, j + 1], held_vel[turn, 1, j])
            vz = jnp.where(top, held_vel[turn, 2, j + 1], held_vel[turn, 2, j])
            upper = (flux[j + 1] - flux[j]) if j + 1 < DEPTH - 1 else -flux[j]
            lower = (flux[j] - flux[j - 1]) if j else flux[j]
            inner = inner_rhs(jnp.where(top, coefs[j + 1], coefs[j]), vy, vz)
            out[(RHS + j) * ny : (RHS + j + 1) * ny, :] = jnp.where(top, upper, lower) + inner
            for t in range(ny // ROWS):
                lane = DEPTH * t + j
                columns = jnp.where(lanes == lane, roll_lanes(vz[t * ROWS : (t + 1) * ROWS], lane + 1), columns)
            lines = jnp.where(rows == j, roll_rows(vy[ny - ROWS :], j + 1), lines)
        out[VX * ny : (VX + 1) * ny, :] = held_vel[turn, 0, DEPTH - 1]
        out[VY * ny : VY * ny + ROWS, :] = lines
        out[VY * ny + ROWS :, :] = columns
        clear_if_alone(out, ("gx", turn))
    for copy in late:
        copy.wait()
    if n_y > 1:
        pack_odd(nx, tile_phase, tile_vel, tile_press, odd_outs)


def row_tile(coef, rhs, vy, top):
    rows = row_index((ROWS, LANES))
    coef = jnp.where(top, roll_rows(coef, DEPTH), coef)
    rhs = jnp.where(top, roll_rows(rhs, -1), roll_rows(rhs, DEPTH))
    return jnp.where(rows == ROWS - 1, vy, jnp.where(rows < DEPTH, coef, rhs))


def pack_odd(nx, tile_phase, tile_vel, tile_press, outs):
    out, *corners = outs
    top = jnp.logical_not(even("gy"))
    lanes = lane_index((ROWS, LANES))
    ends_at, vx_at = nx + nx // ROWS, nx + nx // ROWS + 1
    ends = jnp.zeros((ROWS, LANES), jnp.float32)
    here, old_flux = coefficient(tile_phase[0]), None
    for x in range(nx):
        vy, vz = tile_vel[1, x], tile_vel[2, x]
        answer = inner_rhs(here, vy, vz)
        if old_flux is not None:
            answer = answer - old_flux
        coef = here
        if x + 1 < nx:
            above = coefficient(tile_phase[x + 1])
            old_flux = 0.5 * (here + above) * tile_vel[0, x]
            answer = answer + old_flux
            here = above
        out[x] = row_tile(coef, answer, vy, top)
        ends = jnp.where(lanes == x, roll_lanes(vz, x + 1), ends)
        tile = tile_press[x]
        at = nx + x // ROWS
        out[at, x % ROWS : x % ROWS + 1, :] = jnp.where(top, tile[ROWS - 1 : ROWS], tile[0:1])
    shift = lambda tile: jnp.where(top, roll_rows(tile, -1), roll_rows(tile, DEPTH))
    ends = jnp.where(top, roll_rows(ends, DEPTH - 1), ends)
    out[ends_at] = ends
    out[vx_at] = shift(tile_vel[0, nx - 1])
    for turn, corner in enumerate(corners):
        first = jnp.where(even("gx") == (turn == 0), nx - DEPTH, 0)
        for j in range(DEPTH):
            corner[j] = out[first + j]
        corner[DEPTH] = pltpu.roll(ends, jnp.where(first == 0, 0, (DEPTH - nx) % LANES), 1)
        corner[DEPTH + 1] = out[vx_at]
        clear_if_alone(corner, ("gx", turn), ("gy", 1))
    clear_if_alone(out, ("gy", 1))


def merge_odd(nx, got, *refs):
    corners, out = refs[:-1][::-1], refs[-1]
    total = nx + 2 * DEPTH
    rows, lanes = row_index((ROWS, LANES)), lane_index((ROWS, LANES))
    ends_at, vx_at = nx + nx // ROWS, nx + nx // ROWS + 1
    low, high = zip(*[sides(even("gx"), corners, lambda ref: ref[j]) for j in range(DEPTH + 2)])
    tiles = [got[x] for x in range(nx)] + list(high[:DEPTH]) + list(low[:DEPTH])
    inner = (rows >= DEPTH) & (rows < ROWS - 1)

    def face(below, above, vx):
        weight = 0.5 * (tiles[below] + tiles[above])
        weight = jnp.where(even("gy"), roll_rows(weight, DEPTH - 1), roll_rows(weight, DEPTH))
        return jnp.where(inner, weight * vx, 0.0)

    low_face, high_face = face(total - 1, 0, low[DEPTH + 1]), face(nx - 1, nx, got[vx_at])
    for plane, tile in enumerate(tiles):
        if plane == 0:
            tile = tile - low_face
        if plane == total - 1:
            tile = tile + low_face
        if plane == nx - 1:
            tile = tile + high_face
        if plane == nx:
            tile = tile - high_face
        out[plane] = tile
    for at in range(nx // ROWS):
        out[total + at] = got[nx + at]
    ends = jnp.where(lanes < nx, got[ends_at], roll_lanes(high[DEPTH], nx))
    out[total + nx // ROWS] = jnp.where(lanes < nx + DEPTH, ends, roll_lanes(low[DEPTH], nx + DEPTH))


def load(phase, press, vel, after, coef, press_out, vel_out, rhs, held, sem):
    del after
    copies = []
    for which, (src, dst) in enumerate(((phase, held), (press, press_out), (vel, vel_out))):
        copies.append(pltpu.make_async_copy(src, dst, sem.at[which]))
        copies[-1].start()
    copies[0].wait()
    copies[1].wait()
    copies[2].wait()
    nx = coef.shape[0]
    here = coefficient(held[0])
    old_flux = None
    for x in range(nx):
        coef[x] = here
        answer = inner_rhs(here, vel_out[1, x], vel_out[2, x])
        if old_flux is not None:
            answer = answer - old_flux
        if x + 1 < nx:
            above = coefficient(held[x + 1])
            old_flux = 0.5 * (here + above) * vel_out[0, x]
            answer = answer + old_flux
            here = above
        rhs[x] = answer


class Block:
    def __init__(self, nx, ny, coef, vel, rhs, got_x, row=0, height=None, faces=True):
        self.nx, self.ny = nx, ny
        self.own_coef, self.vel, self.own_rhs, self.got_x = coef, vel, rhs, got_x
        self.even = even("gx")
        self.row, self.height = row, height or ny
        if not faces:
            return
        self.low_face = 0.5 * (self.coef(nx + 2 * DEPTH - 1) + self.coef(0)) * self.halo(VX)[0]
        self.high_face = 0.5 * (self.coef(nx - 1) + self.coef(nx)) * self.take(vel, 0, nx - 1)

    def take(self, ref, *index):
        return ref[(*index, pl.ds(self.row, self.height), slice(None))]

    def halo(self, part):
        return sides(self.even, self.got_x, lambda ref: ref[pl.ds(part * self.ny + self.row, self.height), :])

    def coef(self, plane):
        if plane < self.nx:
            return self.take(self.own_coef, plane)
        above = plane < self.nx + DEPTH
        return self.halo((plane - self.nx) % DEPTH)[1 if above else 0]

    def rhs(self, plane):
        nx = self.nx
        if plane < nx:
            answer = self.take(self.own_rhs, plane)
        else:
            above = plane < nx + DEPTH
            layer = plane - nx if above else plane - nx - DEPTH - 1
            if layer < 0 or layer >= DEPTH - 1:
                return jnp.zeros((self.height, LANES), jnp.float32)
            answer = self.halo(RHS + layer)[1 if above else 0]
        if plane == 0:
            answer = answer - self.low_face
        if plane == nx + 2 * DEPTH - 1:
            answer = answer + self.low_face
        if plane == nx - 1:
            answer = answer + self.high_face
        if plane == nx:
            answer = answer - self.high_face
        return answer

    def layer(self, plane):
        if plane < self.nx + DEPTH:
            place = (1, plane - self.nx)
        else:
            place = (0, plane - self.nx - DEPTH - 1)
        return place if 0 <= place[1] < DEPTH - 1 else None

    def columns(self):
        at = VY * self.ny + ROWS
        return sides(self.even, self.got_x, lambda ref: ref[at : at + ROWS, :])

    def vz_end(self, plane, lane):
        if plane < self.nx:
            return roll_lanes(self.vel[2, plane], lane + 1)
        place = self.layer(plane)
        if place is None:
            return jnp.zeros((self.ny, LANES), jnp.float32)
        source = self.columns()[place[0]]
        return jnp.concatenate(
            [roll_lanes(source, lane - DEPTH * t - place[1]) for t in range(self.ny // ROWS)], 0
        )

    def vy_end(self, plane):
        if plane < self.nx:
            return self.vel[1, plane, self.ny - 1 :, :]
        place = self.layer(plane)
        if place is None:
            return jnp.zeros((1, LANES), jnp.float32)
        at = VY * self.ny + place[1]
        return sides(self.even, self.got_x, lambda ref: ref[at : at + 1, :])[place[0]]


def pack_y(nx, ny, n_x, coef, press, vel, rhs, *refs):
    got_x, out = refs[:n_x], refs[-1]
    total = nx + 2 * DEPTH
    lanes = lane_index((ROWS, LANES))
    top = even("gy")
    row = pl.multiple_of(jnp.where(top, ny - ROWS, 0), ROWS)
    block = Block(nx, ny, coef, vel, rhs, got_x, row, ROWS)
    columns = jnp.zeros((ROWS, LANES), jnp.float32)
    ends = block.columns()
    for plane in range(total):
        out[plane] = row_tile(block.coef(plane), block.rhs(plane), block.vy_end(plane), top)
        if plane < nx:
            source = roll_lanes(vel[2, plane, pl.ds(row, ROWS), :], plane + 1)
        elif block.layer(plane) is None:
            continue
        else:
            side, layer = block.layer(plane)
            high = (plane - layer - DEPTH * (ny // ROWS - 1)) % LANES
            source = pltpu.roll(ends[side], jnp.where(top, high, (plane - layer) % LANES), 1)
        columns = jnp.where(lanes == plane, source, columns)
    out[total + nx // ROWS] = jnp.where(top, roll_rows(columns, DEPTH - 1), columns)
    for plane in range(nx):
        tile = press[plane, pl.ds(row, ROWS), :]
        edge = jnp.where(top, tile[ROWS - 1 : ROWS], tile[0:1])
        out[total + plane // ROWS, plane % ROWS : plane % ROWS + 1, :] = edge
    clear_if_alone(out, ("gy", 0))


def tall_end(block, tile_end, plane, lane):
    return jnp.concatenate([block.vz_end(plane, lane), roll_lanes(tile_end, lane - plane)], 0)


def tile_of_ends(nx, even_y, got_y):
    rows = row_index((ROWS, LANES))
    low, high = sides(even_y, got_y, lambda ref: ref[nx + 2 * DEPTH + nx // ROWS])
    return jnp.where(rows < DEPTH, high, roll_rows(low, DEPTH + 1))


def press_lane(x):
    return GROUP * (x % ROWS) + ROWS + 2 * (x // ROWS)


def pack_plane(lanes, at, top, coef, rhs, end):
    coef = pltpu.roll(coef, jnp.where(top, (at + DEPTH) % LANES, at), 1)
    rhs = pltpu.roll(rhs, jnp.where(top, (at + ROWS - 1) % LANES, at + DEPTH), 1)
    value = jnp.where(lanes == at + ROWS - 1, end, 0.0)
    value = jnp.where((lanes >= at + DEPTH) & (lanes < at + ROWS - 1), rhs, value)
    return jnp.where((lanes >= at) & (lanes < at + DEPTH), coef, value)


def half_tile(tile, below):
    rows = row_index((ROWS, LANES))
    coef = jnp.where(below, jnp.where(rows >= DEPTH, roll_rows(tile, DEPTH), 0.0), jnp.where(rows < DEPTH, tile, 0.0))
    rhs = jnp.where(
        below,
        jnp.where(rows > DEPTH, roll_rows(tile, 1), 0.0),
        jnp.where(rows < DEPTH - 1, roll_rows(tile, -DEPTH), 0.0),
    )
    return coef, rhs


def half_ends(tile, below):
    rows = row_index((ROWS, LANES))
    return jnp.where(
        below, jnp.where(rows > DEPTH, roll_rows(tile, DEPTH + 1), 0.0), jnp.where(rows < DEPTH - 1, tile, 0.0)
    )


def face_y(own_low, own_high, coef_tile, tile, vy_end, below):
    rows = row_index((ROWS, LANES))
    down = 0.5 * (coef_tile[ROWS - 1 :] + own_low) * tile[ROWS - 1 :]
    up = 0.5 * (own_high + coef_tile[:1]) * vy_end
    outside = jnp.where(below, jnp.where(rows == ROWS - 1, down, 0.0), jnp.where(rows == 0, -up, 0.0))
    inside = jnp.where(below, jnp.where(rows == 0, -down, 0.0), jnp.where(rows == ROWS - 1, up, 0.0))
    return outside, inside


def stage_z(nx, ny, n_x, n_z, coef, press, vel, rhs, *refs):
    got_x, (*got_odd, full_coef, full_rhs), sends = refs[:n_x], refs[n_x : len(refs) - n_z], refs[len(refs) - n_z :]
    total, height = nx + 2 * DEPTH, ny + 2 * DEPTH
    groups = total // ROWS
    below = even("gy")
    lanes = lane_index((height, LANES))
    block = Block(nx, ny, coef, vel, rhs, got_x)
    nothing = jnp.zeros((ROWS, LANES), jnp.float32)
    tile_end = half_ends(got_odd[0][total + nx // ROWS], below) if got_odd else nothing
    made = [[jnp.zeros((height, LANES), jnp.float32) for _ in range(groups // 2 + 1)] for _ in sends]
    row = pl.ds(pl.multiple_of(jnp.where(below, 0, ny - ROWS), ROWS), ROWS)
    for plane in range(total):
        c_own, r_own = block.coef(plane), block.rhs(plane)
        c_tile = r_tile = nothing
        full_rhs[plane, :ny, :] = r_own
        if got_odd:
            tile = got_odd[0][plane]
            c_tile, r_tile = half_tile(tile, below)
            outside, inside = face_y(c_own[:1], c_own[ny - 1 :], c_tile, tile, block.vy_end(plane), below)
            r_tile = r_tile + outside
            full_rhs[plane, row, :] = full_rhs[plane, row, :] + inside
        c_all = jnp.concatenate([c_own, c_tile], 0)
        full_coef[plane] = c_all
        full_rhs[plane, ny:, :] = r_tile
        r_all = full_rhs[plane]
        group, seat = plane % groups, plane // groups
        at = GROUP * seat + ROWS * (group % 2)
        end = tall_end(block, tile_end, plane, at + ROWS - 1)
        for turn in range(n_z):
            value = pack_plane(lanes, at, even("gz") == (turn == 0), c_all, r_all, end)
            made[turn][group // 2] = made[turn][group // 2] + value
    for turn, send in enumerate(sends):
        top = even("gz") == (turn == 0)
        value = made[turn][groups // 2][:ny]
        for plane in range(nx):
            at = press_lane(plane)
            moved = pltpu.roll(press[plane], jnp.where(top, (at + 1) % LANES, at), 1)
            value = jnp.where(lanes[:ny] == at, moved, value)
        made[turn][groups // 2] = jnp.concatenate([value, made[turn][groups // 2][ny:]], 0)
        for which, value in enumerate(made[turn]):
            send[which] = value


def pack_z(nx, ny, n_x, n_z, vel, *refs):
    got_x, got, (full_coef, full_rhs, *sends) = refs[:n_x], refs[n_x], refs[-2 - n_z :]
    total = nx + 2 * DEPTH
    groups = total // ROWS
    below = jnp.logical_not(even("gy"))
    lanes = lane_index((ROWS, LANES))
    block = Block(nx, ny, full_coef, vel, full_rhs, got_x, faces=False)
    tile_end = half_ends(got[total + nx // ROWS], below)
    row = pl.ds(pl.multiple_of(jnp.where(below, 0, ny - ROWS), ROWS), ROWS)
    added = [[[jnp.zeros((ROWS, LANES), jnp.float32) for _ in range(2)] for _ in range(groups // 2 + 1)] for _ in sends]
    for plane in range(total):
        if plane in (nx + DEPTH - 1, nx + DEPTH):
            continue
        tile = got[plane]
        c_tile, r_tile = half_tile(tile, below)
        low, high = full_coef[plane, :1, :], full_coef[plane, ny - 1 : ny, :]
        outside, inside = face_y(low, high, c_tile, tile, block.vy_end(plane), below)
        r_tile = r_tile + outside
        full_coef[plane, ny:, :] = full_coef[plane, ny:, :] + c_tile
        full_rhs[plane, ny:, :] = full_rhs[plane, ny:, :] + r_tile
        full_rhs[plane, row, :] = full_rhs[plane, row, :] + inside
        group, seat = plane % groups, plane // groups
        at = GROUP * seat + ROWS * (group % 2)
        end = roll_lanes(tile_end, at + ROWS - 1 - plane)
        for turn in range(n_z):
            top = even("gz") == (turn == 0)
            inside_move = pltpu.roll(inside, jnp.where(top, (at + ROWS - 1) % LANES, at + DEPTH), 1)
            inside_move = jnp.where((lanes >= at + DEPTH) & (lanes < at + ROWS - 1), inside_move, 0.0)
            slot = added[turn][group // 2]
            slot[0] = slot[0] + pack_plane(lanes, at, top, c_tile, r_tile, end)
            slot[1] = slot[1] + inside_move
    for turn, send in enumerate(sends):
        for which, (tile, inside) in enumerate(added[turn]):
            send[which, ny:, :] = send[which, ny:, :] + tile
            send[which, row, :] = send[which, row, :] + inside
        clear_if_alone(send, ("gz", turn))


def tree_sum(parts):
    while len(parts) > 1:
        parts = [parts[i] + parts[i + 1] if i + 1 < len(parts) else parts[i] for i in range(0, len(parts), 2)]
    return parts[0]


class Totals:
    def __init__(self):
        self.stack = []

    def add(self, tile):
        level = 0
        while self.stack and self.stack[-1][0] == level:
            tile = self.stack.pop()[1] + tile
            level += 1
        self.stack.append((level, tile))

    def value(self):
        tiles = [tile for _, tile in self.stack]
        total = tiles.pop()
        while tiles:
            total = tiles.pop() + total
        return total


def prepare(nx, ny, n_x, n_y, coef, vel, rhs, full_coef, full_rhs, *refs):
    got_x, got_y = refs[:n_x], refs[n_x : n_x + n_y]
    basis, ends, shares, wx, wy, wz, inverse = refs[n_x + n_y :]
    total, height = nx + 2 * DEPTH, ny + 2 * DEPTH
    groups = total // ROWS
    lanes = lane_index((height, LANES))
    block = Block(nx, ny, coef, vel, rhs, got_x)
    tile_end = tile_of_ends(nx, even("gy"), got_y)
    for group in range(groups):
        made = [jnp.zeros((height, LANES), jnp.float32) for _ in range(5)]
        for seat in range(ROWS):
            plane = seat * groups + group
            at = GROUP * seat
            for which, source in enumerate((full_coef[plane], full_rhs[plane])):
                here = (lanes >= at + DEPTH) & (lanes < at + GROUP)
                made[2 * which] = jnp.where(here, roll_lanes(source, at + DEPTH), made[2 * which])
                here = (lanes >= at) & (lanes < at + GROUP - DEPTH)
                made[2 * which + 1] = jnp.where(here, roll_lanes(source, at + GROUP - DEPTH), made[2 * which + 1])
            lane = at + GROUP - DEPTH - 1
            made[4] = jnp.where(lanes == lane, tall_end(block, tile_end, plane, lane), made[4])
        for which in range(5):
            ends[which, group] = made[which]
    totals = [Totals() for _ in range(6)]
    trusted = (lanes[:ROWS] >= DEPTH) & (lanes[:ROWS] < LANES - DEPTH)

    def count(which, left, right):
        product = left[:ny] * right[:ny]
        tile = tree_sum([product[i : i + ROWS] for i in range(0, ny, ROWS)])
        totals[which].add(jnp.where(trusted, tile, 0.0))

    old_weight = None
    here = full_coef[nx + DEPTH]
    for x in range(-DEPTH, nx + DEPTH - 1):
        e = x % total
        above = full_coef[(e + 1) % total]
        weight = 0.5 * (here + above)
        wx[e] = weight
        if x > -DEPTH:
            up, down = 0.5 * (here + roll_rows(here, -1)), 0.5 * (here + roll_rows(here, 1))
            right = jnp.where(lanes == LANES - 1, 0.0, 0.5 * (here + roll_lanes(here, -1)))
            left = jnp.where(lanes == 0, 0.0, 0.5 * (here + roll_lanes(here, 1)))
            wy[0, e], wy[1, e], wz[0, e], wz[1, e] = up, down, right, left
            diag = (weight + old_weight) + (up + down) + (right + left)
            inside = here > 0
            scale = jnp.where(inside, 1.0 / jnp.where(inside, diag, 1.0), 0.0)
            inverse[e] = scale
            source = full_rhs[e]
            field = scale * source
            basis[0, e] = field
            if 0 <= x < nx:
                count(0, field, source)
        old_weight, here = weight, above
    for n in range(3):
        reach = 2 - n
        old_flux = None
        here = basis[n, (-reach - 1) % total]
        for x in range(-reach - 1, nx + reach):
            e = x % total
            above = basis[n, (e + 1) % total]
            flux = wx[e] * (above - here)
            if x >= -reach:
                image = old_flux - flux
                image = image + (
                    wy[0, e] * (here - roll_rows(here, -1)) + wy[1, e] * (here - roll_rows(here, 1))
                )
                image = image + (
                    wz[0, e] * (here - roll_lanes(here, -1)) + wz[1, e] * (here - roll_lanes(here, 1))
                )
                own = 0 <= x < nx
                if own:
                    count(2 * n + 1, here, image)
                if n < 2:
                    following = inverse[e] * image
                    basis[n + 1, e] = following
                    if own:
                        count(2 * n + 2, following, image)
            old_flux, here = flux, above
    for which, total_ in enumerate(totals):
        shares[which] = total_.value()


def beside_z(side):
    place = lax.axis_index("gz")
    return place > 0 if side == 0 else place < lax.axis_size("gz") - 1


def solve_end(nx, ny, side, received, ends, basis_z, vz_z, shares, weight_z, inverse_z):
    total, height = nx + 2 * DEPTH, ny + 2 * DEPTH
    groups = total // ROWS
    lanes = lane_index((height, LANES))
    seat_lane, seat = lanes % GROUP, lanes // GROUP
    outer = seat_lane < DEPTH if side == 0 else seat_lane >= GROUP - DEPTH
    coef, rhs, vz = [], [], []
    for g in range(groups):
        got, skip = received(g // 2), ROWS * (g % 2)
        start = 0 if side == 0 else GROUP - DEPTH
        less = 1 if side == 0 else 0
        coef.append(jnp.where(outer, roll_lanes(got, start - skip), ends[side, g]))
        rhs.append(jnp.where(outer, roll_lanes(got, start + less - DEPTH - skip), ends[2 + side, g]))
        if side == 0:
            vz.append(roll_lanes(got, -DEPTH - skip))
            vz_z[g] = vz[-1]
        else:
            vz.append(ends[4, g])

    def along(planes, g, step):
        if 0 <= g + step < groups:
            return planes[g + step]
        return roll_lanes(planes[(g + step) % groups], -GROUP * step)

    totals = [Totals() for _ in range(6)]

    def count(which, g, left, right):
        first = DEPTH if side == 0 else GROUP - 2 * DEPTH
        spot = seat_lane[:ROWS]
        mine = (spot >= first) & (spot < first + DEPTH) & (seat[:ROWS] * groups + g < nx)
        product = left[:ny] * right[:ny]
        tile = tree_sum([product[i : i + ROWS] for i in range(0, ny, ROWS)])
        totals[which].add(jnp.where(mine, tile, 0.0))

    field = []
    for g in range(groups):
        here, q = coef[g], side * groups + g
        neighbours = (along(coef, g, 1), along(coef, g, -1), roll_rows(here, -1), roll_rows(here, 1))
        neighbours += (roll_lanes(here, -1), roll_lanes(here, 1))
        weights = [0.5 * (here + other) for other in neighbours]
        for which, weight in enumerate(weights):
            weight_z[which, g] = weight
        diag = (weights[0] + weights[1]) + (weights[2] + weights[3]) + (weights[4] + weights[5])
        face = DEPTH - 1 if side == 0 else GROUP - DEPTH - 1
        source = rhs[g] + jnp.where(seat_lane == face, weights[4] * vz[g], 0.0)
        source = source - jnp.where(seat_lane == face + 1, weights[5] * roll_lanes(vz[g], 1), 0.0)
        inside = here > 0
        scale = jnp.where(inside, 1.0 / jnp.where(inside, diag, 1.0), 0.0)
        inverse_z[g] = scale
        field.append(scale * source)
        basis_z[0, q] = field[g]
        count(0, g, field[g], source)
    for n in range(3):
        following = []
        for g in range(groups):
            here, q = field[g], side * groups + g
            image = weight_z[0, g] * (here - along(field, g, 1)) + weight_z[1, g] * (here - along(field, g, -1))
            image = image + (
                weight_z[2, g] * (here - roll_rows(here, -1)) + weight_z[3, g] * (here - roll_rows(here, 1))
            )
            image = image + (
                weight_z[4, g] * (here - roll_lanes(here, -1)) + weight_z[5, g] * (here - roll_lanes(here, 1))
            )
            count(2 * n + 1, g, here, image)
            if n < 2:
                following.append(inverse_z[g] * image)
                basis_z[n + 1, q] = following[g]
                count(2 * n + 2, g, following[g], image)
        field = following
    for which, total_ in enumerate(totals):
        shares[which] = shares[which] + total_.value()


def outer_ends(nx, ny, ends, shares_in, basis_z, vz_z, shares, *scratch):
    shares[...] = shares_in[...]
    nothing = jnp.zeros((ny + 2 * DEPTH, LANES), jnp.float32)
    for side in range(2):

        @pl.when(jnp.logical_not(beside_z(side)))
        def _():
            solve_end(nx, ny, side, lambda i: nothing, ends, basis_z, vz_z, shares, *scratch)


def join(nx, ny, n_z, after, ends, *refs):
    del after
    got_z, (basis_z, vz_z, shares, sums, *scratch) = refs[:n_z], refs[n_z + 3 :]
    for side in range(2):

        @pl.when(beside_z(side))
        def _():
            received = lambda i: sides(even("gz"), got_z, lambda ref: ref[i])[side]
            solve_end(nx, ny, side, received, ends, basis_z, vz_z, shares, *scratch)

    rows, lanes = row_index((ROWS, LANES)), lane_index((ROWS, LANES))
    table = jnp.zeros((ROWS, LANES), jnp.float32)
    for which in range(6):
        table = jnp.where(rows == which, jnp.sum(shares[which], 0, keepdims=True), table)
    table = jnp.where(rows == lanes, jnp.sum(table, 1, keepdims=True), 0.0)
    sums[...] = jnp.sum(table, 0, keepdims=True)


def slopes(nx, ny, n_x, n_y, press, vel, *refs):
    got_x, got_y, (slope_x, slope_y, slope_z, base) = refs[:n_x], refs[n_x : n_x + n_y], refs[n_x + n_y :]
    total = nx + 2 * DEPTH
    rows, shape = row_index((ROWS, LANES)), (ROWS, LANES)
    lanes = lane_index((ny, LANES))
    at_low, at_high = lanes == 0, lanes == LANES - 1
    p_low, p_high = sides(even("gx"), got_x, lambda ref: ref[PRESS * ny : (PRESS + 1) * ny, :])
    u_low, _ = sides(even("gx"), got_x, lambda ref: ref[VX * ny : (VX + 1) * ny, :])
    old = p_low - press[0]
    slope_x[0] = old
    old = old * u_low
    for x in range(nx):
        p = press[x]
        slope = p - (press[x + 1] if x + 1 < nx else p_high)
        slope_x[x + 1] = slope
        new = slope * vel[0, x]
        answer, old = old + new, new
        low, high = sides(even("gy"), got_y, lambda ref: ref[total + x // ROWS, x % ROWS : x % ROWS + 1, :])
        p_tile = jnp.where(rows == 0, jnp.broadcast_to(high, shape), jnp.broadcast_to(low, shape))
        p_tall = jnp.concatenate([p, p_tile], 0)
        u_row, _ = sides(even("gy"), got_y, lambda ref: ref[x, ROWS - 1 :, :])
        u_tall = jnp.concatenate([vel[1, x], jnp.broadcast_to(u_row, shape)], 0)
        up, down = p - roll_rows(p_tall, -1)[:ny], roll_rows(p_tall, 1)[:ny] - p
        slope_y[0, x], slope_y[1, x] = up, down
        answer = answer + (up * vel[1, x] + down * roll_rows(u_tall, 1)[:ny])
        up = p - jnp.where(at_high, 0.0, roll_lanes(p, -1))
        down = jnp.where(at_low, 0.0, roll_lanes(p, 1)) - p
        slope_z[0, x], slope_z[1, x] = up, down
        base[x] = answer + (up * vel[2, x] + down * jnp.where(at_low, 0.0, roll_lanes(vel[2, x], 1)))


def finish(nx, ny, n_z, gathered, vel, basis, basis_z, vz_z, slope_x, slope_y, slope_z, base, *refs):
    got_z, (ustar_out, coef_out, ustar, coef_cot, sem) = refs[:n_z], refs[n_z:]
    total, height = nx + 2 * DEPTH, ny + 2 * DEPTH
    groups = total // ROWS
    parts = gathered[...]
    while parts.shape[0] > ROWS:
        half = parts.shape[0] // 2
        parts = parts[:half] + parts[half:]
    sums = jnp.sum(parts, 0, keepdims=True)
    lane = lane_index((1, LANES))
    m0, m1, m2, m3, m4, m5 = [
        jnp.sum(jnp.where(lane == which, sums, 0.0), 1, keepdims=True) for which in range(6)
    ]
    l1, l2 = m2 / m1, m3 / m1
    d1, cross, d2 = m3 - l1 * m2, m4 - l1 * m3, m5 - l2 * m3
    l21 = cross / d1
    d2 = d2 - l21 * cross
    y1 = -l1 * m0 + m1
    y2 = m2 - l2 * m0 - l21 * y1
    c2 = y2 / d2
    c1 = y1 / d1 - l21 * c2
    c0 = (m0 / m1 - l1 * c1 - l2 * c2)[0, 0]
    c1, c2 = c1[0, 0], c2[0, 0]

    lanes = lane_index((height, LANES))
    seat_lane = lanes % GROUP
    spill = []
    for g in range(groups):
        low, high = [
            c0 * basis_z[0, q] + c1 * basis_z[1, q] + c2 * basis_z[2, q] for q in (g, groups + g)
        ]
        cells = jnp.where(seat_lane < DEPTH - 1, roll_lanes(high, DEPTH - GROUP + DEPTH - 1), roll_lanes(low, -1))
        cells = jnp.where(seat_lane == 2 * DEPTH - 2, roll_lanes(high, 2 * DEPTH - 2 - (GROUP - DEPTH)), cells)
        spill.append(jnp.where(seat_lane == 2 * DEPTH - 1, roll_lanes(low, DEPTH), cells))
    spoiled = (lanes < DEPTH - 1) | (lanes > LANES - DEPTH)
    lanes = lane_index((ny, LANES))
    at_low, at_high = lanes == 0, lanes == LANES - 1
    low_z, high_z = sides(even("gz"), got_z, lambda ref: ref[groups // 2, :ny, :])
    press_z = jnp.where(lanes % 2 == 0, high_z, roll_lanes(low_z, 1))

    def solved(x):
        e = x % total
        cells = c0 * basis[0, e] + c1 * basis[1, e] + c2 * basis[2, e]
        return jnp.where(spoiled, roll_lanes(spill[e % groups], 1 - DEPTH - GROUP * (e // groups)), cells)

    copies = []
    below, here = solved(-1), solved(0)
    down = here[:ny] - below[:ny]
    for x in range(nx):
        above = solved(x + 1)
        group, seat = x % groups, x // groups
        own = here[:ny]
        up = above[:ny] - own
        ustar[0, x] = vel[0, x] + up
        answer = base[x] + (slope_x[x + 1] * up + slope_x[x] * down)
        next_down = up
        up, down = roll_rows(here, -1)[:ny] - own, own - roll_rows(here, 1)[:ny]
        ustar[1, x] = vel[1, x] + up
        answer = answer + (slope_y[0, x] * up + slope_y[1, x] * down)
        lam_end = roll_lanes(spill[group][:ny], 1 - 2 * DEPTH - GROUP * seat)
        u_end = roll_lanes(vz_z[group, :ny, :], 1 - DEPTH - GROUP * seat)
        p_end = roll_lanes(press_z, LANES - 1 - press_lane(x))
        up = jnp.where(at_high, lam_end, roll_lanes(own, -1)) - own
        down = own - jnp.where(at_low, lam_end, roll_lanes(own, 1))
        out = vel[2, x] + up
        ustar[2, x] = out
        answer = answer + (slope_z[0, x] * up + slope_z[1, x] * down)
        beyond = jnp.where(at_low, p_end * (u_end + down) + slope_z[1, x] * u_end, 0.0)
        answer = answer + jnp.where(at_high, -p_end * out, beyond)
        down = next_down
        coef_cot[x] = 0.5 * answer
        here = above
        if (x + 1) % STRIDE == 0:
            part = pl.ds(x + 1 - STRIDE, STRIDE)
            for which, (src, dst) in enumerate(
                ((ustar.at[:, part], ustar_out.at[:, part]), (coef_cot.at[part], coef_out.at[part]))
            ):
                copies.append(pltpu.make_async_copy(src, dst, sem.at[which, x // STRIDE]))
                copies[-1].start()
    for copy in copies:
        copy.wait()


def on_device(phase, press, vel):
    nx, ny, nz = phase.shape
    total, height = nx + 2 * DEPTH, ny + 2 * DEPTH
    groups = total // ROWS
    devices = lax.axis_size(AXES)
    n_x, n_y, n_z = (turns(axis) for axis in AXES)
    f32 = lambda *shape: jax.ShapeDtypeStruct(shape, jnp.float32)
    scratch = lambda *shape: pltpu.VMEM(shape, jnp.float32)
    inputs = [pltpu.with_memory_space_constraint(array, pltpu.HBM) for array in (phase, press, vel)]

    def call(kernel, args, in_specs, shapes, name, scratch_shapes=(), out_spec=VMEM, aliases={}):
        return pl.pallas_call(
            kernel,
            out_shape=shapes,
            in_specs=in_specs,
            out_specs=[out_spec] * len(shapes),
            scratch_shapes=list(scratch_shapes),
            input_output_aliases=aliases,
            compiler_params=PARAMS,
            cost_estimate=pl.CostEstimate(flops=3_000_000, bytes_accessed=3_000_000, transcendentals=0),
            name=name,
        )(*args)

    odd = n_y > 1
    sent = call(
        functools.partial(pack_first, nx, ny, n_x, n_y),
        inputs,
        [HBM] * 3,
        [f32(VY * ny + 2 * ROWS, nz)] * n_x
        + ([f32(nx + nx // ROWS + 2, ROWS, nz)] + [f32(DEPTH + 2, ROWS, nz)] * n_x if odd else []),
        "pack_first",
        (
            [pltpu.VMEM((nx, ROWS, nz), jnp.int32), scratch(3, nx, ROWS, nz), scratch(nx, ROWS, nz)]
            + [pltpu.SemaphoreType.DMA((3,))]
            if odd
            else []
        )
        + [pltpu.VMEM((n_x, DEPTH, ny, nz), jnp.int32), scratch(n_x, 3, DEPTH, ny, nz)]
        + [pltpu.SemaphoreType.DMA((n_x, 3))],
    )
    to_x = sent[:n_x]
    got_x = [exchange(send, ("gx", turn)) for turn, send in enumerate(to_x)]
    if odd:
        got_odd = exchange(sent[n_x], ("gy", 1))
        corners = [exchange(send, ("gx", turn), ("gy", 1)) for turn, send in enumerate(sent[n_x + 1 :])]
    coef, press, vel, rhs = call(
        load,
        inputs + [to_x[0]],
        [HBM] * 3 + [ANY],
        [f32(*press.shape), f32(*press.shape), f32(*vel.shape), f32(*press.shape)],
        "load",
        [pltpu.VMEM(phase.shape, jnp.int32), pltpu.SemaphoreType.DMA((3,))],
    )
    rows_y = f32(total + nx // ROWS + 1, ROWS, nz)
    got_y, odd_rows, from_odd = [], [], []
    if odd:
        from_odd = [got_odd, *corners[::-1]]
        odd_rows = call(
            functools.partial(merge_odd, nx),
            from_odd,
            [VMEM] * (1 + n_x),
            [rows_y],
            "merge_odd",
        )
    if n_y:
        to_y = call(
            functools.partial(pack_y, nx, ny, n_x),
            [coef, press, vel, rhs, *got_x, *from_odd],
            [VMEM] * (4 + n_x) + [ANY] * len(from_odd),
            [rows_y],
            "pack_y",
        )
        got_y = [exchange(to_y[0], ("gy", 0)), *odd_rows]
    cube = (total, height, nz)
    packs = [f32(groups // 2 + 1, height, LANES)] * n_z
    staged = call(
        functools.partial(stage_z, nx, ny, n_x, n_z),
        [coef, press, vel, rhs, *got_x, *odd_rows],
        [VMEM] * (4 + n_x + len(odd_rows)),
        [f32(*cube)] * 2 + packs,
        "stage_z",
    )
    full_coef, full_rhs, *to_z = call(
        functools.partial(pack_z, nx, ny, n_x, n_z),
        [vel, *got_x, got_y[0], *staged],
        [VMEM] * (4 + n_x + n_z),
        [f32(*cube)] * 2 + packs,
        "pack_z",
        aliases={2 + n_x + which: which for which in range(2 + n_z)},
    )
    got_z = [exchange(send, ("gz", turn)) for turn, send in enumerate(to_z)]
    basis, ends, shares = call(
        functools.partial(prepare, nx, ny, n_x, n_y),
        [coef, vel, rhs, full_coef, full_rhs, *got_x, *got_y],
        [VMEM] * (5 + n_x + n_y),
        [f32(3, *cube), f32(5, groups, height, LANES), f32(6, ROWS, LANES)],
        "prepare",
        [scratch(*cube), scratch(2, *cube), scratch(2, *cube), scratch(*cube)],
    )
    slope = call(
        functools.partial(slopes, nx, ny, n_x, n_y),
        [press, vel, *got_x, *got_y],
        [VMEM] * (2 + n_x + n_y),
        [f32(nx + 1, ny, nz), f32(2, nx, ny, nz), f32(2, nx, ny, nz), f32(nx, ny, nz)],
        "slopes",
    )
    shapes_z = [f32(3, 2 * groups, height, LANES), f32(groups, height, LANES), f32(6, ROWS, LANES)]
    scratch_z = [scratch(6, groups, height, LANES), scratch(groups, height, LANES)]
    outer = call(
        functools.partial(outer_ends, nx, ny),
        [ends, shares],
        [VMEM] * 2,
        shapes_z,
        "outer_ends",
        scratch_z,
    )
    basis_z, vz_z, _, sums = call(
        functools.partial(join, nx, ny, n_z),
        [slope[-1], ends, *got_z, *outer],
        [ANY] + [VMEM] * (4 + n_z),
        shapes_z + [f32(1, LANES)],
        "join",
        scratch_z,
        aliases={2 + n_z + which: which for which in range(3)},
    )
    spread = jnp.broadcast_to(sums[None], (devices, 1, LANES))
    gathered = lax.all_to_all(spread, AXES, 0, 0).reshape(devices, LANES)
    return call(
        functools.partial(finish, nx, ny, n_z),
        [gathered, vel, basis, basis_z, vz_z, *slope, *got_z],
        [VMEM] * (9 + n_z),
        [f32(*vel.shape), f32(nx, ny, nz)],
        "finish",
        [scratch(*vel.shape), scratch(nx, ny, nz), pltpu.SemaphoreType.DMA((2, nx // STRIDE))],
        HBM,
    )


def solution(mesh):
    cells, faces = P(*AXES), P(None, *AXES)
    return jax.shard_map(
        on_device, mesh=mesh, in_specs=(cells, cells, faces), out_specs=(faces, cells), check_vma=False
    )
```

```python
import functools
import itertools

import jax
import jax.numpy as jnp
from jax import lax
from jax.experimental import pallas as pl
from jax.experimental.pallas import tpu as pltpu
from jax.sharding import PartitionSpec as P

AXES = ("gx", "gy", "gz")
SPARE = dict(gx="gy", gy="gz", gz="gx")
DEPTH = 4
GROUP = 4 * DEPTH
LANES = 128
STRIDE = 4
ROWS = 8
VMEM = pl.BlockSpec(memory_space=pltpu.VMEM)
HBM = pl.BlockSpec(memory_space=pltpu.HBM)
ANY = pl.BlockSpec(memory_space=pl.ANY)
PARAMS = pltpu.CompilerParams(vmem_limit_bytes=40 * 1024 * 1024)


def swaps(moves):
    sizes = [lax.axis_size(name) for name in AXES]
    number = lambda place: (place[0] * sizes[1] + place[1]) * sizes[2] + place[2]
    spare = AXES.index("gz" if len(moves) > 1 else SPARE[moves[0][0]])
    pairs = []
    for place in itertools.product(*map(range, sizes)):
        partner, met = list(place), True
        for axis, turn in moves:
            along = AXES.index(axis)
            partner[along] += 1 if (place[along] - turn) % 2 == 0 else -1
            met = met and 0 <= partner[along] < sizes[along]
        if not met:
            if sizes[spare] % 2:
                continue
            partner = list(place)
            partner[spare] ^= 1
        pairs.append((number(place), number(partner)))
    return pairs


def exchange(send, *moves):
    return lax.ppermute(send, AXES, swaps(moves))


def clear_if_alone(out, *moves):
    for axis, turn in moves:
        count, place = lax.axis_size(axis), lax.axis_index(axis)
        alone = []
        if turn == 1:
            alone.append(place == 0)
        if count % 2 != turn:
            alone.append(place == count - 1)
        for case in alone:

            @pl.when(case)
            def _():
                out[...] = jnp.zeros(out.shape, out.dtype)


def even(axis):
    return lax.axis_index(axis) % 2 == 0


def turns(axis):
    return min(2, lax.axis_size(axis) - 1)


def coefficient(phase):
    return jnp.where(phase == 0, 8.0, jnp.where(phase == 1, 1.0, 2.0)).astype(jnp.float32)


def sides(is_even, got, load):
    one = load(got[0])
    two = load(got[1]) if len(got) > 1 else jnp.zeros_like(one)
    return jnp.where(is_even, two, one), jnp.where(is_even, one, two)


def lane_index(shape):
    return lax.broadcasted_iota(jnp.int32, shape, len(shape) - 1)


def row_index(shape):
    return lax.broadcasted_iota(jnp.int32, shape, len(shape) - 2)


def roll_rows(plane, shift):
    return pltpu.roll(plane, shift % plane.shape[0], 0)


def roll_lanes(plane, shift):
    return pltpu.roll(plane, shift % plane.shape[1], 1)


def inner_rhs(coef, vy, vz):
    rows, lanes = row_index(coef.shape), lane_index(coef.shape)
    up = jnp.where(rows == coef.shape[0] - 1, 0.0, 0.5 * (coef + roll_rows(coef, -1)))
    down = jnp.where(rows == 0, 0.0, 0.5 * (coef + roll_rows(coef, 1)))
    right = jnp.where(lanes == LANES - 1, 0.0, 0.5 * (coef + roll_lanes(coef, -1)))
    left = jnp.where(lanes == 0, 0.0, 0.5 * (coef + roll_lanes(coef, 1)))
    return (up * vy - down * roll_rows(vy, 1)) + (right * vz - left * roll_lanes(vz, 1))


RHS, VX, PRESS, VY = DEPTH, 2 * DEPTH - 1, 2 * DEPTH, 2 * DEPTH + 1


def pack_first(nx, ny, n_x, n_y, phase, press, vel, *refs):
    outs, odd_outs, (held, held_vel, sem) = refs[:n_x], refs[n_x:-3], refs[-3:]
    if n_y > 1:
        *odd_outs, tile_phase, tile_vel, tile_press, tile_sem = odd_outs
    copies, late = [], []
    for turn, out in enumerate(outs):
        top = even("gx") == (turn == 0)
        deep = jnp.where(top, nx - DEPTH, 0)
        last = jnp.where(top, nx - 1, 0)
        parts = [
            (vel.at[:, pl.ds(deep, DEPTH)], held_vel.at[turn]),
            (phase.at[pl.ds(deep, DEPTH)], held.at[turn]),
            (press.at[last], out.at[pl.ds(PRESS * ny, ny)]),
        ]
        for which, (src, dst) in enumerate(parts):
            copy = pltpu.make_async_copy(src, dst, sem.at[turn, which])
            copy.start()
            copies.append(copy)
    if n_y > 1:
        row = pl.multiple_of(jnp.where(even("gy"), 0, ny - ROWS), ROWS)
        parts = [
            (phase.at[:, pl.ds(row, ROWS)], tile_phase),
            (vel.at[:, :, pl.ds(row, ROWS)], tile_vel),
            (press.at[:, pl.ds(row, ROWS)], tile_press),
        ]
        for which, (src, dst) in enumerate(parts):
            copy = pltpu.make_async_copy(src, dst, tile_sem.at[which])
            copy.start()
            late.append(copy)
    lanes = lane_index((ROWS, LANES))
    rows = row_index((ROWS, LANES))
    for turn, out in enumerate(outs):
        for copy in copies[3 * turn : 3 * turn + 3]:
            copy.wait()
        top = even("gx") == (turn == 0)
        coefs = [coefficient(held[turn, j]) for j in range(DEPTH)]
        flux = [0.5 * (coefs[j] + coefs[j + 1]) * held_vel[turn, 0, j] for j in range(DEPTH - 1)]
        columns = jnp.zeros((ROWS, LANES), jnp.float32)
        lines = jnp.zeros((ROWS, LANES), jnp.float32)
        for j in range(DEPTH):
            out[j * ny : (j + 1) * ny, :] = coefs[j]
        for j in range(DEPTH - 1):
            vy = jnp.where(top, held_vel[turn, 1, j + 1], held_vel[turn, 1, j])
            vz = jnp.where(top, held_vel[turn, 2, j + 1], held_vel[turn, 2, j])
            upper = (flux[j + 1] - flux[j]) if j + 1 < DEPTH - 1 else -flux[j]
            lower = (flux[j] - flux[j - 1]) if j else flux[j]
            inner = inner_rhs(jnp.where(top, coefs[j + 1], coefs[j]), vy, vz)
            out[(RHS + j) * ny : (RHS + j + 1) * ny, :] = jnp.where(top, upper, lower) + inner
            for t in range(ny // ROWS):
                lane = DEPTH * t + j
                columns = jnp.where(lanes == lane, roll_lanes(vz[t * ROWS : (t + 1) * ROWS], lane + 1), columns)
            lines = jnp.where(rows == j, roll_rows(vy[ny - ROWS :], j + 1), lines)
        out[VX * ny : (VX + 1) * ny, :] = held_vel[turn, 0, DEPTH - 1]
        out[VY * ny : VY * ny + ROWS, :] = lines
        out[VY * ny + ROWS :, :] = columns
        clear_if_alone(out, ("gx", turn))
    for copy in late:
        copy.wait()
    if n_y > 1:
        pack_odd(nx, tile_phase, tile_vel, tile_press, odd_outs)


def row_tile(coef, rhs, vy, top):
    rows = row_index((ROWS, LANES))
    coef = jnp.where(top, roll_rows(coef, DEPTH), coef)
    rhs = jnp.where(top, roll_rows(rhs, -1), roll_rows(rhs, DEPTH))
    return jnp.where(rows == ROWS - 1, vy, jnp.where(rows < DEPTH, coef, rhs))


def pack_odd(nx, tile_phase, tile_vel, tile_press, outs):
    out, *corners = outs
    top = jnp.logical_not(even("gy"))
    lanes = lane_index((ROWS, LANES))
    ends_at, vx_at = nx + nx // ROWS, nx + nx // ROWS + 1
    ends = jnp.zeros((ROWS, LANES), jnp.float32)
    here, old_flux = coefficient(tile_phase[0]), None
    for x in range(nx):
        vy, vz = tile_vel[1, x], tile_vel[2, x]
        answer = inner_rhs(here, vy, vz)
        if old_flux is not None:
            answer = answer - old_flux
        coef = here
        if x + 1 < nx:
            above = coefficient(tile_phase[x + 1])
            old_flux = 0.5 * (here + above) * tile_vel[0, x]
            answer = answer + old_flux
            here = above
        out[x] = row_tile(coef, answer, vy, top)
        ends = jnp.where(lanes == x, roll_lanes(vz, x + 1), ends)
        tile = tile_press[x]
        at = nx + x // ROWS
        out[at, x % ROWS : x % ROWS + 1, :] = jnp.where(top, tile[ROWS - 1 : ROWS], tile[0:1])
    shift = lambda tile: jnp.where(top, roll_rows(tile, -1), roll_rows(tile, DEPTH))
    ends = jnp.where(top, roll_rows(ends, DEPTH - 1), ends)
    out[ends_at] = ends
    out[vx_at] = shift(tile_vel[0, nx - 1])
    for turn, corner in enumerate(corners):
        first = jnp.where(even("gx") == (turn == 0), nx - DEPTH, 0)
        for j in range(DEPTH):
            corner[j] = out[first + j]
        corner[DEPTH] = pltpu.roll(ends, jnp.where(first == 0, 0, (DEPTH - nx) % LANES), 1)
        corner[DEPTH + 1] = out[vx_at]
        clear_if_alone(corner, ("gx", turn), ("gy", 1))
    clear_if_alone(out, ("gy", 1))


def merge_odd(nx, got, *refs):
    corners, out = refs[:-1][::-1], refs[-1]
    total = nx + 2 * DEPTH
    rows, lanes = row_index((ROWS, LANES)), lane_index((ROWS, LANES))
    ends_at, vx_at = nx + nx // ROWS, nx + nx // ROWS + 1
    low, high = zip(*[sides(even("gx"), corners, lambda ref: ref[j]) for j in range(DEPTH + 2)])
    tiles = [got[x] for x in range(nx)] + list(high[:DEPTH]) + list(low[:DEPTH])
    inner = (rows >= DEPTH) & (rows < ROWS - 1)

    def face(below, above, vx):
        weight = 0.5 * (tiles[below] + tiles[above])
        weight = jnp.where(even("gy"), roll_rows(weight, DEPTH - 1), roll_rows(weight, DEPTH))
        return jnp.where(inner, weight * vx, 0.0)

    low_face, high_face = face(total - 1, 0, low[DEPTH + 1]), face(nx - 1, nx, got[vx_at])
    for plane, tile in enumerate(tiles):
        if plane == 0:
            tile = tile - low_face
        if plane == total - 1:
            tile = tile + low_face
        if plane == nx - 1:
            tile = tile + high_face
        if plane == nx:
            tile = tile - high_face
        out[plane] = tile
    for at in range(nx // ROWS):
        out[total + at] = got[nx + at]
    ends = jnp.where(lanes < nx, got[ends_at], roll_lanes(high[DEPTH], nx))
    out[total + nx // ROWS] = jnp.where(lanes < nx + DEPTH, ends, roll_lanes(low[DEPTH], nx + DEPTH))


def load(phase, press, vel, after, coef, press_out, vel_out, rhs, held, sem):
    del after
    copies = []
    for which, (src, dst) in enumerate(((phase, held), (press, press_out), (vel, vel_out))):
        copies.append(pltpu.make_async_copy(src, dst, sem.at[which]))
        copies[-1].start()
    copies[0].wait()
    copies[1].wait()
    copies[2].wait()
    nx = coef.shape[0]
    here = coefficient(held[0])
    old_flux = None
    for x in range(nx):
        coef[x] = here
        answer = inner_rhs(here, vel_out[1, x], vel_out[2, x])
        if old_flux is not None:
            answer = answer - old_flux
        if x + 1 < nx:
            above = coefficient(held[x + 1])
            old_flux = 0.5 * (here + above) * vel_out[0, x]
            answer = answer + old_flux
            here = above
        rhs[x] = answer


class Block:
    def __init__(self, nx, ny, coef, vel, rhs, got_x, row=0, height=None, faces=True):
        self.nx, self.ny = nx, ny
        self.own_coef, self.vel, self.own_rhs, self.got_x = coef, vel, rhs, got_x
        self.even = even("gx")
        self.row, self.height = row, height or ny
        if not faces:
            return
        self.low_face = 0.5 * (self.coef(nx + 2 * DEPTH - 1) + self.coef(0)) * self.halo(VX)[0]
        self.high_face = 0.5 * (self.coef(nx - 1) + self.coef(nx)) * self.take(vel, 0, nx - 1)

    def take(self, ref, *index):
        return ref[(*index, pl.ds(self.row, self.height), slice(None))]

    def halo(self, part):
        return sides(self.even, self.got_x, lambda ref: ref[pl.ds(part * self.ny + self.row, self.height), :])

    def coef(self, plane):
        if plane < self.nx:
            return self.take(self.own_coef, plane)
        above = plane < self.nx + DEPTH
        return self.halo((plane - self.nx) % DEPTH)[1 if above else 0]

    def rhs(self, plane):
        nx = self.nx
        if plane < nx:
            answer = self.take(self.own_rhs, plane)
        else:
            above = plane < nx + DEPTH
            layer = plane - nx if above else plane - nx - DEPTH - 1
            if layer < 0 or layer >= DEPTH - 1:
                return jnp.zeros((self.height, LANES), jnp.float32)
            answer = self.halo(RHS + layer)[1 if above else 0]
        if plane == 0:
            answer = answer - self.low_face
        if plane == nx + 2 * DEPTH - 1:
            answer = answer + self.low_face
        if plane == nx - 1:
            answer = answer + self.high_face
        if plane == nx:
            answer = answer - self.high_face
        return answer

    def layer(self, plane):
        if plane < self.nx + DEPTH:
            place = (1, plane - self.nx)
        else:
            place = (0, plane - self.nx - DEPTH - 1)
        return place if 0 <= place[1] < DEPTH - 1 else None

    def columns(self):
        at = VY * self.ny + ROWS
        return sides(self.even, self.got_x, lambda ref: ref[at : at + ROWS, :])

    def vz_end(self, plane, lane):
        if plane < self.nx:
            return roll_lanes(self.vel[2, plane], lane + 1)
        place = self.layer(plane)
        if place is None:
            return jnp.zeros((self.ny, LANES), jnp.float32)
        source = self.columns()[place[0]]
        return jnp.concatenate(
            [roll_lanes(source, lane - DEPTH * t - place[1]) for t in range(self.ny // ROWS)], 0
        )

    def vy_end(self, plane):
        if plane < self.nx:
            return self.vel[1, plane, self.ny - 1 :, :]
        place = self.layer(plane)
        if place is None:
            return jnp.zeros((1, LANES), jnp.float32)
        at = VY * self.ny + place[1]
        return sides(self.even, self.got_x, lambda ref: ref[at : at + 1, :])[place[0]]


def pack_y(nx, ny, n_x, coef, press, vel, rhs, *refs):
    got_x, out = refs[:n_x], refs[-1]
    total = nx + 2 * DEPTH
    lanes = lane_index((ROWS, LANES))
    top = even("gy")
    row = pl.multiple_of(jnp.where(top, ny - ROWS, 0), ROWS)
    block = Block(nx, ny, coef, vel, rhs, got_x, row, ROWS)
    columns = jnp.zeros((ROWS, LANES), jnp.float32)
    ends = block.columns()
    for plane in range(total):
        out[plane] = row_tile(block.coef(plane), block.rhs(plane), block.vy_end(plane), top)
        if plane < nx:
            source = roll_lanes(vel[2, plane, pl.ds(row, ROWS), :], plane + 1)
        elif block.layer(plane) is None:
            continue
        else:
            side, layer = block.layer(plane)
            high = (plane - layer - DEPTH * (ny // ROWS - 1)) % LANES
            source = pltpu.roll(ends[side], jnp.where(top, high, (plane - layer) % LANES), 1)
        columns = jnp.where(lanes == plane, source, columns)
    out[total + nx // ROWS] = jnp.where(top, roll_rows(columns, DEPTH - 1), columns)
    for plane in range(nx):
        tile = press[plane, pl.ds(row, ROWS), :]
        edge = jnp.where(top, tile[ROWS - 1 : ROWS], tile[0:1])
        out[total + plane // ROWS, plane % ROWS : plane % ROWS + 1, :] = edge
    clear_if_alone(out, ("gy", 0))


def tall_end(block, tile_end, plane, lane):
    return jnp.concatenate([block.vz_end(plane, lane), roll_lanes(tile_end, lane - plane)], 0)


def tile_of_ends(nx, even_y, got_y):
    rows = row_index((ROWS, LANES))
    low, high = sides(even_y, got_y, lambda ref: ref[nx + 2 * DEPTH + nx // ROWS])
    return jnp.where(rows < DEPTH, high, roll_rows(low, DEPTH + 1))


def press_lane(x):
    return GROUP * (x % ROWS) + ROWS + 2 * (x // ROWS)


def pack_plane(lanes, at, top, coef, rhs, end):
    coef = pltpu.roll(coef, jnp.where(top, (at + DEPTH) % LANES, at), 1)
    rhs = pltpu.roll(rhs, jnp.where(top, (at + ROWS - 1) % LANES, at + DEPTH), 1)
    value = jnp.where(lanes == at + ROWS - 1, end, 0.0)
    value = jnp.where((lanes >= at + DEPTH) & (lanes < at + ROWS - 1), rhs, value)
    return jnp.where((lanes >= at) & (lanes < at + DEPTH), coef, value)


def half_tile(tile, below):
    rows = row_index((ROWS, LANES))
    coef = jnp.where(below, jnp.where(rows >= DEPTH, roll_rows(tile, DEPTH), 0.0), jnp.where(rows < DEPTH, tile, 0.0))
    rhs = jnp.where(
        below,
        jnp.where(rows > DEPTH, roll_rows(tile, 1), 0.0),
        jnp.where(rows < DEPTH - 1, roll_rows(tile, -DEPTH), 0.0),
    )
    return coef, rhs


def half_ends(tile, below):
    rows = row_index((ROWS, LANES))
    return jnp.where(
        below, jnp.where(rows > DEPTH, roll_rows(tile, DEPTH + 1), 0.0), jnp.where(rows < DEPTH - 1, tile, 0.0)
    )


def face_y(own_low, own_high, coef_tile, tile, vy_end, below):
    rows = row_index((ROWS, LANES))
    down = 0.5 * (coef_tile[ROWS - 1 :] + own_low) * tile[ROWS - 1 :]
    up = 0.5 * (own_high + coef_tile[:1]) * vy_end
    outside = jnp.where(below, jnp.where(rows == ROWS - 1, down, 0.0), jnp.where(rows == 0, -up, 0.0))
    inside = jnp.where(below, jnp.where(rows == 0, -down, 0.0), jnp.where(rows == ROWS - 1, up, 0.0))
    return outside, inside


def stage_z(nx, ny, n_x, n_z, coef, press, vel, rhs, *refs):
    got_x, (*got_odd, full_coef, full_rhs), sends = refs[:n_x], refs[n_x : len(refs) - n_z], refs[len(refs) - n_z :]
    total, height = nx + 2 * DEPTH, ny + 2 * DEPTH
    groups = total // ROWS
    below = even("gy")
    lanes = lane_index((height, LANES))
    block = Block(nx, ny, coef, vel, rhs, got_x)
    nothing = jnp.zeros((ROWS, LANES), jnp.float32)
    tile_end = half_ends(got_odd[0][total + nx // ROWS], below) if got_odd else nothing
    made = [[jnp.zeros((height, LANES), jnp.float32) for _ in range(groups // 2 + 1)] for _ in sends]
    row = pl.ds(pl.multiple_of(jnp.where(below, 0, ny - ROWS), ROWS), ROWS)
    for plane in range(total):
        c_own, r_own = block.coef(plane), block.rhs(plane)
        c_tile = r_tile = nothing
        full_rhs[plane, :ny, :] = r_own
        if got_odd:
            tile = got_odd[0][plane]
            c_tile, r_tile = half_tile(tile, below)
            outside, inside = face_y(c_own[:1], c_own[ny - 1 :], c_tile, tile, block.vy_end(plane), below)
            r_tile = r_tile + outside
            full_rhs[plane, row, :] = full_rhs[plane, row, :] + inside
        c_all = jnp.concatenate([c_own, c_tile], 0)
        full_coef[plane] = c_all
        full_rhs[plane, ny:, :] = r_tile
        r_all = full_rhs[plane]
        group, seat = plane % groups, plane // groups
        at = GROUP * seat + ROWS * (group % 2)
        end = tall_end(block, tile_end, plane, at + ROWS - 1)
        for turn in range(n_z):
            value = pack_plane(lanes, at, even("gz") == (turn == 0), c_all, r_all, end)
            made[turn][group // 2] = made[turn][group // 2] + value
    for turn, send in enumerate(sends):
        top = even("gz") == (turn == 0)
        value = made[turn][groups // 2][:ny]
        for plane in range(nx):
            at = press_lane(plane)
            moved = pltpu.roll(press[plane], jnp.where(top, (at + 1) % LANES, at), 1)
            value = jnp.where(lanes[:ny] == at, moved, value)
        made[turn][groups // 2] = jnp.concatenate([value, made[turn][groups // 2][ny:]], 0)
        for which, value in enumerate(made[turn]):
            send[which] = value


def pack_z(nx, ny, n_x, n_z, vel, *refs):
    got_x, got, (full_coef, full_rhs, *sends) = refs[:n_x], refs[n_x], refs[-2 - n_z :]
    total = nx + 2 * DEPTH
    groups = total // ROWS
    below = jnp.logical_not(even("gy"))
    lanes = lane_index((ROWS, LANES))
    block = Block(nx, ny, full_coef, vel, full_rhs, got_x, faces=False)
    tile_end = half_ends(got[total + nx // ROWS], below)
    row = pl.ds(pl.multiple_of(jnp.where(below, 0, ny - ROWS), ROWS), ROWS)
    added = [[[jnp.zeros((ROWS, LANES), jnp.float32) for _ in range(2)] for _ in range(groups // 2 + 1)] for _ in sends]
    for plane in range(total):
        if plane in (nx + DEPTH - 1, nx + DEPTH):
            continue
        tile = got[plane]
        c_tile, r_tile = half_tile(tile, below)
        low, high = full_coef[plane, :1, :], full_coef[plane, ny - 1 : ny, :]
        outside, inside = face_y(low, high, c_tile, tile, block.vy_end(plane), below)
        r_tile = r_tile + outside
        full_coef[plane, ny:, :] = full_coef[plane, ny:, :] + c_tile
        full_rhs[plane, ny:, :] = full_rhs[plane, ny:, :] + r_tile
        full_rhs[plane, row, :] = full_rhs[plane, row, :] + inside
        group, seat = plane % groups, plane // groups
        at = GROUP * seat + ROWS * (group % 2)
        end = roll_lanes(tile_end, at + ROWS - 1 - plane)
        for turn in range(n_z):
            top = even("gz") == (turn == 0)
            inside_move = pltpu.roll(inside, jnp.where(top, (at + ROWS - 1) % LANES, at + DEPTH), 1)
            inside_move = jnp.where((lanes >= at + DEPTH) & (lanes < at + ROWS - 1), inside_move, 0.0)
            slot = added[turn][group // 2]
            slot[0] = slot[0] + pack_plane(lanes, at, top, c_tile, r_tile, end)
            slot[1] = slot[1] + inside_move
    for turn, send in enumerate(sends):
        for which, (tile, inside) in enumerate(added[turn]):
            send[which, ny:, :] = send[which, ny:, :] + tile
            send[which, row, :] = send[which, row, :] + inside
        clear_if_alone(send, ("gz", turn))


def tree_sum(parts):
    while len(parts) > 1:
        parts = [parts[i] + parts[i + 1] if i + 1 < len(parts) else parts[i] for i in range(0, len(parts), 2)]
    return parts[0]


class Totals:
    def __init__(self):
        self.stack = []

    def add(self, tile):
        level = 0
        while self.stack and self.stack[-1][0] == level:
            tile = self.stack.pop()[1] + tile
            level += 1
        self.stack.append((level, tile))

    def value(self):
        tiles = [tile for _, tile in self.stack]
        total = tiles.pop()
        while tiles:
            total = tiles.pop() + total
        return total


def prepare(nx, ny, n_x, n_y, coef, vel, rhs, full_coef, full_rhs, *refs):
    got_x, got_y = refs[:n_x], refs[n_x : n_x + n_y]
    basis, ends, shares, wx, wy, wz, inverse = refs[n_x + n_y :]
    total, height = nx + 2 * DEPTH, ny + 2 * DEPTH
    groups = total // ROWS
    lanes = lane_index((height, LANES))
    block = Block(nx, ny, coef, vel, rhs, got_x)
    tile_end = tile_of_ends(nx, even("gy"), got_y)
    for group in range(groups):
        made = [jnp.zeros((height, LANES), jnp.float32) for _ in range(5)]
        for seat in range(ROWS):
            plane = seat * groups + group
            at = GROUP * seat
            for which, source in enumerate((full_coef[plane], full_rhs[plane])):
                here = (lanes >= at + DEPTH) & (lanes < at + GROUP)
                made[2 * which] = jnp.where(here, roll_lanes(source, at + DEPTH), made[2 * which])
                here = (lanes >= at) & (lanes < at + GROUP - DEPTH)
                made[2 * which + 1] = jnp.where(here, roll_lanes(source, at + GROUP - DEPTH), made[2 * which + 1])
            lane = at + GROUP - DEPTH - 1
            made[4] = jnp.where(lanes == lane, tall_end(block, tile_end, plane, lane), made[4])
        for which in range(5):
            ends[which, group] = made[which]
    totals = [Totals() for _ in range(6)]
    trusted = (lanes[:ROWS] >= DEPTH) & (lanes[:ROWS] < LANES - DEPTH)

    def count(which, left, right):
        product = left[:ny] * right[:ny]
        tile = tree_sum([product[i : i + ROWS] for i in range(0, ny, ROWS)])
        totals[which].add(jnp.where(trusted, tile, 0.0))

    old_weight = None
    here = full_coef[nx + DEPTH]
    for x in range(-DEPTH, nx + DEPTH - 1):
        e = x % total
        above = full_coef[(e + 1) % total]
        weight = 0.5 * (here + above)
        wx[e] = weight
        if x > -DEPTH:
            up, down = 0.5 * (here + roll_rows(here, -1)), 0.5 * (here + roll_rows(here, 1))
            right = jnp.where(lanes == LANES - 1, 0.0, 0.5 * (here + roll_lanes(here, -1)))
            left = jnp.where(lanes == 0, 0.0, 0.5 * (here + roll_lanes(here, 1)))
            wy[0, e], wy[1, e], wz[0, e], wz[1, e] = up, down, right, left
            diag = (weight + old_weight) + (up + down) + (right + left)
            inside = here > 0
            scale = jnp.where(inside, 1.0 / jnp.where(inside, diag, 1.0), 0.0)
            inverse[e] = scale
            source = full_rhs[e]
            field = scale * source
            basis[0, e] = field
            if 0 <= x < nx:
                count(0, field, source)
        old_weight, here = weight, above
    for n in range(3):
        reach = 2 - n
        old_flux = None
        here = basis[n, (-reach - 1) % total]
        for x in range(-reach - 1, nx + reach):
            e = x % total
            above = basis[n, (e + 1) % total]
            flux = wx[e] * (above - here)
            if x >= -reach:
                image = old_flux - flux
                image = image + (
                    wy[0, e] * (here - roll_rows(here, -1)) + wy[1, e] * (here - roll_rows(here, 1))
                )
                image = image + (
                    wz[0, e] * (here - roll_lanes(here, -1)) + wz[1, e] * (here - roll_lanes(here, 1))
                )
                own = 0 <= x < nx
                if own:
                    count(2 * n + 1, here, image)
                if n < 2:
                    following = inverse[e] * image
                    basis[n + 1, e] = following
                    if own:
                        count(2 * n + 2, following, image)
            old_flux, here = flux, above
    for which, total_ in enumerate(totals):
        shares[which] = total_.value()


def beside_z(side):
    place = lax.axis_index("gz")
    return place > 0 if side == 0 else place < lax.axis_size("gz") - 1


def solve_end(nx, ny, side, received, ends, basis_z, vz_z, shares, weight_z, inverse_z):
    total, height = nx + 2 * DEPTH, ny + 2 * DEPTH
    groups = total // ROWS
    lanes = lane_index((height, LANES))
    seat_lane, seat = lanes % GROUP, lanes // GROUP
    outer = seat_lane < DEPTH if side == 0 else seat_lane >= GROUP - DEPTH
    coef, rhs, vz = [], [], []
    for g in range(groups):
        got, skip = received(g // 2), ROWS * (g % 2)
        start = 0 if side == 0 else GROUP - DEPTH
        less = 1 if side == 0 else 0
        coef.append(jnp.where(outer, roll_lanes(got, start - skip), ends[side, g]))
        rhs.append(jnp.where(outer, roll_lanes(got, start + less - DEPTH - skip), ends[2 + side, g]))
        if side == 0:
            vz.append(roll_lanes(got, -DEPTH - skip))
            vz_z[g] = vz[-1]
        else:
            vz.append(ends[4, g])

    def along(planes, g, step):
        if 0 <= g + step < groups:
            return planes[g + step]
        return roll_lanes(planes[(g + step) % groups], -GROUP * step)

    totals = [Totals() for _ in range(6)]

    def count(which, g, left, right):
        first = DEPTH if side == 0 else GROUP - 2 * DEPTH
        spot = seat_lane[:ROWS]
        mine = (spot >= first) & (spot < first + DEPTH) & (seat[:ROWS] * groups + g < nx)
        product = left[:ny] * right[:ny]
        tile = tree_sum([product[i : i + ROWS] for i in range(0, ny, ROWS)])
        totals[which].add(jnp.where(mine, tile, 0.0))

    field = []
    for g in range(groups):
        here, q = coef[g], side * groups + g
        neighbours = (along(coef, g, 1), along(coef, g, -1), roll_rows(here, -1), roll_rows(here, 1))
        neighbours += (roll_lanes(here, -1), roll_lanes(here, 1))
        weights = [0.5 * (here + other) for other in neighbours]
        for which, weight in enumerate(weights):
            weight_z[which, g] = weight
        diag = (weights[0] + weights[1]) + (weights[2] + weights[3]) + (weights[4] + weights[5])
        face = DEPTH - 1 if side == 0 else GROUP - DEPTH - 1
        source = rhs[g] + jnp.where(seat_lane == face, weights[4] * vz[g], 0.0)
        source = source - jnp.where(seat_lane == face + 1, weights[5] * roll_lanes(vz[g], 1), 0.0)
        inside = here > 0
        scale = jnp.where(inside, 1.0 / jnp.where(inside, diag, 1.0), 0.0)
        inverse_z[g] = scale
        field.append(scale * source)
        basis_z[0, q] = field[g]
        count(0, g, field[g], source)
    for n in range(3):
        following = []
        for g in range(groups):
            here, q = field[g], side * groups + g
            image = weight_z[0, g] * (here - along(field, g, 1)) + weight_z[1, g] * (here - along(field, g, -1))
            image = image + (
                weight_z[2, g] * (here - roll_rows(here, -1)) + weight_z[3, g] * (here - roll_rows(here, 1))
            )
            image = image + (
                weight_z[4, g] * (here - roll_lanes(here, -1)) + weight_z[5, g] * (here - roll_lanes(here, 1))
            )
            count(2 * n + 1, g, here, image)
            if n < 2:
                following.append(inverse_z[g] * image)
                basis_z[n + 1, q] = following[g]
                count(2 * n + 2, g, following[g], image)
        field = following
    for which, total_ in enumerate(totals):
        shares[which] = shares[which] + total_.value()


def outer_ends(nx, ny, ends, shares_in, basis_z, vz_z, shares, *scratch):
    shares[...] = shares_in[...]
    nothing = jnp.zeros((ny + 2 * DEPTH, LANES), jnp.float32)
    for side in range(2):

        @pl.when(jnp.logical_not(beside_z(side)))
        def _():
            solve_end(nx, ny, side, lambda i: nothing, ends, basis_z, vz_z, shares, *scratch)


def join(nx, ny, n_z, after, ends, *refs):
    del after
    got_z, (basis_z, vz_z, shares, sums, *scratch) = refs[:n_z], refs[n_z + 3 :]
    for side in range(2):

        @pl.when(beside_z(side))
        def _():
            received = lambda i: sides(even("gz"), got_z, lambda ref: ref[i])[side]
            solve_end(nx, ny, side, received, ends, basis_z, vz_z, shares, *scratch)

    rows, lanes = row_index((ROWS, LANES)), lane_index((ROWS, LANES))
    table = jnp.zeros((ROWS, LANES), jnp.float32)
    for which in range(6):
        table = jnp.where(rows == which, jnp.sum(shares[which], 0, keepdims=True), table)
    table = jnp.where(rows == lanes, jnp.sum(table, 1, keepdims=True), 0.0)
    sums[...] = jnp.sum(table, 0, keepdims=True)


def slopes(nx, ny, n_x, n_y, press, vel, *refs):
    got_x, got_y, (slope_x, slope_y, slope_z, base) = refs[:n_x], refs[n_x : n_x + n_y], refs[n_x + n_y :]
    total = nx + 2 * DEPTH
    rows, shape = row_index((ROWS, LANES)), (ROWS, LANES)
    lanes = lane_index((ny, LANES))
    at_low, at_high = lanes == 0, lanes == LANES - 1
    p_low, p_high = sides(even("gx"), got_x, lambda ref: ref[PRESS * ny : (PRESS + 1) * ny, :])
    u_low, _ = sides(even("gx"), got_x, lambda ref: ref[VX * ny : (VX + 1) * ny, :])
    old = p_low - press[0]
    slope_x[0] = old
    old = old * u_low
    for x in range(nx):
        p = press[x]
        slope = p - (press[x + 1] if x + 1 < nx else p_high)
        slope_x[x + 1] = slope
        new = slope * vel[0, x]
        answer, old = old + new, new
        low, high = sides(even("gy"), got_y, lambda ref: ref[total + x // ROWS, x % ROWS : x % ROWS + 1, :])
        p_tile = jnp.where(rows == 0, jnp.broadcast_to(high, shape), jnp.broadcast_to(low, shape))
        p_tall = jnp.concatenate([p, p_tile], 0)
        u_row, _ = sides(even("gy"), got_y, lambda ref: ref[x, ROWS - 1 :, :])
        u_tall = jnp.concatenate([vel[1, x], jnp.broadcast_to(u_row, shape)], 0)
        up, down = p - roll_rows(p_tall, -1)[:ny], roll_rows(p_tall, 1)[:ny] - p
        slope_y[0, x], slope_y[1, x] = up, down
        answer = answer + (up * vel[1, x] + down * roll_rows(u_tall, 1)[:ny])
        up = p - jnp.where(at_high, 0.0, roll_lanes(p, -1))
        down = jnp.where(at_low, 0.0, roll_lanes(p, 1)) - p
        slope_z[0, x], slope_z[1, x] = up, down
        base[x] = answer + (up * vel[2, x] + down * jnp.where(at_low, 0.0, roll_lanes(vel[2, x], 1)))


def finish(nx, ny, n_z, gathered, vel, basis, basis_z, vz_z, slope_x, slope_y, slope_z, base, *refs):
    got_z, (ustar_out, coef_out, ustar, coef_cot, sem) = refs[:n_z], refs[n_z:]
    total, height = nx + 2 * DEPTH, ny + 2 * DEPTH
    groups = total // ROWS
    parts = gathered[...]
    while parts.shape[0] > ROWS:
        half = parts.shape[0] // 2
        parts = parts[:half] + parts[half:]
    sums = jnp.sum(parts, 0, keepdims=True)
    shape = (ROWS, LANES)
    table = jnp.sum(jnp.where(row_index(shape) == lane_index(shape), sums, 0.0), 1, keepdims=True)
    m0, m1, m2, m3, m4, m5 = [table[which : which + 1] for which in range(6)]
    l1, l2 = m2 / m1, m3 / m1
    d1, cross, d2 = m3 - l1 * m2, m4 - l1 * m3, m5 - l2 * m3
    l21 = cross / d1
    d2 = d2 - l21 * cross
    y1 = -l1 * m0 + m1
    y2 = m2 - l2 * m0 - l21 * y1
    c2 = y2 / d2
    c1 = y1 / d1 - l21 * c2
    c0 = (m0 / m1 - l1 * c1 - l2 * c2)[0, 0]
    c1, c2 = c1[0, 0], c2[0, 0]

    lanes = lane_index((height, LANES))
    seat_lane = lanes % GROUP
    spill = []
    for g in range(groups):
        low, high = [
            c0 * basis_z[0, q] + c1 * basis_z[1, q] + c2 * basis_z[2, q] for q in (g, groups + g)
        ]
        cells = jnp.where(seat_lane < DEPTH - 1, roll_lanes(high, DEPTH - GROUP + DEPTH - 1), roll_lanes(low, -1))
        cells = jnp.where(seat_lane == 2 * DEPTH - 2, roll_lanes(high, 2 * DEPTH - 2 - (GROUP - DEPTH)), cells)
        spill.append(jnp.where(seat_lane == 2 * DEPTH - 1, roll_lanes(low, DEPTH), cells))
    spoiled = (lanes < DEPTH - 1) | (lanes > LANES - DEPTH)
    lanes = lane_index((ny, LANES))
    at_low, at_high = lanes == 0, lanes == LANES - 1
    low_z, high_z = sides(even("gz"), got_z, lambda ref: ref[groups // 2, :ny, :])
    press_z = jnp.where(lanes % 2 == 0, high_z, roll_lanes(low_z, 1))

    def solved(x):
        e = x % total
        cells = c0 * basis[0, e] + c1 * basis[1, e] + c2 * basis[2, e]
        return jnp.where(spoiled, roll_lanes(spill[e % groups], 1 - DEPTH - GROUP * (e // groups)), cells)

    copies = []
    below, here = solved(-1), solved(0)
    down = here[:ny] - below[:ny]
    for x in range(nx):
        above = solved(x + 1)
        group, seat = x % groups, x // groups
        own = here[:ny]
        up = above[:ny] - own
        ustar[0, x] = vel[0, x] + up
        answer = base[x] + (slope_x[x + 1] * up + slope_x[x] * down)
        next_down = up
        up, down = roll_rows(here, -1)[:ny] - own, own - roll_rows(here, 1)[:ny]
        ustar[1, x] = vel[1, x] + up
        answer = answer + (slope_y[0, x] * up + slope_y[1, x] * down)
        lam_end = roll_lanes(spill[group][:ny], 1 - 2 * DEPTH - GROUP * seat)
        u_end = roll_lanes(vz_z[group, :ny, :], 1 - DEPTH - GROUP * seat)
        p_end = roll_lanes(press_z, LANES - 1 - press_lane(x))
        up = jnp.where(at_high, lam_end, roll_lanes(own, -1)) - own
        down = own - jnp.where(at_low, lam_end, roll_lanes(own, 1))
        out = vel[2, x] + up
        ustar[2, x] = out
        answer = answer + (slope_z[0, x] * up + slope_z[1, x] * down)
        beyond = jnp.where(at_low, p_end * (u_end + down) + slope_z[1, x] * u_end, 0.0)
        answer = answer + jnp.where(at_high, -p_end * out, beyond)
        down = next_down
        coef_cot[x] = 0.5 * answer
        here = above
        if (x + 1) % STRIDE == 0:
            part = pl.ds(x + 1 - STRIDE, STRIDE)
            for which, (src, dst) in enumerate(
                ((ustar.at[:, part], ustar_out.at[:, part]), (coef_cot.at[part], coef_out.at[part]))
            ):
                copies.append(pltpu.make_async_copy(src, dst, sem.at[which, x // STRIDE]))
                copies[-1].start()
    for copy in copies:
        copy.wait()


def on_device(phase, press, vel):
    nx, ny, nz = phase.shape
    total, height = nx + 2 * DEPTH, ny + 2 * DEPTH
    groups = total // ROWS
    devices = lax.axis_size(AXES)
    n_x, n_y, n_z = (turns(axis) for axis in AXES)
    f32 = lambda *shape: jax.ShapeDtypeStruct(shape, jnp.float32)
    scratch = lambda *shape: pltpu.VMEM(shape, jnp.float32)
    inputs = [pltpu.with_memory_space_constraint(array, pltpu.HBM) for array in (phase, press, vel)]

    def call(kernel, args, in_specs, shapes, name, scratch_shapes=(), out_spec=VMEM, aliases={}):
        return pl.pallas_call(
            kernel,
            out_shape=shapes,
            in_specs=in_specs,
            out_specs=[out_spec] * len(shapes),
            scratch_shapes=list(scratch_shapes),
            input_output_aliases=aliases,
            compiler_params=PARAMS,
            cost_estimate=pl.CostEstimate(flops=3_000_000, bytes_accessed=3_000_000, transcendentals=0),
            name=name,
        )(*args)

    odd = n_y > 1
    sent = call(
        functools.partial(pack_first, nx, ny, n_x, n_y),
        inputs,
        [HBM] * 3,
        [f32(VY * ny + 2 * ROWS, nz)] * n_x
        + ([f32(nx + nx // ROWS + 2, ROWS, nz)] + [f32(DEPTH + 2, ROWS, nz)] * n_x if odd else []),
        "pack_first",
        (
            [pltpu.VMEM((nx, ROWS, nz), jnp.int32), scratch(3, nx, ROWS, nz), scratch(nx, ROWS, nz)]
            + [pltpu.SemaphoreType.DMA((3,))]
            if odd
            else []
        )
        + [pltpu.VMEM((n_x, DEPTH, ny, nz), jnp.int32), scratch(n_x, 3, DEPTH, ny, nz)]
        + [pltpu.SemaphoreType.DMA((n_x, 3))],
    )
    to_x = sent[:n_x]
    got_x = [exchange(send, ("gx", turn)) for turn, send in enumerate(to_x)]
    if odd:
        got_odd = exchange(sent[n_x], ("gy", 1))
        corners = [exchange(send, ("gx", turn), ("gy", 1)) for turn, send in enumerate(sent[n_x + 1 :])]
    coef, press, vel, rhs = call(
        load,
        inputs + [to_x[0]],
        [HBM] * 3 + [ANY],
        [f32(*press.shape), f32(*press.shape), f32(*vel.shape), f32(*press.shape)],
        "load",
        [pltpu.VMEM(phase.shape, jnp.int32), pltpu.SemaphoreType.DMA((3,))],
    )
    rows_y = f32(total + nx // ROWS + 1, ROWS, nz)
    got_y, odd_rows, from_odd = [], [], []
    if odd:
        from_odd = [got_odd, *corners[::-1]]
        odd_rows = call(
            functools.partial(merge_odd, nx),
            from_odd,
            [VMEM] * (1 + n_x),
            [rows_y],
            "merge_odd",
        )
    if n_y:
        to_y = call(
            functools.partial(pack_y, nx, ny, n_x),
            [coef, press, vel, rhs, *got_x, *from_odd],
            [VMEM] * (4 + n_x) + [ANY] * len(from_odd),
            [rows_y],
            "pack_y",
        )
        got_y = [exchange(to_y[0], ("gy", 0)), *odd_rows]
    cube = (total, height, nz)
    packs = [f32(groups // 2 + 1, height, LANES)] * n_z
    staged = call(
        functools.partial(stage_z, nx, ny, n_x, n_z),
        [coef, press, vel, rhs, *got_x, *odd_rows],
        [VMEM] * (4 + n_x + len(odd_rows)),
        [f32(*cube)] * 2 + packs,
        "stage_z",
    )
    full_coef, full_rhs, *to_z = call(
        functools.partial(pack_z, nx, ny, n_x, n_z),
        [vel, *got_x, got_y[0], *staged],
        [VMEM] * (4 + n_x + n_z),
        [f32(*cube)] * 2 + packs,
        "pack_z",
        aliases={2 + n_x + which: which for which in range(2 + n_z)},
    )
    got_z = [exchange(send, ("gz", turn)) for turn, send in enumerate(to_z)]
    basis, ends, shares = call(
        functools.partial(prepare, nx, ny, n_x, n_y),
        [coef, vel, rhs, full_coef, full_rhs, *got_x, *got_y],
        [VMEM] * (5 + n_x + n_y),
        [f32(3, *cube), f32(5, groups, height, LANES), f32(6, ROWS, LANES)],
        "prepare",
        [scratch(*cube), scratch(2, *cube), scratch(2, *cube), scratch(*cube)],
    )
    slope = call(
        functools.partial(slopes, nx, ny, n_x, n_y),
        [press, vel, *got_x, *got_y],
        [VMEM] * (2 + n_x + n_y),
        [f32(nx + 1, ny, nz), f32(2, nx, ny, nz), f32(2, nx, ny, nz), f32(nx, ny, nz)],
        "slopes",
    )
    shapes_z = [f32(3, 2 * groups, height, LANES), f32(groups, height, LANES), f32(6, ROWS, LANES)]
    scratch_z = [scratch(6, groups, height, LANES), scratch(groups, height, LANES)]
    outer = call(
        functools.partial(outer_ends, nx, ny),
        [ends, shares],
        [VMEM] * 2,
        shapes_z,
        "outer_ends",
        scratch_z,
    )
    basis_z, vz_z, _, sums = call(
        functools.partial(join, nx, ny, n_z),
        [slope[-1], ends, *got_z, *outer],
        [ANY] + [VMEM] * (4 + n_z),
        shapes_z + [f32(1, LANES)],
        "join",
        scratch_z,
        aliases={2 + n_z + which: which for which in range(3)},
    )
    spread = jnp.broadcast_to(sums[None], (devices, 1, LANES))
    gathered = lax.all_to_all(spread, AXES, 0, 0).reshape(devices, LANES)
    return call(
        functools.partial(finish, nx, ny, n_z),
        [gathered, vel, basis, basis_z, vz_z, *slope, *got_z],
        [VMEM] * (9 + n_z),
        [f32(*vel.shape), f32(nx, ny, nz)],
        "finish",
        [scratch(*vel.shape), scratch(nx, ny, nz), pltpu.SemaphoreType.DMA((2, nx // STRIDE))],
        HBM,
    )


def solution(mesh):
    cells, faces = P(*AXES), P(None, *AXES)
    return jax.shard_map(
        on_device, mesh=mesh, in_specs=(cells, cells, faces), out_specs=(faces, cells), check_vma=False
    )
```
